32 devices in a mesh: loop: 2 (over x), dp: 16 (over z, y, core).
Axes of the slice: x: 2, y: 2, z: 4, core: 2. Of those that a mesh axis runs over, the one named last changes fastest.
Arguments:
- layer_input_stream: bfloat16 [2, 2048, 2048], P('loop', 'dp'), may hold values from -6 to 6
- layer_output_gradient: bfloat16 [2, 2048, 2048], P('loop', 'dp'), may hold values from -6 to 6
- attention_in_weight: bfloat16 [2048, 2560], P('dp'), may hold values from -0.125 to 0.125
- attention_out_weight: bfloat16 [2048, 2048], P('dp'), may hold values from -1.5 to 1.5
- feedforward_weight: bfloat16 [16384, 3, 2048], P('dp'), may hold values from -0.125 to 0.125
- layer_norm_gains: float32 [2, 2048], replicated, may hold values from 0.5 to 1.5
- adapter_first_factors: bfloat16 [2, 2048, 1536], P('loop'), may hold values from -0.125 to 0.125
- adapter_second_factors: bfloat16 [2, 256, 6656], P('loop'), may hold values from -0.15625 to 0.15625
- adapter_hidden_factors: bfloat16 [2, 16384, 768], P('loop'), may hold values from -0.09375 to 0.09375
- group_sequence_lengths: int32 [2, 8], P('loop'), may hold values from 1 to 1529, as said below
- token_per_row: int32 [2, 2048], P('loop'), may hold values from -1 to 1535, as said below
- token_exit_depth: int32 [2, 2048], P('loop', 'dp'), may hold values from 0 to 2
Outputs:
- hidden_out: bfloat16 [2, 2048, 2048], P('loop', 'dp')
- hidden_grad: float32 [2, 2048, 2048], P('loop', 'dp')
- attn_in_grad: float32 [2048, 2560], P('dp')
- attn_out_grad: float32 [2048, 2048], P('dp')
- mlp_grad: float32 [16384, 3, 2048], P('dp')
- gains_grad: float32 [2, 2048], P(None, 'dp')
- lora_in_grad: float32 [2, 2048, 1536], P('loop', 'dp')
- lora_out_grad: float32 [2, 256, 6656], P('loop', None, 'dp')
- lora_ff_grad: float32 [2, 16384, 768], P('loop', 'dp')
- exit_counts: int32 [3], replicated
- mean_confidence: float32 [], replicated
The draws below stay inside these ranges and needn't reach their ends.
Inputs may be any that keep to these rules, and one draw needn't show every extreme that they name: `group_sequence_lengths`: in each loop group the 8 lengths add up to 1536 and the longest is exactly 1529. `token_per_row`: in each loop group every token index from 0 to 1535 stands in exactly one row, sequences following one another in the order of group_sequence_lengths; -1 marks an unused row. A device's used rows are its first rows, and some device uses all 128.
All inputs are finite; a program needn't handle non-finite values.
Results may differ from the reference program's by a relative error of at most 0.019.
Values may be sent and summed in bfloat16 or wider, within the bound.
A program may use at most 512 MiB of HBM per device.

```python
import jax
import jax.numpy as jnp
from jax import lax

MODEL_WIDTH = 2048
HEADS = 8
HEAD_SIZE = 256
HIDDEN_UNITS = 16384
ADAPTER_RANK = 256
TOK_DEV = 128
SEQS = 8
LOOP_TOTAL = 2
TOKENS = 2048
LIVE = 1536
SEQ_MAX = 1529
QUERY_WIDTH = 2048
PROJECTED_WIDTH = 2560
ADAPTER_OUTPUTS = 6656


def group_layout(key):
    device_count = TOKENS // TOK_DEV
    subkeys = jax.random.split(key, 5)
    others = SEQS - 1
    remainder = LIVE - SEQ_MAX
    even_share = remainder // others
    leftover = remainder - even_share * others
    other_ids = jnp.arange(others, dtype=jnp.int32)
    other_lengths = even_share + (other_ids < leftover).astype(jnp.int32)
    pair_count = others // 2
    shifts = jax.random.randint(subkeys[0], (pair_count,), -(even_share // 2), even_share // 2 + 1, dtype=jnp.int32)
    moved_tokens = jnp.zeros((others,), jnp.int32).at[0:2 * pair_count:2].add(shifts).at[1:2 * pair_count:2].add(-shifts)
    other_lengths = other_lengths + moved_tokens
    long_slot = jax.random.randint(subkeys[1], (), 0, SEQS, dtype=jnp.int32)
    seq_slots = jnp.arange(SEQS, dtype=jnp.int32)
    source_slot = jnp.clip(seq_slots - (seq_slots > long_slot).astype(jnp.int32), 0, others - 1)
    sequence_length = jnp.where(seq_slots == long_slot, SEQ_MAX, other_lengths[source_slot])
    long_start = jnp.sum(jnp.where(seq_slots < long_slot, sequence_length, 0))
    capacity = TOK_DEV // 2
    full_device = jax.random.randint(subkeys[2], (), 0, device_count, dtype=jnp.int32)
    chosen_slots = jax.random.permutation(subkeys[3], (device_count - 1) * capacity)[:TOKENS - LIVE]
    slot_device = chosen_slots // capacity
    slot_device = slot_device + (slot_device >= full_device).astype(jnp.int32)
    dropped = jnp.sum((slot_device[:, None] == jnp.arange(device_count, dtype=jnp.int32)[None, :]).astype(jnp.int32), axis=0)
    live_count = TOK_DEV - dropped
    row_ids = jnp.arange(TOKENS, dtype=jnp.int32)
    local_row = row_ids % TOK_DEV
    live_row = local_row < live_count[row_ids // TOK_DEV]
    jitter_range = max(2 ** 23 // TOKENS, 1)
    jitter = jax.random.randint(subkeys[4], (TOKENS,), 0, jitter_range, dtype=jnp.int32)
    band_offset = jnp.where(local_row == 0, 0, jnp.where(live_row, 2 ** 24, 2 ** 30))
    row_score = jitter * TOKENS + row_ids + band_offset
    row_rank = jnp.argsort(jnp.argsort(row_score, stable=True), stable=True).astype(jnp.int32)
    later = row_rank - device_count
    token_index = jnp.where(row_rank < device_count, long_start + row_rank, jnp.where(later < long_start, later, row_rank))
    token_index = jnp.where(live_row, token_index, -1)
    return (sequence_length.astype(jnp.int32), token_index.astype(jnp.int32))


def layout_tables(key):
    length_list = []
    token_list = []
    for group_index in range(LOOP_TOTAL):
        sequence_length, token_index = group_layout(jax.random.fold_in(key, 100 + group_index))
        length_list.append(sequence_length)
        token_list.append(token_index)
    return (jnp.stack(length_list), jnp.stack(token_list))


def draw_group_sequence_lengths(key, part):
    return layout_tables(key)[0]


def draw_token_per_row(key, part):
    return layout_tables(key)[1]


def touch_ends(entries, rng, smallest, high):
    longest = entries.shape.index(max(entries.shape))
    spots = []
    for shift in (0, 1):
        where = [jax.random.randint(jax.random.fold_in(rng, axis), (), 0, length) for axis, length in enumerate(entries.shape)]
        where[longest] = (where[longest] + shift) % entries.shape[longest]
        spots.append(tuple(where))
    return entries.at[spots[0]].set(smallest).at[spots[1]].set(high)


def block_levels(own_key, shape, cuts, low, largest):
    factor_of = 1.0
    for axis_at, shards_of in cuts:
        steps = jax.random.uniform(jax.random.fold_in(jax.random.fold_in(own_key, 6), axis_at), (shards_of,), jnp.float32, low / len(cuts), largest / len(cuts))
        factor_of = factor_of * jnp.repeat(jnp.exp(steps), shape[axis_at] // shards_of).reshape((-1,) + (1,) * (len(shape) - 1 - axis_at))
    return factor_of


def noise(rng, extent, scale, reach, cuts=(), kind=jnp.bfloat16):
    drawn = scale * jax.random.normal(rng, extent, jnp.float32)
    if cuts:
        drawn = drawn * block_levels(rng, extent, cuts, -0.22, 0.18)
    return jnp.clip(drawn, -reach, reach).astype(kind)


def setup_inputs(seed: int = 0) -> dict:
    arg_keys = jax.random.split(jax.random.key(seed), 13)
    layer_input_stream = noise(arg_keys[0], (LOOP_TOTAL, TOKENS, MODEL_WIDTH), 1.0, 6.0, ((0, 2), (1, 16)))
    layer_output_gradient = noise(arg_keys[1], (LOOP_TOTAL, TOKENS, MODEL_WIDTH), 1.0, 6.0, ((0, 2), (1, 16)))
    attention_in_weight = noise(arg_keys[2], (MODEL_WIDTH, PROJECTED_WIDTH), MODEL_WIDTH ** -0.5, 0.125, ((0, 16),))
    attention_out_weight = noise(arg_keys[3], (QUERY_WIDTH, MODEL_WIDTH), (max(QUERY_WIDTH // 128, 1)) ** -0.5, 1.5, ((0, 16),))
    feedforward_weight = noise(arg_keys[4], (HIDDEN_UNITS, 3, MODEL_WIDTH), MODEL_WIDTH ** -0.5, 0.125, ((0, 16),))
    layer_norm_gains = jnp.clip(1.0 + 0.1 * jax.random.normal(arg_keys[5], (2, MODEL_WIDTH), jnp.float32), 0.5, 1.5)
    adapter_first_factors = noise(arg_keys[6], (LOOP_TOTAL, MODEL_WIDTH, 6 * ADAPTER_RANK), MODEL_WIDTH ** -0.5, 0.125, ((0, 2),))
    adapter_second_factors = noise(arg_keys[7], (LOOP_TOTAL, ADAPTER_RANK, ADAPTER_OUTPUTS), (6 * ADAPTER_RANK) ** -0.5, 0.15625, ((0, 2),))
    adapter_hidden_factors = noise(arg_keys[8], (LOOP_TOTAL, HIDDEN_UNITS, 3 * ADAPTER_RANK), (HIDDEN_UNITS // 4) ** -0.5, 0.09375, ((0, 2),))
    group_sequence_lengths = draw_group_sequence_lengths(jax.random.fold_in(arg_keys[12], 71), 0)
    token_per_row = draw_token_per_row(jax.random.fold_in(arg_keys[12], 71), 0)
    token_exit_depth = touch_ends(jax.random.randint(arg_keys[11], (LOOP_TOTAL, TOKENS), 0, LOOP_TOTAL + 1), jax.random.fold_in(arg_keys[11], 1), 0, LOOP_TOTAL).astype(jnp.int32)
    return {"layer_input_stream": layer_input_stream, "layer_output_gradient": layer_output_gradient, "attention_in_weight": attention_in_weight, "attention_out_weight": attention_out_weight, "feedforward_weight": feedforward_weight, "layer_norm_gains": layer_norm_gains, "adapter_first_factors": adapter_first_factors, "adapter_second_factors": adapter_second_factors, "adapter_hidden_factors": adapter_hidden_factors, "group_sequence_lengths": group_sequence_lengths, "token_per_row": token_per_row, "token_exit_depth": token_exit_depth}


@jax.custom_vjp
def lowrank_values(v):
    return lax.optimization_barrier(v.astype(jnp.bfloat16)).astype(jnp.float32)

@jax.custom_vjp
def lowrank_backward(v):
    return v

def low_keep(v):
    return (lowrank_values(v), None)

def low_pass(kept, grad):
    return (grad,)

def back_keep(v):
    return (v, None)

def back_low(kept, grad):
    return (lowrank_values(grad),)
lowrank_values.defvjp(low_keep, low_pass)
lowrank_backward.defvjp(back_keep, back_low)
EPSILON = 1e-06
HIGHEST = lax.Precision.HIGHEST
FLOOR_SCORE = -1e+30

def matrix_product(left, right):
    return jnp.dot(left, right, preferred_element_type=jnp.float32, precision=HIGHEST)

def norm_rows(values, gain):
    return values * lax.rsqrt(lax.optimization_barrier(jnp.mean(values * values, axis=-1, keepdims=True)) + EPSILON) * gain

def rotate(values, positions):
    half_dim = values.shape[-1] // 2
    freqs = 10000.0 ** (-jnp.arange(half_dim, dtype=jnp.float32) / half_dim)
    angles = positions.astype(jnp.float32)[:, None, None] * freqs
    cosine = jnp.cos(angles)
    sine = jnp.sin(angles)
    first_half = values[..., :half_dim]
    second_half = values[..., half_dim:]
    return jnp.concatenate([first_half * cosine - second_half * sine, first_half * sine + second_half * cosine], axis=-1)

def token_facts(row_of_tokens, sequence_length):
    row_total = row_of_tokens.shape[0]
    live_row = row_of_tokens >= 0
    seq_ends = jnp.cumsum(sequence_length).astype(jnp.int32)
    seq_index = lax.optimization_barrier(jnp.sum((row_of_tokens[:, None] >= seq_ends[None, :]).astype(jnp.int32), axis=1))
    seq_starts = seq_ends - sequence_length
    own_start = lax.optimization_barrier(jnp.sum(jnp.where(seq_index[:, None] == jnp.arange(sequence_length.shape[0], dtype=jnp.int32)[None, :], seq_starts[None, :], 0), axis=1))
    row_ids = jnp.arange(row_total, dtype=jnp.int32)
    sequence = jnp.where(live_row, seq_index, -1 - row_ids)
    ordering = jnp.where(live_row, row_of_tokens, 0)
    positions = jnp.where(live_row, row_of_tokens - own_start, 0)
    return (live_row, sequence, ordering, positions)

def attend_group(queries, keys, values, sequence, ordering):
    block_rows = min(TOKENS, 512)
    block_count = TOKENS // block_rows
    scale = HEAD_SIZE ** (-0.5)

    def one_block(pieces):
        query_block, seq_block, order_block = pieces
        scores = jnp.einsum('qhd,kd->qhk', query_block, keys, precision=HIGHEST) * scale
        scores = lowrank_backward(scores)
        allowed = (seq_block[:, None] == sequence[None, :]) & (ordering[None, :] <= order_block[:, None])
        scores = jnp.where(allowed[:, None, :], scores, FLOOR_SCORE)
        top_score = lax.optimization_barrier(jnp.max(scores, axis=-1, keepdims=True))
        expo = jnp.exp(scores - top_score)
        prob_low = lowrank_values(expo / lax.optimization_barrier(jnp.sum(expo, axis=-1, keepdims=True)))
        return jnp.einsum('qhk,kd->qhd', prob_low, values, precision=HIGHEST)
    result = lax.map(jax.checkpoint(one_block), (queries.reshape(block_count, block_rows, HEADS, HEAD_SIZE), sequence.reshape(block_count, block_rows), ordering.reshape(block_count, block_rows)))
    return result.reshape(TOKENS, QUERY_WIDTH)

def single_loop(current_loop, residual_stream, input_weight, output_weight, feedforward_matrix, norm_gain_pair, adapter_first, adapter_second, adapter_feedforward, row_of_tokens, sequence_length, row_depth):
    live_row, sequence, ordering, positions = token_facts(row_of_tokens, sequence_length)
    active_mask = (live_row & (row_depth > current_loop)).astype(jnp.float32)[:, None]
    normed_input = lowrank_values(norm_rows(residual_stream, norm_gain_pair[0]))
    lowrank_projection = lowrank_values(lowrank_backward(matrix_product(normed_input, adapter_first[:, :3 * ADAPTER_RANK])))
    query_linear = lowrank_backward(matrix_product(normed_input, input_weight[:, :QUERY_WIDTH]) + matrix_product(lowrank_projection[:, :ADAPTER_RANK], adapter_second[:, :QUERY_WIDTH]))
    key_linear = lowrank_backward(matrix_product(normed_input, input_weight[:, QUERY_WIDTH:QUERY_WIDTH + HEAD_SIZE]) + matrix_product(lowrank_projection[:, ADAPTER_RANK:2 * ADAPTER_RANK], adapter_second[:, QUERY_WIDTH:QUERY_WIDTH + HEAD_SIZE]))
    value_linear = lowrank_backward(matrix_product(normed_input, input_weight[:, QUERY_WIDTH + HEAD_SIZE:PROJECTED_WIDTH]) + matrix_product(lowrank_projection[:, 2 * ADAPTER_RANK:3 * ADAPTER_RANK], adapter_second[:, QUERY_WIDTH + HEAD_SIZE:PROJECTED_WIDTH]))
    queries = lowrank_values(rotate(query_linear.reshape(TOKENS, HEADS, HEAD_SIZE), positions))
    keys = lowrank_values(rotate(key_linear.reshape(TOKENS, 1, HEAD_SIZE), positions)[:, 0])
    values = lowrank_values(value_linear)
    attended_rows = lowrank_values(lowrank_backward(attend_group(queries, keys, values, sequence, ordering)))
    output_projection = lowrank_values(lowrank_backward(matrix_product(attended_rows, adapter_first[:, 3 * ADAPTER_RANK:4 * ADAPTER_RANK])))
    branch_output = lowrank_backward(matrix_product(attended_rows, output_weight) + matrix_product(output_projection, adapter_second[:, PROJECTED_WIDTH:PROJECTED_WIDTH + MODEL_WIDTH]))
    middle_state = residual_stream + active_mask * branch_output
    second_normed_input = lowrank_values(norm_rows(middle_state, norm_gain_pair[1]))
    feedforward_projection = lowrank_values(lowrank_backward(matrix_product(second_normed_input, adapter_first[:, 4 * ADAPTER_RANK:6 * ADAPTER_RANK])))
    gate_values = lowrank_backward(matrix_product(second_normed_input, feedforward_matrix[:, 0, :].T) + matrix_product(feedforward_projection[:, :ADAPTER_RANK], adapter_feedforward[:, ADAPTER_RANK:2 * ADAPTER_RANK].T))
    up_projection_value = lowrank_backward(matrix_product(second_normed_input, feedforward_matrix[:, 1, :].T) + matrix_product(feedforward_projection[:, ADAPTER_RANK:], adapter_feedforward[:, 2 * ADAPTER_RANK:].T))
    hidden_activations = lowrank_values(jax.nn.gelu(gate_values, approximate=True) * up_projection_value)
    down_lowrank = lowrank_values(lowrank_backward(matrix_product(hidden_activations, adapter_feedforward[:, :ADAPTER_RANK])))
    feedforward_output = lowrank_backward(matrix_product(hidden_activations, feedforward_matrix[:, 2, :]) + matrix_product(down_lowrank, adapter_second[:, PROJECTED_WIDTH + MODEL_WIDTH:]))
    return middle_state + active_mask * feedforward_output

def reference(layer_input_stream, layer_output_gradient, attention_in_weight, attention_out_weight, feedforward_weight, layer_norm_gains, adapter_first_factors, adapter_second_factors, adapter_hidden_factors, group_sequence_lengths, token_per_row, token_exit_depth):

    def forward_function(hidden_state, input_weight, output_weight, feedforward_matrix, norm_gain_pair, adapter_first, adapter_second, adapter_feedforward):
        result_list = []
        for current_loop in range(LOOP_TOTAL):
            result_list.append(single_loop(current_loop, hidden_state[current_loop], input_weight, output_weight, feedforward_matrix, norm_gain_pair, adapter_first[current_loop], adapter_second[current_loop], adapter_feedforward[current_loop], token_per_row[current_loop], group_sequence_lengths[current_loop], token_exit_depth[current_loop]))
        return jnp.stack(result_list)
    base_value = layer_input_stream.astype(jnp.float32)
    layer_output, pullback_function = jax.vjp(forward_function, base_value, attention_in_weight.astype(jnp.float32), attention_out_weight.astype(jnp.float32), feedforward_weight.astype(jnp.float32), layer_norm_gains.astype(jnp.float32), adapter_first_factors.astype(jnp.float32), adapter_second_factors.astype(jnp.float32), adapter_hidden_factors.astype(jnp.float32))
    grads = pullback_function(layer_output_gradient.astype(jnp.float32))

    def root_mean(values):
        return jnp.sqrt(lax.optimization_barrier(jnp.mean(values * values, axis=-1)) + EPSILON)
    confidence = root_mean(base_value) / (root_mean(base_value) + root_mean(layer_output - base_value))
    live_all = token_per_row >= 0
    mean_confidence = jnp.sum(jnp.where(live_all, confidence, 0.0)) / jnp.sum(live_all.astype(jnp.float32))
    depth_hits = (token_exit_depth[:, :, None] == jnp.arange(LOOP_TOTAL + 1, dtype=jnp.int32)[None, None, :]) & live_all[:, :, None]
    exit_counts = lax.optimization_barrier(jnp.sum(depth_hits.astype(jnp.int32), axis=(0, 1)))
    return (layer_output.astype(jnp.bfloat16), grads[0], grads[1], grads[2], grads[3], grads[4], grads[5], grads[6], grads[7], exit_counts, mean_confidence)
```

```python
import functools

import jax
import jax.numpy as jnp
from jax import lax
from jax.experimental import pallas as pl
from jax.experimental.pallas import tpu as pltpu
from jax.sharding import PartitionSpec as P

MODEL_WIDTH = 2048
HEADS = 8
HEAD_SIZE = 256
ADAPTER_RANK = 256
QUERY_WIDTH = 2048
PROJECTED_WIDTH = 2560


EPSILON = 1e-06
FLOOR_SCORE = -1e30
MESH = pl.DeviceIdType.MESH
VMEM_LIMIT = 60 * 1024 * 1024
LINE_DEVICES = 16


def matrix_product(left, right):
    return jnp.dot(left, right, preferred_element_type=jnp.float32)


def inner_rows(left, right):
    return lax.dot_general(
        left, right, (((0,), (0,)), ((), ())), preferred_element_type=jnp.float32
    )


def outer_columns(left, right):
    return lax.dot_general(
        left, right, (((1,), (1,)), ((), ())), preferred_element_type=jnp.float32
    )


def norm_rows(values, gain):
    return values * lax.rsqrt(jnp.mean(values * values, axis=-1, keepdims=True) + EPSILON) * gain


def rotate(values, positions):
    half_dim = values.shape[-1] // 2
    freqs = 10000.0 ** (-jnp.arange(half_dim, dtype=jnp.float32) / half_dim)
    angles = positions.astype(jnp.float32)[:, None, None] * freqs
    cosine = jnp.cos(angles)
    sine = jnp.sin(angles)
    first_half = values[..., :half_dim]
    second_half = values[..., half_dim:]
    return jnp.concatenate(
        [first_half * cosine - second_half * sine, first_half * sine + second_half * cosine],
        axis=-1,
    )


def rotate_back(grads, positions):

    def turned(values):
        return rotate(values, positions)

    return jax.vjp(turned, jnp.zeros_like(grads))[1](grads)[0]


def geglu(gate_values, up_projection_value):
    return jax.nn.gelu(gate_values, approximate=True) * up_projection_value


def root_mean(values):
    return jnp.sqrt(jnp.mean(values * values, axis=-1) + EPSILON)


def token_facts(row_of_tokens, sequence_length):
    row_total = row_of_tokens.shape[0]
    live_row = row_of_tokens >= 0
    seq_ends = jnp.cumsum(sequence_length)
    seq_index = jnp.sum((row_of_tokens[:, None] >= seq_ends[None, :]).astype(jnp.int32), axis=1)
    seq_starts = seq_ends - sequence_length
    own_start = jnp.sum(
        jnp.where(
            seq_index[:, None] == jnp.arange(sequence_length.shape[0], dtype=jnp.int32)[None, :],
            seq_starts[None, :],
            0,
        ),
        axis=1,
    )
    row_ids = jnp.arange(row_total, dtype=jnp.int32)
    sequence = jnp.where(live_row, seq_index, -1 - row_ids)
    ordering = jnp.where(live_row, row_of_tokens, 0)
    positions = jnp.where(live_row, row_of_tokens - own_start, 0)
    return (live_row, sequence, ordering, positions)


def place(count):
    me = lax.axis_index("dp")
    return me, count // 4, me // 4, (me // 2) % 2, me % 2


def greet(count):
    me, depth, z, y, c = place(count)
    barrier = pltpu.get_barrier_semaphore()

    def signal(where):
        pl.semaphore_signal(barrier, inc=1, device_id={"dp": where}, device_id_type=MESH)

    signal(me + 1 - 2 * c)
    signal(me + 2 - 4 * y)

    @pl.when(z > 0)
    def _():
        signal(me - 4)

    @pl.when(z < depth - 1)
    def _():
        signal(me + 4)

    ends = jnp.where((z > 0) & (z < depth - 1), 4, 3)
    pl.semaphore_wait(barrier, ends)


def gather_body(count, parts, arrays, *refs):
    own = refs[:arrays]
    full = refs[arrays : 2 * arrays]
    keep, recv, send_core, send_pair, send_right, send_left = refs[2 * arrays :]
    me, depth, z, y, c = place(count)
    greet(count)

    def spans(a):
        rows = own[a].shape[0]
        step = rows // parts
        return [(s, pl.ds(s * step, step)) for s in range(parts)]

    def copy(a, block, span, target, sem, first=False):
        s, rows = span
        source = own[a].at[rows] if first else full[a].at[block, rows]
        return pltpu.make_async_remote_copy(
            src_ref=source,
            dst_ref=full[a].at[block, rows],
            send_sem=sem,
            recv_sem=recv.at[a, block, s],
            device_id={"dp": target},
            device_id_type=MESH,
        )

    def to_core(a, block, span, first=False):
        return copy(a, block, span, me + 1 - 2 * c, send_core.at[a, block // 2, span[0]], first)

    def to_pair(a, block, span, first=False):
        return copy(a, block, span, me + 2 - 4 * y, send_pair.at[a, block // 4, span[0]], first)

    def to_right(a, block, span, first=False):
        return copy(a, block, span, me + 4, send_right.at[a, block // 4, span[0]], first)

    def to_left(a, block, span, first=False):
        return copy(a, block, span, me - 4, send_left.at[a, block // 4, span[0]], first)

    local = [
        pltpu.make_async_copy(own[a], full[a].at[me], keep.at[a]) for a in range(arrays)
    ]
    units = [(a, span) for a in range(arrays) for span in spans(a)]
    for a, span in units:

        @pl.when(z < depth - 1)
        def _(a=a, span=span):
            to_right(a, me, span, True).start()

        @pl.when(z > 0)
        def _(a=a, span=span):
            to_left(a, me, span, True).start()

        to_pair(a, me, span, True).start()
        to_core(a, me, span, True).start()
    for item in local:
        item.start()
    mate = me + 2 - 4 * y
    for k in range(1, depth):
        for a, span in units:

            @pl.when(z - k >= 0)
            def _(a=a, span=span):
                block = me - 4 * k
                to_right(a, block, span).wait_recv()

                @pl.when(z < depth - 1)
                def _():
                    to_right(a, block, span).start()

                to_pair(a, block, span).start()
                to_core(a, block, span).start()

            @pl.when(z + k < depth)
            def _(a=a, span=span):
                block = me + 4 * k
                to_left(a, block, span).wait_recv()

                @pl.when(z > 0)
                def _():
                    to_left(a, block, span).start()

                to_pair(a, block, span).start()
                to_core(a, block, span).start()

    def from_pair(a, block, span):
        to_pair(a, block, span).wait_recv()
        to_core(a, block, span).start()

    for a, span in units:
        from_pair(a, mate, span)
    for k in range(1, depth):
        for a, span in units:

            @pl.when(z - k >= 0)
            def _(a=a, span=span):
                from_pair(a, mate - 4 * k, span)

            @pl.when(z + k < depth)
            def _(a=a, span=span):
                from_pair(a, mate + 4 * k, span)

    for a, span in units:
        for j in range(count // 2):
            to_core(a, 2 * j + 1 - c, span).wait_recv()
    for item in local:
        item.wait()
    for a, span in units:
        for j in range(count // 2):
            to_core(a, 2 * j + c, span).wait_send()
        for j in range(depth):
            block = 4 * j + 2 * y + c
            to_pair(a, block, span).wait_send()

            @pl.when((z >= j) & (z < depth - 1))
            def _():
                to_right(a, block, span).wait_send()

            @pl.when((z <= j) & (z > 0))
            def _():
                to_left(a, block, span).wait_send()


def gather_rows(count, ident, *arrays, parts=2):
    if count != LINE_DEVICES:
        return [lax.all_gather(item, "dp", axis=0, tiled=True) for item in arrays]
    number = len(arrays)
    depth = count // 4
    sem = pltpu.SemaphoreType.DMA
    full = pl.pallas_call(
        functools.partial(gather_body, count, parts, number),
        out_shape=[
            jax.ShapeDtypeStruct((count,) + item.shape, item.dtype) for item in arrays
        ],
        in_specs=[pl.BlockSpec(memory_space=pl.ANY)] * number,
        out_specs=[pl.BlockSpec(memory_space=pl.ANY)] * number,
        scratch_shapes=[
            sem((number,)),
            sem((number, count, parts)),
            sem((number, count // 2, parts)),
            sem((number, depth, parts)),
            sem((number, depth, parts)),
            sem((number, depth, parts)),
        ],
        compiler_params=pltpu.CompilerParams(
            collective_id=ident, has_side_effects=True, vmem_limit_bytes=VMEM_LIMIT
        ),
        name="gather_rows",
    )(*arrays)
    return [
        item.reshape((count * item.shape[1],) + item.shape[2:]) for item in full
    ]


def scatter_body(count, parts, arrays, *refs):
    terms = refs[:arrays]
    total = refs[arrays : 2 * arrays]
    scratch = refs[2 * arrays :]
    held, loaded, core_in, pair_in, line_in = [
        scratch[i * arrays : (i + 1) * arrays] for i in range(5)
    ]
    (load_sem, core_send, core_recv, pair_send, pair_recv, line_send, line_recv) = scratch[
        5 * arrays :
    ]
    me, depth, z, y, c = place(count)
    greet(count)
    near = z < depth // 2

    def turn(k):
        even = depth - 1 - k // 2 if k % 2 == 0 else k // 2
        return jnp.where(near, even, depth - 1 - even)

    def rows_of(a, s):
        step = terms[a].shape[1] // parts[a]
        return pl.ds(s * step, step)

    def to_core(a, s, line, pair):
        slot = 2 * line + pair
        return pltpu.make_async_remote_copy(
            src_ref=terms[a].at[2 * slot + 1 - c, rows_of(a, s)],
            dst_ref=core_in[a].at[slot, rows_of(a, s)],
            send_sem=core_send.at[a, slot, s],
            recv_sem=core_recv.at[a, slot, s],
            device_id={"dp": me + 1 - 2 * c},
            device_id_type=MESH,
        )

    def load(a, s, line, pair):
        slot = 2 * line + pair
        return pltpu.make_async_copy(
            terms[a].at[2 * slot + c, rows_of(a, s)],
            loaded[a].at[slot, rows_of(a, s)],
            load_sem.at[a, slot, s],
        )

    def to_pair(a, s, line):
        return pltpu.make_async_remote_copy(
            src_ref=loaded[a].at[2 * line + 1 - y, rows_of(a, s)],
            dst_ref=pair_in[a].at[line, rows_of(a, s)],
            send_sem=pair_send.at[a, line, s],
            recv_sem=pair_recv.at[a, line, s],
            device_id={"dp": me + 2 - 4 * y},
            device_id_type=MESH,
        )

    def along(a, s, line, slot, target):
        return pltpu.make_async_remote_copy(
            src_ref=loaded[a].at[2 * line + y, rows_of(a, s)],
            dst_ref=line_in[a].at[slot, rows_of(a, s)],
            send_sem=line_send.at[a, line, s],
            recv_sem=line_recv.at[a, slot, s],
            device_id={"dp": target},
            device_id_type=MESH,
        )

    def to_right(a, s, line):
        return along(a, s, line, line, me + 4)

    def to_left(a, s, line):
        return along(a, s, line, jnp.where(line == z - 1, depth, line), me - 4)

    def from_right(a, s, line):
        return along(a, s, line, jnp.where(line == z, depth, line), me)

    order = [turn(k) for k in range(depth)]
    units = [(a, s) for a in range(arrays) for s in range(parts[a])]
    for pair in (1 - y, y):
        for line in order:
            for a, s in units:
                to_core(a, s, line, pair).start()
                load(a, s, line, pair).start()

    for line in order:
        for a, s in units:
            slot = 2 * line + 1 - y
            rows = rows_of(a, s)
            load(a, s, line, 1 - y).wait()
            to_core(a, s, line, 1 - y).wait_recv()
            loaded[a][slot, rows] = loaded[a][slot, rows] + core_in[a][slot, rows]
            to_pair(a, s, line).start()

    def own_sum(a, s, line):
        slot = 2 * line + y
        rows = rows_of(a, s)
        load(a, s, line, y).wait()
        to_core(a, s, line, y).wait_recv()
        to_pair(a, s, line).wait_recv()
        part = loaded[a][slot, rows].astype(jnp.float32)
        part += core_in[a][slot, rows].astype(jnp.float32)
        held[a][...] = part + pair_in[a][line, rows].astype(jnp.float32)

    def add_line(a, s, slot):
        along(a, s, z, slot, me).wait_recv()
        held[a][...] += line_in[a][slot, rows_of(a, s)].astype(jnp.float32)

    for line in order:
        for a, s in units:

            @pl.when(line != z)
            def _(a=a, s=s, line=line):
                own_sum(a, s, line)

                @pl.when(((line > z) & (z > 0)) | ((line < z) & (z < depth - 1)))
                def _():
                    add_line(a, s, line)

                loaded[a][2 * line + y, rows_of(a, s)] = held[a][...].astype(loaded[a].dtype)

                @pl.when(line > z)
                def _():
                    to_right(a, s, line).start()

                @pl.when(line < z)
                def _():
                    to_left(a, s, line).start()

    for a, s in units:
        own_sum(a, s, z)

        @pl.when(z > 0)
        def _(a=a, s=s):
            add_line(a, s, z)

        @pl.when(z < depth - 1)
        def _(a=a, s=s):
            add_line(a, s, depth)

        total[a][rows_of(a, s)] = held[a][...]

    for a, s in units:
        for line in range(depth):
            for pair in range(2):
                to_core(a, s, line, pair).wait_send()
            to_pair(a, s, line).wait_send()

            @pl.when(z != line)
            def _():
                to_right(a, s, line).wait_send()


def scatter_rows(count, ident, *arrays):
    if count != LINE_DEVICES:
        return [
            lax.psum_scatter(
                item.astype(jnp.float32), "dp", scatter_dimension=0, tiled=True
            )
            for item in arrays
        ]
    depth = count // 4
    number = len(arrays)
    blocks = [
        item.reshape(count, item.shape[0] // count, item.shape[1]) for item in arrays
    ]
    parts = [2 if item.shape[1] % 32 == 0 and item.shape[1] > 32 else 1 for item in blocks]
    most = max(parts)

    def room(slots):
        return [pltpu.VMEM((slots,) + item.shape[1:], item.dtype) for item in blocks]

    def sems(slots):
        return pltpu.SemaphoreType.DMA((number, slots, most))

    return pl.pallas_call(
        functools.partial(scatter_body, count, parts, number),
        out_shape=[jax.ShapeDtypeStruct(item.shape[1:], jnp.float32) for item in blocks],
        in_specs=[pl.BlockSpec(memory_space=pl.ANY)] * number,
        out_specs=[pl.BlockSpec(memory_space=pltpu.VMEM)] * number,
        scratch_shapes=[
            pltpu.VMEM((item.shape[1] // part, item.shape[2]), jnp.float32)
            for item, part in zip(blocks, parts)
        ]
        + room(2 * depth)
        + room(2 * depth)
        + room(depth)
        + room(depth + 1)
        + [
            sems(2 * depth),
            sems(2 * depth),
            sems(2 * depth),
            sems(depth),
            sems(depth),
            sems(depth),
            sems(depth + 1),
        ],
        compiler_params=pltpu.CompilerParams(
            collective_id=ident, has_side_effects=True, vmem_limit_bytes=VMEM_LIMIT
        ),
        name="scatter_rows",
    )(*blocks)


def swap_loops(values):
    if lax.axis_size("loop") == 1:
        return values
    return lax.ppermute(values, "loop", [(0, 1), (1, 0)])


def both_loops(values):
    if lax.axis_size("loop") != 2:
        return lax.psum(values.astype(jnp.float32), "loop")
    return values.astype(jnp.float32) + swap_loops(values).astype(jnp.float32)


def per_device(
    layer_input_stream,
    layer_output_gradient,
    attention_in_weight,
    attention_out_weight,
    feedforward_weight,
    layer_norm_gains,
    adapter_first_factors,
    adapter_second_factors,
    adapter_hidden_factors,
    group_sequence_lengths,
    token_per_row,
    token_exit_depth,
):
    current_loop = lax.axis_index("loop")
    dp_index = lax.axis_index("dp")
    loop_count = lax.axis_size("loop")
    count = lax.axis_size("dp")
    local_rows = layer_input_stream.shape[1]
    ffn_rows = feedforward_weight.shape[0]
    weight_rows = attention_in_weight.shape[0]
    low = jnp.bfloat16
    rank = ADAPTER_RANK
    scale = HEAD_SIZE ** (-0.5)
    key_at = QUERY_WIDTH
    value_at = QUERY_WIDTH + HEAD_SIZE
    down_at = PROJECTED_WIDTH + MODEL_WIDTH
    live_all, seq_all, order_all, pos_all = token_facts(token_per_row[0], group_sequence_lengths[0])
    first_row = dp_index * local_rows

    def own_slice(values):
        return lax.dynamic_slice_in_dim(values, first_row, local_rows, 0)

    live_own = own_slice(live_all)
    seq_own = own_slice(seq_all)
    order_own = own_slice(order_all)
    pos_own = own_slice(pos_all)
    active_mask = (live_own & (token_exit_depth[0] > current_loop)).astype(jnp.float32)[:, None]
    residual_stream = layer_input_stream[0].astype(jnp.float32)
    grad_out = layer_output_gradient[0].astype(jnp.float32)
    adapter_first = adapter_first_factors[0]
    adapter_second = adapter_second_factors[0]
    ffn_own = lax.dynamic_slice_in_dim(adapter_hidden_factors[0], dp_index * ffn_rows, ffn_rows, 0)
    first_own = lax.dynamic_slice_in_dim(adapter_first, dp_index * weight_rows, weight_rows, 0)
    second_query = adapter_second[:, :key_at]
    second_key = adapter_second[:, key_at:value_at]
    second_value = adapter_second[:, value_at:PROJECTED_WIDTH]
    second_output = adapter_second[:, PROJECTED_WIDTH:down_at]
    second_down = adapter_second[:, down_at:]

    in_own = (
        attention_in_weight.astype(jnp.float32)
        + jnp.concatenate(
            [
                matrix_product(first_own[:, :rank], second_query),
                matrix_product(first_own[:, rank : 2 * rank], second_key),
                matrix_product(first_own[:, 2 * rank : 3 * rank], second_value),
            ],
            axis=1,
        )
    ).astype(low)
    out_own = (
        attention_out_weight.astype(jnp.float32)
        + matrix_product(first_own[:, 3 * rank : 4 * rank], second_output)
    ).astype(low)
    down_factor = ffn_own[:, :rank]
    gate_factor = ffn_own[:, rank : 2 * rank]
    up_factor = ffn_own[:, 2 * rank :]
    first_gate = adapter_first[:, 4 * rank : 5 * rank]
    first_up = adapter_first[:, 5 * rank :]
    gate_weight = (
        feedforward_weight[:, 0, :].astype(jnp.float32) + outer_columns(gate_factor, first_gate)
    ).astype(low)
    up_weight = (
        feedforward_weight[:, 1, :].astype(jnp.float32) + outer_columns(up_factor, first_up)
    ).astype(low)
    down_weight = (
        feedforward_weight[:, 2, :].astype(jnp.float32) + matrix_product(down_factor, second_down)
    ).astype(low)

    feedforward_gradient = (active_mask * grad_out).astype(low)
    normed_input = norm_rows(residual_stream, layer_norm_gains[0]).astype(low)
    input_weight, output_weight, grad_ffn_all = gather_rows(
        count, 1, in_own, out_own, feedforward_gradient
    )
    query_key_value_linear = matrix_product(normed_input, input_weight)
    queries = rotate(
        query_key_value_linear[:, :QUERY_WIDTH].reshape(local_rows, HEADS, HEAD_SIZE), pos_own
    ).astype(low)
    key_rot = rotate(
        query_key_value_linear[:, key_at:value_at].reshape(local_rows, 1, HEAD_SIZE), pos_own
    )[:, 0]
    kv_send = jnp.concatenate([key_rot, query_key_value_linear[:, value_at:]], axis=1).astype(low)
    (kv_all,) = gather_rows(count, 2, kv_send)
    keys = kv_all[:, :HEAD_SIZE]
    values = kv_all[:, HEAD_SIZE:]
    key_total = kv_all.shape[0]
    allowed = ((seq_own[:, None] == seq_all[None, :]) & (order_all[None, :] <= order_own[:, None]))[
        :, None, :
    ]
    query_rows = queries.reshape(local_rows * HEADS, HEAD_SIZE)

    def score_rows():
        raw_scores = (outer_columns(query_rows, keys) * scale).reshape(local_rows, HEADS, key_total)
        return jnp.where(allowed, raw_scores, FLOOR_SCORE)

    scores = score_rows()
    top_score = jnp.max(scores, axis=-1, keepdims=True)
    expo = jnp.exp(scores - top_score)
    mass = jnp.sum(expo, axis=-1, keepdims=True)
    prob_low = (expo / mass).astype(low)
    attended_rows = (
        matrix_product(prob_low.reshape(local_rows * HEADS, key_total), values)
        .reshape(local_rows, QUERY_WIDTH)
        .astype(low)
    )
    branch_output = matrix_product(attended_rows, output_weight)
    middle_state = residual_stream + active_mask * branch_output
    second_normed_input = norm_rows(middle_state, layer_norm_gains[1]).astype(low)
    (normed_all,) = gather_rows(count, 3, second_normed_input)

    gate_own = outer_columns(normed_all, gate_weight)
    up_own = outer_columns(normed_all, up_weight)
    hidden_unit_gradient = outer_columns(grad_ffn_all, down_weight)
    units_own = geglu(gate_own, up_own).astype(low)
    grad_gate_own, grad_up_own = jax.vjp(geglu, gate_own, up_own)[1](hidden_unit_gradient)
    grad_gate_own = grad_gate_own.astype(low)
    grad_up_own = grad_up_own.astype(low)
    gate_grad = inner_rows(grad_gate_own, normed_all).astype(low)
    up_grad = inner_rows(grad_up_own, normed_all).astype(low)
    down_grad = inner_rows(units_own, grad_ffn_all).astype(low)
    gate_other, up_other, down_other = (
        swap_loops(gate_grad),
        swap_loops(up_grad),
        swap_loops(down_grad),
    )
    ffn_terms = matrix_product(units_own, down_weight).astype(low)
    input_terms = (
        matrix_product(grad_gate_own, gate_weight) + matrix_product(grad_up_own, up_weight)
    ).astype(low)
    ffn_sum, second_normed_gradient = scatter_rows(count, 4, ffn_terms, input_terms)
    complete_output = middle_state + active_mask * ffn_sum
    confidence = root_mean(residual_stream) / (
        root_mean(residual_stream) + root_mean(complete_output - residual_stream)
    )
    conf_sum = jnp.sum(jnp.where(live_own, confidence, 0.0))
    depth_hits = (
        (token_exit_depth[0][:, None] == jnp.arange(loop_count + 1, dtype=jnp.int32)[None, :])
        & live_own[:, None]
    ).astype(jnp.float32)
    stats = jnp.concatenate([conf_sum[None], jnp.sum(depth_hits, axis=0)])

    adapter_hidden_gradient = jnp.concatenate(
        [
            outer_columns(down_grad, second_down),
            matrix_product(gate_grad, first_gate),
            matrix_product(up_grad, first_up),
        ],
        axis=1,
    )
    first_terms = jnp.concatenate(
        [inner_rows(gate_grad, gate_factor), inner_rows(up_grad, up_factor)], axis=1
    ).astype(low)
    grad_middle_part, grad_gain_two = jax.vjp(norm_rows, middle_state, layer_norm_gains[1])[1](
        second_normed_gradient
    )
    grad_middle = grad_out + grad_middle_part
    branch_gradient = (active_mask * grad_middle).astype(low)
    grad_attended = outer_columns(branch_gradient, output_weight).astype(low)
    grad_att_rows = grad_attended.reshape(local_rows * HEADS, HEAD_SIZE)
    prob = jnp.exp(score_rows() - top_score) / mass
    grad_prob = outer_columns(grad_att_rows, values).reshape(local_rows, HEADS, key_total)
    centre = jnp.sum(prob * grad_prob, axis=-1, keepdims=True)
    grad_scores = (
        (prob * (grad_prob - centre)).astype(low).reshape(local_rows * HEADS, key_total)
    )
    prob_again = prob.astype(low).reshape(local_rows * HEADS, key_total)
    kv_terms = jnp.concatenate(
        [inner_rows(grad_scores, query_rows) * scale, inner_rows(prob_again, grad_att_rows)], axis=1
    ).astype(low)
    grad_kv, first_grad_hidden = scatter_rows(count, 5, kv_terms, first_terms)
    grad_queries = (matrix_product(grad_scores, keys) * scale).reshape(local_rows, HEADS, HEAD_SIZE)
    query_linear_gradient = (
        rotate_back(grad_queries, pos_own).reshape(local_rows, QUERY_WIDTH).astype(low)
    )
    key_linear_gradient = rotate_back(grad_kv[:, None, :HEAD_SIZE], pos_own)[:, 0].astype(low)
    value_linear_gradient = grad_kv[:, HEAD_SIZE:].astype(low)
    query_key_value_gradient = jnp.concatenate(
        [query_linear_gradient, key_linear_gradient, value_linear_gradient], axis=1
    )
    normed_gradient = outer_columns(query_key_value_gradient, input_weight)
    grad_resid_part, grad_gain_one = jax.vjp(norm_rows, residual_stream, layer_norm_gains[0])[1](
        normed_gradient
    )
    hidden_grad = grad_middle + grad_resid_part

    lowrank_projection = matrix_product(normed_input, adapter_first[:, : 3 * rank]).astype(low)
    output_projection = matrix_product(
        attended_rows, adapter_first[:, 3 * rank : 4 * rank]
    ).astype(low)
    second_terms = jnp.concatenate(
        [
            inner_rows(query_linear_gradient, lowrank_projection[:, :rank]),
            inner_rows(key_linear_gradient, lowrank_projection[:, rank : 2 * rank]),
            inner_rows(value_linear_gradient, lowrank_projection[:, 2 * rank :]),
            inner_rows(branch_gradient, output_projection),
            inner_rows(down_grad, down_factor),
        ],
        axis=0,
    ).astype(low)
    in_terms = inner_rows(normed_input, query_key_value_gradient).astype(low)
    out_terms = inner_rows(attended_rows, branch_gradient).astype(low)
    width_own = MODEL_WIDTH // count
    gain_rows = jnp.stack([grad_gain_one, grad_gain_two]).reshape(2, count, width_own)
    small = jnp.zeros((count, 8, 128), jnp.float32)
    small = small.at[:, :2, :width_own].set(jnp.swapaxes(gain_rows, 0, 1))
    small = small.at[:, 2, : loop_count + 2].set(stats[None])
    in_portion, out_portion, second_grad, small_sum = scatter_rows(
        count, 6, in_terms, out_terms, second_terms, small.reshape(count * 8, 128)
    )
    in_low = in_portion.astype(low)
    out_low = out_portion.astype(low)
    adapter_first_gradient = jnp.concatenate(
        [
            outer_columns(in_low[:, :key_at], second_query),
            outer_columns(in_low[:, key_at:value_at], second_key),
            outer_columns(in_low[:, value_at:], second_value),
            outer_columns(out_low, second_output),
            first_grad_hidden,
        ],
        axis=1,
    )
    small_total = both_loops(small_sum)
    sum_gains = small_total[:2, :width_own]
    depth_total = small_total[2, 1 : loop_count + 2]
    mean_confidence = small_total[2, 0] / jnp.sum(depth_total)
    exit_counts = depth_total.astype(jnp.int32)
    sum_mlp = jnp.stack(
        [
            gate_grad.astype(jnp.float32) + gate_other.astype(jnp.float32),
            up_grad.astype(jnp.float32) + up_other.astype(jnp.float32),
            down_grad.astype(jnp.float32) + down_other.astype(jnp.float32),
        ],
        axis=1,
    )
    return (
        complete_output.astype(low)[None],
        hidden_grad[None],
        both_loops(in_low),
        both_loops(out_low),
        sum_mlp,
        sum_gains,
        adapter_first_gradient[None],
        jnp.swapaxes(second_grad, 0, 1)[None],
        adapter_hidden_gradient[None],
        exit_counts,
        mean_confidence,
    )


def solution(mesh):
    return jax.shard_map(
        per_device,
        mesh=mesh,
        in_specs=(
            P("loop", "dp", None),
            P("loop", "dp", None),
            P("dp", None),
            P("dp", None),
            P("dp", None, None),
            P(),
            P("loop", None, None),
            P("loop", None, None),
            P("loop", None, None),
            P("loop", None),
            P("loop", None),
            P("loop", "dp"),
        ),
        out_specs=(
            P("loop", "dp", None),
            P("loop", "dp", None),
            P("dp", None),
            P("dp", None),
            P("dp", None, None),
            P(None, "dp"),
            P("loop", "dp", None),
            P("loop", None, "dp"),
            P("loop", "dp", None),
            P(),
            P(),
        ),
        check_vma=False,
    )
```

```python
import functools

import jax
import jax.numpy as jnp
from jax import lax
from jax.experimental import pallas as pl
from jax.experimental.pallas import tpu as pltpu
from jax.sharding import PartitionSpec as P

MODEL_WIDTH = 2048
HEADS = 8
HEAD_SIZE = 256
ADAPTER_RANK = 256
QUERY_WIDTH = 2048
PROJECTED_WIDTH = 2560


EPSILON = 1e-06
FLOOR_SCORE = -1e30
MESH = pl.DeviceIdType.MESH
VMEM_LIMIT = 60 * 1024 * 1024
LINE_DEVICES = 16


def matrix_product(left, right):
    return jnp.dot(left, right, preferred_element_type=jnp.float32)


def inner_rows(left, right):
    return lax.dot_general(
        left, right, (((0,), (0,)), ((), ())), preferred_element_type=jnp.float32
    )


def outer_columns(left, right):
    return lax.dot_general(
        left, right, (((1,), (1,)), ((), ())), preferred_element_type=jnp.float32
    )


def norm_rows(values, gain):
    return values * lax.rsqrt(jnp.mean(values * values, axis=-1, keepdims=True) + EPSILON) * gain


def rotate(values, positions):
    half_dim = values.shape[-1] // 2
    freqs = 10000.0 ** (-jnp.arange(half_dim, dtype=jnp.float32) / half_dim)
    angles = positions.astype(jnp.float32)[:, None, None] * freqs
    cosine = jnp.cos(angles)
    sine = jnp.sin(angles)
    first_half = values[..., :half_dim]
    second_half = values[..., half_dim:]
    return jnp.concatenate(
        [first_half * cosine - second_half * sine, first_half * sine + second_half * cosine],
        axis=-1,
    )


def rotate_back(grads, positions):

    def turned(values):
        return rotate(values, positions)

    return jax.vjp(turned, jnp.zeros_like(grads))[1](grads)[0]


def geglu(gate_values, up_projection_value):
    return jax.nn.gelu(gate_values, approximate=True) * up_projection_value


def root_mean(values):
    return jnp.sqrt(jnp.mean(values * values, axis=-1) + EPSILON)


def token_facts(row_of_tokens, sequence_length):
    row_total = row_of_tokens.shape[0]
    live_row = row_of_tokens >= 0
    seq_ends = jnp.cumsum(sequence_length)
    seq_index = jnp.sum((row_of_tokens[:, None] >= seq_ends[None, :]).astype(jnp.int32), axis=1)
    seq_starts = seq_ends - sequence_length
    own_start = jnp.sum(
        jnp.where(
            seq_index[:, None] == jnp.arange(sequence_length.shape[0], dtype=jnp.int32)[None, :],
            seq_starts[None, :],
            0,
        ),
        axis=1,
    )
    row_ids = jnp.arange(row_total, dtype=jnp.int32)
    sequence = jnp.where(live_row, seq_index, -1 - row_ids)
    ordering = jnp.where(live_row, row_of_tokens, 0)
    positions = jnp.where(live_row, row_of_tokens - own_start, 0)
    return (live_row, sequence, ordering, positions)


def place(count):
    me = lax.axis_index("dp")
    return me, count // 4, me // 4, (me // 2) % 2, me % 2


def greet(count):
    me, depth, z, y, c = place(count)
    barrier = pltpu.get_barrier_semaphore()

    def signal(where):
        pl.semaphore_signal(barrier, inc=1, device_id={"dp": where}, device_id_type=MESH)

    signal(me + 1 - 2 * c)
    signal(me + 2 - 4 * y)

    @pl.when(z > 0)
    def _():
        signal(me - 4)

    @pl.when(z < depth - 1)
    def _():
        signal(me + 4)

    ends = jnp.where((z > 0) & (z < depth - 1), 4, 3)
    pl.semaphore_wait(barrier, ends)


def contract(left, right, left_axis, right_axis):
    return lax.dot_general(
        left,
        right,
        (((left_axis,), (right_axis,)), ((), ())),
        preferred_element_type=jnp.float32,
    )


def gather_plan(count, parts, own, full, keep, recv, send_core, send_pair, send_right, send_left):
    arrays = len(own)
    me, depth, z, y, c = place(count)
    mate = me + 2 - 4 * y

    def rows_of(a, s):
        step = own[a].shape[0] // parts
        return pl.ds(s * step, step)

    def copy(unit, block, target, sem, first=False):
        a, s = unit
        rows = rows_of(a, s)
        return pltpu.make_async_remote_copy(
            src_ref=own[a].at[rows] if first else full[a].at[block, rows],
            dst_ref=full[a].at[block, rows],
            send_sem=sem,
            recv_sem=recv.at[a, block, s],
            device_id={"dp": target},
            device_id_type=MESH,
        )

    def to_core(unit, block, first=False):
        a, s = unit
        return copy(unit, block, me + 1 - 2 * c, send_core.at[a, block // 2, s], first)

    def to_pair(unit, block, first=False):
        a, s = unit
        return copy(unit, block, mate, send_pair.at[a, block // 4, s], first)

    def to_right(unit, block, first=False):
        a, s = unit
        return copy(unit, block, me + 4, send_right.at[a, block // 4, s], first)

    def to_left(unit, block, first=False):
        a, s = unit
        return copy(unit, block, me - 4, send_left.at[a, block // 4, s], first)

    local = [pltpu.make_async_copy(own[a], full[a].at[me], keep.at[a]) for a in range(arrays)]
    units = [(a, s) for a in range(arrays) for s in range(parts)]

    def begin():
        for unit in units:

            @pl.when(z < depth - 1)
            def _(unit=unit):
                to_right(unit, me, True).start()

            @pl.when(z > 0)
            def _(unit=unit):
                to_left(unit, me, True).start()

            to_pair(unit, me, True).start()
            to_core(unit, me, True).start()
        for item in local:
            item.start()

    def from_line(k, unit):
        @pl.when(z - k >= 0)
        def _():
            block = me - 4 * k
            to_right(unit, block).wait_recv()

            @pl.when(z < depth - 1)
            def _():
                to_right(unit, block).start()

            to_pair(unit, block).start()
            to_core(unit, block).start()

        @pl.when(z + k < depth)
        def _():
            block = me + 4 * k
            to_left(unit, block).wait_recv()

            @pl.when(z > 0)
            def _():
                to_left(unit, block).start()

            to_pair(unit, block).start()
            to_core(unit, block).start()

    def pass_on(unit, block):
        to_pair(unit, block).wait_recv()
        to_core(unit, block).start()

    def from_pair(k, unit):
        if k == 0:
            pass_on(unit, mate)
            return

        @pl.when(z - k >= 0)
        def _():
            pass_on(unit, mate - 4 * k)

        @pl.when(z + k < depth)
        def _():
            pass_on(unit, mate + 4 * k)

    def arrive():
        for unit in units:
            for j in range(count // 2):
                to_core(unit, 2 * j + 1 - c).wait_recv()
        for item in local:
            item.wait()

    def finish():
        for unit in units:
            for j in range(count // 2):
                to_core(unit, 2 * j + c).wait_send()
            for j in range(depth):
                block = 4 * j + 2 * y + c
                to_pair(unit, block).wait_send()

                @pl.when((z >= j) & (z < depth - 1))
                def _():
                    to_right(unit, block).wait_send()

                @pl.when((z <= j) & (z > 0))
                def _():
                    to_left(unit, block).wait_send()

    return units, begin, from_line, from_pair, arrive, finish


def gather_sems(count, number, parts):
    depth = count // 4
    sem = pltpu.SemaphoreType.DMA
    return [
        sem((number,)),
        sem((number, count, parts)),
        sem((number, count // 2, parts)),
        sem((number, depth, parts)),
        sem((number, depth, parts)),
        sem((number, depth, parts)),
    ]


def gather_body(count, parts, arrays, *refs):
    depth = count // 4
    greet(count)
    units, begin, from_line, from_pair, arrive, finish = gather_plan(
        count, parts, refs[:arrays], refs[arrays : 2 * arrays], *refs[2 * arrays :]
    )
    begin()
    for k in range(1, depth):
        for unit in units:
            from_line(k, unit)
        for unit in units:
            from_pair(k - 1, unit)
    for unit in units:
        from_pair(depth - 1, unit)
    arrive()
    finish()


def kernel_params(ident):
    return pltpu.CompilerParams(
        collective_id=ident, has_side_effects=True, vmem_limit_bytes=VMEM_LIMIT
    )


def gather_rows(count, ident, *arrays, parts=2):
    if count != LINE_DEVICES:
        return [lax.all_gather(item, "dp", axis=0, tiled=True) for item in arrays]
    number = len(arrays)
    anywhere = pl.BlockSpec(memory_space=pl.ANY)
    full = pl.pallas_call(
        functools.partial(gather_body, count, parts, number),
        out_shape=[
            jax.ShapeDtypeStruct((count,) + item.shape, item.dtype) for item in arrays
        ],
        in_specs=[anywhere] * number,
        out_specs=[anywhere] * number,
        scratch_shapes=gather_sems(count, number, parts),
        compiler_params=kernel_params(ident),
        name="gather_rows",
    )(*arrays)
    return [
        item.reshape((count * item.shape[1],) + item.shape[2:]) for item in full
    ]


def opening_body(count, parts, arrays, *refs):
    own = refs[:arrays]
    weights, factors, first, second = refs[arrays : arrays + 4]
    full = refs[arrays + 4 : 2 * arrays + 4]
    folded = refs[2 * arrays + 4]
    scratch = refs[2 * arrays + 5 :]
    bank, factor_bank, first_bank, second_bank, bank_sem, factor_sem, out_sem = scratch[:7]
    me, depth, z, y, c = place(count)
    rank = ADAPTER_RANK
    width, wide = bank.shape[1:]
    greet(count)
    units, begin, from_line, from_pair, arrive, finish = gather_plan(
        count, parts, own, full, *scratch[7:]
    )
    begin()
    fills = [
        pltpu.make_async_copy(weights.at[i], bank.at[i], bank_sem.at[i]) for i in range(3)
    ]
    sources = [
        pltpu.make_async_copy(
            factors.at[pl.ds(me * width, width)], factor_bank, factor_sem.at[0]
        ),
        pltpu.make_async_copy(
            first.at[:, pl.ds(4 * rank, 2 * rank)], first_bank, factor_sem.at[1]
        ),
        pltpu.make_async_copy(
            second.at[:, pl.ds(PROJECTED_WIDTH + MODEL_WIDTH, wide)], second_bank, factor_sem.at[2]
        ),
    ]
    for item in sources + fills:
        item.start()

    def put(i):
        return pltpu.make_async_copy(bank.at[i], folded.at[i], out_sem.at[i])

    def fold(i):
        high, tile = 256, 512

        def inner(n, carry):
            rows = pl.ds(pl.multiple_of((n // (wide // tile)) * high, high), high)
            cols = pl.ds(pl.multiple_of((n % (wide // tile)) * tile, tile), tile)
            if i == 2:
                extra = contract(factor_bank[rows, :rank], second_bank[:, cols], 1, 0)
            else:
                extra = contract(
                    factor_bank[rows, (i + 1) * rank : (i + 2) * rank],
                    first_bank[cols, i * rank : (i + 1) * rank],
                    1,
                    1,
                )
            bank[i, rows, cols] = (bank[i, rows, cols].astype(jnp.float32) + extra).astype(
                bank.dtype
            )
            return carry

        lax.fori_loop(0, (width // high) * (wide // tile), inner, 0)
        put(i).start()

    for item in sources:
        item.wait()
    fills[0].wait()
    fold(0)
    for k in range(1, depth):
        for unit in units:
            from_line(k, unit)
        if k < 3:
            fills[k].wait()
            fold(k)
        for unit in units:
            from_pair(k - 1, unit)
    for unit in units:
        from_pair(depth - 1, unit)
    arrive()
    finish()
    for i in range(3):
        put(i).wait()


def opening(count, ident, arrays, weights, factors, first, second, parts=2):
    number = len(arrays)
    _, width, wide = weights.shape
    low = jnp.bfloat16
    sem = pltpu.SemaphoreType.DMA
    anywhere = pl.BlockSpec(memory_space=pl.ANY)
    out = pl.pallas_call(
        functools.partial(opening_body, count, parts, number),
        out_shape=[
            jax.ShapeDtypeStruct((count,) + item.shape, item.dtype) for item in arrays
        ]
        + [jax.ShapeDtypeStruct(weights.shape, low)],
        in_specs=[anywhere] * (number + 4),
        out_specs=[anywhere] * (number + 1),
        scratch_shapes=[
            pltpu.VMEM(weights.shape, low),
            pltpu.VMEM((width, factors.shape[1]), low),
            pltpu.VMEM((wide, 2 * ADAPTER_RANK), low),
            pltpu.VMEM((ADAPTER_RANK, wide), low),
            sem((3,)),
            sem((3,)),
            sem((3,)),
        ]
        + gather_sems(count, number, parts),
        compiler_params=kernel_params(ident),
        name="opening",
    )(*arrays, weights, factors, first, second)
    return [
        item.reshape((count * item.shape[1],) + item.shape[2:]) for item in out[:number]
    ] + [out[number]]


def scatter_body(count, parts, arrays, *refs):
    terms = refs[:arrays]
    total = refs[arrays : 2 * arrays]
    scratch = refs[2 * arrays :]
    held, loaded, core_in, pair_in, line_in = [
        scratch[i * arrays : (i + 1) * arrays] for i in range(5)
    ]
    (load_sem, core_send, core_recv, pair_send, pair_recv, line_send, line_recv) = scratch[
        5 * arrays :
    ]
    me, depth, z, y, c = place(count)
    greet(count)
    near = z < depth // 2

    def turn(k):
        even = depth - 1 - k // 2 if k % 2 == 0 else k // 2
        return jnp.where(near, even, depth - 1 - even)

    def rows_of(a, s):
        step = terms[a].shape[1] // parts[a]
        return pl.ds(s * step, step)

    def to_core(a, s, line, pair):
        slot = 2 * line + pair
        return pltpu.make_async_remote_copy(
            src_ref=terms[a].at[2 * slot + 1 - c, rows_of(a, s)],
            dst_ref=core_in[a].at[slot, rows_of(a, s)],
            send_sem=core_send.at[a, slot, s],
            recv_sem=core_recv.at[a, slot, s],
            device_id={"dp": me + 1 - 2 * c},
            device_id_type=MESH,
        )

    def load(a, s, line, pair):
        slot = 2 * line + pair
        return pltpu.make_async_copy(
            terms[a].at[2 * slot + c, rows_of(a, s)],
            loaded[a].at[slot, rows_of(a, s)],
            load_sem.at[a, slot, s],
        )

    def to_pair(a, s, line):
        return pltpu.make_async_remote_copy(
            src_ref=loaded[a].at[2 * line + 1 - y, rows_of(a, s)],
            dst_ref=pair_in[a].at[line, rows_of(a, s)],
            send_sem=pair_send.at[a, line, s],
            recv_sem=pair_recv.at[a, line, s],
            device_id={"dp": me + 2 - 4 * y},
            device_id_type=MESH,
        )

    def along(a, s, line, slot, target):
        return pltpu.make_async_remote_copy(
            src_ref=loaded[a].at[2 * line + y, rows_of(a, s)],
            dst_ref=line_in[a].at[slot, rows_of(a, s)],
            send_sem=line_send.at[a, line, s],
            recv_sem=line_recv.at[a, slot, s],
            device_id={"dp": target},
            device_id_type=MESH,
        )

    def to_right(a, s, line):
        return along(a, s, line, line, me + 4)

    def to_left(a, s, line):
        return along(a, s, line, jnp.where(line == z - 1, depth, line), me - 4)

    def from_right(a, s, line):
        return along(a, s, line, jnp.where(line == z, depth, line), me)

    order = [turn(k) for k in range(depth)]
    units = [(a, s) for a in range(arrays) for s in range(parts[a])]
    for pair in (1 - y, y):
        for line in order:
            for a, s in units:
                to_core(a, s, line, pair).start()
                load(a, s, line, pair).start()

    for line in order:
        for a, s in units:
            slot = 2 * line + 1 - y
            rows = rows_of(a, s)
            load(a, s, line, 1 - y).wait()
            to_core(a, s, line, 1 - y).wait_recv()
            loaded[a][slot, rows] = loaded[a][slot, rows] + core_in[a][slot, rows]
            to_pair(a, s, line).start()

    def own_sum(a, s, line):
        slot = 2 * line + y
        rows = rows_of(a, s)
        load(a, s, line, y).wait()
        to_core(a, s, line, y).wait_recv()
        to_pair(a, s, line).wait_recv()
        part = loaded[a][slot, rows].astype(jnp.float32)
        part += core_in[a][slot, rows].astype(jnp.float32)
        held[a][...] = part + pair_in[a][line, rows].astype(jnp.float32)

    def add_line(a, s, slot):
        along(a, s, z, slot, me).wait_recv()
        held[a][...] += line_in[a][slot, rows_of(a, s)].astype(jnp.float32)

    for line in order:
        for a, s in units:

            @pl.when(line != z)
            def _(a=a, s=s, line=line):
                own_sum(a, s, line)

                @pl.when(((line > z) & (z > 0)) | ((line < z) & (z < depth - 1)))
                def _():
                    add_line(a, s, line)

                loaded[a][2 * line + y, rows_of(a, s)] = held[a][...].astype(loaded[a].dtype)

                @pl.when(line > z)
                def _():
                    to_right(a, s, line).start()

                @pl.when(line < z)
                def _():
                    to_left(a, s, line).start()

    for a, s in units:
        own_sum(a, s, z)

        @pl.when(z > 0)
        def _(a=a, s=s):
            add_line(a, s, z)

        @pl.when(z < depth - 1)
        def _(a=a, s=s):
            add_line(a, s, depth)

        total[a][rows_of(a, s)] = held[a][...]

    for a, s in units:
        for line in range(depth):
            for pair in range(2):
                to_core(a, s, line, pair).wait_send()
            to_pair(a, s, line).wait_send()

            @pl.when(z != line)
            def _():
                to_right(a, s, line).wait_send()


def scatter_rows(count, ident, *arrays):
    if count != LINE_DEVICES:
        return [
            lax.psum_scatter(
                item.astype(jnp.float32), "dp", scatter_dimension=0, tiled=True
            )
            for item in arrays
        ]
    depth = count // 4
    number = len(arrays)
    blocks = [
        item.reshape(count, item.shape[0] // count, item.shape[1]) for item in arrays
    ]
    parts = [2 if item.shape[1] % 32 == 0 and item.shape[1] > 32 else 1 for item in blocks]
    most = max(parts)

    def room(slots):
        return [pltpu.VMEM((slots,) + item.shape[1:], item.dtype) for item in blocks]

    def sems(slots):
        return pltpu.SemaphoreType.DMA((number, slots, most))

    return pl.pallas_call(
        functools.partial(scatter_body, count, parts, number),
        out_shape=[jax.ShapeDtypeStruct(item.shape[1:], jnp.float32) for item in blocks],
        in_specs=[pl.BlockSpec(memory_space=pl.ANY)] * number,
        out_specs=[pl.BlockSpec(memory_space=pltpu.VMEM)] * number,
        scratch_shapes=[
            pltpu.VMEM((item.shape[1] // part, item.shape[2]), jnp.float32)
            for item, part in zip(blocks, parts)
        ]
        + room(2 * depth)
        + room(2 * depth)
        + room(depth)
        + room(depth + 1)
        + [
            sems(2 * depth),
            sems(2 * depth),
            sems(2 * depth),
            sems(depth),
            sems(depth),
            sems(depth),
            sems(depth + 1),
        ],
        compiler_params=kernel_params(ident),
        name="scatter_rows",
    )(*blocks)


def line_order(z):
    near = z < 2
    return [z, z + 1 - 2 * (z % 2), jnp.where(near, 2, 1), jnp.where(near, 3, 0)]


def unit_values(gate, up, grad):
    slope = 0.7978845608028654
    cubic = 0.044715
    square = gate * gate
    curve = jnp.tanh(slope * (gate + cubic * square * gate))
    half = 0.5 * (1.0 + curve)
    turned = gate * half
    rise = half + 0.5 * gate * (1.0 - curve * curve) * slope * (1.0 + 3.0 * cubic * square)
    low = jnp.bfloat16
    return (turned * up).astype(low), (grad * up * rise).astype(low), (grad * turned).astype(low)


def hidden_body(count, parts, own, grads, weights, units, gate_grads, up_grads, rows_out,
                held, bank, coming, done, recv, send_core, send_pair, send_line, keep, bank_sem,
                coming_sem, done_sem, rows_sem):
    me, depth, z, y, c = place(count)
    height = own.shape[0]
    width = bank.shape[1]
    step = height // parts
    tile = 512
    core, mate = me + 1 - 2 * c, me + 2 - 4 * y
    lines = line_order(z)
    greet(count)

    def hop(block, s, target, sem, first=False):
        rows = pl.ds(s * step, step)
        return pltpu.make_async_remote_copy(
            src_ref=own.at[rows] if first else held.at[block, rows],
            dst_ref=held.at[block, rows],
            send_sem=sem,
            recv_sem=recv.at[block, s],
            device_id={"dp": target},
            device_id_type=MESH,
        )

    def to_core(block, s, first=False):
        return hop(block, s, core, send_core.at[block // 2, s], first)

    def to_pair(block, s, first=False):
        return hop(block, s, mate, send_pair.at[block // 4, s], first)

    def to_right(block, s, first=False):
        return hop(block, s, me + 4, send_line.at[0, block // 4, s], first)

    def to_left(block, s, first=False):
        return hop(block, s, me - 4, send_line.at[1, block // 4, s], first)

    for s in range(parts):

        @pl.when(z > 0)
        def _():
            to_left(me, s, True).start()

        @pl.when(z < depth - 1)
        def _():
            to_right(me, s, True).start()

        to_core(me, s, True).start()
        to_pair(me, s, True).start()
    mine = pltpu.make_async_copy(own, held.at[me], keep)
    mine.start()
    fills = [
        pltpu.make_async_copy(weights.at[i], bank.at[i], bank_sem.at[i]) for i in range(3)
    ]
    for fill in fills:
        fill.start()

    def first_of(line, pair):
        return 4 * line + 2 * pair

    def fetch(line, pair, slot):
        return pltpu.make_async_copy(
            grads.at[pl.ds(first_of(line, pair), 2)], coming.at[slot], coming_sem.at[slot]
        )

    def store(line, pair, slot):
        rows = pl.ds(first_of(line, pair) * height, 2 * height)
        return [
            pltpu.make_async_copy(done.at[slot, i], out.at[rows], done_sem.at[slot, i])
            for i, out in enumerate((units, gate_grads, up_grads))
        ]

    def keep_rows(line, pair):
        some = pl.ds(first_of(line, pair), 2)
        return pltpu.make_async_copy(held.at[some], rows_out.at[some], rows_sem.at[line, pair])

    def from_line(line):
        block = first_of(line, y) + c
        for s in range(parts):
            hop(block, s, core, send_core.at[block // 2, s]).wait_recv()

            @pl.when((line < z) & (z < depth - 1))
            def _():
                to_right(block, s).start()

            @pl.when((line > z) & (z > 0))
            def _():
                to_left(block, s).start()

            to_pair(block, s).start()
            to_core(block, s).start()

    def from_pair(line):
        block = first_of(line, 1 - y) + c
        for s in range(parts):
            to_core(block, s).wait_recv()
            to_core(block, s).start()

    steps = [(line, pair) for line in lines for pair in (y, 1 - y)]

    def work(index):
        line, pair = steps[index]
        slot = index % 2
        for s in range(parts):
            to_core(first_of(line, pair) + 1 - c, s).wait_recv()
        if index == 0:
            mine.wait()
            fetch(line, pair, slot).start()
            for fill in fills:
                fill.wait()
        if index + 1 < len(steps):
            fetch(*steps[index + 1], 1 - slot).start()
        fetch(line, pair, slot).wait()
        keep_rows(line, pair).start()
        if index >= 2:
            for item in store(*steps[index - 2], slot):
                item.wait()
        some = pl.ds(first_of(line, pair), 2)

        def inner(n, carry):
            cols = pl.ds(pl.multiple_of(n * tile, tile), tile)
            block = held[some].reshape(2 * height, held.shape[2])
            gate = contract(block, bank[0, cols], 1, 1)
            up = contract(block, bank[1, cols], 1, 1)
            grad = contract(coming[slot].reshape(2 * height, held.shape[2]), bank[2, cols], 1, 1)
            for i, value in enumerate(unit_values(gate, up, grad)):
                done[slot, i, :, cols] = value
            return carry

        lax.fori_loop(0, width // tile, inner, 0)
        for item in store(line, pair, slot):
            item.start()

    work(0)
    from_pair(lines[0])
    from_line(lines[1])
    work(1)
    for k in range(1, depth):
        from_pair(lines[k])
        work(2 * k)
        if k + 1 < depth:
            from_line(lines[k + 1])
        work(2 * k + 1)

    for index in (len(steps) - 2, len(steps) - 1):
        for item in store(*steps[index], index % 2):
            item.wait()
    for line, pair in steps:
        keep_rows(line, pair).wait()
    for j in range(depth):
        block = first_of(j, y) + c
        for s in range(parts):
            to_core(block, s).wait_send()
            to_core(first_of(j, 1 - y) + c, s).wait_send()
            to_pair(block, s).wait_send()

            @pl.when((z >= j) & (z < depth - 1))
            def _():
                to_right(block, s).wait_send()

            @pl.when((z <= j) & (z > 0))
            def _():
                to_left(block, s).wait_send()


def hidden_units(count, ident, own, grads, weights, parts=2):
    height, wide = own.shape
    width = weights.shape[1]
    depth = count // 4
    low = jnp.bfloat16
    sem = pltpu.SemaphoreType.DMA
    anywhere = pl.BlockSpec(memory_space=pl.ANY)
    acts = jax.ShapeDtypeStruct((count * height, width), low)
    return pl.pallas_call(
        functools.partial(hidden_body, count, parts),
        out_shape=[acts, acts, acts, jax.ShapeDtypeStruct((count, height, wide), low)],
        in_specs=[anywhere] * 3,
        out_specs=[anywhere] * 4,
        scratch_shapes=[
            pltpu.VMEM((count, height, wide), low),
            pltpu.VMEM((3, width, wide), low),
            pltpu.VMEM((2, 2, height, wide), low),
            pltpu.VMEM((2, 3, 2 * height, width), low),
            sem((count, parts)),
            sem((2 * depth, parts)),
            sem((depth, parts)),
            sem((2, depth, parts)),
            sem,
            sem((3,)),
            sem((2,)),
            sem((2, 3)),
            sem((depth, 2)),
        ],
        compiler_params=kernel_params(ident),
        cost_estimate=pl.CostEstimate(
            flops=6 * count * height * width * wide,
            bytes_accessed=20 * width * wide,
            transcendentals=0,
        ),
        name="hidden_units",
    )(own, grads, weights)


def unit_grads_body(count, parts, units, gate_grads, up_grads, weights, rows_all, grads_all,
                    input_sum, output_sum, weight_grads,
                    bank, rows_in, units_in, made, held, loaded, leaving, core_in, pair_in,
                    line_in, bank_sem, rows_sem, fill_sems, units_sem, made_sem, core_send, core_recv,
                    pair_send, pair_recv, line_send, line_recv):
    me, depth, z, y, c = place(count)
    height, wide = input_sum.shape
    width = weights.shape[1]
    step = height // parts
    low = jnp.bfloat16
    core, mate = me + 1 - 2 * c, me + 2 - 4 * y
    near = z < 2
    order = [jnp.where(near, 3, 0), jnp.where(near, 0, 3), jnp.where(near, 2, 1),
             jnp.where(near, 1, 2)]
    greet(count)

    def fill(source, at):
        return pltpu.make_async_copy(source, bank.at[at], bank_sem.at[at])

    blocks = width // height

    def fill_rows(source, half, at):
        return [
            pltpu.make_async_copy(
                source.at[half * blocks + i],
                bank.at[at, pl.ds(i * height, height)],
                fill_sems.at[at, i],
            )
            for i in range(blocks)
        ]

    first_fills = [fill(weights.at[i], i) for i in range(3)]
    for item in first_fills:
        item.start()
    grad_tail = fill_rows(grads_all, 1, 3)
    steps = [(line, pair) for line in order for pair in (1 - y, y)]

    def fetch(line, pair, slot, sources):
        rows = pl.ds((4 * line + 2 * pair) * height, 2 * height)
        return [
            pltpu.make_async_copy(source.at[rows], rows_in.at[slot, i], rows_sem.at[slot, i])
            for i, source in enumerate(sources)
        ]

    def rows_of(s):
        return pl.ds(s * step, step)

    def to_core(a, line, pair, slot, s):
        at = 2 * line + pair
        return pltpu.make_async_remote_copy(
            src_ref=leaving.at[a, slot, rows_of(s)],
            dst_ref=core_in.at[a, at, rows_of(s)],
            send_sem=core_send.at[a, slot, s],
            recv_sem=core_recv.at[a, at, s],
            device_id={"dp": core},
            device_id_type=MESH,
        )

    def to_pair(a, line, s):
        return pltpu.make_async_remote_copy(
            src_ref=loaded.at[a, 2 * line + 1 - y, rows_of(s)],
            dst_ref=pair_in.at[a, line, rows_of(s)],
            send_sem=pair_send.at[a, line, s],
            recv_sem=pair_recv.at[a, line, s],
            device_id={"dp": mate},
            device_id_type=MESH,
        )

    def along(a, line, slot, s, target):
        return pltpu.make_async_remote_copy(
            src_ref=loaded.at[a, 2 * line + y, rows_of(s)],
            dst_ref=line_in.at[a, slot, rows_of(s)],
            send_sem=line_send.at[a, line, s],
            recv_sem=line_recv.at[a, slot, s],
            device_id={"dp": target},
            device_id_type=MESH,
        )

    def product(a, index):
        line, pair = steps[index]
        slot = index % 2
        sources = (gate_grads, up_grads) if a == 0 else (units,)
        if index == 0:
            for item in fetch(line, pair, slot, sources):
                item.start()
        if index + 1 < len(steps):
            for item in fetch(*steps[index + 1], 1 - slot, sources):
                item.start()
        if index >= 2:
            for s in range(parts):
                to_core(a, *steps[index - 2], slot, s).wait_send()
        for item in fetch(line, pair, slot, sources):
            item.wait()
        tile = 512

        def inner(n, carry):
            cols = pl.ds(pl.multiple_of(n * tile, tile), tile)
            if a == 0:
                value = contract(rows_in[slot, 0], bank[0, :, cols], 1, 0)
                value += contract(rows_in[slot, 1], bank[1, :, cols], 1, 0)
            else:
                value = contract(rows_in[slot, 0], bank[2, :, cols], 1, 0)
            value = value.astype(low)

            @pl.when(c == 0)
            def _():
                loaded[a, 2 * line + pair, :, cols] = value[:height]
                leaving[a, slot, :, cols] = value[height:]

            @pl.when(c == 1)
            def _():
                loaded[a, 2 * line + pair, :, cols] = value[height:]
                leaving[a, slot, :, cols] = value[:height]

            return carry

        lax.fori_loop(0, wide // tile, inner, 0)
        for s in range(parts):
            to_core(a, line, pair, slot, s).start()

    def finish_sends(a):
        for index in (len(steps) - 2, len(steps) - 1):
            for s in range(parts):
                to_core(a, *steps[index], index % 2, s).wait_send()

    def pair_step(a, k):
        line = order[k]
        at = 2 * line + 1 - y
        for s in range(parts):
            to_core(a, line, 1 - y, 0, s).wait_recv()
            loaded[a, at, rows_of(s)] = loaded[a, at, rows_of(s)] + core_in[a, at, rows_of(s)]
            to_pair(a, line, s).start()

    def own_sum(a, line, s):
        at = 2 * line + y
        to_core(a, line, y, 0, s).wait_recv()
        to_pair(a, line, s).wait_recv()
        part = loaded[a, at, rows_of(s)].astype(jnp.float32)
        part += core_in[a, at, rows_of(s)].astype(jnp.float32)
        held[...] = part + pair_in[a, line, rows_of(s)].astype(jnp.float32)

    def add_line(a, slot, s):
        along(a, z, slot, s, me + 4).wait_recv()
        held[...] += line_in[a, slot, rows_of(s)].astype(jnp.float32)

    def line_step(a, k):
        line = order[k]

        @pl.when(line != z)
        def _():
            for s in range(parts):
                own_sum(a, line, s)

                @pl.when(((line > z) & (z > 0)) | ((line < z) & (z < depth - 1)))
                def _():
                    add_line(a, line, s)

                loaded[a, 2 * line + y, rows_of(s)] = held[...].astype(low)

                @pl.when(line > z)
                def _():
                    along(a, line, line, s, me + 4).start()

                @pl.when(line < z)
                def _():
                    along(a, line, jnp.where(line == z - 1, depth, line), s, me - 4).start()

    def last_step(a, total):
        for s in range(parts):
            own_sum(a, z, s)

            @pl.when(z > 0)
            def _():
                add_line(a, z, s)

            @pl.when(z < depth - 1)
            def _():
                add_line(a, depth, s)

            total[rows_of(s)] = held[...]

    tall = units_in.shape[2]

    def bring(g, slot):
        source = (gate_grads, up_grads, units)[g // (width // tall)]
        cols = pl.ds((g % (width // tall)) * tall, tall)
        return pltpu.make_async_copy(source.at[:, cols], units_in.at[slot], units_sem.at[slot])

    def put(g, slot):
        rows = pl.ds((g % (width // tall)) * tall, tall)
        return pltpu.make_async_copy(
            made.at[slot], weight_grads.at[g // (width // tall), rows], made_sem.at[slot]
        )

    number = 3 * (width // tall)

    def weight_product(g):
        slot = g % 2
        if g + 1 < number:
            bring(g + 1, 1 - slot).start()
        bring(g, slot).wait()
        if g >= 2:
            put(g - 2, slot).wait()
        at = 0 if g < 2 * (width // tall) else 2
        tile = 512

        def inner(n, carry):
            cols = pl.ds(pl.multiple_of(n * tile, tile), tile)
            whole = bank[at : at + 2, :, cols].reshape(2 * width, tile)
            made[slot, :, cols] = contract(units_in[slot], whole, 0, 0).astype(low)
            return carry

        lax.fori_loop(0, wide // tile, inner, 0)
        put(g, slot).start()

    for item in first_fills[:2]:
        item.wait()
    for index in range(8):
        product(0, index)
        if index >= 2 and index % 2 == 0:
            pair_step(0, index // 2 - 1)
    finish_sends(0)
    row_fills = fill_rows(rows_all, 0, 0) + fill_rows(rows_all, 1, 1)
    for item in row_fills:
        item.start()
    for item in grad_tail:
        item.start()
    first_fills[2].wait()
    for index in range(8):
        product(1, index)
        if index == 0:
            pair_step(0, 3)
        if index >= 2 and index % 2 == 0:
            pair_step(1, index // 2 - 1)
        if index == 4:
            line_step(0, 0)
    finish_sends(1)
    grad_fills = fill_rows(grads_all, 0, 2)
    for item in grad_fills:
        item.start()
    bring(0, 0).start()
    for item in row_fills:
        item.wait()
    weight_product(0)
    pair_step(1, 3)
    line_step(0, 1)
    weight_product(1)
    weight_product(2)
    line_step(0, 2)
    weight_product(3)
    weight_product(4)
    line_step(0, 3)
    weight_product(5)
    weight_product(6)
    last_step(0, input_sum)
    weight_product(7)
    for item in grad_tail + grad_fills:
        item.wait()
    weight_product(8)
    line_step(1, 0)
    weight_product(9)
    weight_product(10)
    line_step(1, 1)
    weight_product(11)
    line_step(1, 2)
    line_step(1, 3)
    last_step(1, output_sum)

    for g in (number - 2, number - 1):
        put(g, g % 2).wait()
    for a in range(2):
        for line in range(depth):
            for s in range(parts):
                to_pair(a, line, s).wait_send()

                @pl.when(z != line)
                def _():
                    along(a, line, line, s, me + 4).wait_send()


def unit_grads(count, ident, units, gate_grads, up_grads, weights, rows_all, grads_all, parts=2):
    width, wide = weights.shape[1:]
    height = rows_all.shape[1]
    depth = count // 4
    low = jnp.bfloat16
    sem = pltpu.SemaphoreType.DMA
    anywhere = pl.BlockSpec(memory_space=pl.ANY)
    inside = pl.BlockSpec(memory_space=pltpu.VMEM)
    total = jax.ShapeDtypeStruct((height, wide), jnp.float32)

    return pl.pallas_call(
        functools.partial(unit_grads_body, count, parts),
        out_shape=[total, total, jax.ShapeDtypeStruct((3, width, wide), low)],
        in_specs=[anywhere] * 6,
        out_specs=[inside, inside, anywhere],
        scratch_shapes=[
            pltpu.VMEM((4, width, wide), low),
            pltpu.VMEM((2, 2, 2 * height, width), low),
            pltpu.VMEM((2, count * height, 256), low),
            pltpu.VMEM((2, 256, wide), low),
            pltpu.VMEM((height // parts, wide), jnp.float32),
            pltpu.VMEM((2, 2 * depth, height, wide), low),
            pltpu.VMEM((2, 2, height, wide), low),
            pltpu.VMEM((2, 2 * depth, height, wide), low),
            pltpu.VMEM((2, depth, height, wide), low),
            pltpu.VMEM((2, depth + 1, height, wide), low),
            sem((4,)),
            sem((2, 2)),
            sem((4, width // height)),
            sem((2,)),
            sem((2,)),
            sem((2, 2, parts)),
            sem((2, 2 * depth, parts)),
            sem((2, depth, parts)),
            sem((2, depth, parts)),
            sem((2, depth, parts)),
            sem((2, depth + 1, parts)),
        ],
        compiler_params=kernel_params(ident),
        cost_estimate=pl.CostEstimate(
            flops=12 * count * height * width * wide,
            bytes_accessed=40 * width * wide,
            transcendentals=0,
        ),
        name="unit_grads",
    )(units, gate_grads, up_grads, weights, rows_all, grads_all)


def swap_loops(values):
    if lax.axis_size("loop") == 1:
        return values
    return lax.ppermute(values, "loop", [(0, 1), (1, 0)])


def both_loops(values):
    if lax.axis_size("loop") != 2:
        return lax.psum(values.astype(jnp.float32), "loop")
    return values.astype(jnp.float32) + swap_loops(values).astype(jnp.float32)


def per_device(
    layer_input_stream,
    layer_output_gradient,
    attention_in_weight,
    attention_out_weight,
    feedforward_weight,
    layer_norm_gains,
    adapter_first_factors,
    adapter_second_factors,
    adapter_hidden_factors,
    group_sequence_lengths,
    token_per_row,
    token_exit_depth,
):
    current_loop = lax.axis_index("loop")
    dp_index = lax.axis_index("dp")
    loop_count = lax.axis_size("loop")
    count = lax.axis_size("dp")
    local_rows = layer_input_stream.shape[1]
    ffn_rows = feedforward_weight.shape[0]
    weight_rows = attention_in_weight.shape[0]
    low = jnp.bfloat16
    rank = ADAPTER_RANK
    scale = HEAD_SIZE ** (-0.5)
    key_at = QUERY_WIDTH
    value_at = QUERY_WIDTH + HEAD_SIZE
    down_at = PROJECTED_WIDTH + MODEL_WIDTH
    live_all, seq_all, order_all, pos_all = token_facts(token_per_row[0], group_sequence_lengths[0])
    first_row = dp_index * local_rows

    def own_slice(values):
        return lax.dynamic_slice_in_dim(values, first_row, local_rows, 0)

    live_own = own_slice(live_all)
    seq_own = own_slice(seq_all)
    order_own = own_slice(order_all)
    pos_own = own_slice(pos_all)
    active_mask = (live_own & (token_exit_depth[0] > current_loop)).astype(jnp.float32)[:, None]
    residual_stream = layer_input_stream[0].astype(jnp.float32)
    grad_out = layer_output_gradient[0].astype(jnp.float32)
    adapter_first = adapter_first_factors[0]
    adapter_second = adapter_second_factors[0]
    ffn_own = lax.dynamic_slice_in_dim(adapter_hidden_factors[0], dp_index * ffn_rows, ffn_rows, 0)
    first_own = lax.dynamic_slice_in_dim(adapter_first, dp_index * weight_rows, weight_rows, 0)
    second_query = adapter_second[:, :key_at]
    second_key = adapter_second[:, key_at:value_at]
    second_value = adapter_second[:, value_at:PROJECTED_WIDTH]
    second_output = adapter_second[:, PROJECTED_WIDTH:down_at]
    second_down = adapter_second[:, down_at:]

    in_own = (
        attention_in_weight.astype(jnp.float32)
        + jnp.concatenate(
            [
                matrix_product(first_own[:, :rank], second_query),
                matrix_product(first_own[:, rank : 2 * rank], second_key),
                matrix_product(first_own[:, 2 * rank : 3 * rank], second_value),
            ],
            axis=1,
        )
    ).astype(low)
    out_own = (
        attention_out_weight.astype(jnp.float32)
        + matrix_product(first_own[:, 3 * rank : 4 * rank], second_output)
    ).astype(low)
    down_factor = ffn_own[:, :rank]
    gate_factor = ffn_own[:, rank : 2 * rank]
    up_factor = ffn_own[:, 2 * rank :]
    first_gate = adapter_first[:, 4 * rank : 5 * rank]
    first_up = adapter_first[:, 5 * rank :]
    ffn_weight = jnp.swapaxes(feedforward_weight, 0, 1)

    feedforward_gradient = (active_mask * grad_out).astype(low)
    normed_input = norm_rows(residual_stream, layer_norm_gains[0]).astype(low)
    if count == LINE_DEVICES:
        input_weight, output_weight, ffn_folded = opening(
            count, 1, (in_own, out_own), ffn_weight, adapter_hidden_factors[0],
            adapter_first, adapter_second,
        )
    else:
        input_weight, output_weight = gather_rows(count, 1, in_own, out_own)
        extra = jnp.stack(
            [
                outer_columns(gate_factor, first_gate),
                outer_columns(up_factor, first_up),
                matrix_product(down_factor, second_down),
            ]
        )
        ffn_folded = (ffn_weight.astype(jnp.float32) + extra).astype(low)
    feedforward_gradient, input_weight = lax.optimization_barrier(
        (feedforward_gradient, input_weight)
    )
    grad_ffn_all = lax.all_gather(feedforward_gradient, "dp", axis=0, tiled=True)
    query_key_value_linear = matrix_product(normed_input, input_weight)
    queries = rotate(
        query_key_value_linear[:, :QUERY_WIDTH].reshape(local_rows, HEADS, HEAD_SIZE), pos_own
    ).astype(low)
    key_rot = rotate(
        query_key_value_linear[:, key_at:value_at].reshape(local_rows, 1, HEAD_SIZE), pos_own
    )[:, 0]
    kv_send = jnp.concatenate([key_rot, query_key_value_linear[:, value_at:]], axis=1).astype(low)
    (kv_all,) = gather_rows(count, 2, kv_send)
    keys = kv_all[:, :HEAD_SIZE]
    values = kv_all[:, HEAD_SIZE:]
    key_total = kv_all.shape[0]
    allowed = ((seq_own[:, None] == seq_all[None, :]) & (order_all[None, :] <= order_own[:, None]))[
        :, None, :
    ]
    query_rows = queries.reshape(local_rows * HEADS, HEAD_SIZE)

    def score_rows():
        raw_scores = (outer_columns(query_rows, keys) * scale).reshape(local_rows, HEADS, key_total)
        return jnp.where(allowed, raw_scores, FLOOR_SCORE)

    scores = score_rows()
    top_score = jnp.max(scores, axis=-1, keepdims=True)
    expo = jnp.exp(scores - top_score)
    mass = jnp.sum(expo, axis=-1, keepdims=True)
    prob_low = (expo / mass).astype(low)
    attended_rows = (
        matrix_product(prob_low.reshape(local_rows * HEADS, key_total), values)
        .reshape(local_rows, QUERY_WIDTH)
        .astype(low)
    )
    branch_output = matrix_product(attended_rows, output_weight)
    middle_state = residual_stream + active_mask * branch_output
    second_normed_input = norm_rows(middle_state, layer_norm_gains[1]).astype(low)
    if count == LINE_DEVICES:
        grad_blocks = grad_ffn_all.reshape(count, local_rows, MODEL_WIDTH)
        units_own, grad_gate_own, grad_up_own, normed_blocks = hidden_units(
            count, 3, second_normed_input, grad_blocks, ffn_folded
        )
        second_normed_gradient, ffn_sum, weight_grads = unit_grads(
            count, 4, units_own, grad_gate_own, grad_up_own, ffn_folded, normed_blocks, grad_blocks
        )
        gate_grad, up_grad, down_grad = weight_grads
    else:
        (normed_all,) = gather_rows(count, 3, second_normed_input)
        gate_weight, up_weight, down_weight = ffn_folded
        gate_own = outer_columns(normed_all, gate_weight)
        up_own = outer_columns(normed_all, up_weight)
        hidden_unit_gradient = outer_columns(grad_ffn_all, down_weight)
        units_own = geglu(gate_own, up_own).astype(low)
        grad_gate_own, grad_up_own = jax.vjp(geglu, gate_own, up_own)[1](hidden_unit_gradient)
        grad_gate_own = grad_gate_own.astype(low)
        grad_up_own = grad_up_own.astype(low)
        gate_grad = inner_rows(grad_gate_own, normed_all).astype(low)
        up_grad = inner_rows(grad_up_own, normed_all).astype(low)
        down_grad = inner_rows(units_own, grad_ffn_all).astype(low)
        ffn_terms = matrix_product(units_own, down_weight).astype(low)
        input_terms = (
            matrix_product(grad_gate_own, gate_weight) + matrix_product(grad_up_own, up_weight)
        ).astype(low)
        ffn_sum, second_normed_gradient = scatter_rows(count, 4, ffn_terms, input_terms)
        weight_grads = jnp.stack([gate_grad, up_grad, down_grad])
    weight_other = swap_loops(weight_grads)
    complete_output = middle_state + active_mask * ffn_sum
    confidence = root_mean(residual_stream) / (
        root_mean(residual_stream) + root_mean(complete_output - residual_stream)
    )
    conf_sum = jnp.sum(jnp.where(live_own, confidence, 0.0))
    depth_hits = (
        (token_exit_depth[0][:, None] == jnp.arange(loop_count + 1, dtype=jnp.int32)[None, :])
        & live_own[:, None]
    ).astype(jnp.float32)
    stats = jnp.concatenate([conf_sum[None], jnp.sum(depth_hits, axis=0)])

    adapter_hidden_gradient = jnp.concatenate(
        [
            outer_columns(down_grad, second_down),
            matrix_product(gate_grad, first_gate),
            matrix_product(up_grad, first_up),
        ],
        axis=1,
    )
    first_terms = jnp.concatenate(
        [inner_rows(gate_grad, gate_factor), inner_rows(up_grad, up_factor)], axis=1
    ).astype(low)
    grad_middle_part, grad_gain_two = jax.vjp(norm_rows, middle_state, layer_norm_gains[1])[1](
        second_normed_gradient
    )
    grad_middle = grad_out + grad_middle_part
    branch_gradient = (active_mask * grad_middle).astype(low)
    grad_attended = outer_columns(branch_gradient, output_weight).astype(low)
    grad_att_rows = grad_attended.reshape(local_rows * HEADS, HEAD_SIZE)
    prob = jnp.exp(score_rows() - top_score) / mass
    grad_prob = outer_columns(grad_att_rows, values).reshape(local_rows, HEADS, key_total)
    centre = jnp.sum(prob * grad_prob, axis=-1, keepdims=True)
    grad_scores = (
        (prob * (grad_prob - centre)).astype(low).reshape(local_rows * HEADS, key_total)
    )
    prob_again = prob.astype(low).reshape(local_rows * HEADS, key_total)
    kv_terms = jnp.concatenate(
        [inner_rows(grad_scores, query_rows) * scale, inner_rows(prob_again, grad_att_rows)], axis=1
    ).astype(low)
    grad_kv, first_grad_hidden = scatter_rows(count, 5, kv_terms, first_terms)
    grad_queries = (matrix_product(grad_scores, keys) * scale).reshape(local_rows, HEADS, HEAD_SIZE)
    query_linear_gradient = (
        rotate_back(grad_queries, pos_own).reshape(local_rows, QUERY_WIDTH).astype(low)
    )
    key_linear_gradient = rotate_back(grad_kv[:, None, :HEAD_SIZE], pos_own)[:, 0].astype(low)
    value_linear_gradient = grad_kv[:, HEAD_SIZE:].astype(low)
    query_key_value_gradient = jnp.concatenate(
        [query_linear_gradient, key_linear_gradient, value_linear_gradient], axis=1
    )
    normed_gradient = outer_columns(query_key_value_gradient, input_weight)
    grad_resid_part, grad_gain_one = jax.vjp(norm_rows, residual_stream, layer_norm_gains[0])[1](
        normed_gradient
    )
    hidden_grad = grad_middle + grad_resid_part

    lowrank_projection = matrix_product(normed_input, adapter_first[:, : 3 * rank]).astype(low)
    output_projection = matrix_product(
        attended_rows, adapter_first[:, 3 * rank : 4 * rank]
    ).astype(low)
    second_terms = jnp.concatenate(
        [
            inner_rows(query_linear_gradient, lowrank_projection[:, :rank]),
            inner_rows(key_linear_gradient, lowrank_projection[:, rank : 2 * rank]),
            inner_rows(value_linear_gradient, lowrank_projection[:, 2 * rank :]),
            inner_rows(branch_gradient, output_projection),
            inner_rows(down_grad, down_factor),
        ],
        axis=0,
    ).astype(low)
    in_terms = inner_rows(normed_input, query_key_value_gradient).astype(low)
    out_terms = inner_rows(attended_rows, branch_gradient).astype(low)
    width_own = MODEL_WIDTH // count
    gain_rows = jnp.stack([grad_gain_one, grad_gain_two]).reshape(2, count, width_own)
    small = jnp.zeros((count, 8, 128), jnp.float32)
    small = small.at[:, :2, :width_own].set(jnp.swapaxes(gain_rows, 0, 1))
    small = small.at[:, 2, : loop_count + 2].set(stats[None])
    in_portion, out_portion, second_grad, small_sum = scatter_rows(
        count, 6, in_terms, out_terms, second_terms, small.reshape(count * 8, 128)
    )
    in_low = in_portion.astype(low)
    out_low = out_portion.astype(low)
    adapter_first_gradient = jnp.concatenate(
        [
            outer_columns(in_low[:, :key_at], second_query),
            outer_columns(in_low[:, key_at:value_at], second_key),
            outer_columns(in_low[:, value_at:], second_value),
            outer_columns(out_low, second_output),
            first_grad_hidden,
        ],
        axis=1,
    )
    small_total = both_loops(small_sum)
    sum_gains = small_total[:2, :width_own]
    depth_total = small_total[2, 1 : loop_count + 2]
    mean_confidence = small_total[2, 0] / jnp.sum(depth_total)
    exit_counts = depth_total.astype(jnp.int32)
    sum_mlp = jnp.swapaxes(
        weight_grads.astype(jnp.float32) + weight_other.astype(jnp.float32), 0, 1
    )
    return (
        complete_output.astype(low)[None],
        hidden_grad[None],
        both_loops(in_low),
        both_loops(out_low),
        sum_mlp,
        sum_gains,
        adapter_first_gradient[None],
        jnp.swapaxes(second_grad, 0, 1)[None],
        adapter_hidden_gradient[None],
        exit_counts,
        mean_confidence,
    )


def solution(mesh):
    return jax.shard_map(
        per_device,
        mesh=mesh,
        in_specs=(
            P("loop", "dp", None),
            P("loop", "dp", None),
            P("dp", None),
            P("dp", None),
            P("dp", None, None),
            P(),
            P("loop", None, None),
            P("loop", None, None),
            P("loop", None, None),
            P("loop", None),
            P("loop", None),
            P("loop", "dp"),
        ),
        out_specs=(
            P("loop", "dp", None),
            P("loop", "dp", None),
            P("dp", None),
            P("dp", None),
            P("dp", None, None),
            P(None, "dp"),
            P("loop", "dp", None),
            P("loop", None, "dp"),
            P("loop", "dp", None),
            P(),
            P(),
        ),
        check_vma=False,
    )
```

```python
import functools

import jax
import jax.numpy as jnp
from jax import lax
from jax.experimental import pallas as pl
from jax.experimental.pallas import tpu as pltpu
from jax.sharding import PartitionSpec as P

MODEL_WIDTH = 2048
HEADS = 8
HEAD_SIZE = 256
ADAPTER_RANK = 256
QUERY_WIDTH = 2048
PROJECTED_WIDTH = 2560


EPSILON = 1e-06
FLOOR_SCORE = -1e30
MESH = pl.DeviceIdType.MESH
VMEM_LIMIT = 60 * 1024 * 1024
LINE_DEVICES = 16


def matrix_product(left, right):
    return jnp.dot(left, right, preferred_element_type=jnp.float32)


def inner_rows(left, right):
    return lax.dot_general(
        left, right, (((0,), (0,)), ((), ())), preferred_element_type=jnp.float32
    )


def outer_columns(left, right):
    return lax.dot_general(
        left, right, (((1,), (1,)), ((), ())), preferred_element_type=jnp.float32
    )


def norm_rows(values, gain):
    return values * lax.rsqrt(jnp.mean(values * values, axis=-1, keepdims=True) + EPSILON) * gain


def rotate(values, positions):
    half_dim = values.shape[-1] // 2
    freqs = 10000.0 ** (-jnp.arange(half_dim, dtype=jnp.float32) / half_dim)
    angles = positions.astype(jnp.float32)[:, None, None] * freqs
    cosine = jnp.cos(angles)
    sine = jnp.sin(angles)
    first_half = values[..., :half_dim]
    second_half = values[..., half_dim:]
    return jnp.concatenate(
        [first_half * cosine - second_half * sine, first_half * sine + second_half * cosine],
        axis=-1,
    )


def rotate_back(grads, positions):

    def turned(values):
        return rotate(values, positions)

    return jax.vjp(turned, jnp.zeros_like(grads))[1](grads)[0]


def geglu(gate_values, up_projection_value):
    return jax.nn.gelu(gate_values, approximate=True) * up_projection_value


def root_mean(values):
    return jnp.sqrt(jnp.mean(values * values, axis=-1) + EPSILON)


def token_facts(row_of_tokens, sequence_length):
    row_total = row_of_tokens.shape[0]
    live_row = row_of_tokens >= 0
    seq_ends = jnp.cumsum(sequence_length)
    seq_index = jnp.sum((row_of_tokens[:, None] >= seq_ends[None, :]).astype(jnp.int32), axis=1)
    seq_starts = seq_ends - sequence_length
    own_start = jnp.sum(
        jnp.where(
            seq_index[:, None] == jnp.arange(sequence_length.shape[0], dtype=jnp.int32)[None, :],
            seq_starts[None, :],
            0,
        ),
        axis=1,
    )
    row_ids = jnp.arange(row_total, dtype=jnp.int32)
    sequence = jnp.where(live_row, seq_index, -1 - row_ids)
    ordering = jnp.where(live_row, row_of_tokens, 0)
    positions = jnp.where(live_row, row_of_tokens - own_start, 0)
    return (live_row, sequence, ordering, positions)


def place(count):
    me = lax.axis_index("dp")
    return me, count // 4, me // 4, (me // 2) % 2, me % 2


def greet(count, across=False):
    me, depth, z, y, c = place(count)
    barrier = pltpu.get_barrier_semaphore()

    def signal(where):
        pl.semaphore_signal(barrier, inc=1, device_id={"dp": where}, device_id_type=MESH)

    signal(me + 1 - 2 * c)
    signal(me + 2 - 4 * y)
    if across:
        other = 1 - lax.axis_index("loop")
        pl.semaphore_signal(barrier, inc=1, device_id={"loop": other}, device_id_type=MESH)

    @pl.when(z > 0)
    def _():
        signal(me - 4)

    @pl.when(z < depth - 1)
    def _():
        signal(me + 4)

    ends = jnp.where((z > 0) & (z < depth - 1), 4, 3)
    pl.semaphore_wait(barrier, ends + 1 if across else ends)


def contract(left, right, left_axis, right_axis):
    return lax.dot_general(
        left,
        right,
        (((left_axis,), (right_axis,)), ((), ())),
        preferred_element_type=jnp.float32,
    )


def gather_plan(count, parts, own, full, keep, recv, send_core, send_pair, send_right, send_left):
    arrays = len(own)
    me, depth, z, y, c = place(count)
    mate = me + 2 - 4 * y

    def rows_of(a, s):
        step = own[a].shape[0] // parts
        return pl.ds(s * step, step)

    def copy(unit, block, target, sem, first=False):
        a, s = unit
        rows = rows_of(a, s)
        return pltpu.make_async_remote_copy(
            src_ref=own[a].at[rows] if first else full[a].at[block, rows],
            dst_ref=full[a].at[block, rows],
            send_sem=sem,
            recv_sem=recv.at[a, block, s],
            device_id={"dp": target},
            device_id_type=MESH,
        )

    def to_core(unit, block, first=False):
        a, s = unit
        return copy(unit, block, me + 1 - 2 * c, send_core.at[a, block // 2, s], first)

    def to_pair(unit, block, first=False):
        a, s = unit
        return copy(unit, block, mate, send_pair.at[a, block // 4, s], first)

    def to_right(unit, block, first=False):
        a, s = unit
        return copy(unit, block, me + 4, send_right.at[a, block // 4, s], first)

    def to_left(unit, block, first=False):
        a, s = unit
        return copy(unit, block, me - 4, send_left.at[a, block // 4, s], first)

    local = [pltpu.make_async_copy(own[a], full[a].at[me], keep.at[a]) for a in range(arrays)]
    units = [(a, s) for a in range(arrays) for s in range(parts)]

    def begin():
        for unit in units:

            @pl.when(z < depth - 1)
            def _(unit=unit):
                to_right(unit, me, True).start()

            @pl.when(z > 0)
            def _(unit=unit):
                to_left(unit, me, True).start()

            to_pair(unit, me, True).start()
            to_core(unit, me, True).start()
        for item in local:
            item.start()

    def from_line(k, unit):
        @pl.when(z - k >= 0)
        def _():
            block = me - 4 * k
            to_right(unit, block).wait_recv()

            @pl.when(z < depth - 1)
            def _():
                to_right(unit, block).start()

            to_pair(unit, block).start()
            to_core(unit, block).start()

        @pl.when(z + k < depth)
        def _():
            block = me + 4 * k
            to_left(unit, block).wait_recv()

            @pl.when(z > 0)
            def _():
                to_left(unit, block).start()

            to_pair(unit, block).start()
            to_core(unit, block).start()

    def pass_on(unit, block):
        to_pair(unit, block).wait_recv()
        to_core(unit, block).start()

    def from_pair(k, unit):
        if k == 0:
            pass_on(unit, mate)
            return

        @pl.when(z - k >= 0)
        def _():
            pass_on(unit, mate - 4 * k)

        @pl.when(z + k < depth)
        def _():
            pass_on(unit, mate + 4 * k)

    def arrive():
        for unit in units:
            for j in range(count // 2):
                to_core(unit, 2 * j + 1 - c).wait_recv()
        for item in local:
            item.wait()

    def finish():
        for unit in units:
            for j in range(count // 2):
                to_core(unit, 2 * j + c).wait_send()
            for j in range(depth):
                block = 4 * j + 2 * y + c
                to_pair(unit, block).wait_send()

                @pl.when((z >= j) & (z < depth - 1))
                def _():
                    to_right(unit, block).wait_send()

                @pl.when((z <= j) & (z > 0))
                def _():
                    to_left(unit, block).wait_send()

    return units, begin, from_line, from_pair, arrive, finish


def gather_sems(count, number, parts):
    depth = count // 4
    sem = pltpu.SemaphoreType.DMA
    return [
        sem((number,)),
        sem((number, count, parts)),
        sem((number, count // 2, parts)),
        sem((number, depth, parts)),
        sem((number, depth, parts)),
        sem((number, depth, parts)),
    ]


def gather_body(count, parts, arrays, *refs):
    depth = count // 4
    greet(count)
    units, begin, from_line, from_pair, arrive, finish = gather_plan(
        count, parts, refs[:arrays], refs[arrays : 2 * arrays], *refs[2 * arrays :]
    )
    begin()
    for k in range(1, depth):
        for unit in units:
            from_line(k, unit)
        for unit in units:
            from_pair(k - 1, unit)
    for unit in units:
        from_pair(depth - 1, unit)
    arrive()
    finish()


def kernel_params(ident):
    return pltpu.CompilerParams(
        collective_id=ident, has_side_effects=True, vmem_limit_bytes=VMEM_LIMIT
    )


def gather_rows(count, ident, *arrays, parts=2):
    if count != LINE_DEVICES:
        return [lax.all_gather(item, "dp", axis=0, tiled=True) for item in arrays]
    number = len(arrays)
    anywhere = pl.BlockSpec(memory_space=pl.ANY)
    full = pl.pallas_call(
        functools.partial(gather_body, count, parts, number),
        out_shape=[
            jax.ShapeDtypeStruct((count,) + item.shape, item.dtype) for item in arrays
        ],
        in_specs=[anywhere] * number,
        out_specs=[anywhere] * number,
        scratch_shapes=gather_sems(count, number, parts),
        compiler_params=kernel_params(ident),
        name="gather_rows",
    )(*arrays)
    return [
        item.reshape((count * item.shape[1],) + item.shape[2:]) for item in full
    ]


def opening_body(count, parts, arrays, *refs):
    own = refs[:arrays]
    weights, factors, first, second = refs[arrays : arrays + 4]
    full = refs[arrays + 4 : 2 * arrays + 4]
    folded = refs[2 * arrays + 4]
    scratch = refs[2 * arrays + 5 :]
    bank, factor_bank, first_bank, second_bank, bank_sem, factor_sem, out_sem = scratch[:7]
    me, depth, z, y, c = place(count)
    rank = ADAPTER_RANK
    width, wide = bank.shape[1:]
    greet(count)
    units, begin, from_line, from_pair, arrive, finish = gather_plan(
        count, parts, own, full, *scratch[7:]
    )
    begin()
    fills = [
        pltpu.make_async_copy(weights.at[i], bank.at[i], bank_sem.at[i]) for i in range(3)
    ]
    sources = [
        pltpu.make_async_copy(
            factors.at[pl.ds(me * width, width)], factor_bank, factor_sem.at[0]
        ),
        pltpu.make_async_copy(
            first.at[:, pl.ds(4 * rank, 2 * rank)], first_bank, factor_sem.at[1]
        ),
        pltpu.make_async_copy(
            second.at[:, pl.ds(PROJECTED_WIDTH + MODEL_WIDTH, wide)], second_bank, factor_sem.at[2]
        ),
    ]
    for item in sources + fills:
        item.start()

    def put(i):
        return pltpu.make_async_copy(bank.at[i], folded.at[i], out_sem.at[i])

    def fold(i):
        high, tile = 256, 512

        def inner(n, carry):
            rows = pl.ds(pl.multiple_of((n // (wide // tile)) * high, high), high)
            cols = pl.ds(pl.multiple_of((n % (wide // tile)) * tile, tile), tile)
            if i == 2:
                extra = contract(factor_bank[rows, :rank], second_bank[:, cols], 1, 0)
            else:
                extra = contract(
                    factor_bank[rows, (i + 1) * rank : (i + 2) * rank],
                    first_bank[cols, i * rank : (i + 1) * rank],
                    1,
                    1,
                )
            bank[i, rows, cols] = (bank[i, rows, cols].astype(jnp.float32) + extra).astype(
                bank.dtype
            )
            return carry

        lax.fori_loop(0, (width // high) * (wide // tile), inner, 0)
        put(i).start()

    for item in sources:
        item.wait()
    fills[0].wait()
    fold(0)
    for k in range(1, depth):
        for unit in units:
            from_line(k, unit)
        if k < 3:
            fills[k].wait()
            fold(k)
        for unit in units:
            from_pair(k - 1, unit)
    for unit in units:
        from_pair(depth - 1, unit)
    arrive()
    finish()
    for i in range(3):
        put(i).wait()


def opening(count, ident, arrays, weights, factors, first, second, parts=2):
    number = len(arrays)
    _, width, wide = weights.shape
    low = jnp.bfloat16
    sem = pltpu.SemaphoreType.DMA
    anywhere = pl.BlockSpec(memory_space=pl.ANY)
    out = pl.pallas_call(
        functools.partial(opening_body, count, parts, number),
        out_shape=[
            jax.ShapeDtypeStruct((count,) + item.shape, item.dtype) for item in arrays
        ]
        + [jax.ShapeDtypeStruct(weights.shape, low)],
        in_specs=[anywhere] * (number + 4),
        out_specs=[anywhere] * (number + 1),
        scratch_shapes=[
            pltpu.VMEM(weights.shape, low),
            pltpu.VMEM((width, factors.shape[1]), low),
            pltpu.VMEM((wide, 2 * ADAPTER_RANK), low),
            pltpu.VMEM((ADAPTER_RANK, wide), low),
            sem((3,)),
            sem((3,)),
            sem((3,)),
        ]
        + gather_sems(count, number, parts),
        compiler_params=kernel_params(ident),
        name="opening",
    )(*arrays, weights, factors, first, second)
    return [
        item.reshape((count * item.shape[1],) + item.shape[2:]) for item in out[:number]
    ] + [out[number]]


def scatter_body(count, parts, arrays, *refs):
    terms = refs[:arrays]
    total = refs[arrays : 2 * arrays]
    scratch = refs[2 * arrays :]
    held, loaded, core_in, pair_in, line_in = [
        scratch[i * arrays : (i + 1) * arrays] for i in range(5)
    ]
    (load_sem, core_send, core_recv, pair_send, pair_recv, line_send, line_recv) = scratch[
        5 * arrays :
    ]
    me, depth, z, y, c = place(count)
    greet(count)
    near = z < depth // 2

    def turn(k):
        even = depth - 1 - k // 2 if k % 2 == 0 else k // 2
        return jnp.where(near, even, depth - 1 - even)

    def rows_of(a, s):
        step = terms[a].shape[1] // parts[a]
        return pl.ds(s * step, step)

    def to_core(a, s, line, pair):
        slot = 2 * line + pair
        return pltpu.make_async_remote_copy(
            src_ref=terms[a].at[2 * slot + 1 - c, rows_of(a, s)],
            dst_ref=core_in[a].at[slot, rows_of(a, s)],
            send_sem=core_send.at[a, slot, s],
            recv_sem=core_recv.at[a, slot, s],
            device_id={"dp": me + 1 - 2 * c},
            device_id_type=MESH,
        )

    def load(a, s, line, pair):
        slot = 2 * line + pair
        return pltpu.make_async_copy(
            terms[a].at[2 * slot + c, rows_of(a, s)],
            loaded[a].at[slot, rows_of(a, s)],
            load_sem.at[a, slot, s],
        )

    def to_pair(a, s, line):
        return pltpu.make_async_remote_copy(
            src_ref=loaded[a].at[2 * line + 1 - y, rows_of(a, s)],
            dst_ref=pair_in[a].at[line, rows_of(a, s)],
            send_sem=pair_send.at[a, line, s],
            recv_sem=pair_recv.at[a, line, s],
            device_id={"dp": me + 2 - 4 * y},
            device_id_type=MESH,
        )

    def along(a, s, line, slot, target):
        return pltpu.make_async_remote_copy(
            src_ref=loaded[a].at[2 * line + y, rows_of(a, s)],
            dst_ref=line_in[a].at[slot, rows_of(a, s)],
            send_sem=line_send.at[a, line, s],
            recv_sem=line_recv.at[a, slot, s],
            device_id={"dp": target},
            device_id_type=MESH,
        )

    def to_right(a, s, line):
        return along(a, s, line, line, me + 4)

    def to_left(a, s, line):
        return along(a, s, line, jnp.where(line == z - 1, depth, line), me - 4)

    def from_right(a, s, line):
        return along(a, s, line, jnp.where(line == z, depth, line), me)

    order = [turn(k) for k in range(depth)]
    units = [(a, s) for a in range(arrays) for s in range(parts[a])]
    for pair in (1 - y, y):
        for line in order:
            for a, s in units:
                to_core(a, s, line, pair).start()
                load(a, s, line, pair).start()

    for line in order:
        for a, s in units:
            slot = 2 * line + 1 - y
            rows = rows_of(a, s)
            load(a, s, line, 1 - y).wait()
            to_core(a, s, line, 1 - y).wait_recv()
            loaded[a][slot, rows] = loaded[a][slot, rows] + core_in[a][slot, rows]
            to_pair(a, s, line).start()

    def own_sum(a, s, line):
        slot = 2 * line + y
        rows = rows_of(a, s)
        load(a, s, line, y).wait()
        to_core(a, s, line, y).wait_recv()
        to_pair(a, s, line).wait_recv()
        part = loaded[a][slot, rows].astype(jnp.float32)
        part += core_in[a][slot, rows].astype(jnp.float32)
        held[a][...] = part + pair_in[a][line, rows].astype(jnp.float32)

    def add_line(a, s, slot):
        along(a, s, z, slot, me).wait_recv()
        held[a][...] += line_in[a][slot, rows_of(a, s)].astype(jnp.float32)

    for line in order:
        for a, s in units:

            @pl.when(line != z)
            def _(a=a, s=s, line=line):
                own_sum(a, s, line)

                @pl.when(((line > z) & (z > 0)) | ((line < z) & (z < depth - 1)))
                def _():
                    add_line(a, s, line)

                loaded[a][2 * line + y, rows_of(a, s)] = held[a][...].astype(loaded[a].dtype)

                @pl.when(line > z)
                def _():
                    to_right(a, s, line).start()

                @pl.when(line < z)
                def _():
                    to_left(a, s, line).start()

    for a, s in units:
        own_sum(a, s, z)

        @pl.when(z > 0)
        def _(a=a, s=s):
            add_line(a, s, z)

        @pl.when(z < depth - 1)
        def _(a=a, s=s):
            add_line(a, s, depth)

        total[a][rows_of(a, s)] = held[a][...]

    for a, s in units:
        for line in range(depth):
            for pair in range(2):
                to_core(a, s, line, pair).wait_send()
            to_pair(a, s, line).wait_send()

            @pl.when(z != line)
            def _():
                to_right(a, s, line).wait_send()


def scatter_rows(count, ident, *arrays):
    if count != LINE_DEVICES:
        return [
            lax.psum_scatter(
                item.astype(jnp.float32), "dp", scatter_dimension=0, tiled=True
            )
            for item in arrays
        ]
    depth = count // 4
    number = len(arrays)
    blocks = [
        item.reshape(count, item.shape[0] // count, item.shape[1]) for item in arrays
    ]
    parts = [2 if item.shape[1] % 32 == 0 and item.shape[1] > 32 else 1 for item in blocks]
    most = max(parts)

    def room(slots):
        return [pltpu.VMEM((slots,) + item.shape[1:], item.dtype) for item in blocks]

    def sems(slots):
        return pltpu.SemaphoreType.DMA((number, slots, most))

    return pl.pallas_call(
        functools.partial(scatter_body, count, parts, number),
        out_shape=[jax.ShapeDtypeStruct(item.shape[1:], jnp.float32) for item in blocks],
        in_specs=[pl.BlockSpec(memory_space=pl.ANY)] * number,
        out_specs=[pl.BlockSpec(memory_space=pltpu.VMEM)] * number,
        scratch_shapes=[
            pltpu.VMEM((item.shape[1] // part, item.shape[2]), jnp.float32)
            for item, part in zip(blocks, parts)
        ]
        + room(2 * depth)
        + room(2 * depth)
        + room(depth)
        + room(depth + 1)
        + [
            sems(2 * depth),
            sems(2 * depth),
            sems(2 * depth),
            sems(depth),
            sems(depth),
            sems(depth),
            sems(depth + 1),
        ],
        compiler_params=kernel_params(ident),
        name="scatter_rows",
    )(*blocks)


FAR_TILES = 3


def line_order(z):
    near = z < 2
    return [z, z + 1 - 2 * (z % 2), jnp.where(near, 2, 1), jnp.where(near, 3, 0)]


def unit_values(gate, up, grad):
    slope = 0.7978845608028654
    cubic = 0.044715
    square = gate * gate
    curve = jnp.tanh(slope * (gate + cubic * square * gate))
    half = 0.5 * (1.0 + curve)
    turned = gate * half
    rise = half + 0.5 * gate * (1.0 - curve * curve) * slope * (1.0 + 3.0 * cubic * square)
    low = jnp.bfloat16
    return (turned * up).astype(low), (grad * up * rise).astype(low), (grad * turned).astype(low)


def hidden_body(count, parts, own, grads, weights, units, gate_grads, up_grads, rows_out,
                held, bank, coming, done, recv, send_core, send_pair, send_line, keep, bank_sem,
                coming_sem, done_sem, rows_sem):
    me, depth, z, y, c = place(count)
    height = own.shape[0]
    width = bank.shape[1]
    step = height // parts
    tile = 512
    core, mate = me + 1 - 2 * c, me + 2 - 4 * y
    lines = line_order(z)
    greet(count)

    def hop(block, s, target, sem, first=False):
        rows = pl.ds(s * step, step)
        return pltpu.make_async_remote_copy(
            src_ref=own.at[rows] if first else held.at[block, rows],
            dst_ref=held.at[block, rows],
            send_sem=sem,
            recv_sem=recv.at[block, s],
            device_id={"dp": target},
            device_id_type=MESH,
        )

    def to_core(block, s, first=False):
        return hop(block, s, core, send_core.at[block // 2, s], first)

    def to_pair(block, s, first=False):
        return hop(block, s, mate, send_pair.at[block // 4, s], first)

    def to_right(block, s, first=False):
        return hop(block, s, me + 4, send_line.at[0, block // 4, s], first)

    def to_left(block, s, first=False):
        return hop(block, s, me - 4, send_line.at[1, block // 4, s], first)

    for s in range(parts):

        @pl.when(z > 0)
        def _():
            to_left(me, s, True).start()

        @pl.when(z < depth - 1)
        def _():
            to_right(me, s, True).start()

        to_core(me, s, True).start()
        to_pair(me, s, True).start()
    mine = pltpu.make_async_copy(own, held.at[me], keep)
    mine.start()
    fills = [
        pltpu.make_async_copy(weights.at[i], bank.at[i], bank_sem.at[i]) for i in range(3)
    ]
    for fill in fills:
        fill.start()

    def first_of(line, pair):
        return 4 * line + 2 * pair

    def fetch(line, pair, slot):
        return pltpu.make_async_copy(
            grads.at[pl.ds(first_of(line, pair), 2)], coming.at[slot], coming_sem.at[slot]
        )

    def store(line, pair, slot):
        rows = pl.ds(first_of(line, pair) * height, 2 * height)
        return [
            pltpu.make_async_copy(done.at[slot, i], out.at[rows], done_sem.at[slot, i])
            for i, out in enumerate((units, gate_grads, up_grads))
        ]

    def keep_rows(line, pair):
        some = pl.ds(first_of(line, pair), 2)
        return pltpu.make_async_copy(held.at[some], rows_out.at[some], rows_sem.at[line, pair])

    def from_line(line):
        block = first_of(line, y) + c
        for s in range(parts):
            hop(block, s, core, send_core.at[block // 2, s]).wait_recv()

            @pl.when((line < z) & (z < depth - 1))
            def _():
                to_right(block, s).start()

            @pl.when((line > z) & (z > 0))
            def _():
                to_left(block, s).start()

            to_pair(block, s).start()
            to_core(block, s).start()

    def from_pair(line):
        block = first_of(line, 1 - y) + c
        for s in range(parts):
            to_core(block, s).wait_recv()
            to_core(block, s).start()

    steps = [(line, pair) for line in lines for pair in (y, 1 - y)]

    def work(index):
        line, pair = steps[index]
        slot = index % 2
        for s in range(parts):
            to_core(first_of(line, pair) + 1 - c, s).wait_recv()
        if index == 0:
            mine.wait()
            fetch(line, pair, slot).start()
            for fill in fills:
                fill.wait()
        if index + 1 < len(steps):
            fetch(*steps[index + 1], 1 - slot).start()
        fetch(line, pair, slot).wait()
        keep_rows(line, pair).start()
        if index >= 2:
            for item in store(*steps[index - 2], slot):
                item.wait()
        some = pl.ds(first_of(line, pair), 2)

        def inner(n, carry):
            cols = pl.ds(pl.multiple_of(n * tile, tile), tile)
            block = held[some].reshape(2 * height, held.shape[2])
            gate = contract(block, bank[0, cols], 1, 1)
            up = contract(block, bank[1, cols], 1, 1)
            grad = contract(coming[slot].reshape(2 * height, held.shape[2]), bank[2, cols], 1, 1)
            for i, value in enumerate(unit_values(gate, up, grad)):
                done[slot, i, :, cols] = value
            return carry

        lax.fori_loop(0, width // tile, inner, 0)
        for item in store(line, pair, slot):
            item.start()

    work(0)
    from_pair(lines[0])
    from_line(lines[1])
    work(1)
    for k in range(1, depth):
        from_pair(lines[k])
        work(2 * k)
        if k + 1 < depth:
            from_line(lines[k + 1])
        work(2 * k + 1)

    for index in (len(steps) - 2, len(steps) - 1):
        for item in store(*steps[index], index % 2):
            item.wait()
    for line, pair in steps:
        keep_rows(line, pair).wait()
    for j in range(depth):
        block = first_of(j, y) + c
        for s in range(parts):
            to_core(block, s).wait_send()
            to_core(first_of(j, 1 - y) + c, s).wait_send()
            to_pair(block, s).wait_send()

            @pl.when((z >= j) & (z < depth - 1))
            def _():
                to_right(block, s).wait_send()

            @pl.when((z <= j) & (z > 0))
            def _():
                to_left(block, s).wait_send()


def hidden_units(count, ident, own, grads, weights, parts=2):
    height, wide = own.shape
    width = weights.shape[1]
    depth = count // 4
    low = jnp.bfloat16
    sem = pltpu.SemaphoreType.DMA
    anywhere = pl.BlockSpec(memory_space=pl.ANY)
    acts = jax.ShapeDtypeStruct((count * height, width), low)
    return pl.pallas_call(
        functools.partial(hidden_body, count, parts),
        out_shape=[acts, acts, acts, jax.ShapeDtypeStruct((count, height, wide), low)],
        in_specs=[anywhere] * 3,
        out_specs=[anywhere] * 4,
        scratch_shapes=[
            pltpu.VMEM((count, height, wide), low),
            pltpu.VMEM((3, width, wide), low),
            pltpu.VMEM((2, 2, height, wide), low),
            pltpu.VMEM((2, 3, 2 * height, width), low),
            sem((count, parts)),
            sem((2 * depth, parts)),
            sem((depth, parts)),
            sem((2, depth, parts)),
            sem,
            sem((3,)),
            sem((2,)),
            sem((2, 3)),
            sem((depth, 2)),
        ],
        compiler_params=kernel_params(ident),
        name="hidden_units",
    )(own, grads, weights)


def unit_grads_body(count, parts, units, gate_grads, up_grads, weights, rows_all, grads_all,
                    input_sum, output_sum, gate_out, up_out, down_out, gate_far,
                    bank, rows_in, units_in, made, held, loaded, leaving, core_in, pair_in,
                    line_in, bank_sem, rows_sem, fill_sems, units_sem, made_sem, core_send, core_recv,
                    pair_send, pair_recv, line_send, line_recv,
                    far_send, far_recv):
    me, depth, z, y, c = place(count)
    height, wide = input_sum.shape
    width = weights.shape[1]
    step = height // parts
    low = jnp.bfloat16
    core, mate = me + 1 - 2 * c, me + 2 - 4 * y
    near = z < 2
    order = [jnp.where(near, 3, 0), jnp.where(near, 0, 3), jnp.where(near, 2, 1),
             jnp.where(near, 1, 2)]
    greet(count, True)

    def fill(source, at):
        return pltpu.make_async_copy(source, bank.at[at], bank_sem.at[at])

    blocks = width // height

    def fill_rows(source, half, at):
        return [
            pltpu.make_async_copy(
                source.at[half * blocks + i],
                bank.at[at, pl.ds(i * height, height)],
                fill_sems.at[at, i],
            )
            for i in range(blocks)
        ]

    first_fills = [fill(weights.at[i], i) for i in range(3)]
    for item in first_fills:
        item.start()
    grad_tail = fill_rows(grads_all, 1, 3)
    steps = [(line, pair) for line in order for pair in (1 - y, y)]

    def fetch(line, pair, slot, sources):
        rows = pl.ds((4 * line + 2 * pair) * height, 2 * height)
        return [
            pltpu.make_async_copy(source.at[rows], rows_in.at[slot, i], rows_sem.at[slot, i])
            for i, source in enumerate(sources)
        ]

    def rows_of(s):
        return pl.ds(s * step, step)

    def to_core(a, line, pair, slot, s):
        at = 2 * line + pair
        return pltpu.make_async_remote_copy(
            src_ref=leaving.at[a, slot, rows_of(s)],
            dst_ref=core_in.at[a, at, rows_of(s)],
            send_sem=core_send.at[a, slot, s],
            recv_sem=core_recv.at[a, at, s],
            device_id={"dp": core},
            device_id_type=MESH,
        )

    def to_pair(a, line, s):
        return pltpu.make_async_remote_copy(
            src_ref=loaded.at[a, 2 * line + 1 - y, rows_of(s)],
            dst_ref=pair_in.at[a, line, rows_of(s)],
            send_sem=pair_send.at[a, line, s],
            recv_sem=pair_recv.at[a, line, s],
            device_id={"dp": mate},
            device_id_type=MESH,
        )

    def along(a, line, slot, s, target):
        return pltpu.make_async_remote_copy(
            src_ref=loaded.at[a, 2 * line + y, rows_of(s)],
            dst_ref=line_in.at[a, slot, rows_of(s)],
            send_sem=line_send.at[a, line, s],
            recv_sem=line_recv.at[a, slot, s],
            device_id={"dp": target},
            device_id_type=MESH,
        )

    def product(a, index):
        line, pair = steps[index]
        slot = index % 2
        sources = (gate_grads, up_grads) if a == 0 else (units,)
        if index == 0:
            for item in fetch(line, pair, slot, sources):
                item.start()
        if index + 1 < len(steps):
            for item in fetch(*steps[index + 1], 1 - slot, sources):
                item.start()
        if index >= 2:
            for s in range(parts):
                to_core(a, *steps[index - 2], slot, s).wait_send()
        for item in fetch(line, pair, slot, sources):
            item.wait()
        tile = 512

        def inner(n, carry):
            cols = pl.ds(pl.multiple_of(n * tile, tile), tile)
            if a == 0:
                value = contract(rows_in[slot, 0], bank[0, :, cols], 1, 0)
                value += contract(rows_in[slot, 1], bank[1, :, cols], 1, 0)
            else:
                value = contract(rows_in[slot, 0], bank[2, :, cols], 1, 0)
            value = value.astype(low)

            @pl.when(c == 0)
            def _():
                loaded[a, 2 * line + pair, :, cols] = value[:height]
                leaving[a, slot, :, cols] = value[height:]

            @pl.when(c == 1)
            def _():
                loaded[a, 2 * line + pair, :, cols] = value[height:]
                leaving[a, slot, :, cols] = value[:height]

            return carry

        lax.fori_loop(0, wide // tile, inner, 0)
        for s in range(parts):
            to_core(a, line, pair, slot, s).start()

    def finish_sends(a):
        for index in (len(steps) - 2, len(steps) - 1):
            for s in range(parts):
                to_core(a, *steps[index], index % 2, s).wait_send()

    def pair_step(a, k):
        line = order[k]
        at = 2 * line + 1 - y
        for s in range(parts):
            to_core(a, line, 1 - y, 0, s).wait_recv()
            loaded[a, at, rows_of(s)] = loaded[a, at, rows_of(s)] + core_in[a, at, rows_of(s)]
            to_pair(a, line, s).start()

    def own_sum(a, line, s):
        at = 2 * line + y
        to_core(a, line, y, 0, s).wait_recv()
        to_pair(a, line, s).wait_recv()
        part = loaded[a, at, rows_of(s)].astype(jnp.float32)
        part += core_in[a, at, rows_of(s)].astype(jnp.float32)
        held[...] = part + pair_in[a, line, rows_of(s)].astype(jnp.float32)

    def add_line(a, slot, s):
        along(a, z, slot, s, me + 4).wait_recv()
        held[...] += line_in[a, slot, rows_of(s)].astype(jnp.float32)

    def line_step(a, k):
        line = order[k]

        @pl.when(line != z)
        def _():
            for s in range(parts):
                own_sum(a, line, s)

                @pl.when(((line > z) & (z > 0)) | ((line < z) & (z < depth - 1)))
                def _():
                    add_line(a, line, s)

                loaded[a, 2 * line + y, rows_of(s)] = held[...].astype(low)

                @pl.when(line > z)
                def _():
                    along(a, line, line, s, me + 4).start()

                @pl.when(line < z)
                def _():
                    along(a, line, jnp.where(line == z - 1, depth, line), s, me - 4).start()

    def last_step(a, total):
        for s in range(parts):
            own_sum(a, z, s)

            @pl.when(z > 0)
            def _():
                add_line(a, z, s)

            @pl.when(z < depth - 1)
            def _():
                add_line(a, depth, s)

            total[rows_of(s)] = held[...]

    tall = units_in.shape[2]
    each = width // tall

    def bring(g, slot):
        source = (gate_grads, up_grads, units)[g // each]
        cols = pl.ds((g % each) * tall, tall)
        return pltpu.make_async_copy(source.at[:, cols], units_in.at[slot], units_sem.at[slot])

    def put(g, slot):
        rows = pl.ds((g % each) * tall, tall)
        return pltpu.make_async_copy(
            made.at[slot], (gate_out, up_out, down_out)[g // each].at[rows], made_sem.at[slot]
        )

    def swap(g):
        rows = pl.ds(g * tall, tall)
        return pltpu.make_async_remote_copy(
            src_ref=gate_out.at[rows],
            dst_ref=gate_far.at[rows],
            send_sem=far_send.at[g],
            recv_sem=far_recv.at[g],
            device_id={"loop": 1 - lax.axis_index("loop")},
            device_id_type=MESH,
        )

    number = 3 * each

    def weight_product(g):
        slot = g % 2
        if g + 1 < number:
            bring(g + 1, 1 - slot).start()
        bring(g, slot).wait()
        if g >= 2:
            put(g - 2, slot).wait()
            if g - 2 < FAR_TILES:
                swap(g - 2).start()
        at = 0 if g < 2 * each else 2
        tile = 512

        def inner(n, carry):
            cols = pl.ds(pl.multiple_of(n * tile, tile), tile)
            whole = bank[at : at + 2, :, cols].reshape(2 * width, tile)
            made[slot, :, cols] = contract(units_in[slot], whole, 0, 0).astype(low)
            return carry

        lax.fori_loop(0, wide // tile, inner, 0)
        put(g, slot).start()

    for item in first_fills[:2]:
        item.wait()
    for index in range(8):
        product(0, index)
        if index >= 2 and index % 2 == 0:
            pair_step(0, index // 2 - 1)
    finish_sends(0)
    row_fills = fill_rows(rows_all, 0, 0) + fill_rows(rows_all, 1, 1)
    for item in row_fills:
        item.start()
    for item in grad_tail:
        item.start()
    bring(0, 0).start()
    first_fills[2].wait()
    product(1, 0)
    pair_step(0, 3)
    product(1, 1)
    for item in row_fills:
        item.wait()
    weight_product(0)
    weight_product(1)
    line_step(0, 0)
    weight_product(2)
    weight_product(3)
    line_step(0, 1)
    for index in range(2, 8):
        product(1, index)
        if index % 2 == 0:
            pair_step(1, index // 2 - 1)
        if index == 6:
            line_step(0, 2)
    finish_sends(1)
    grad_fills = fill_rows(grads_all, 0, 2)
    for item in grad_fills:
        item.start()
    weight_product(4)
    pair_step(1, 3)
    line_step(0, 3)
    weight_product(5)
    last_step(0, input_sum)
    weight_product(6)
    weight_product(7)
    line_step(1, 0)
    for item in grad_tail + grad_fills:
        item.wait()
    weight_product(8)
    weight_product(9)
    line_step(1, 1)
    weight_product(10)
    weight_product(11)
    line_step(1, 2)
    line_step(1, 3)
    last_step(1, output_sum)

    for g in (number - 2, number - 1):
        put(g, g % 2).wait()
    for g in range(FAR_TILES):
        swap(g).wait()
    for a in range(2):
        for line in range(depth):
            for s in range(parts):
                to_pair(a, line, s).wait_send()

                @pl.when(z != line)
                def _():
                    along(a, line, line, s, me + 4).wait_send()


def unit_grads(count, ident, units, gate_grads, up_grads, weights, rows_all, grads_all, parts=2):
    width, wide = weights.shape[1:]
    height = rows_all.shape[1]
    depth = count // 4
    low = jnp.bfloat16
    sem = pltpu.SemaphoreType.DMA
    anywhere = pl.BlockSpec(memory_space=pl.ANY)
    inside = pl.BlockSpec(memory_space=pltpu.VMEM)
    total = jax.ShapeDtypeStruct((height, wide), jnp.float32)

    return pl.pallas_call(
        functools.partial(unit_grads_body, count, parts),
        out_shape=[total, total] + [jax.ShapeDtypeStruct((width, wide), low)] * 3
        + [jax.ShapeDtypeStruct((FAR_TILES * 256, wide), low)],
        in_specs=[anywhere] * 6,
        out_specs=[inside, inside] + [anywhere] * 4,
        scratch_shapes=[
            pltpu.VMEM((4, width, wide), low),
            pltpu.VMEM((2, 2, 2 * height, width), low),
            pltpu.VMEM((2, count * height, 256), low),
            pltpu.VMEM((2, 256, wide), low),
            pltpu.VMEM((height // parts, wide), jnp.float32),
            pltpu.VMEM((2, 2 * depth, height, wide), low),
            pltpu.VMEM((2, 2, height, wide), low),
            pltpu.VMEM((2, 2 * depth, height, wide), low),
            pltpu.VMEM((2, depth, height, wide), low),
            pltpu.VMEM((2, depth + 1, height, wide), low),
            sem((4,)),
            sem((2, 2)),
            sem((4, width // height)),
            sem((2,)),
            sem((2,)),
            sem((2, 2, parts)),
            sem((2, 2 * depth, parts)),
            sem((2, depth, parts)),
            sem((2, depth, parts)),
            sem((2, depth, parts)),
            sem((2, depth + 1, parts)),
            sem((FAR_TILES,)),
            sem((FAR_TILES,)),
        ],
        compiler_params=kernel_params(ident),
        name="unit_grads",
    )(units, gate_grads, up_grads, weights, rows_all, grads_all)


OUT_SPLIT = 1536


def sum_plan(count, parts, mine, theirs, core_in, pair_in, line_in, sems):
    me, depth, z, y, c = place(count)
    core_send, core_recv, pair_send, pair_recv, line_send, line_recv = sems
    rows = core_in.shape[1]
    step = rows // parts
    near = z < 2
    order = [
        jnp.where(near, 3, 0),
        jnp.where(near, 0, 3),
        jnp.where(near, 2, 1),
        jnp.where(near, 1, 2),
    ]

    def rows_of(s):
        return pl.ds(s * step, step)

    def to_core(line, pair, s):
        at = 2 * line + pair
        return pltpu.make_async_remote_copy(
            src_ref=theirs(at, rows_of(s)),
            dst_ref=core_in.at[at, rows_of(s)],
            send_sem=core_send.at[at, s],
            recv_sem=core_recv.at[at, s],
            device_id={"dp": me + 1 - 2 * c},
            device_id_type=MESH,
        )

    def to_pair(line, s):
        return pltpu.make_async_remote_copy(
            src_ref=mine(2 * line + 1 - y, rows_of(s)),
            dst_ref=pair_in.at[line, rows_of(s)],
            send_sem=pair_send.at[line, s],
            recv_sem=pair_recv.at[line, s],
            device_id={"dp": me + 2 - 4 * y},
            device_id_type=MESH,
        )

    def along(line, slot, s, target):
        return pltpu.make_async_remote_copy(
            src_ref=mine(2 * line + y, rows_of(s)),
            dst_ref=line_in.at[slot, rows_of(s)],
            send_sem=line_send.at[line, s],
            recv_sem=line_recv.at[slot, s],
            device_id={"dp": target},
            device_id_type=MESH,
        )

    def send_core(line, pair):
        for s in range(parts):
            to_core(line, pair, s).start()

    def pair_step(k):
        line = order[k]
        at = 2 * line + 1 - y
        for s in range(parts):
            to_core(line, 1 - y, s).wait_recv()
            block = mine(at, rows_of(s))
            block[...] = block[...] + core_in[at, rows_of(s)]
            to_pair(line, s).start()

    def own_sum(line, s):
        at = 2 * line + y
        to_core(line, y, s).wait_recv()
        to_pair(line, s).wait_recv()
        part = mine(at, rows_of(s))[...].astype(jnp.float32)
        part += core_in[at, rows_of(s)].astype(jnp.float32)
        return part + pair_in[line, rows_of(s)].astype(jnp.float32)

    def line_step(k):
        line = order[k]

        @pl.when(line != z)
        def _():
            for s in range(parts):
                block = mine(2 * line + y, rows_of(s))
                follows = ((line > z) & (z > 0)) | ((line < z) & (z < depth - 1))
                part = own_sum(line, s)

                @pl.when(follows)
                def _():
                    along(z, line, s, me + 4).wait_recv()
                    extra = line_in[line, rows_of(s)].astype(jnp.float32)
                    block[...] = (part + extra).astype(block.dtype)

                @pl.when(jnp.logical_not(follows))
                def _():
                    block[...] = part.astype(block.dtype)

                @pl.when(line > z)
                def _():
                    along(line, line, s, me + 4).start()

                @pl.when(line < z)
                def _():
                    along(line, jnp.where(line == z - 1, depth, line), s, me - 4).start()

    def last_step(total):
        for s in range(parts):
            total[rows_of(s)] = own_sum(z, s)

            @pl.when(z > 0)
            def _():
                along(z, z, s, me + 4).wait_recv()
                total[rows_of(s)] += line_in[z, rows_of(s)].astype(jnp.float32)

            @pl.when(z < depth - 1)
            def _():
                along(z, depth, s, me + 4).wait_recv()
                total[rows_of(s)] += line_in[depth, rows_of(s)].astype(jnp.float32)

    def finish():
        for line in range(depth):
            for s in range(parts):
                for pair in range(2):
                    to_core(line, pair, s).wait_send()
                to_pair(line, s).wait_send()

                @pl.when(z != line)
                def _():
                    along(line, line, s, me + 4).wait_send()

    return order, send_core, pair_step, line_step, last_step, finish


def sum_sems(count, parts):
    depth = count // 4
    sem = pltpu.SemaphoreType.DMA
    return [
        sem((2 * depth, parts)),
        sem((2 * depth, parts)),
        sem((depth, parts)),
        sem((depth, parts)),
        sem((depth, parts)),
        sem((depth + 1, parts)),
    ]


def sum_rooms(count, rows, cols, kind=jnp.bfloat16):
    depth = count // 4
    return [
        pltpu.VMEM((2 * depth, rows, cols), kind),
        pltpu.VMEM((depth, rows, cols), kind),
        pltpu.VMEM((depth + 1, rows, cols), kind),
    ]


def sum_terms(count, parts, terms, rooms, sems):
    me, depth, z, y, c = place(count)

    def mine(at, rows):
        return terms.at[2 * at + c, rows]

    def theirs(at, rows):
        return terms.at[2 * at + 1 - c, rows]

    return sum_plan(count, parts, mine, theirs, *rooms, sems)


def turn_back(values, cosine, sine):
    half = values.shape[-1] // 2
    first, second = values[:, :half], values[:, half:]
    return jnp.concatenate(
        [first * cosine + second * sine, second * cosine - first * sine], axis=1
    )


def attention_grads_body(count, attended, grad_rows, weight, queries, keys_values, level,
                         cosine, sine, own_seq, own_order, all_seq, all_order,
                         joint_grads, out_sum,
                         weight_in, grad_att, allowed, kv_total, kv_terms, kv_sum, out_terms,
                         out_core, out_pair, out_line, kv_core, kv_pair, kv_line,
                         weight_sem, *sems):
    me, depth, z, y, c = place(count)
    height, wide = grad_rows.shape
    size = HEAD_SIZE
    scale = size ** (-0.5)
    low = jnp.bfloat16
    greet(count)
    load = pltpu.make_async_copy(weight, weight_in, weight_sem)
    load.start()
    order, send_out, pair_out, line_out, last_out, finish_out = sum_terms(
        count, 2, out_terms, (out_core, out_pair, out_line), sems[:6]
    )
    _, send_kv, pair_kv, line_kv, last_kv, finish_kv = sum_terms(
        count, 1, kv_terms, (kv_core, kv_pair, kv_line), sems[6:]
    )
    feature, some = out_terms.shape[1:]

    def out_product(line):
        def inner(n, carry):
            into = pl.ds(pl.multiple_of(n * 512, 512), 512)
            cols = pl.ds(pl.multiple_of(line * 4 * feature, 4 * feature), 4 * feature)
            value = contract(attended[:, cols], grad_rows[:, into], 0, 0).astype(low)
            out_terms[pl.ds(4 * line, 4), :, into] = value.reshape(4, feature, 512)
            return carry

        lax.fori_loop(0, some // 512, inner, 0)
        for pair in (1 - y, y):
            send_out(line, pair)

    for line in order:
        out_product(line)
    load.wait()
    tile = 256

    def product(n, carry):
        cols = pl.ds(pl.multiple_of(n * tile, tile), tile)
        grad_att[:, cols] = contract(grad_rows[...], weight_in[cols], 1, 1).astype(low)
        return carry

    lax.fori_loop(0, wide // tile, product, 0)
    same = own_seq[...] == all_seq[...]
    allowed[...] = jnp.where(same & (all_order[...] <= own_order[...]), 1.0, 0.0)
    for k in range(depth):
        pair_out(k)
    keys = keys_values[:, :size]
    values = keys_values[:, size:]

    def heads(pair):
        def both(ref):
            return jnp.concatenate(
                [
                    ref[:, 2 * pair * size : (2 * pair + 1) * size],
                    ref[:, (2 * pair + 1) * size : (2 * pair + 2) * size],
                ],
                axis=0,
            )

        query = both(queries)
        grad = both(grad_att)
        keep = jnp.concatenate([allowed[...], allowed[...]], axis=0) > 0.5
        scores = jnp.where(keep, contract(query, keys, 1, 1) * scale, FLOOR_SCORE)
        prob = jnp.exp(scores - level[pair][:, :1])
        grad_prob = contract(grad, values, 1, 1)
        centre = jnp.sum(prob * grad_prob, axis=-1, keepdims=True)
        grad_scores = (prob * (grad_prob - centre)).astype(low)
        back = contract(grad_scores, keys, 1, 0) * scale
        for i in range(2):
            part = turn_back(back[i * height : (i + 1) * height], cosine[...], sine[...])
            joint_grads[:, (2 * pair + i) * size : (2 * pair + i + 1) * size] = part.astype(low)
        key_part = contract(grad_scores, query, 0, 0) * scale
        value_part = contract(prob.astype(low), grad, 0, 0)
        if pair == 0:
            kv_total[:, :size] = key_part
            kv_total[:, size:] = value_part
        else:
            kv_total[:, :size] += key_part
            kv_total[:, size:] += value_part

    for pair in range(wide // size // 2):
        heads(pair)
    for block in range(count):
        kv_terms[block] = kv_total[block * height : (block + 1) * height].astype(low)
    for pair in (1 - y, y):
        for line in order:
            send_kv(line, pair)
    for k in range(depth):
        pair_kv(k)
    for k in range(depth):
        line_out(k)
    for k in range(depth):
        line_kv(k)
    last_kv(kv_sum)
    part = turn_back(kv_sum[:, :size], cosine[...], sine[...])
    joint_grads[:, wide : wide + size] = part.astype(low)
    joint_grads[:, wide + size :] = kv_sum[:, size:].astype(low)
    last_out(out_sum)
    finish_out()
    finish_kv()


def attention_grads(count, ident, attended, grad_rows, weight, queries, keys_values, level,
                    cosine, sine, own_seq, own_order, all_seq, all_order):
    height, wide = grad_rows.shape
    total = keys_values.shape[0]
    low = jnp.bfloat16
    inside = pl.BlockSpec(memory_space=pltpu.VMEM)
    anywhere = pl.BlockSpec(memory_space=pl.ANY)
    feature = attended.shape[1] // count
    both = 2 * HEAD_SIZE
    return pl.pallas_call(
        functools.partial(attention_grads_body, count),
        out_shape=[
            jax.ShapeDtypeStruct((height, wide + both), low),
            jax.ShapeDtypeStruct((feature, OUT_SPLIT), jnp.float32),
        ],
        in_specs=[inside] * 2 + [anywhere] + [inside] * 9,
        out_specs=[inside] * 2,
        scratch_shapes=[
            pltpu.VMEM(weight.shape, low),
            pltpu.VMEM(attended.shape, low),
            pltpu.VMEM((height, total), jnp.float32),
            pltpu.VMEM((total, both), jnp.float32),
            pltpu.VMEM((count, height, both), low),
            pltpu.VMEM((height, both), jnp.float32),
            pltpu.VMEM((count, feature, OUT_SPLIT), low),
        ]
        + sum_rooms(count, feature, OUT_SPLIT)
        + sum_rooms(count, height, both)
        + [pltpu.SemaphoreType.DMA]
        + sum_sems(count, 2)
        + sum_sems(count, 1),
        compiler_params=kernel_params(ident),
        name="attention_grads",
    )(
        attended, grad_rows, weight, queries, keys_values, level,
        cosine, sine, own_seq, own_order, all_seq, all_order,
    )


def closing_body(count, normed, joint_grads, attended, grad_rows, lowrank, lowrank_out, stream,
                 gain, grad_middle, small, weight, gate_grads, up_grads, down_grads, factors,
                 first, second,
                 in_sum, out_sum, second_sum, first_sum, small_sum, stream_grad, factor_grads,
                 bank, factor_bank, first_bank, second_bank, made, in_terms, out_terms,
                 second_terms, first_terms, small_terms, *scratch):
    me, depth, z, y, c = place(count)
    height, wide = normed.shape
    rank = ADAPTER_RANK
    width = gate_grads.shape[0]
    low = jnp.bfloat16
    rooms = [scratch[3 * i : 3 * i + 3] for i in range(5)]
    weight_sem, grads_sem, factor_sem, made_sem = scratch[15:19]
    sems = [scratch[19 + 6 * i : 25 + 6 * i] for i in range(5)]
    greet(count)
    halves = [
        pltpu.make_async_copy(weight.at[pl.ds(i * width, width)], bank, weight_sem.at[i])
        for i in range(wide // width)
    ]
    halves[0].start()
    loads = [
        pltpu.make_async_copy(
            factors.at[pl.ds(me * width, width)], factor_bank, factor_sem.at[0]
        ),
        pltpu.make_async_copy(
            first.at[:, pl.ds(4 * rank, 2 * rank)], first_bank, factor_sem.at[1]
        ),
        pltpu.make_async_copy(
            second.at[:, pl.ds(PROJECTED_WIDTH + MODEL_WIDTH, wide)], second_bank, factor_sem.at[2]
        ),
    ]
    for item in loads:
        item.start()
    terms = (in_terms, out_terms, second_terms, first_terms, small_terms)
    parts = (2, 2, 1, 1, 1)
    plans = [sum_terms(count, parts[i], terms[i], rooms[i], sems[i]) for i in range(5)]
    order = plans[0][0]
    send = [plan[1] for plan in plans]
    pair_step = [plan[2] for plan in plans]
    line_step = [plan[3] for plan in plans]
    last_step = [plan[4] for plan in plans]
    finish = [plan[5] for plan in plans]

    def block_products(i, left, right, at):
        feature, some = terms[i].shape[1:]

        def product(line):
            def inner(n, carry):
                cols = pl.ds(pl.multiple_of(line * 4 * feature, 4 * feature), 4 * feature)
                into = pl.ds(pl.multiple_of(n * 512, 512), 512)
                from_ = pl.ds(pl.multiple_of(at + n * 512, 512), 512)
                value = contract(left[:, cols], right[:, from_], 0, 0).astype(low)
                terms[i][pl.ds(4 * line, 4), :, into] = value.reshape(4, feature, 512)
                return carry

            lax.fori_loop(0, some // 512, inner, 0)
            for pair in (1 - y, y):
                send[i](line, pair)

        for line in order:
            product(line)

    def send_all(i):
        for pair in (1 - y, y):
            for line in order:
                send[i](line, pair)
        for k in range(depth):
            pair_step[i](k)

    def put_second(at, value):
        size = second_terms.shape[1]
        value = value.astype(low)
        start = at
        while start < at + value.shape[0]:
            block, inner = start // size, start % size
            rows = min(size - inner, at + value.shape[0] - start)
            second_terms[block, inner : inner + rows, :] = value[start - at : start - at + rows]
            start += rows

    def half_product(i):
        halves[i].wait()

        def product(n, carry):
            some = pl.ds(pl.multiple_of(n * 256, 256), 256)
            cols = pl.ds(pl.multiple_of(i * width + n * 256, 256), 256)
            stream_grad[:, cols] = contract(joint_grads[...], bank[some], 1, 1)
            return carry

        lax.fori_loop(0, width // 256, product, 0)
        if i + 1 < len(halves):
            halves[i + 1].start()

    block_products(0, normed, joint_grads, 0)
    for k in range(depth):
        pair_step[0](k)
    half_product(0)
    block_products(1, attended, grad_rows, OUT_SPLIT)
    for k in range(depth):
        pair_step[1](k)
    for i in range(1, len(halves)):
        half_product(i)

    rows = stream[...].astype(jnp.float32)
    inverse = lax.rsqrt(jnp.mean(rows * rows, axis=-1, keepdims=True) + EPSILON)
    grad = stream_grad[...]
    unit = rows * inverse
    gain_grad = jnp.sum(grad * unit, axis=0, keepdims=True)
    scaled = grad * gain[...]
    centre = jnp.mean(scaled * unit, axis=-1, keepdims=True)
    stream_grad[...] = grad_middle[...] + inverse * (scaled - unit * centre)
    small_terms[...] = small[...]
    share = wide // count
    for block in range(count):
        small_terms[block, 0:1, :share] = gain_grad[:, block * share : (block + 1) * share]
    send_all(4)

    def bring(i):
        source = (gate_grads, up_grads, down_grads)[i]
        return pltpu.make_async_copy(source, bank.at[:, pl.ds(0, wide)], grads_sem.at[i])

    bring(0).start()
    line_step[0](0)
    value_at = QUERY_WIDTH + HEAD_SIZE
    for at, stop, left, own in (
        (0, QUERY_WIDTH, joint_grads, lowrank[:, :rank]),
        (QUERY_WIDTH, value_at, joint_grads, lowrank[:, rank : 2 * rank]),
        (value_at, PROJECTED_WIDTH, joint_grads, lowrank[:, 2 * rank :]),
    ):
        put_second(at, contract(left[:, at:stop], own, 0, 0))
    put_second(PROJECTED_WIDTH, contract(grad_rows[...], lowrank_out[...], 0, 0))
    for item in loads:
        item.wait()

    def put_factor(slot, cols):
        return pltpu.make_async_copy(
            made.at[slot], factor_grads.at[:, pl.ds(cols * rank, rank)], made_sem.at[slot]
        )

    line_step[0](1)
    held = bank.at[:, pl.ds(0, wide)]
    for i in range(2):
        bring(i).wait()
        made[i] = contract(held[...], first_bank[:, i * rank : (i + 1) * rank], 1, 0)
        put_factor(i, i + 1).start()
        value = contract(held[...], factor_bank[:, (i + 1) * rank : (i + 2) * rank], 0, 0)
        first_terms[:, :, i * rank : (i + 1) * rank] = value.astype(low).reshape(
            count, wide // count, rank
        )
        bring(i + 1).start()
        if i == 0:
            line_step[0](2)
    send_all(3)
    bring(2).wait()
    put_factor(0, 1).wait()
    made[0] = contract(held[...], second_bank[...], 1, 1)
    put_factor(0, 0).start()
    put_second(
        PROJECTED_WIDTH + MODEL_WIDTH, contract(held[...], factor_bank[:, :rank], 0, 0)
    )
    send_all(2)
    line_step[0](3)
    for k in range(depth):
        line_step[1](k)
    last_step[0](in_sum)
    last_step[1](out_sum)
    for i, total in ((4, small_sum), (3, first_sum), (2, second_sum)):
        for k in range(depth):
            line_step[i](k)
        last_step[i](total)
    for item in finish:
        item()
    put_factor(0, 0).wait()
    put_factor(1, 2).wait()


def closing(count, ident, normed, joint_grads, attended, grad_rows, lowrank, lowrank_out, stream,
            gain, grad_middle, small, weight, gate_grads, up_grads, down_grads, factors, first,
            second):
    height, wide = normed.shape
    width = gate_grads.shape[0]
    low, high = jnp.bfloat16, jnp.float32
    rank = ADAPTER_RANK
    inside = pl.BlockSpec(memory_space=pltpu.VMEM)
    anywhere = pl.BlockSpec(memory_space=pl.ANY)
    share = wide // count
    shapes = [
        (share, joint_grads.shape[1], low),
        (share, wide - OUT_SPLIT, low),
        (second.shape[1] // count, rank, low),
        (share, 2 * rank, low),
        (8, 128, high),
    ]
    sem = pltpu.SemaphoreType.DMA
    rooms, sems = [], []
    for (rows, cols, kind), parts in zip(shapes, (2, 2, 1, 1, 1)):
        rooms += sum_rooms(count, rows, cols, kind)
        sems += sum_sems(count, parts)
    return pl.pallas_call(
        functools.partial(closing_body, count),
        out_shape=[jax.ShapeDtypeStruct((rows, cols), high) for rows, cols, _ in shapes]
        + [
            jax.ShapeDtypeStruct((height, wide), high),
            jax.ShapeDtypeStruct((width, 3 * rank), high),
        ],
        in_specs=[inside] * 10 + [anywhere] * 7,
        out_specs=[inside] * 6 + [anywhere],
        scratch_shapes=[
            pltpu.VMEM((width, weight.shape[1]), low),
            pltpu.VMEM((width, 3 * rank), low),
            pltpu.VMEM((wide, 2 * rank), low),
            pltpu.VMEM((rank, wide), low),
            pltpu.VMEM((2, width, rank), high),
        ]
        + [pltpu.VMEM((count, rows, cols), kind) for rows, cols, kind in shapes]
        + rooms
        + [sem((wide // width,)), sem((3,)), sem((3,)), sem((2,))]
        + sems,
        compiler_params=kernel_params(ident),
        name="closing",
    )(
        normed, joint_grads, attended, grad_rows, lowrank, lowrank_out, stream, gain, grad_middle,
        small, weight, gate_grads, up_grads, down_grads, factors, first, second,
    )


def swap_loops(values):
    if lax.axis_size("loop") == 1:
        return values
    return lax.ppermute(values, "loop", [(0, 1), (1, 0)])


def both_loops(values):
    if lax.axis_size("loop") != 2:
        return lax.psum(values.astype(jnp.float32), "loop")
    return values.astype(jnp.float32) + swap_loops(values).astype(jnp.float32)


def per_device(
    layer_input_stream,
    layer_output_gradient,
    attention_in_weight,
    attention_out_weight,
    feedforward_weight,
    layer_norm_gains,
    adapter_first_factors,
    adapter_second_factors,
    adapter_hidden_factors,
    group_sequence_lengths,
    token_per_row,
    token_exit_depth,
):
    current_loop = lax.axis_index("loop")
    dp_index = lax.axis_index("dp")
    loop_count = lax.axis_size("loop")
    count = lax.axis_size("dp")
    local_rows = layer_input_stream.shape[1]
    ffn_rows = feedforward_weight.shape[0]
    weight_rows = attention_in_weight.shape[0]
    low = jnp.bfloat16
    rank = ADAPTER_RANK
    scale = HEAD_SIZE ** (-0.5)
    key_at = QUERY_WIDTH
    value_at = QUERY_WIDTH + HEAD_SIZE
    down_at = PROJECTED_WIDTH + MODEL_WIDTH
    live_all, seq_all, order_all, pos_all = token_facts(token_per_row[0], group_sequence_lengths[0])
    first_row = dp_index * local_rows

    def own_slice(values):
        return lax.dynamic_slice_in_dim(values, first_row, local_rows, 0)

    live_own = own_slice(live_all)
    seq_own = own_slice(seq_all)
    order_own = own_slice(order_all)
    pos_own = own_slice(pos_all)
    active_mask = (live_own & (token_exit_depth[0] > current_loop)).astype(jnp.float32)[:, None]
    residual_stream = layer_input_stream[0].astype(jnp.float32)
    grad_out = layer_output_gradient[0].astype(jnp.float32)
    adapter_first = adapter_first_factors[0]
    adapter_second = adapter_second_factors[0]
    ffn_own = lax.dynamic_slice_in_dim(adapter_hidden_factors[0], dp_index * ffn_rows, ffn_rows, 0)
    first_own = lax.dynamic_slice_in_dim(adapter_first, dp_index * weight_rows, weight_rows, 0)
    second_query = adapter_second[:, :key_at]
    second_key = adapter_second[:, key_at:value_at]
    second_value = adapter_second[:, value_at:PROJECTED_WIDTH]
    second_output = adapter_second[:, PROJECTED_WIDTH:down_at]
    second_down = adapter_second[:, down_at:]

    in_own = (
        attention_in_weight.astype(jnp.float32)
        + jnp.concatenate(
            [
                matrix_product(first_own[:, :rank], second_query),
                matrix_product(first_own[:, rank : 2 * rank], second_key),
                matrix_product(first_own[:, 2 * rank : 3 * rank], second_value),
            ],
            axis=1,
        )
    ).astype(low)
    out_own = (
        attention_out_weight.astype(jnp.float32)
        + matrix_product(first_own[:, 3 * rank : 4 * rank], second_output)
    ).astype(low)
    down_factor = ffn_own[:, :rank]
    gate_factor = ffn_own[:, rank : 2 * rank]
    up_factor = ffn_own[:, 2 * rank :]
    first_gate = adapter_first[:, 4 * rank : 5 * rank]
    first_up = adapter_first[:, 5 * rank :]
    ffn_weight = jnp.swapaxes(feedforward_weight, 0, 1)

    feedforward_gradient = (active_mask * grad_out).astype(low)
    normed_input = norm_rows(residual_stream, layer_norm_gains[0]).astype(low)
    if count == LINE_DEVICES:
        input_weight, output_weight, ffn_folded = opening(
            count, 1, (in_own, out_own), ffn_weight, adapter_hidden_factors[0],
            adapter_first, adapter_second,
        )
    else:
        input_weight, output_weight = gather_rows(count, 1, in_own, out_own)
        extra = jnp.stack(
            [
                outer_columns(gate_factor, first_gate),
                outer_columns(up_factor, first_up),
                matrix_product(down_factor, second_down),
            ]
        )
        ffn_folded = (ffn_weight.astype(jnp.float32) + extra).astype(low)
    feedforward_gradient, input_weight = lax.optimization_barrier(
        (feedforward_gradient, input_weight)
    )
    grad_ffn_all = lax.all_gather(feedforward_gradient, "dp", axis=0, tiled=True)
    query_key_value_linear = matrix_product(normed_input, input_weight)
    half = HEAD_SIZE // 2
    freqs = 10000.0 ** (-jnp.arange(half, dtype=jnp.float32) / half)
    angles = pos_own.astype(jnp.float32)[:, None] * freqs
    cosine, sine = jnp.cos(angles), jnp.sin(angles)
    queries = rotate(
        query_key_value_linear[:, :QUERY_WIDTH].reshape(local_rows, HEADS, HEAD_SIZE), pos_own
    ).astype(low)
    key_rot = rotate(
        query_key_value_linear[:, key_at:value_at].reshape(local_rows, 1, HEAD_SIZE), pos_own
    )[:, 0]
    kv_send = jnp.concatenate([key_rot, query_key_value_linear[:, value_at:]], axis=1).astype(low)
    (kv_all,) = gather_rows(count, 2, kv_send)
    keys = kv_all[:, :HEAD_SIZE]
    values = kv_all[:, HEAD_SIZE:]
    key_total = kv_all.shape[0]
    allowed = ((seq_own[:, None] == seq_all[None, :]) & (order_all[None, :] <= order_own[:, None]))[
        :, None, :
    ]
    query_rows = queries.reshape(local_rows * HEADS, HEAD_SIZE)
    queries_flat = queries.reshape(local_rows, QUERY_WIDTH)

    def score_rows():
        raw_scores = (outer_columns(query_rows, keys) * scale).reshape(local_rows, HEADS, key_total)
        return jnp.where(allowed, raw_scores, FLOOR_SCORE)

    scores = score_rows()
    top_score = jnp.max(scores, axis=-1, keepdims=True)
    expo = jnp.exp(scores - top_score)
    mass = jnp.sum(expo, axis=-1, keepdims=True)
    level = (top_score + jnp.log(mass))[:, :, 0]
    prob_low = (expo / mass).astype(low)
    attended_rows = (
        matrix_product(prob_low.reshape(local_rows * HEADS, key_total), values)
        .reshape(local_rows, QUERY_WIDTH)
        .astype(low)
    )
    branch_output = matrix_product(attended_rows, output_weight)
    middle_state = residual_stream + active_mask * branch_output
    second_normed_input = norm_rows(middle_state, layer_norm_gains[1]).astype(low)
    if count == LINE_DEVICES:
        grad_blocks = grad_ffn_all.reshape(count, local_rows, MODEL_WIDTH)
        units_own, grad_gate_own, grad_up_own, normed_blocks = hidden_units(
            count, 3, second_normed_input, grad_blocks, ffn_folded
        )
        second_normed_gradient, ffn_sum, gate_grad, up_grad, down_grad, gate_other = unit_grads(
            count, 4, units_own, grad_gate_own, grad_up_own, ffn_folded, normed_blocks, grad_blocks
        )
    else:
        (normed_all,) = gather_rows(count, 3, second_normed_input)
        gate_weight, up_weight, down_weight = ffn_folded
        gate_own = outer_columns(normed_all, gate_weight)
        up_own = outer_columns(normed_all, up_weight)
        hidden_unit_gradient = outer_columns(grad_ffn_all, down_weight)
        units_own = geglu(gate_own, up_own).astype(low)
        grad_gate_own, grad_up_own = jax.vjp(geglu, gate_own, up_own)[1](hidden_unit_gradient)
        grad_gate_own = grad_gate_own.astype(low)
        grad_up_own = grad_up_own.astype(low)
        gate_grad = inner_rows(grad_gate_own, normed_all).astype(low)
        up_grad = inner_rows(grad_up_own, normed_all).astype(low)
        down_grad = inner_rows(units_own, grad_ffn_all).astype(low)
        ffn_terms = matrix_product(units_own, down_weight).astype(low)
        input_terms = (
            matrix_product(grad_gate_own, gate_weight) + matrix_product(grad_up_own, up_weight)
        ).astype(low)
        ffn_sum, second_normed_gradient = scatter_rows(count, 4, ffn_terms, input_terms)
        gate_other = swap_loops(gate_grad)
    if count == LINE_DEVICES:
        gate_last = swap_loops(gate_grad[FAR_TILES * 256 :])
        gate_other = jnp.concatenate([gate_other, gate_last], axis=0)
    up_other = swap_loops(up_grad)
    down_other = swap_loops(down_grad)
    complete_output = middle_state + active_mask * ffn_sum.astype(jnp.float32)
    confidence = root_mean(residual_stream) / (
        root_mean(residual_stream) + root_mean(complete_output - residual_stream)
    )
    conf_sum = jnp.sum(jnp.where(live_own, confidence, 0.0))
    depth_hits = (
        (token_exit_depth[0][:, None] == jnp.arange(loop_count + 1, dtype=jnp.int32)[None, :])
        & live_own[:, None]
    ).astype(jnp.float32)
    stats = jnp.concatenate([conf_sum[None], jnp.sum(depth_hits, axis=0)])

    grad_middle_part, grad_gain_two = jax.vjp(norm_rows, middle_state, layer_norm_gains[1])[1](
        second_normed_gradient
    )
    grad_middle = grad_out + grad_middle_part
    branch_gradient = (active_mask * grad_middle).astype(low)
    width_own = MODEL_WIDTH // count
    small = jnp.zeros((count, 8, 128), jnp.float32)
    small = small.at[:, 1, :width_own].set(grad_gain_two.reshape(count, width_own))
    small = small.at[:, 2, : loop_count + 2].set(stats[None])
    lowrank_projection = matrix_product(normed_input, adapter_first[:, : 3 * rank]).astype(low)
    output_projection = matrix_product(
        attended_rows, adapter_first[:, 3 * rank : 4 * rank]
    ).astype(low)
    if count == LINE_DEVICES:
        steps = jnp.transpose(level).reshape(HEADS // 2, 2 * local_rows, 1)
        joint_grads, out_first = attention_grads(
            count, 5, attended_rows, branch_gradient, output_weight, queries_flat, kv_all,
            jnp.broadcast_to(steps, steps.shape[:2] + (128,)), cosine, sine, seq_own[:, None],
            order_own[:, None], seq_all[None], order_all[None],
        )
        (
            in_portion, out_last, second_grad, first_grad_hidden, small_sum, hidden_grad,
            adapter_hidden_gradient,
        ) = closing(
            count, 6, normed_input, joint_grads, attended_rows, branch_gradient, lowrank_projection,
            output_projection, layer_input_stream[0], layer_norm_gains[:1], grad_middle, small,
            input_weight, gate_grad, up_grad, down_grad, adapter_hidden_factors[0], adapter_first,
            adapter_second,
        )
        out_portion = jnp.concatenate([out_first, out_last], axis=1)
    else:
        grad_attended = outer_columns(branch_gradient, output_weight).astype(low)
        grad_att_rows = grad_attended.reshape(local_rows * HEADS, HEAD_SIZE)
        prob = jnp.exp(score_rows() - level[:, :, None])
        grad_prob = outer_columns(grad_att_rows, values).reshape(local_rows, HEADS, key_total)
        centre = jnp.sum(prob * grad_prob, axis=-1, keepdims=True)
        grad_scores = (
            (prob * (grad_prob - centre)).astype(low).reshape(local_rows * HEADS, key_total)
        )
        prob_again = prob.astype(low).reshape(local_rows * HEADS, key_total)
        kv_terms = jnp.concatenate(
            [inner_rows(grad_scores, query_rows) * scale, inner_rows(prob_again, grad_att_rows)],
            axis=1,
        ).astype(low)
        (grad_kv,) = scatter_rows(count, 5, kv_terms)
        grad_queries = (matrix_product(grad_scores, keys) * scale).reshape(
            local_rows, HEADS, HEAD_SIZE
        )
        query_key_value_gradient = jnp.concatenate(
            [
                rotate_back(grad_queries, pos_own).reshape(local_rows, QUERY_WIDTH),
                rotate_back(grad_kv[:, None, :HEAD_SIZE], pos_own)[:, 0],
                grad_kv[:, HEAD_SIZE:],
            ],
            axis=1,
        ).astype(low)
        normed_gradient = outer_columns(query_key_value_gradient, input_weight)
        grad_resid_part, grad_gain_one = jax.vjp(norm_rows, residual_stream, layer_norm_gains[0])[1](
            normed_gradient
        )
        hidden_grad = grad_middle + grad_resid_part
        small = small.at[:, 0, :width_own].set(grad_gain_one.reshape(count, width_own))
        second_terms = jnp.concatenate(
            [
                inner_rows(query_key_value_gradient[:, :key_at], lowrank_projection[:, :rank]),
                inner_rows(
                    query_key_value_gradient[:, key_at:value_at],
                    lowrank_projection[:, rank : 2 * rank],
                ),
                inner_rows(query_key_value_gradient[:, value_at:], lowrank_projection[:, 2 * rank :]),
                inner_rows(branch_gradient, output_projection),
                inner_rows(down_grad, down_factor),
            ],
            axis=0,
        ).astype(low)
        in_terms = inner_rows(normed_input, query_key_value_gradient).astype(low)
        out_terms = inner_rows(attended_rows, branch_gradient).astype(low)
        first_terms = jnp.concatenate(
            [inner_rows(gate_grad, gate_factor), inner_rows(up_grad, up_factor)], axis=1
        ).astype(low)
        in_portion, out_portion, second_grad, first_grad_hidden, small_sum = scatter_rows(
            count, 6, in_terms, out_terms, second_terms, first_terms, small.reshape(count * 8, 128)
        )
        adapter_hidden_gradient = jnp.concatenate(
            [
                outer_columns(down_grad, second_down),
                matrix_product(gate_grad, first_gate),
                matrix_product(up_grad, first_up),
            ],
            axis=1,
        )
    gate_other, up_other, down_other, small_sum = lax.optimization_barrier(
        (gate_other, up_other, down_other, small_sum)
    )
    in_low = in_portion.astype(low)
    out_low = out_portion.astype(low)
    adapter_first_gradient = jnp.concatenate(
        [
            outer_columns(in_low[:, :key_at], second_query),
            outer_columns(in_low[:, key_at:value_at], second_key),
            outer_columns(in_low[:, value_at:], second_value),
            outer_columns(out_low, second_output),
            first_grad_hidden,
        ],
        axis=1,
    )
    small_total = both_loops(small_sum)
    sum_gains = small_total[:2, :width_own]
    depth_total = small_total[2, 1 : loop_count + 2]
    mean_confidence = small_total[2, 0] / jnp.sum(depth_total)
    exit_counts = depth_total.astype(jnp.int32)
    sum_mlp = jnp.stack(
        [
            gate_grad.astype(jnp.float32) + gate_other.astype(jnp.float32),
            up_grad.astype(jnp.float32) + up_other.astype(jnp.float32),
            down_grad.astype(jnp.float32) + down_other.astype(jnp.float32),
        ],
        axis=1,
    )
    return (
        complete_output.astype(low)[None],
        hidden_grad[None],
        both_loops(in_low),
        both_loops(out_low),
        sum_mlp,
        sum_gains,
        adapter_first_gradient[None],
        jnp.swapaxes(second_grad, 0, 1)[None],
        adapter_hidden_gradient[None],
        exit_counts,
        mean_confidence,
    )


def solution(mesh):
    return jax.shard_map(
        per_device,
        mesh=mesh,
        in_specs=(
            P("loop", "dp", None),
            P("loop", "dp", None),
            P("dp", None),
            P("dp", None),
            P("dp", None, None),
            P(),
            P("loop", None, None),
            P("loop", None, None),
            P("loop", None, None),
            P("loop", None),
            P("loop", None),
            P("loop", "dp"),
        ),
        out_specs=(
            P("loop", "dp", None),
            P("loop", "dp", None),
            P("dp", None),
            P("dp", None),
            P("dp", None, None),
            P(None, "dp"),
            P("loop", "dp", None),
            P("loop", None, "dp"),
            P("loop", "dp", None),
            P(),
            P(),
        ),
        check_vma=False,
    )
```

```python
import functools

import jax
import jax.numpy as jnp
from jax import lax
from jax.experimental import pallas as pl
from jax.experimental.pallas import tpu as pltpu
from jax.sharding import PartitionSpec as P

MODEL_WIDTH = 2048
HEADS = 8
HEAD_SIZE = 256
ADAPTER_RANK = 256
QUERY_WIDTH = 2048
PROJECTED_WIDTH = 2560


EPSILON = 1e-06
FLOOR_SCORE = -1e30
MESH = pl.DeviceIdType.MESH
VMEM_LIMIT = 60 * 1024 * 1024
LINE_DEVICES = 16
FAR_TILES = 3
OUT_SPLIT = 1536
IN_SHARE = 48
OUT_SHARE = 32


def matrix_product(left, right):
    return jnp.dot(left, right, preferred_element_type=jnp.float32)


def inner_rows(left, right):
    return lax.dot_general(
        left, right, (((0,), (0,)), ((), ())), preferred_element_type=jnp.float32
    )


def outer_columns(left, right):
    return lax.dot_general(
        left, right, (((1,), (1,)), ((), ())), preferred_element_type=jnp.float32
    )


def norm_rows(values, gain):
    return values * lax.rsqrt(jnp.mean(values * values, axis=-1, keepdims=True) + EPSILON) * gain


def rotate(values, positions):
    half_dim = values.shape[-1] // 2
    freqs = 10000.0 ** (-jnp.arange(half_dim, dtype=jnp.float32) / half_dim)
    angles = positions.astype(jnp.float32)[:, None, None] * freqs
    cosine = jnp.cos(angles)
    sine = jnp.sin(angles)
    first_half = values[..., :half_dim]
    second_half = values[..., half_dim:]
    return jnp.concatenate(
        [first_half * cosine - second_half * sine, first_half * sine + second_half * cosine],
        axis=-1,
    )


def rotate_back(grads, positions):

    def turned(values):
        return rotate(values, positions)

    return jax.vjp(turned, jnp.zeros_like(grads))[1](grads)[0]


def geglu(gate_values, up_projection_value):
    return jax.nn.gelu(gate_values, approximate=True) * up_projection_value


def root_mean(values):
    return jnp.sqrt(jnp.mean(values * values, axis=-1) + EPSILON)


def token_facts(row_of_tokens, sequence_length):
    row_total = row_of_tokens.shape[0]
    live_row = row_of_tokens >= 0
    seq_ends = jnp.cumsum(sequence_length)
    seq_index = jnp.sum((row_of_tokens[:, None] >= seq_ends[None, :]).astype(jnp.int32), axis=1)
    seq_starts = seq_ends - sequence_length
    own_start = jnp.sum(
        jnp.where(
            seq_index[:, None] == jnp.arange(sequence_length.shape[0], dtype=jnp.int32)[None, :],
            seq_starts[None, :],
            0,
        ),
        axis=1,
    )
    row_ids = jnp.arange(row_total, dtype=jnp.int32)
    sequence = jnp.where(live_row, seq_index, -1 - row_ids)
    ordering = jnp.where(live_row, row_of_tokens, 0)
    positions = jnp.where(live_row, row_of_tokens - own_start, 0)
    return (live_row, sequence, ordering, positions)


def place(count):
    me = lax.axis_index("dp")
    return me, count // 4, me // 4, (me // 2) % 2, me % 2


def greet(count, across=False):
    me, depth, z, y, c = place(count)
    barrier = pltpu.get_barrier_semaphore()

    def signal(where):
        pl.semaphore_signal(barrier, inc=1, device_id={"dp": where}, device_id_type=MESH)

    signal(me + 1 - 2 * c)
    signal(me + 2 - 4 * y)
    if across:
        other = 1 - lax.axis_index("loop")
        pl.semaphore_signal(barrier, inc=1, device_id={"loop": other}, device_id_type=MESH)

    @pl.when(z > 0)
    def _():
        signal(me - 4)

    @pl.when(z < depth - 1)
    def _():
        signal(me + 4)

    ends = jnp.where((z > 0) & (z < depth - 1), 4, 3)
    pl.semaphore_wait(barrier, ends + 1 if across else ends)


def contract(left, right, left_axis, right_axis):
    return lax.dot_general(
        left,
        right,
        (((left_axis,), (right_axis,)), ((), ())),
        preferred_element_type=jnp.float32,
    )


def gather_plan(count, spans, own, full, sems, far_sems=None):
    keep, recv, send_core, send_pair, send_right, send_left = sems
    arrays = len(own)
    me, depth, z, y, c = place(count)
    mate = me + 2 - 4 * y
    core = me + 1 - 2 * c

    def copy(unit, block, target, sem, first=False):
        a, s = unit
        rows = pl.ds(*spans[a][s])
        return pltpu.make_async_remote_copy(
            src_ref=own[a].at[rows] if first else full[a].at[block, rows],
            dst_ref=full[a].at[block, rows],
            send_sem=sem,
            recv_sem=recv.at[a, block, s],
            device_id={"dp": target},
            device_id_type=MESH,
        )

    def to_core(unit, block, first=False):
        a, s = unit
        return copy(unit, block, core, send_core.at[a, block // 2, s], first)

    def to_pair(unit, block, first=False):
        a, s = unit
        return copy(unit, block, mate, send_pair.at[a, block // 4, s], first)

    def to_right(unit, block, first=False):
        a, s = unit
        return copy(unit, block, me + 4, send_right.at[a, block // 4, s], first)

    def to_left(unit, block, first=False):
        a, s = unit
        return copy(unit, block, me - 4, send_left.at[a, block // 4, s], first)

    def to_far(a, block):
        rows = pl.ds(*spans[a][0])
        return pltpu.make_async_remote_copy(
            src_ref=full[a].at[block, rows],
            dst_ref=full[a].at[block, rows],
            send_sem=far_sems[0].at[a, block // 2],
            recv_sem=far_sems[1].at[a, block],
            device_id={"loop": 1 - lax.axis_index("loop")},
            device_id_type=MESH,
        )

    def far_core(a, block, first=False):
        rows = pl.ds(*spans[a][2])
        return pltpu.make_async_remote_copy(
            src_ref=own[a].at[rows] if first else full[a].at[block, rows],
            dst_ref=full[a].at[block, rows],
            send_sem=far_sems[2].at[a, block // 2],
            recv_sem=far_sems[3].at[a, block],
            device_id={"dp": core},
            device_id_type=MESH,
        )

    def cross(unit, block):
        if far_sems is not None and unit[1] == 0:
            to_far(unit[0], block).start()

    local = [pltpu.make_async_copy(own[a], full[a].at[me], keep.at[a]) for a in range(arrays)]
    units = [(a, s) for a in range(arrays) for s in range(2 if far_sems else len(spans[a]))]

    def begin():
        for unit in units:

            @pl.when(z < depth - 1)
            def _(unit=unit):
                to_right(unit, me, True).start()

            @pl.when(z > 0)
            def _(unit=unit):
                to_left(unit, me, True).start()

            to_pair(unit, me, True).start()
            to_core(unit, me, True).start()
        if far_sems is not None:
            for a in range(arrays):
                far_core(a, me, True).start()
        for item in local:
            item.start()

    def from_line(k, unit):
        @pl.when(z - k >= 0)
        def _():
            block = me - 4 * k
            to_right(unit, block).wait_recv()

            @pl.when(z < depth - 1)
            def _():
                to_right(unit, block).start()

            to_pair(unit, block).start()
            to_core(unit, block).start()
            cross(unit, block)

        @pl.when(z + k < depth)
        def _():
            block = me + 4 * k
            to_left(unit, block).wait_recv()

            @pl.when(z > 0)
            def _():
                to_left(unit, block).start()

            to_pair(unit, block).start()
            to_core(unit, block).start()
            cross(unit, block)

    def pass_on(unit, block):
        to_pair(unit, block).wait_recv()
        to_core(unit, block).start()
        cross(unit, block)

    def from_pair(k, unit):
        if k == 0:
            pass_on(unit, mate)
            return

        @pl.when(z - k >= 0)
        def _():
            pass_on(unit, mate - 4 * k)

        @pl.when(z + k < depth)
        def _():
            pass_on(unit, mate + 4 * k)

    def far_on(a, block):
        to_far(a, block).wait_recv()
        far_core(a, block).start()

    def from_far(k, a):
        if k == 0:
            far_on(a, mate)
            return

        @pl.when(z - k >= 0)
        def _():
            far_on(a, me - 4 * k)
            far_on(a, mate - 4 * k)

        @pl.when(z + k < depth)
        def _():
            far_on(a, me + 4 * k)
            far_on(a, mate + 4 * k)

    def arrive():
        for unit in units:
            for j in range(count // 2):
                to_core(unit, 2 * j + 1 - c).wait_recv()
        if far_sems is not None:
            for a in range(arrays):
                for j in range(count // 2):
                    far_core(a, 2 * j + 1 - c).wait_recv()
        for item in local:
            item.wait()

    def finish():
        for unit in units:
            for j in range(count // 2):
                to_core(unit, 2 * j + c).wait_send()
            for j in range(depth):
                block = 4 * j + 2 * y + c
                to_pair(unit, block).wait_send()

                @pl.when((z >= j) & (z < depth - 1))
                def _():
                    to_right(unit, block).wait_send()

                @pl.when((z <= j) & (z > 0))
                def _():
                    to_left(unit, block).wait_send()

        if far_sems is not None:
            for a in range(arrays):
                for j in range(count // 2):
                    far_core(a, 2 * j + c).wait_send()

                    @pl.when(2 * j + c != me)
                    def _():
                        to_far(a, 2 * j + c).wait_send()

    return units, begin, from_line, from_pair, from_far, arrive, finish


def gather_sems(count, number, parts):
    depth = count // 4
    sem = pltpu.SemaphoreType.DMA
    return [
        sem((number,)),
        sem((number, count, parts)),
        sem((number, count // 2, parts)),
        sem((number, depth, parts)),
        sem((number, depth, parts)),
        sem((number, depth, parts)),
    ]


def even_spans(rows, parts):
    return [(s * (rows // parts), rows // parts) for s in range(parts)]


def kernel_params(ident):
    return pltpu.CompilerParams(
        collective_id=ident, has_side_effects=True, vmem_limit_bytes=VMEM_LIMIT
    )


def opening_body(count, shares, arrays, stream, gain, *refs):
    own = refs[:arrays]
    weights, factors, first, second = refs[arrays : arrays + 4]
    full = refs[arrays + 4 : 2 * arrays + 4]
    folded, normed, lowrank = refs[2 * arrays + 4 : 2 * arrays + 7]
    scratch = refs[2 * arrays + 7 :]
    (bank, factor_bank, first_bank, in_bank, second_bank, bank_sem, factor_sem, out_sem) = scratch[
        :8
    ]
    me, depth, z, y, c = place(count)
    rank = ADAPTER_RANK
    width, wide = bank.shape[1:]
    loop = lax.axis_index("loop")
    greet(count, True)
    spans = []
    for a in range(arrays):
        rows, share = own[a].shape[0], shares[a]
        spans.append(
            [
                (pl.multiple_of(loop * (rows - share), 16), share),
                (share, rows - 2 * share),
                (pl.multiple_of((1 - loop) * (rows - share), 16), share),
            ]
        )
    units, begin, from_line, from_pair, from_far, arrive, finish = gather_plan(
        count, spans, own, full, scratch[8:14], scratch[14:18]
    )
    begin()
    fills = [
        pltpu.make_async_copy(weights.at[i], bank.at[i], bank_sem.at[i]) for i in range(3)
    ]
    sources = [
        pltpu.make_async_copy(first.at[:, pl.ds(0, 3 * rank)], in_bank, factor_sem.at[0]),
        pltpu.make_async_copy(
            factors.at[pl.ds(me * width, width)], factor_bank, factor_sem.at[1]
        ),
        pltpu.make_async_copy(
            first.at[:, pl.ds(4 * rank, 2 * rank)], first_bank, factor_sem.at[2]
        ),
        pltpu.make_async_copy(
            second.at[:, pl.ds(PROJECTED_WIDTH + MODEL_WIDTH, wide)], second_bank, factor_sem.at[3]
        ),
    ]
    for item in sources + fills:
        item.start()

    def put(i):
        return pltpu.make_async_copy(bank.at[i], folded.at[i], out_sem.at[i])

    def fold(i):
        high, tile = 256, 512

        def inner(n, carry):
            rows = pl.ds(pl.multiple_of((n // (wide // tile)) * high, high), high)
            cols = pl.ds(pl.multiple_of((n % (wide // tile)) * tile, tile), tile)
            if i == 2:
                extra = contract(factor_bank[rows, :rank], second_bank[:, cols], 1, 0)
            else:
                extra = contract(
                    factor_bank[rows, (i + 1) * rank : (i + 2) * rank],
                    first_bank[cols, i * rank : (i + 1) * rank],
                    1,
                    1,
                )
            bank[i, rows, cols] = (bank[i, rows, cols].astype(jnp.float32) + extra).astype(
                bank.dtype
            )
            return carry

        lax.fori_loop(0, (width // high) * (wide // tile), inner, 0)
        put(i).start()

    rows = stream[...].astype(jnp.float32)
    inverse = lax.rsqrt(jnp.mean(rows * rows, axis=-1, keepdims=True) + EPSILON)
    normed[...] = (rows * inverse * gain[...]).astype(normed.dtype)
    sources[0].wait()
    lowrank[...] = contract(normed[...], in_bank[...], 1, 0).astype(lowrank.dtype)
    for item in sources[1:]:
        item.wait()
    for k in range(1, depth):
        for a in range(arrays):
            for unit in units:
                if unit[0] == a:
                    from_line(k, unit)
                    from_pair(k - 1, unit)
            if k > 1 or a > 0:
                stage = (k - 1) * arrays + a - 1
                from_far(stage // arrays, stage % arrays)
        fills[k - 1].wait()
        fold(k - 1)
    for unit in units:
        from_pair(depth - 1, unit)
    for stage in range((depth - 1) * arrays - 1, depth * arrays):
        from_far(stage // arrays, stage % arrays)
    arrive()
    finish()
    for i in range(3):
        put(i).wait()


def opening(count, ident, stream, gain, arrays, shares, weights, factors, first, second):
    number = len(arrays)
    _, width, wide = weights.shape
    low = jnp.bfloat16
    rank = ADAPTER_RANK
    sem = pltpu.SemaphoreType.DMA
    anywhere = pl.BlockSpec(memory_space=pl.ANY)
    inside = pl.BlockSpec(memory_space=pltpu.VMEM)
    out = pl.pallas_call(
        functools.partial(opening_body, count, shares, number),
        out_shape=[
            jax.ShapeDtypeStruct((count,) + item.shape, item.dtype) for item in arrays
        ]
        + [
            jax.ShapeDtypeStruct(weights.shape, low),
            jax.ShapeDtypeStruct(stream.shape, low),
            jax.ShapeDtypeStruct((stream.shape[0], 3 * rank), low),
        ],
        in_specs=[inside] * 2 + [anywhere] * (number + 4),
        out_specs=[anywhere] * (number + 1) + [inside] * 2,
        scratch_shapes=[
            pltpu.VMEM(weights.shape, low),
            pltpu.VMEM((width, factors.shape[1]), low),
            pltpu.VMEM((wide, 2 * rank), low),
            pltpu.VMEM((wide, 3 * rank), low),
            pltpu.VMEM((rank, wide), low),
            sem((3,)),
            sem((4,)),
            sem((3,)),
        ]
        + gather_sems(count, number, 2)
        + [
            sem((number, count // 2)),
            sem((number, count)),
            sem((number, count // 2)),
            sem((number, count)),
        ],
        compiler_params=kernel_params(ident),
        name="opening",
    )(stream, gain, *arrays, weights, factors, first, second)
    return [
        item.reshape((count * item.shape[1],) + item.shape[2:]) for item in out[:number]
    ] + list(out[number:])


def turn(values, cosine, sine):
    half = values.shape[-1] // 2
    first, second = values[:, :half], values[:, half:]
    return jnp.concatenate(
        [first * cosine - second * sine, first * sine + second * cosine], axis=1
    )


def attention_body(count, normed, lowrank, stream, active, gain, cosine, sine, own_seq, own_order,
                   all_seq, all_order, in_weight, out_weight, first, second, grads,
                   queries, attended, lowrank_out, level, middle, normed_next, keys_values, grads_all,
                   in_bank, out_bank, in_second, out_second, out_first, allowed, kv_own, kv_full,
                   load_sem, put_sem, *sems):
    me, depth, z, y, c = place(count)
    height, wide = normed.shape
    size = HEAD_SIZE
    scale = size ** (-0.5)
    rank = ADAPTER_RANK
    low = jnp.bfloat16
    greet(count)
    kv_units, kv_begin, kv_line, kv_pair, _, kv_arrive, kv_finish = gather_plan(
        count, [even_spans(height, 1)], (kv_own,), (kv_full,), sems[:6]
    )
    units, begin, from_line, from_pair, _, arrive, finish = gather_plan(
        count, [even_spans(height, 2)], (grads,), (grads_all,), sems[6:]
    )
    loads = [
        pltpu.make_async_copy(source, bank, load_sem.at[i])
        for i, (source, bank) in enumerate(
            (
                (in_weight, in_bank),
                (second.at[:, pl.ds(0, PROJECTED_WIDTH)], in_second),
                (out_weight, out_bank),
                (second.at[:, pl.ds(PROJECTED_WIDTH, MODEL_WIDTH)], out_second),
                (first.at[:, pl.ds(3 * rank, rank)], out_first),
            )
        )
    ]
    for item in loads:
        item.start()
    loads[0].wait()
    loads[1].wait()

    def head(at, part):
        value = contract(normed[...], in_bank[:, at : at + size], 1, 0)
        return value + contract(
            lowrank[:, part * rank : (part + 1) * rank], in_second[:, at : at + size], 1, 0
        )

    kv_own[:, :size] = turn(head(QUERY_WIDTH, 1), cosine[...], sine[...]).astype(low)
    kv_own[:, size:] = head(QUERY_WIDTH + size, 2).astype(low)
    kv_begin()
    begin()
    heads = wide // size

    def some_heads(start, stop):
        for i in range(start, stop):
            value = turn(head(i * size, 0), cosine[...], sine[...])
            queries[:, i * size : (i + 1) * size] = value.astype(low)

    some_heads(0, 4)
    (kv_unit,) = kv_units
    kv_line(1, kv_unit)
    kv_pair(0, kv_unit)
    some_heads(4, heads)
    same = own_seq[...] == all_seq[...]
    allowed[...] = jnp.where(same & (all_order[...] <= own_order[...]), 1.0, 0.0)
    kv_line(2, kv_unit)
    kv_pair(1, kv_unit)
    kv_line(3, kv_unit)
    kv_pair(2, kv_unit)
    kv_pair(3, kv_unit)
    for unit in units:
        from_line(1, unit)
        from_pair(0, unit)
    kv_arrive()
    put_kv = pltpu.make_async_copy(kv_full, keys_values, put_sem)
    put_kv.start()
    total = count * height
    keys = kv_full[:, :, :size].reshape(total, size)
    values = kv_full[:, :, size:].reshape(total, size)

    def attend(pair):
        query = jnp.concatenate(
            [
                queries[:, 2 * pair * size : (2 * pair + 1) * size],
                queries[:, (2 * pair + 1) * size : (2 * pair + 2) * size],
            ],
            axis=0,
        )
        keep = jnp.concatenate([allowed[...], allowed[...]], axis=0) > 0.5
        scores = jnp.where(keep, contract(query, keys, 1, 1) * scale, FLOOR_SCORE)
        top = jnp.max(scores, axis=-1, keepdims=True)
        expo = jnp.exp(scores - top)
        mass = jnp.sum(expo, axis=-1, keepdims=True)
        level[pair] = jnp.broadcast_to(top + jnp.log(mass), level.shape[1:])
        value = contract((expo / mass).astype(low), values, 1, 0).astype(low)
        for i in range(2):
            attended[:, (2 * pair + i) * size : (2 * pair + i + 1) * size] = value[
                i * height : (i + 1) * height
            ]

    for pair in range(heads // 2):
        attend(pair)
        if pair == 0:
            for unit in units:
                from_line(2, unit)
        if pair == 1:
            for unit in units:
                from_pair(1, unit)
        if pair == 2:
            for unit in units:
                from_line(3, unit)
        if pair == 3:
            for unit in units:
                from_pair(2, unit)
    for item in loads[2:]:
        item.wait()
    lowrank_out[...] = contract(attended[...], out_first[...], 1, 0).astype(low)
    tile = 256

    def product(n, carry):
        cols = pl.ds(pl.multiple_of(n * tile, tile), tile)
        value = contract(attended[...], out_bank[:, cols], 1, 0)
        value += contract(lowrank_out[...], out_second[:, cols], 1, 0)
        middle[:, cols] = stream[:, cols].astype(jnp.float32) + active[...] * value
        return carry

    lax.fori_loop(0, wide // tile, product, 0)
    rows = middle[...]
    inverse = lax.rsqrt(jnp.mean(rows * rows, axis=-1, keepdims=True) + EPSILON)
    normed_next[...] = (rows * inverse * gain[...]).astype(low)
    for unit in units:
        from_pair(3, unit)
    arrive()
    finish()
    kv_finish()
    put_kv.wait()


def attention(count, ident, normed, lowrank, stream, active, gain, cosine, sine, own_seq,
              own_order, all_seq, all_order, in_weight, out_weight, first, second, grads):
    height, wide = normed.shape
    low, high = jnp.bfloat16, jnp.float32
    inside = pl.BlockSpec(memory_space=pltpu.VMEM)
    anywhere = pl.BlockSpec(memory_space=pl.ANY)
    rank = ADAPTER_RANK
    both = 2 * HEAD_SIZE
    total = count * height
    sem = pltpu.SemaphoreType.DMA
    shape = jax.ShapeDtypeStruct
    return pl.pallas_call(
        functools.partial(attention_body, count),
        out_shape=[
            shape((height, wide), low),
            shape((height, wide), low),
            shape((height, rank), low),
            shape((wide // both, 2 * height, 128), high),
            shape((height, wide), high),
            shape((height, wide), low),
            shape((count, height, both), low),
            shape((count, height, wide), low),
        ],
        in_specs=[inside] * 11 + [anywhere] * 5,
        out_specs=[inside] * 6 + [anywhere] * 2,
        scratch_shapes=[
            pltpu.VMEM(in_weight.shape, low),
            pltpu.VMEM(out_weight.shape, low),
            pltpu.VMEM((rank, PROJECTED_WIDTH), low),
            pltpu.VMEM((rank, wide), low),
            pltpu.VMEM((wide, rank), low),
            pltpu.VMEM((height, total), high),
            pltpu.VMEM((height, both), low),
            pltpu.VMEM((count, height, both), low),
            sem((5,)),
            sem,
        ]
        + gather_sems(count, 1, 1)
        + gather_sems(count, 1, 2),
        compiler_params=kernel_params(ident),
        name="attention",
    )(
        normed, lowrank, stream, active, gain, cosine, sine, own_seq, own_order, all_seq,
        all_order, in_weight, out_weight, first, second, grads,
    )


def line_order(z):
    near = z < 2
    return [z, z + 1 - 2 * (z % 2), jnp.where(near, 2, 1), jnp.where(near, 3, 0)]


def unit_values(gate, up, grad):
    slope = 0.7978845608028654
    cubic = 0.044715
    square = gate * gate
    curve = jnp.tanh(slope * (gate + cubic * square * gate))
    half = 0.5 * (1.0 + curve)
    turned = gate * half
    rise = half + 0.5 * gate * (1.0 - curve * curve) * slope * (1.0 + 3.0 * cubic * square)
    low = jnp.bfloat16
    return (turned * up).astype(low), (grad * up * rise).astype(low), (grad * turned).astype(low)


def hidden_body(count, parts, own, grads, weights, units, gate_grads, up_grads, rows_out,
                held, bank, coming, done, recv, send_core, send_pair, send_line, keep, bank_sem,
                coming_sem, done_sem, rows_sem):
    me, depth, z, y, c = place(count)
    height = own.shape[0]
    width = bank.shape[1]
    step = height // parts
    tile = 512
    core, mate = me + 1 - 2 * c, me + 2 - 4 * y
    lines = line_order(z)
    greet(count)

    def hop(block, s, target, sem, first=False):
        rows = pl.ds(s * step, step)
        return pltpu.make_async_remote_copy(
            src_ref=own.at[rows] if first else held.at[block, rows],
            dst_ref=held.at[block, rows],
            send_sem=sem,
            recv_sem=recv.at[block, s],
            device_id={"dp": target},
            device_id_type=MESH,
        )

    def to_core(block, s, first=False):
        return hop(block, s, core, send_core.at[block // 2, s], first)

    def to_pair(block, s, first=False):
        return hop(block, s, mate, send_pair.at[block // 4, s], first)

    def to_right(block, s, first=False):
        return hop(block, s, me + 4, send_line.at[0, block // 4, s], first)

    def to_left(block, s, first=False):
        return hop(block, s, me - 4, send_line.at[1, block // 4, s], first)

    for s in range(parts):

        @pl.when(z > 0)
        def _():
            to_left(me, s, True).start()

        @pl.when(z < depth - 1)
        def _():
            to_right(me, s, True).start()

        to_core(me, s, True).start()
        to_pair(me, s, True).start()
    mine = pltpu.make_async_copy(own, held.at[me], keep)
    mine.start()
    fills = [
        pltpu.make_async_copy(weights.at[i], bank.at[i], bank_sem.at[i]) for i in range(3)
    ]
    for fill in fills:
        fill.start()

    def first_of(line, pair):
        return 4 * line + 2 * pair

    def fetch(line, pair, slot):
        return pltpu.make_async_copy(
            grads.at[pl.ds(first_of(line, pair), 2)], coming.at[slot], coming_sem.at[slot]
        )

    def store(line, pair, slot):
        rows = pl.ds(first_of(line, pair) * height, 2 * height)
        return [
            pltpu.make_async_copy(done.at[slot, i], out.at[rows], done_sem.at[slot, i])
            for i, out in enumerate((units, gate_grads, up_grads))
        ]

    def keep_rows(line, pair):
        some = pl.ds(first_of(line, pair), 2)
        return pltpu.make_async_copy(held.at[some], rows_out.at[some], rows_sem.at[line, pair])

    def from_line(line):
        block = first_of(line, y) + c
        for s in range(parts):
            hop(block, s, core, send_core.at[block // 2, s]).wait_recv()

            @pl.when((line < z) & (z < depth - 1))
            def _():
                to_right(block, s).start()

            @pl.when((line > z) & (z > 0))
            def _():
                to_left(block, s).start()

            to_pair(block, s).start()
            to_core(block, s).start()

    def from_pair(line):
        block = first_of(line, 1 - y) + c
        for s in range(parts):
            to_core(block, s).wait_recv()
            to_core(block, s).start()

    steps = [(line, pair) for line in lines for pair in (y, 1 - y)]

    def work(index):
        line, pair = steps[index]
        slot = index % 2
        for s in range(parts):
            to_core(first_of(line, pair) + 1 - c, s).wait_recv()
        if index == 0:
            mine.wait()
            fetch(line, pair, slot).start()
            for fill in fills:
                fill.wait()
        if index + 1 < len(steps):
            fetch(*steps[index + 1], 1 - slot).start()
        fetch(line, pair, slot).wait()
        keep_rows(line, pair).start()
        if index >= 2:
            for item in store(*steps[index - 2], slot):
                item.wait()
        some = pl.ds(first_of(line, pair), 2)

        def inner(n, carry):
            cols = pl.ds(pl.multiple_of(n * tile, tile), tile)
            block = held[some].reshape(2 * height, held.shape[2])
            gate = contract(block, bank[0, cols], 1, 1)
            up = contract(block, bank[1, cols], 1, 1)
            grad = contract(coming[slot].reshape(2 * height, held.shape[2]), bank[2, cols], 1, 1)
            for i, value in enumerate(unit_values(gate, up, grad)):
                done[slot, i, :, cols] = value
            return carry

        lax.fori_loop(0, width // tile, inner, 0)
        for item in store(line, pair, slot):
            item.start()

    work(0)
    from_pair(lines[0])
    from_line(lines[1])
    work(1)
    for k in range(1, depth):
        from_pair(lines[k])
        work(2 * k)
        if k + 1 < depth:
            from_line(lines[k + 1])
        work(2 * k + 1)

    for index in (len(steps) - 2, len(steps) - 1):
        for item in store(*steps[index], index % 2):
            item.wait()
    for line, pair in steps:
        keep_rows(line, pair).wait()
    for j in range(depth):
        block = first_of(j, y) + c
        for s in range(parts):
            to_core(block, s).wait_send()
            to_core(first_of(j, 1 - y) + c, s).wait_send()
            to_pair(block, s).wait_send()

            @pl.when((z >= j) & (z < depth - 1))
            def _():
                to_right(block, s).wait_send()

            @pl.when((z <= j) & (z > 0))
            def _():
                to_left(block, s).wait_send()


def hidden_units(count, ident, own, grads, weights, parts=2):
    height, wide = own.shape
    width = weights.shape[1]
    depth = count // 4
    low = jnp.bfloat16
    sem = pltpu.SemaphoreType.DMA
    anywhere = pl.BlockSpec(memory_space=pl.ANY)
    acts = jax.ShapeDtypeStruct((count * height, width), low)
    return pl.pallas_call(
        functools.partial(hidden_body, count, parts),
        out_shape=[acts, acts, acts, jax.ShapeDtypeStruct((count, height, wide), low)],
        in_specs=[anywhere] * 3,
        out_specs=[anywhere] * 4,
        scratch_shapes=[
            pltpu.VMEM((count, height, wide), low),
            pltpu.VMEM((3, width, wide), low),
            pltpu.VMEM((2, 2, height, wide), low),
            pltpu.VMEM((2, 3, 2 * height, width), low),
            sem((count, parts)),
            sem((2 * depth, parts)),
            sem((depth, parts)),
            sem((2, depth, parts)),
            sem,
            sem((3,)),
            sem((2,)),
            sem((2, 3)),
            sem((depth, 2)),
        ],
        compiler_params=kernel_params(ident),
        name="hidden_units",
    )(own, grads, weights)


def unit_grads_body(count, parts, units, gate_grads, up_grads, weights, rows_all, grads_all,
                    input_sum, output_sum, gate_out, up_out, down_out, gate_far,
                    bank, rows_in, units_in, made, held, loaded, leaving, core_in, pair_in,
                    line_in, bank_sem, rows_sem, fill_sems, units_sem, made_sem, core_send, core_recv,
                    pair_send, pair_recv, line_send, line_recv,
                    far_send, far_recv):
    me, depth, z, y, c = place(count)
    height, wide = input_sum.shape
    width = weights.shape[1]
    step = height // parts
    low = jnp.bfloat16
    core, mate = me + 1 - 2 * c, me + 2 - 4 * y
    near = z < 2
    order = [jnp.where(near, 3, 0), jnp.where(near, 0, 3), jnp.where(near, 2, 1),
             jnp.where(near, 1, 2)]
    greet(count, True)

    def fill(source, at):
        return pltpu.make_async_copy(source, bank.at[at], bank_sem.at[at])

    blocks = width // height

    def fill_rows(source, half, at):
        return [
            pltpu.make_async_copy(
                source.at[half * blocks + i],
                bank.at[at, pl.ds(i * height, height)],
                fill_sems.at[at, i],
            )
            for i in range(blocks)
        ]

    first_fills = [fill(weights.at[i], i) for i in range(3)]
    for item in first_fills:
        item.start()
    grad_tail = fill_rows(grads_all, 1, 3)
    steps = [(line, pair) for line in order for pair in (1 - y, y)]

    def fetch(line, pair, slot, sources):
        rows = pl.ds((4 * line + 2 * pair) * height, 2 * height)
        return [
            pltpu.make_async_copy(source.at[rows], rows_in.at[slot, i], rows_sem.at[slot, i])
            for i, source in enumerate(sources)
        ]

    def rows_of(s):
        return pl.ds(s * step, step)

    def to_core(a, line, pair, slot, s):
        at = 2 * line + pair
        return pltpu.make_async_remote_copy(
            src_ref=leaving.at[a, slot, rows_of(s)],
            dst_ref=core_in.at[a, at, rows_of(s)],
            send_sem=core_send.at[a, slot, s],
            recv_sem=core_recv.at[a, at, s],
            device_id={"dp": core},
            device_id_type=MESH,
        )

    def to_pair(a, line, s):
        return pltpu.make_async_remote_copy(
            src_ref=loaded.at[a, 2 * line + 1 - y, rows_of(s)],
            dst_ref=pair_in.at[a, line, rows_of(s)],
            send_sem=pair_send.at[a, line, s],
            recv_sem=pair_recv.at[a, line, s],
            device_id={"dp": mate},
            device_id_type=MESH,
        )

    def along(a, line, slot, s, target):
        return pltpu.make_async_remote_copy(
            src_ref=loaded.at[a, 2 * line + y, rows_of(s)],
            dst_ref=line_in.at[a, slot, rows_of(s)],
            send_sem=line_send.at[a, line, s],
            recv_sem=line_recv.at[a, slot, s],
            device_id={"dp": target},
            device_id_type=MESH,
        )

    def product(a, index):
        line, pair = steps[index]
        slot = index % 2
        sources = (gate_grads, up_grads) if a == 0 else (units,)
        if index == 0:
            for item in fetch(line, pair, slot, sources):
                item.start()
        if index + 1 < len(steps):
            for item in fetch(*steps[index + 1], 1 - slot, sources):
                item.start()
        if index >= 2:
            for s in range(parts):
                to_core(a, *steps[index - 2], slot, s).wait_send()
        for item in fetch(line, pair, slot, sources):
            item.wait()
        tile = 512

        def inner(n, carry):
            cols = pl.ds(pl.multiple_of(n * tile, tile), tile)
            if a == 0:
                value = contract(rows_in[slot, 0], bank[0, :, cols], 1, 0)
                value += contract(rows_in[slot, 1], bank[1, :, cols], 1, 0)
            else:
                value = contract(rows_in[slot, 0], bank[2, :, cols], 1, 0)
            value = value.astype(low)

            @pl.when(c == 0)
            def _():
                loaded[a, 2 * line + pair, :, cols] = value[:height]
                leaving[a, slot, :, cols] = value[height:]

            @pl.when(c == 1)
            def _():
                loaded[a, 2 * line + pair, :, cols] = value[height:]
                leaving[a, slot, :, cols] = value[:height]

            return carry

        lax.fori_loop(0, wide // tile, inner, 0)
        for s in range(parts):
            to_core(a, line, pair, slot, s).start()

    def finish_sends(a):
        for index in (len(steps) - 2, len(steps) - 1):
            for s in range(parts):
                to_core(a, *steps[index], index % 2, s).wait_send()

    def pair_step(a, k):
        line = order[k]
        at = 2 * line + 1 - y
        for s in range(parts):
            to_core(a, line, 1 - y, 0, s).wait_recv()
            loaded[a, at, rows_of(s)] = loaded[a, at, rows_of(s)] + core_in[a, at, rows_of(s)]
            to_pair(a, line, s).start()

    def own_sum(a, line, s):
        at = 2 * line + y
        to_core(a, line, y, 0, s).wait_recv()
        to_pair(a, line, s).wait_recv()
        part = loaded[a, at, rows_of(s)].astype(jnp.float32)
        part += core_in[a, at, rows_of(s)].astype(jnp.float32)
        held[...] = part + pair_in[a, line, rows_of(s)].astype(jnp.float32)

    def add_line(a, slot, s):
        along(a, z, slot, s, me + 4).wait_recv()
        held[...] += line_in[a, slot, rows_of(s)].astype(jnp.float32)

    def line_step(a, k):
        line = order[k]

        @pl.when(line != z)
        def _():
            for s in range(parts):
                own_sum(a, line, s)

                @pl.when(((line > z) & (z > 0)) | ((line < z) & (z < depth - 1)))
                def _():
                    add_line(a, line, s)

                loaded[a, 2 * line + y, rows_of(s)] = held[...].astype(low)

                @pl.when(line > z)
                def _():
                    along(a, line, line, s, me + 4).start()

                @pl.when(line < z)
                def _():
                    along(a, line, jnp.where(line == z - 1, depth, line), s, me - 4).start()

    def last_step(a, total):
        for s in range(parts):
            own_sum(a, z, s)

            @pl.when(z > 0)
            def _():
                add_line(a, z, s)

            @pl.when(z < depth - 1)
            def _():
                add_line(a, depth, s)

            total[rows_of(s)] = held[...]

    tall = units_in.shape[2]
    each = width // tall

    def bring(g, slot):
        source = (gate_grads, up_grads, units)[g // each]
        cols = pl.ds((g % each) * tall, tall)
        return pltpu.make_async_copy(source.at[:, cols], units_in.at[slot], units_sem.at[slot])

    def put(g, slot):
        rows = pl.ds((g % each) * tall, tall)
        return pltpu.make_async_copy(
            made.at[slot], (gate_out, up_out, down_out)[g // each].at[rows], made_sem.at[slot]
        )

    def swap(g):
        rows = pl.ds(g * tall, tall)
        return pltpu.make_async_remote_copy(
            src_ref=gate_out.at[rows],
            dst_ref=gate_far.at[rows],
            send_sem=far_send.at[g],
            recv_sem=far_recv.at[g],
            device_id={"loop": 1 - lax.axis_index("loop")},
            device_id_type=MESH,
        )

    number = 3 * each

    def weight_product(g):
        slot = g % 2
        if g + 1 < number:
            bring(g + 1, 1 - slot).start()
        bring(g, slot).wait()
        if g >= 2:
            put(g - 2, slot).wait()
            if g - 2 < FAR_TILES:
                swap(g - 2).start()
        at = 0 if g < 2 * each else 2
        tile = 512

        def inner(n, carry):
            cols = pl.ds(pl.multiple_of(n * tile, tile), tile)
            whole = bank[at : at + 2, :, cols].reshape(2 * width, tile)
            made[slot, :, cols] = contract(units_in[slot], whole, 0, 0).astype(low)
            return carry

        lax.fori_loop(0, wide // tile, inner, 0)
        put(g, slot).start()

    for item in first_fills[:2]:
        item.wait()
    for index in range(8):
        product(0, index)
        if index >= 2 and index % 2 == 0:
            pair_step(0, index // 2 - 1)
    finish_sends(0)
    row_fills = fill_rows(rows_all, 0, 0) + fill_rows(rows_all, 1, 1)
    for item in row_fills:
        item.start()
    for item in grad_tail:
        item.start()
    bring(0, 0).start()
    first_fills[2].wait()
    product(1, 0)
    pair_step(0, 3)
    product(1, 1)
    for item in row_fills:
        item.wait()
    weight_product(0)
    weight_product(1)
    line_step(0, 0)
    weight_product(2)
    weight_product(3)
    line_step(0, 1)
    for index in range(2, 8):
        product(1, index)
        if index % 2 == 0:
            pair_step(1, index // 2 - 1)
        if index == 6:
            line_step(0, 2)
    finish_sends(1)
    grad_fills = fill_rows(grads_all, 0, 2)
    for item in grad_fills:
        item.start()
    weight_product(4)
    pair_step(1, 3)
    line_step(0, 3)
    weight_product(5)
    last_step(0, input_sum)
    weight_product(6)
    weight_product(7)
    line_step(1, 0)
    for item in grad_tail + grad_fills:
        item.wait()
    weight_product(8)
    weight_product(9)
    line_step(1, 1)
    weight_product(10)
    weight_product(11)
    line_step(1, 2)
    line_step(1, 3)
    last_step(1, output_sum)

    for g in (number - 2, number - 1):
        put(g, g % 2).wait()
    for g in range(FAR_TILES):
        swap(g).wait()
    for a in range(2):
        for line in range(depth):
            for s in range(parts):
                to_pair(a, line, s).wait_send()

                @pl.when(z != line)
                def _():
                    along(a, line, line, s, me + 4).wait_send()


def unit_grads(count, ident, units, gate_grads, up_grads, weights, rows_all, grads_all, parts=2):
    width, wide = weights.shape[1:]
    height = rows_all.shape[1]
    depth = count // 4
    low = jnp.bfloat16
    sem = pltpu.SemaphoreType.DMA
    anywhere = pl.BlockSpec(memory_space=pl.ANY)
    inside = pl.BlockSpec(memory_space=pltpu.VMEM)
    total = jax.ShapeDtypeStruct((height, wide), jnp.float32)

    return pl.pallas_call(
        functools.partial(unit_grads_body, count, parts),
        out_shape=[total, total] + [jax.ShapeDtypeStruct((width, wide), low)] * 3
        + [jax.ShapeDtypeStruct((FAR_TILES * 256, wide), low)],
        in_specs=[anywhere] * 6,
        out_specs=[inside, inside] + [anywhere] * 4,
        scratch_shapes=[
            pltpu.VMEM((4, width, wide), low),
            pltpu.VMEM((2, 2, 2 * height, width), low),
            pltpu.VMEM((2, count * height, 256), low),
            pltpu.VMEM((2, 256, wide), low),
            pltpu.VMEM((height // parts, wide), jnp.float32),
            pltpu.VMEM((2, 2 * depth, height, wide), low),
            pltpu.VMEM((2, 2, height, wide), low),
            pltpu.VMEM((2, 2 * depth, height, wide), low),
            pltpu.VMEM((2, depth, height, wide), low),
            pltpu.VMEM((2, depth + 1, height, wide), low),
            sem((4,)),
            sem((2, 2)),
            sem((4, width // height)),
            sem((2,)),
            sem((2,)),
            sem((2, 2, parts)),
            sem((2, 2 * depth, parts)),
            sem((2, depth, parts)),
            sem((2, depth, parts)),
            sem((2, depth, parts)),
            sem((2, depth + 1, parts)),
            sem((FAR_TILES,)),
            sem((FAR_TILES,)),
        ],
        compiler_params=kernel_params(ident),
        name="unit_grads",
    )(units, gate_grads, up_grads, weights, rows_all, grads_all)


def sum_plan(count, parts, mine, theirs, core_in, pair_in, line_in, sems):
    me, depth, z, y, c = place(count)
    core_send, core_recv, pair_send, pair_recv, line_send, line_recv = sems
    rows = core_in.shape[1]
    step = rows // parts
    near = z < 2
    order = [
        jnp.where(near, 3, 0),
        jnp.where(near, 0, 3),
        jnp.where(near, 2, 1),
        jnp.where(near, 1, 2),
    ]

    def rows_of(s):
        return pl.ds(s * step, step)

    def to_core(line, pair, s):
        at = 2 * line + pair
        return pltpu.make_async_remote_copy(
            src_ref=theirs(at, rows_of(s)),
            dst_ref=core_in.at[at, rows_of(s)],
            send_sem=core_send.at[at, s],
            recv_sem=core_recv.at[at, s],
            device_id={"dp": me + 1 - 2 * c},
            device_id_type=MESH,
        )

    def to_pair(line, s):
        return pltpu.make_async_remote_copy(
            src_ref=mine(2 * line + 1 - y, rows_of(s)),
            dst_ref=pair_in.at[line, rows_of(s)],
            send_sem=pair_send.at[line, s],
            recv_sem=pair_recv.at[line, s],
            device_id={"dp": me + 2 - 4 * y},
            device_id_type=MESH,
        )

    def along(line, slot, s, target):
        return pltpu.make_async_remote_copy(
            src_ref=mine(2 * line + y, rows_of(s)),
            dst_ref=line_in.at[slot, rows_of(s)],
            send_sem=line_send.at[line, s],
            recv_sem=line_recv.at[slot, s],
            device_id={"dp": target},
            device_id_type=MESH,
        )

    def send_core(line, pair):
        for s in range(parts):
            to_core(line, pair, s).start()

    def pair_step(k):
        line = order[k]
        at = 2 * line + 1 - y
        for s in range(parts):
            to_core(line, 1 - y, s).wait_recv()
            block = mine(at, rows_of(s))
            block[...] = block[...] + core_in[at, rows_of(s)]
            to_pair(line, s).start()

    def own_sum(line, s):
        at = 2 * line + y
        to_core(line, y, s).wait_recv()
        to_pair(line, s).wait_recv()
        part = mine(at, rows_of(s))[...].astype(jnp.float32)
        part += core_in[at, rows_of(s)].astype(jnp.float32)
        return part + pair_in[line, rows_of(s)].astype(jnp.float32)

    def line_step(k):
        line = order[k]

        @pl.when(line != z)
        def _():
            for s in range(parts):
                block = mine(2 * line + y, rows_of(s))
                follows = ((line > z) & (z > 0)) | ((line < z) & (z < depth - 1))
                part = own_sum(line, s)

                @pl.when(follows)
                def _():
                    along(z, line, s, me + 4).wait_recv()
                    extra = line_in[line, rows_of(s)].astype(jnp.float32)
                    block[...] = (part + extra).astype(block.dtype)

                @pl.when(jnp.logical_not(follows))
                def _():
                    block[...] = part.astype(block.dtype)

                @pl.when(line > z)
                def _():
                    along(line, line, s, me + 4).start()

                @pl.when(line < z)
                def _():
                    along(line, jnp.where(line == z - 1, depth, line), s, me - 4).start()

    def last_step(total):
        for s in range(parts):
            total[rows_of(s)] = own_sum(z, s)

            @pl.when(z > 0)
            def _():
                along(z, z, s, me + 4).wait_recv()
                total[rows_of(s)] += line_in[z, rows_of(s)].astype(jnp.float32)

            @pl.when(z < depth - 1)
            def _():
                along(z, depth, s, me + 4).wait_recv()
                total[rows_of(s)] += line_in[depth, rows_of(s)].astype(jnp.float32)

    def finish():
        for line in range(depth):
            for s in range(parts):
                for pair in range(2):
                    to_core(line, pair, s).wait_send()
                to_pair(line, s).wait_send()

                @pl.when(z != line)
                def _():
                    along(line, line, s, me + 4).wait_send()

    return order, send_core, pair_step, line_step, last_step, finish


def sum_sems(count, parts):
    depth = count // 4
    sem = pltpu.SemaphoreType.DMA
    return [
        sem((2 * depth, parts)),
        sem((2 * depth, parts)),
        sem((depth, parts)),
        sem((depth, parts)),
        sem((depth, parts)),
        sem((depth + 1, parts)),
    ]


def sum_rooms(count, rows, cols, kind=jnp.bfloat16):
    depth = count // 4
    return [
        pltpu.VMEM((2 * depth, rows, cols), kind),
        pltpu.VMEM((depth, rows, cols), kind),
        pltpu.VMEM((depth + 1, rows, cols), kind),
    ]


def sum_terms(count, parts, terms, rooms, sems):
    me, depth, z, y, c = place(count)

    def mine(at, rows):
        return terms.at[2 * at + c, rows]

    def theirs(at, rows):
        return terms.at[2 * at + 1 - c, rows]

    return sum_plan(count, parts, mine, theirs, *rooms, sems)


def turn_back(values, cosine, sine):
    half = values.shape[-1] // 2
    first, second = values[:, :half], values[:, half:]
    return jnp.concatenate(
        [first * cosine + second * sine, second * cosine - first * sine], axis=1
    )


def attention_grads_body(count, attended, grad_rows, weight, queries, keys_values, level,
                         cosine, sine, own_seq, own_order, all_seq, all_order, first, second,
                         joint_grads, lowrank_grads, out_sum,
                         weight_in, out_first, both_second, grad_att, allowed, kv_total, kv_terms, kv_sum, out_terms,
                         out_core, out_pair, out_line, kv_core, kv_pair, kv_line,
                         weight_sem, *sems):
    me, depth, z, y, c = place(count)
    height, wide = grad_rows.shape
    size = HEAD_SIZE
    scale = size ** (-0.5)
    low = jnp.bfloat16
    greet(count)
    rank = ADAPTER_RANK
    loads = [
        pltpu.make_async_copy(source, bank, weight_sem.at[i])
        for i, (source, bank) in enumerate(
            (
                (weight, weight_in),
                (first.at[:, pl.ds(3 * rank, rank)], out_first),
                (second.at[:, pl.ds(0, PROJECTED_WIDTH + wide)], both_second),
            )
        )
    ]
    for item in loads:
        item.start()
    order, send_out, pair_out, line_out, last_out, finish_out = sum_terms(
        count, 2, out_terms, (out_core, out_pair, out_line), sems[:6]
    )
    _, send_kv, pair_kv, line_kv, last_kv, finish_kv = sum_terms(
        count, 1, kv_terms, (kv_core, kv_pair, kv_line), sems[6:]
    )
    feature, some = out_terms.shape[1:]

    def out_product(line):
        def inner(n, carry):
            into = pl.ds(pl.multiple_of(n * 512, 512), 512)
            cols = pl.ds(pl.multiple_of(line * 4 * feature, 4 * feature), 4 * feature)
            value = contract(attended[:, cols], grad_rows[:, into], 0, 0).astype(low)
            out_terms[pl.ds(4 * line, 4), :, into] = value.reshape(4, feature, 512)
            return carry

        lax.fori_loop(0, some // 512, inner, 0)
        for pair in (1 - y, y):
            send_out(line, pair)

    for line in order:
        out_product(line)
    for item in loads:
        item.wait()
    tile = 256
    back_out = contract(grad_rows[...], both_second[:, PROJECTED_WIDTH:], 1, 1).astype(low)

    def product(n, carry):
        cols = pl.ds(pl.multiple_of(n * tile, tile), tile)
        value = contract(grad_rows[...], weight_in[cols], 1, 1)
        value += contract(back_out, out_first[cols], 1, 1)
        grad_att[:, cols] = value.astype(low)
        return carry

    lax.fori_loop(0, wide // tile, product, 0)
    same = own_seq[...] == all_seq[...]
    allowed[...] = jnp.where(same & (all_order[...] <= own_order[...]), 1.0, 0.0)
    for k in range(depth):
        pair_out(k)
    keys = keys_values[:, :size]
    values = keys_values[:, size:]

    def heads(pair):
        def both(ref):
            return jnp.concatenate(
                [
                    ref[:, 2 * pair * size : (2 * pair + 1) * size],
                    ref[:, (2 * pair + 1) * size : (2 * pair + 2) * size],
                ],
                axis=0,
            )

        query = both(queries)
        grad = both(grad_att)
        keep = jnp.concatenate([allowed[...], allowed[...]], axis=0) > 0.5
        scores = jnp.where(keep, contract(query, keys, 1, 1) * scale, FLOOR_SCORE)
        prob = jnp.exp(scores - level[pair][:, :1])
        grad_prob = contract(grad, values, 1, 1)
        centre = jnp.sum(prob * grad_prob, axis=-1, keepdims=True)
        grad_scores = (prob * (grad_prob - centre)).astype(low)
        back = contract(grad_scores, keys, 1, 0) * scale
        for i in range(2):
            part = turn_back(back[i * height : (i + 1) * height], cosine[...], sine[...])
            joint_grads[:, (2 * pair + i) * size : (2 * pair + i + 1) * size] = part.astype(low)
        key_part = contract(grad_scores, query, 0, 0) * scale
        value_part = contract(prob.astype(low), grad, 0, 0)
        if pair == 0:
            kv_total[:, :size] = key_part
            kv_total[:, size:] = value_part
        else:
            kv_total[:, :size] += key_part
            kv_total[:, size:] += value_part

    for pair in range(wide // size // 2):
        heads(pair)
    for block in range(count):
        kv_terms[block] = kv_total[block * height : (block + 1) * height].astype(low)
    for pair in (1 - y, y):
        for line in order:
            send_kv(line, pair)
    for k in range(depth):
        pair_kv(k)
    for k in range(depth):
        line_out(k)
    for k in range(depth):
        line_kv(k)
    last_kv(kv_sum)
    part = turn_back(kv_sum[:, :size], cosine[...], sine[...])
    joint_grads[:, wide : wide + size] = part.astype(low)
    joint_grads[:, wide + size :] = kv_sum[:, size:].astype(low)
    for i, (at, stop) in enumerate(
        ((0, wide), (wide, wide + size), (wide + size, wide + 2 * size))
    ):
        value = contract(joint_grads[:, at:stop], both_second[:, at:stop], 1, 1)
        lowrank_grads[:, i * rank : (i + 1) * rank] = value.astype(low)
    last_out(out_sum)
    finish_out()
    finish_kv()


def attention_grads(count, ident, attended, grad_rows, weight, queries, keys_values, level,
                    cosine, sine, own_seq, own_order, all_seq, all_order, first, second):
    height, wide = grad_rows.shape
    total = keys_values.shape[0]
    low = jnp.bfloat16
    inside = pl.BlockSpec(memory_space=pltpu.VMEM)
    anywhere = pl.BlockSpec(memory_space=pl.ANY)
    feature = attended.shape[1] // count
    both = 2 * HEAD_SIZE
    return pl.pallas_call(
        functools.partial(attention_grads_body, count),
        out_shape=[
            jax.ShapeDtypeStruct((height, wide + both), low),
            jax.ShapeDtypeStruct((height, 3 * ADAPTER_RANK), low),
            jax.ShapeDtypeStruct((feature, OUT_SPLIT), jnp.float32),
        ],
        in_specs=[inside] * 2 + [anywhere] + [inside] * 9 + [anywhere] * 2,
        out_specs=[inside] * 3,
        scratch_shapes=[
            pltpu.VMEM(weight.shape, low),
            pltpu.VMEM((wide, ADAPTER_RANK), low),
            pltpu.VMEM((ADAPTER_RANK, PROJECTED_WIDTH + wide), low),
            pltpu.VMEM(attended.shape, low),
            pltpu.VMEM((height, total), jnp.float32),
            pltpu.VMEM((total, both), jnp.float32),
            pltpu.VMEM((count, height, both), low),
            pltpu.VMEM((height, both), jnp.float32),
            pltpu.VMEM((count, feature, OUT_SPLIT), low),
        ]
        + sum_rooms(count, feature, OUT_SPLIT)
        + sum_rooms(count, height, both)
        + [pltpu.SemaphoreType.DMA((3,))]
        + sum_sems(count, 2)
        + sum_sems(count, 1),
        compiler_params=kernel_params(ident),
        name="attention_grads",
    )(
        attended, grad_rows, weight, queries, keys_values, level,
        cosine, sine, own_seq, own_order, all_seq, all_order, first, second,
    )


def closing_body(count, normed, joint_grads, attended, grad_rows, lowrank, lowrank_out, stream,
                 gain, grad_middle, small, lowrank_grads, weight, gate_grads, up_grads, down_grads, factors,
                 first, second,
                 in_sum, out_sum, second_sum, first_sum, small_sum, stream_grad, factor_grads,
                 bank, in_bank, factor_bank, second_bank, made, in_terms, out_terms,
                 second_terms, first_terms, small_terms, *scratch):
    me, depth, z, y, c = place(count)
    height, wide = normed.shape
    rank = ADAPTER_RANK
    width = gate_grads.shape[0]
    low = jnp.bfloat16
    rooms = [scratch[3 * i : 3 * i + 3] for i in range(5)]
    weight_sem, grads_sem, factor_sem, made_sem, side_sem = scratch[15:20]
    sems = [scratch[20 + 6 * i : 26 + 6 * i] for i in range(5)]
    greet(count)
    halves = [
        pltpu.make_async_copy(weight.at[pl.ds(i * width, width)], bank, weight_sem.at[i])
        for i in range(wide // width)
    ]
    halves[0].start()
    loads = [
        pltpu.make_async_copy(
            factors.at[pl.ds(me * width, width), pl.ds(0, rank)], factor_bank, factor_sem.at[0]
        ),
        pltpu.make_async_copy(
            second.at[:, pl.ds(PROJECTED_WIDTH + MODEL_WIDTH, wide)], second_bank, factor_sem.at[2]
        ),
    ]
    in_load = pltpu.make_async_copy(first.at[:, pl.ds(0, 3 * rank)], in_bank, factor_sem.at[3])
    first_load = pltpu.make_async_copy(
        first.at[:, pl.ds(4 * rank, 2 * rank)], in_bank.at[:, pl.ds(0, 2 * rank)], factor_sem.at[1]
    )
    side_load = pltpu.make_async_copy(
        factors.at[pl.ds(me * width, width), pl.ds(rank, 2 * rank)],
        bank.at[:, pl.ds(wide, 2 * rank)],
        side_sem,
    )
    for item in [in_load] + loads:
        item.start()
    terms = (in_terms, out_terms, second_terms, first_terms, small_terms)
    parts = (2, 2, 1, 1, 1)
    plans = [sum_terms(count, parts[i], terms[i], rooms[i], sems[i]) for i in range(5)]
    order = plans[0][0]
    send = [plan[1] for plan in plans]
    pair_step = [plan[2] for plan in plans]
    line_step = [plan[3] for plan in plans]
    last_step = [plan[4] for plan in plans]
    finish = [plan[5] for plan in plans]

    def block_products(i, left, right, at):
        feature, some = terms[i].shape[1:]

        def product(line):
            def inner(n, carry):
                cols = pl.ds(pl.multiple_of(line * 4 * feature, 4 * feature), 4 * feature)
                into = pl.ds(pl.multiple_of(n * 512, 512), 512)
                from_ = pl.ds(pl.multiple_of(at + n * 512, 512), 512)
                value = contract(left[:, cols], right[:, from_], 0, 0).astype(low)
                terms[i][pl.ds(4 * line, 4), :, into] = value.reshape(4, feature, 512)
                return carry

            lax.fori_loop(0, some // 512, inner, 0)
            for pair in (1 - y, y):
                send[i](line, pair)

        for line in order:
            product(line)

    def send_all(i):
        for pair in (1 - y, y):
            for line in order:
                send[i](line, pair)
        for k in range(depth):
            pair_step[i](k)

    def put_second(at, value):
        size = second_terms.shape[1]
        value = value.astype(low)
        start = at
        while start < at + value.shape[0]:
            block, inner = start // size, start % size
            rows = min(size - inner, at + value.shape[0] - start)
            second_terms[block, inner : inner + rows, :] = value[start - at : start - at + rows]
            start += rows

    def half_product(i):
        halves[i].wait()

        def product(n, carry):
            some = pl.ds(pl.multiple_of(n * 256, 256), 256)
            cols = pl.ds(pl.multiple_of(i * width + n * 256, 256), 256)
            value = contract(joint_grads[...], bank[some], 1, 1)
            stream_grad[:, cols] = value + contract(lowrank_grads[...], in_bank[cols], 1, 1)
            return carry

        lax.fori_loop(0, width // 256, product, 0)
        if i + 1 < len(halves):
            halves[i + 1].start()

    block_products(0, normed, joint_grads, 0)
    for k in range(depth):
        pair_step[0](k)
    in_load.wait()
    half_product(0)
    block_products(1, attended, grad_rows, OUT_SPLIT)
    for k in range(depth):
        pair_step[1](k)
    for i in range(1, len(halves)):
        half_product(i)
    first_load.start()
    side_load.start()

    rows = stream[...].astype(jnp.float32)
    inverse = lax.rsqrt(jnp.mean(rows * rows, axis=-1, keepdims=True) + EPSILON)
    grad = stream_grad[...]
    unit = rows * inverse
    gain_grad = jnp.sum(grad * unit, axis=0, keepdims=True)
    scaled = grad * gain[...]
    centre = jnp.mean(scaled * unit, axis=-1, keepdims=True)
    stream_grad[...] = grad_middle[...] + inverse * (scaled - unit * centre)
    small_terms[...] = small[...]
    share = wide // count
    for block in range(count):
        small_terms[block, 0:1, :share] = gain_grad[:, block * share : (block + 1) * share]
    send_all(4)

    def bring(i):
        source = (gate_grads, up_grads, down_grads)[i]
        return pltpu.make_async_copy(source, bank.at[:, pl.ds(0, wide)], grads_sem.at[i])

    bring(0).start()
    line_step[0](0)
    value_at = QUERY_WIDTH + HEAD_SIZE
    for at, stop, left, own in (
        (0, QUERY_WIDTH, joint_grads, lowrank[:, :rank]),
        (QUERY_WIDTH, value_at, joint_grads, lowrank[:, rank : 2 * rank]),
        (value_at, PROJECTED_WIDTH, joint_grads, lowrank[:, 2 * rank :]),
    ):
        put_second(at, contract(left[:, at:stop], own, 0, 0))
    put_second(PROJECTED_WIDTH, contract(grad_rows[...], lowrank_out[...], 0, 0))
    for item in loads + [first_load, side_load]:
        item.wait()

    def put_factor(cols):
        return pltpu.make_async_copy(
            made, factor_grads.at[:, pl.ds(cols * rank, rank)], made_sem.at[cols]
        )

    line_step[0](1)
    held = bank.at[:, pl.ds(0, wide)]
    for i in range(2):
        bring(i).wait()
        if i > 0:
            put_factor(i).wait()
        made[...] = contract(held[...], in_bank[:, i * rank : (i + 1) * rank], 1, 0)
        put_factor(i + 1).start()
        value = contract(held[...], bank[:, wide + i * rank : wide + (i + 1) * rank], 0, 0)
        first_terms[:, :, i * rank : (i + 1) * rank] = value.astype(low).reshape(
            count, wide // count, rank
        )
        bring(i + 1).start()
        if i == 0:
            line_step[0](2)
    send_all(3)
    bring(2).wait()
    put_factor(2).wait()
    made[...] = contract(held[...], second_bank[...], 1, 1)
    put_factor(0).start()
    put_second(
        PROJECTED_WIDTH + MODEL_WIDTH, contract(held[...], factor_bank[...], 0, 0)
    )
    send_all(2)
    line_step[0](3)
    for k in range(depth):
        line_step[1](k)
    last_step[0](in_sum)
    last_step[1](out_sum)
    for i, total in ((4, small_sum), (3, first_sum), (2, second_sum)):
        for k in range(depth):
            line_step[i](k)
        last_step[i](total)
    for item in finish:
        item()
    put_factor(0).wait()


def closing(count, ident, normed, joint_grads, attended, grad_rows, lowrank, lowrank_out, stream,
            gain, grad_middle, small, lowrank_grads, weight, gate_grads, up_grads, down_grads, factors, first,
            second):
    height, wide = normed.shape
    width = gate_grads.shape[0]
    low, high = jnp.bfloat16, jnp.float32
    rank = ADAPTER_RANK
    inside = pl.BlockSpec(memory_space=pltpu.VMEM)
    anywhere = pl.BlockSpec(memory_space=pl.ANY)
    share = wide // count
    shapes = [
        (share, joint_grads.shape[1], low),
        (share, wide - OUT_SPLIT, low),
        (second.shape[1] // count, rank, low),
        (share, 2 * rank, low),
        (8, 128, high),
    ]
    sem = pltpu.SemaphoreType.DMA
    rooms, sems = [], []
    for (rows, cols, kind), parts in zip(shapes, (2, 2, 1, 1, 1)):
        rooms += sum_rooms(count, rows, cols, kind)
        sems += sum_sems(count, parts)
    return pl.pallas_call(
        functools.partial(closing_body, count),
        out_shape=[jax.ShapeDtypeStruct((rows, cols), high) for rows, cols, _ in shapes]
        + [
            jax.ShapeDtypeStruct((height, wide), high),
            jax.ShapeDtypeStruct((width, 3 * rank), high),
        ],
        in_specs=[inside] * 11 + [anywhere] * 7,
        out_specs=[inside] * 6 + [anywhere],
        scratch_shapes=[
            pltpu.VMEM((width, weight.shape[1]), low),
            pltpu.VMEM((wide, 3 * rank), low),
            pltpu.VMEM((width, rank), low),
            pltpu.VMEM((rank, wide), low),
            pltpu.VMEM((width, rank), high),
        ]
        + [pltpu.VMEM((count, rows, cols), kind) for rows, cols, kind in shapes]
        + rooms
        + [sem((wide // width,)), sem((3,)), sem((4,)), sem((3,)), sem]
        + sems,
        compiler_params=kernel_params(ident),
        name="closing",
    )(
        normed, joint_grads, attended, grad_rows, lowrank, lowrank_out, stream, gain, grad_middle,
        small, lowrank_grads, weight, gate_grads, up_grads, down_grads, factors, first, second,
    )


def swap_loops(values):
    return lax.ppermute(values, "loop", [(0, 1), (1, 0)])


def both_loops(values):
    return values.astype(jnp.float32) + swap_loops(values).astype(jnp.float32)


def per_device(
    layer_input_stream,
    layer_output_gradient,
    attention_in_weight,
    attention_out_weight,
    feedforward_weight,
    layer_norm_gains,
    adapter_first_factors,
    adapter_second_factors,
    adapter_hidden_factors,
    group_sequence_lengths,
    token_per_row,
    token_exit_depth,
):
    current_loop = lax.axis_index("loop")
    dp_index = lax.axis_index("dp")
    loop_count = lax.axis_size("loop")
    count = lax.axis_size("dp")
    local_rows = layer_input_stream.shape[1]
    low = jnp.bfloat16
    key_at = QUERY_WIDTH
    value_at = QUERY_WIDTH + HEAD_SIZE
    down_at = PROJECTED_WIDTH + MODEL_WIDTH
    live_all, seq_all, order_all, pos_all = token_facts(token_per_row[0], group_sequence_lengths[0])
    first_row = dp_index * local_rows

    def own_slice(values):
        return lax.dynamic_slice_in_dim(values, first_row, local_rows, 0)

    live_own = own_slice(live_all)
    seq_own = own_slice(seq_all)
    order_own = own_slice(order_all)
    pos_own = own_slice(pos_all)
    active_mask = (live_own & (token_exit_depth[0] > current_loop)).astype(jnp.float32)[:, None]
    stream = layer_input_stream[0]
    residual_stream = stream.astype(jnp.float32)
    grad_out = layer_output_gradient[0].astype(jnp.float32)
    adapter_first = adapter_first_factors[0]
    adapter_second = adapter_second_factors[0]
    ffn_weight = jnp.swapaxes(feedforward_weight, 0, 1)
    feedforward_gradient = (active_mask * grad_out).astype(low)

    input_weight, output_weight, ffn_folded, normed_input, lowrank_projection = opening(
        count, 1, stream, layer_norm_gains[:1], (attention_in_weight, attention_out_weight),
        (IN_SHARE, OUT_SHARE), ffn_weight, adapter_hidden_factors[0], adapter_first,
        adapter_second,
    )
    half = HEAD_SIZE // 2
    freqs = 10000.0 ** (-jnp.arange(half, dtype=jnp.float32) / half)
    angles = pos_own.astype(jnp.float32)[:, None] * freqs
    cosine, sine = jnp.cos(angles), jnp.sin(angles)
    facts = (cosine, sine, seq_own[:, None], order_own[:, None], seq_all[None], order_all[None])
    (
        queries, attended_rows, output_projection, level, middle_state, second_normed_input,
        kv_blocks, grad_blocks,
    ) = attention(
        count, 2, normed_input, lowrank_projection, stream, active_mask, layer_norm_gains[1:],
        *facts, input_weight, output_weight, adapter_first, adapter_second, feedforward_gradient,
    )
    units_own, grad_gate_own, grad_up_own, normed_blocks = hidden_units(
        count, 3, second_normed_input, grad_blocks, ffn_folded
    )
    second_normed_gradient, ffn_sum, gate_grad, up_grad, down_grad, gate_other = unit_grads(
        count, 4, units_own, grad_gate_own, grad_up_own, ffn_folded, normed_blocks, grad_blocks
    )
    gate_last = swap_loops(gate_grad[FAR_TILES * 256 :])
    up_other = swap_loops(up_grad)
    down_other = swap_loops(down_grad)

    complete_output = middle_state + active_mask * ffn_sum
    confidence = root_mean(residual_stream) / (
        root_mean(residual_stream) + root_mean(complete_output - residual_stream)
    )
    conf_sum = jnp.sum(jnp.where(live_own, confidence, 0.0))
    depth_hits = (
        (token_exit_depth[0][:, None] == jnp.arange(loop_count + 1, dtype=jnp.int32)[None, :])
        & live_own[:, None]
    ).astype(jnp.float32)
    stats = jnp.concatenate([conf_sum[None], jnp.sum(depth_hits, axis=0)])
    grad_middle_part, grad_gain_two = jax.vjp(norm_rows, middle_state, layer_norm_gains[1])[1](
        second_normed_gradient
    )
    grad_middle = grad_out + grad_middle_part
    branch_gradient = (active_mask * grad_middle).astype(low)
    joint_grads, lowrank_grads, out_first = attention_grads(
        count, 5, attended_rows, branch_gradient, output_weight, queries,
        kv_blocks.reshape(count * local_rows, 2 * HEAD_SIZE), level, *facts, adapter_first,
        adapter_second,
    )
    width_own = MODEL_WIDTH // count
    small = jnp.zeros((count, 8, 128), jnp.float32)
    small = small.at[:, 1, :width_own].set(grad_gain_two.reshape(count, width_own))
    small = small.at[:, 2, : loop_count + 2].set(stats[None])
    (
        in_portion, out_last, second_grad, first_grad_hidden, small_sum, hidden_grad,
        adapter_hidden_gradient,
    ) = closing(
        count, 6, normed_input, joint_grads, attended_rows, branch_gradient, lowrank_projection,
        output_projection, stream, layer_norm_gains[:1], grad_middle, small, lowrank_grads,
        input_weight, gate_grad, up_grad, down_grad, adapter_hidden_factors[0], adapter_first,
        adapter_second,
    )
    gate_other, gate_last, up_other, down_other, small_sum = lax.optimization_barrier(
        (gate_other, gate_last, up_other, down_other, small_sum)
    )
    gate_other = jnp.concatenate([gate_other, gate_last], axis=0)
    in_low = in_portion.astype(low)
    out_low = jnp.concatenate([out_first, out_last], axis=1).astype(low)
    adapter_first_gradient = jnp.concatenate(
        [
            outer_columns(in_low[:, :key_at], adapter_second[:, :key_at]),
            outer_columns(in_low[:, key_at:value_at], adapter_second[:, key_at:value_at]),
            outer_columns(in_low[:, value_at:], adapter_second[:, value_at:PROJECTED_WIDTH]),
            outer_columns(out_low, adapter_second[:, PROJECTED_WIDTH:down_at]),
            first_grad_hidden,
        ],
        axis=1,
    )
    small_total = both_loops(small_sum)
    sum_gains = small_total[:2, :width_own]
    depth_total = small_total[2, 1 : loop_count + 2]
    mean_confidence = small_total[2, 0] / jnp.sum(depth_total)
    exit_counts = depth_total.astype(jnp.int32)
    sum_mlp = jnp.stack(
        [
            gate_grad.astype(jnp.float32) + gate_other.astype(jnp.float32),
            up_grad.astype(jnp.float32) + up_other.astype(jnp.float32),
            down_grad.astype(jnp.float32) + down_other.astype(jnp.float32),
        ],
        axis=1,
    )
    return (
        complete_output.astype(low)[None],
        hidden_grad[None],
        both_loops(in_low),
        both_loops(out_low),
        sum_mlp,
        sum_gains,
        adapter_first_gradient[None],
        jnp.swapaxes(second_grad, 0, 1)[None],
        adapter_hidden_gradient[None],
        exit_counts,
        mean_confidence,
    )


def per_device_any(
    layer_input_stream,
    layer_output_gradient,
    attention_in_weight,
    attention_out_weight,
    feedforward_weight,
    layer_norm_gains,
    adapter_first_factors,
    adapter_second_factors,
    adapter_hidden_factors,
    group_sequence_lengths,
    token_per_row,
    token_exit_depth,
):
    current_loop = lax.axis_index("loop")
    dp_index = lax.axis_index("dp")
    loop_count = lax.axis_size("loop")
    local_rows = layer_input_stream.shape[1]
    ffn_rows = feedforward_weight.shape[0]
    scale = HEAD_SIZE ** (-0.5)
    live_all, seq_all, order_all, pos_all = token_facts(token_per_row[0], group_sequence_lengths[0])
    first_row = dp_index * local_rows

    def own_slice(values):
        return lax.dynamic_slice_in_dim(values, first_row, local_rows, 0)

    live_own = own_slice(live_all)
    seq_own = own_slice(seq_all)
    order_own = own_slice(order_all)
    pos_own = own_slice(pos_all)
    active_mask = (live_own & (token_exit_depth[0] > current_loop)).astype(jnp.float32)[:, None]
    residual_stream = layer_input_stream[0].astype(jnp.float32)
    adapter_first = adapter_first_factors[0]
    adapter_second = adapter_second_factors[0]
    adapter_feedforward = adapter_hidden_factors[0]
    ffn_own = lax.dynamic_slice_in_dim(adapter_feedforward, dp_index * ffn_rows, ffn_rows, 0)
    input_weight, output_weight = (
        lax.all_gather(attention_in_weight, "dp", axis=0, tiled=True),
        lax.all_gather(attention_out_weight, "dp", axis=0, tiled=True),
    )
    normed_input = norm_rows(residual_stream, layer_norm_gains[0]).astype(jnp.bfloat16)
    lowrank_projection = matrix_product(normed_input, adapter_first[:, : 3 * ADAPTER_RANK]).astype(
        jnp.bfloat16
    )
    adapter_query_key_value = jnp.concatenate(
        [
            matrix_product(lowrank_projection[:, :ADAPTER_RANK], adapter_second[:, :QUERY_WIDTH]),
            matrix_product(
                lowrank_projection[:, ADAPTER_RANK : 2 * ADAPTER_RANK],
                adapter_second[:, QUERY_WIDTH : QUERY_WIDTH + HEAD_SIZE],
            ),
            matrix_product(
                lowrank_projection[:, 2 * ADAPTER_RANK :],
                adapter_second[:, QUERY_WIDTH + HEAD_SIZE : PROJECTED_WIDTH],
            ),
        ],
        axis=1,
    )
    query_key_value_linear = matrix_product(normed_input, input_weight) + adapter_query_key_value
    queries = rotate(
        query_key_value_linear[:, :QUERY_WIDTH].reshape(local_rows, HEADS, HEAD_SIZE), pos_own
    ).astype(jnp.bfloat16)
    key_rot = rotate(
        query_key_value_linear[:, QUERY_WIDTH : QUERY_WIDTH + HEAD_SIZE].reshape(
            local_rows, 1, HEAD_SIZE
        ),
        pos_own,
    )[:, 0]
    kv_send = jnp.concatenate(
        [key_rot, query_key_value_linear[:, QUERY_WIDTH + HEAD_SIZE :]], axis=1
    ).astype(jnp.bfloat16)
    kv_all = lax.all_gather(kv_send, "dp", axis=0, tiled=True)
    keys = kv_all[:, :HEAD_SIZE]
    values = kv_all[:, HEAD_SIZE:]
    key_total = kv_all.shape[0]
    allowed = ((seq_own[:, None] == seq_all[None, :]) & (order_all[None, :] <= order_own[:, None]))[
        :, None, :
    ]
    query_rows = queries.reshape(local_rows * HEADS, HEAD_SIZE)

    def score_rows():
        raw_scores = (outer_columns(query_rows, keys) * scale).reshape(local_rows, HEADS, key_total)
        return jnp.where(allowed, raw_scores, FLOOR_SCORE)

    scores = score_rows()
    top_score = jnp.max(scores, axis=-1, keepdims=True)
    expo = jnp.exp(scores - top_score)
    mass = jnp.sum(expo, axis=-1, keepdims=True)
    prob_low = (expo / mass).astype(jnp.bfloat16)
    attended_rows = (
        matrix_product(prob_low.reshape(local_rows * HEADS, key_total), values)
        .reshape(local_rows, QUERY_WIDTH)
        .astype(jnp.bfloat16)
    )
    output_projection = matrix_product(
        attended_rows, adapter_first[:, 3 * ADAPTER_RANK : 4 * ADAPTER_RANK]
    ).astype(jnp.bfloat16)
    branch_output = matrix_product(attended_rows, output_weight) + matrix_product(
        output_projection, adapter_second[:, PROJECTED_WIDTH : PROJECTED_WIDTH + MODEL_WIDTH]
    )
    middle_state = residual_stream + active_mask * branch_output
    second_normed_input = norm_rows(middle_state, layer_norm_gains[1]).astype(jnp.bfloat16)
    feedforward_projection = matrix_product(
        second_normed_input, adapter_first[:, 4 * ADAPTER_RANK :]
    ).astype(jnp.bfloat16)
    normed_all, proj_all = (
        lax.all_gather(second_normed_input, "dp", axis=0, tiled=True),
        lax.all_gather(feedforward_projection, "dp", axis=0, tiled=True),
    )
    gate_own = outer_columns(normed_all, feedforward_weight[:, 0, :]) + outer_columns(
        proj_all[:, :ADAPTER_RANK], ffn_own[:, ADAPTER_RANK : 2 * ADAPTER_RANK]
    )
    up_own = outer_columns(normed_all, feedforward_weight[:, 1, :]) + outer_columns(
        proj_all[:, ADAPTER_RANK:], ffn_own[:, 2 * ADAPTER_RANK :]
    )
    units_own = geglu(gate_own, up_own).astype(jnp.bfloat16)
    ffn_sum, low_sum = (
        lax.psum_scatter(
            matrix_product(units_own, feedforward_weight[:, 2, :]),
            "dp",
            scatter_dimension=0,
            tiled=True,
        ),
        lax.psum_scatter(
            matrix_product(units_own, ffn_own[:, :ADAPTER_RANK]),
            "dp",
            scatter_dimension=0,
            tiled=True,
        ),
    )
    down_lowrank = low_sum.astype(jnp.bfloat16)
    complete_output = middle_state + active_mask * (
        ffn_sum + matrix_product(down_lowrank, adapter_second[:, PROJECTED_WIDTH + MODEL_WIDTH :])
    )
    confidence = root_mean(residual_stream) / (
        root_mean(residual_stream) + root_mean(complete_output - residual_stream)
    )
    conf_sum = jnp.sum(jnp.where(live_own, confidence, 0.0))
    depth_hits = (
        (token_exit_depth[0][:, None] == jnp.arange(loop_count + 1, dtype=jnp.int32)[None, :])
        & live_own[:, None]
    ).astype(jnp.float32)
    conf_total, depth_total = lax.psum((conf_sum, jnp.sum(depth_hits, axis=0)), ("loop", "dp"))
    mean_confidence = conf_total / jnp.sum(depth_total)
    exit_counts = depth_total.astype(jnp.int32)
    grad_out = layer_output_gradient[0].astype(jnp.float32)
    feedforward_gradient = (active_mask * grad_out).astype(jnp.bfloat16)
    lowrank_gradient = outer_columns(
        feedforward_gradient, adapter_second[:, PROJECTED_WIDTH + MODEL_WIDTH :]
    ).astype(jnp.bfloat16)
    grad_ffn_all, grad_low_all = (
        lax.all_gather(feedforward_gradient, "dp", axis=0, tiled=True),
        lax.all_gather(lowrank_gradient, "dp", axis=0, tiled=True),
    )
    hidden_unit_gradient = outer_columns(grad_ffn_all, feedforward_weight[:, 2, :]) + outer_columns(
        grad_low_all, ffn_own[:, :ADAPTER_RANK]
    )
    grad_gate_own, grad_up_own = jax.vjp(geglu, gate_own, up_own)[1](hidden_unit_gradient)
    grad_gate_own = grad_gate_own.astype(jnp.bfloat16)
    grad_up_own = grad_up_own.astype(jnp.bfloat16)
    input_terms = matrix_product(grad_gate_own, feedforward_weight[:, 0, :]) + matrix_product(
        grad_up_own, feedforward_weight[:, 1, :]
    )
    proj_terms = jnp.concatenate(
        [
            matrix_product(grad_gate_own, ffn_own[:, ADAPTER_RANK : 2 * ADAPTER_RANK]),
            matrix_product(grad_up_own, ffn_own[:, 2 * ADAPTER_RANK :]),
        ],
        axis=1,
    )
    grad_norm_base, grad_proj = (
        lax.psum_scatter(input_terms, "dp", scatter_dimension=0, tiled=True),
        lax.psum_scatter(proj_terms, "dp", scatter_dimension=0, tiled=True),
    )
    ffn_grad = jnp.concatenate(
        [
            inner_rows(grad_gate_own, normed_all),
            inner_rows(grad_up_own, normed_all),
            inner_rows(units_own, grad_ffn_all),
            inner_rows(units_own, grad_low_all),
            inner_rows(grad_gate_own, proj_all[:, :ADAPTER_RANK]),
            inner_rows(grad_up_own, proj_all[:, ADAPTER_RANK:]),
        ],
        axis=1,
    )
    lowrank_projection_gradient = grad_proj.astype(jnp.bfloat16)
    second_normed_gradient = grad_norm_base + outer_columns(
        lowrank_projection_gradient, adapter_first[:, 4 * ADAPTER_RANK :]
    )
    grad_middle_part, grad_gain_two = jax.vjp(norm_rows, middle_state, layer_norm_gains[1])[1](
        second_normed_gradient
    )
    grad_middle = grad_out + grad_middle_part
    branch_gradient = (active_mask * grad_middle).astype(jnp.bfloat16)
    output_projection_gradient = outer_columns(
        branch_gradient, adapter_second[:, PROJECTED_WIDTH : PROJECTED_WIDTH + MODEL_WIDTH]
    ).astype(jnp.bfloat16)
    grad_attended = (
        outer_columns(branch_gradient, output_weight)
        + outer_columns(
            output_projection_gradient, adapter_first[:, 3 * ADAPTER_RANK : 4 * ADAPTER_RANK]
        )
    ).astype(jnp.bfloat16)
    grad_att_rows = grad_attended.reshape(local_rows * HEADS, HEAD_SIZE)
    prob = jnp.exp(score_rows() - top_score) / mass
    grad_prob = outer_columns(grad_att_rows, values).reshape(local_rows, HEADS, key_total)
    centre = jnp.sum(prob * grad_prob, axis=-1, keepdims=True)
    grad_scores = (
        (prob * (grad_prob - centre)).astype(jnp.bfloat16).reshape(local_rows * HEADS, key_total)
    )
    grad_queries = (matrix_product(grad_scores, keys) * scale).reshape(local_rows, HEADS, HEAD_SIZE)
    prob_again = prob.astype(jnp.bfloat16).reshape(local_rows * HEADS, key_total)
    kv_terms = jnp.concatenate(
        [inner_rows(grad_scores, query_rows) * scale, inner_rows(prob_again, grad_att_rows)], axis=1
    )
    grad_kv = lax.psum_scatter(kv_terms, "dp", scatter_dimension=0, tiled=True)
    query_linear_gradient = (
        rotate_back(grad_queries, pos_own).reshape(local_rows, QUERY_WIDTH).astype(jnp.bfloat16)
    )
    key_linear_gradient = rotate_back(grad_kv[:, None, :HEAD_SIZE], pos_own)[:, 0].astype(
        jnp.bfloat16
    )
    value_linear_gradient = grad_kv[:, HEAD_SIZE:].astype(jnp.bfloat16)
    query_key_value_gradient = jnp.concatenate(
        [query_linear_gradient, key_linear_gradient, value_linear_gradient], axis=1
    )
    attention_projection_gradient = jnp.concatenate(
        [
            outer_columns(query_linear_gradient, adapter_second[:, :QUERY_WIDTH]),
            outer_columns(
                key_linear_gradient, adapter_second[:, QUERY_WIDTH : QUERY_WIDTH + HEAD_SIZE]
            ),
            outer_columns(
                value_linear_gradient, adapter_second[:, QUERY_WIDTH + HEAD_SIZE : PROJECTED_WIDTH]
            ),
        ],
        axis=1,
    ).astype(jnp.bfloat16)
    normed_gradient = outer_columns(query_key_value_gradient, input_weight) + outer_columns(
        attention_projection_gradient, adapter_first[:, : 3 * ADAPTER_RANK]
    )
    grad_resid_part, grad_gain_one = jax.vjp(norm_rows, residual_stream, layer_norm_gains[0])[1](
        normed_gradient
    )
    hidden_grad = grad_middle + grad_resid_part
    grad_w_in = inner_rows(normed_input, query_key_value_gradient)
    grad_w_out = inner_rows(attended_rows, branch_gradient)
    grad_gains = jnp.stack([grad_gain_one, grad_gain_two])
    adapter_first_gradient = jnp.concatenate(
        [
            inner_rows(normed_input, attention_projection_gradient),
            inner_rows(attended_rows, output_projection_gradient),
            inner_rows(second_normed_input, lowrank_projection_gradient),
        ],
        axis=1,
    )
    adapter_second_gradient = jnp.concatenate(
        [
            inner_rows(lowrank_projection[:, :ADAPTER_RANK], query_linear_gradient),
            inner_rows(lowrank_projection[:, ADAPTER_RANK : 2 * ADAPTER_RANK], key_linear_gradient),
            inner_rows(lowrank_projection[:, 2 * ADAPTER_RANK :], value_linear_gradient),
            inner_rows(output_projection, branch_gradient),
            inner_rows(down_lowrank, feedforward_gradient),
        ],
        axis=1,
    )
    input_portion, output_portion, gain_portion, adapter_first_grads, adapter_second_grads = (
        lax.psum_scatter(grad_w_in, "dp", scatter_dimension=0, tiled=True),
        lax.psum_scatter(grad_w_out, "dp", scatter_dimension=0, tiled=True),
        lax.psum_scatter(grad_gains, "dp", scatter_dimension=1, tiled=True),
        lax.psum_scatter(adapter_first_gradient, "dp", scatter_dimension=0, tiled=True),
        lax.psum_scatter(adapter_second_gradient, "dp", scatter_dimension=1, tiled=True),
    )
    mlp_part = ffn_grad[:, : 3 * MODEL_WIDTH].reshape(ffn_rows, 3, MODEL_WIDTH)
    sum_in, sum_out, sum_gains, sum_mlp = (
        lax.psum(input_portion.astype(jnp.bfloat16), "loop").astype(jnp.float32),
        lax.psum(output_portion.astype(jnp.bfloat16), "loop").astype(jnp.float32),
        lax.psum(gain_portion.astype(jnp.bfloat16), "loop").astype(jnp.float32),
        lax.psum(mlp_part.astype(jnp.bfloat16), "loop").astype(jnp.float32),
    )
    return (
        complete_output.astype(jnp.bfloat16)[None],
        hidden_grad[None],
        sum_in,
        sum_out,
        sum_mlp,
        sum_gains,
        adapter_first_grads[None],
        adapter_second_grads[None],
        ffn_grad[:, 3 * MODEL_WIDTH :][None],
        exit_counts,
        mean_confidence,
    )


def solution(mesh):
    return jax.shard_map(
        per_device if mesh.shape == {"loop": 2, "dp": LINE_DEVICES} else per_device_any,
        mesh=mesh,
        in_specs=(
            P("loop", "dp", None),
            P("loop", "dp", None),
            P("dp", None),
            P("dp", None),
            P("dp", None, None),
            P(),
            P("loop", None, None),
            P("loop", None, None),
            P("loop", None, None),
            P("loop", None),
            P("loop", None),
            P("loop", "dp"),
        ),
        out_specs=(
            P("loop", "dp", None),
            P("loop", "dp", None),
            P("dp", None),
            P("dp", None),
            P("dp", None, None),
            P(None, "dp"),
            P("loop", "dp", None),
            P("loop", None, "dp"),
            P("loop", "dp", None),
            P(),
            P(),
        ),
        check_vma=False,
    )
```

```python
import functools

import jax
import jax.numpy as jnp
from jax import lax
from jax.experimental import pallas as pl
from jax.experimental.pallas import tpu as pltpu
from jax.sharding import PartitionSpec as P

MODEL_WIDTH = 2048
HEADS = 8
HEAD_SIZE = 256
ADAPTER_RANK = 256
QUERY_WIDTH = 2048
PROJECTED_WIDTH = 2560


EPSILON = 1e-06
FLOOR_SCORE = -1e30
MESH = pl.DeviceIdType.MESH
VMEM_LIMIT = 60 * 1024 * 1024
LINE_DEVICES = 16
FAR_TILES = 3
OUT_SPLIT = 1536
IN_SHARE = 48
OUT_SHARE = 32


def matrix_product(left, right):
    return jnp.dot(left, right, preferred_element_type=jnp.float32)


def inner_rows(left, right):
    return lax.dot_general(
        left, right, (((0,), (0,)), ((), ())), preferred_element_type=jnp.float32
    )


def outer_columns(left, right):
    return lax.dot_general(
        left, right, (((1,), (1,)), ((), ())), preferred_element_type=jnp.float32
    )


def norm_rows(values, gain):
    return values * lax.rsqrt(jnp.mean(values * values, axis=-1, keepdims=True) + EPSILON) * gain


def rotate(values, positions):
    half_dim = values.shape[-1] // 2
    freqs = 10000.0 ** (-jnp.arange(half_dim, dtype=jnp.float32) / half_dim)
    angles = positions.astype(jnp.float32)[:, None, None] * freqs
    cosine = jnp.cos(angles)
    sine = jnp.sin(angles)
    first_half = values[..., :half_dim]
    second_half = values[..., half_dim:]
    return jnp.concatenate(
        [first_half * cosine - second_half * sine, first_half * sine + second_half * cosine],
        axis=-1,
    )


def rotate_back(grads, positions):

    def turned(values):
        return rotate(values, positions)

    return jax.vjp(turned, jnp.zeros_like(grads))[1](grads)[0]


def geglu(gate_values, up_projection_value):
    return jax.nn.gelu(gate_values, approximate=True) * up_projection_value


def root_mean(values):
    return jnp.sqrt(jnp.mean(values * values, axis=-1) + EPSILON)


def token_facts(row_of_tokens, sequence_length):
    row_total = row_of_tokens.shape[0]
    live_row = row_of_tokens >= 0
    seq_ends = jnp.cumsum(sequence_length)
    seq_index = jnp.sum((row_of_tokens[:, None] >= seq_ends[None, :]).astype(jnp.int32), axis=1)
    seq_starts = seq_ends - sequence_length
    own_start = jnp.sum(
        jnp.where(
            seq_index[:, None] == jnp.arange(sequence_length.shape[0], dtype=jnp.int32)[None, :],
            seq_starts[None, :],
            0,
        ),
        axis=1,
    )
    row_ids = jnp.arange(row_total, dtype=jnp.int32)
    sequence = jnp.where(live_row, seq_index, -1 - row_ids)
    ordering = jnp.where(live_row, row_of_tokens, 0)
    positions = jnp.where(live_row, row_of_tokens - own_start, 0)
    return (live_row, sequence, ordering, positions)


def place(count):
    me = lax.axis_index("dp")
    return me, count // 4, me // 4, (me // 2) % 2, me % 2


def greet(count, across=False):
    me, depth, z, y, c = place(count)
    barrier = pltpu.get_barrier_semaphore()

    def signal(where):
        pl.semaphore_signal(barrier, inc=1, device_id={"dp": where}, device_id_type=MESH)

    signal(me + 1 - 2 * c)
    signal(me + 2 - 4 * y)
    if across:
        other = 1 - lax.axis_index("loop")
        pl.semaphore_signal(barrier, inc=1, device_id={"loop": other}, device_id_type=MESH)

    @pl.when(z > 0)
    def _():
        signal(me - 4)

    @pl.when(z < depth - 1)
    def _():
        signal(me + 4)

    ends = jnp.where((z > 0) & (z < depth - 1), 4, 3)
    pl.semaphore_wait(barrier, ends + 1 if across else ends)


def contract(left, right, left_axis, right_axis):
    return lax.dot_general(
        left,
        right,
        (((left_axis,), (right_axis,)), ((), ())),
        preferred_element_type=jnp.float32,
    )


def gather_plan(count, spans, own, full, sems, far_sems=None, twins=False):
    keep, recv, send_core, send_pair, send_right, send_left, send_twin = sems
    arrays = len(own)
    me, depth, z, y, c = place(count)
    mate = me + 2 - 4 * y
    core = me + 1 - 2 * c

    def copy(unit, block, target, sem, first=False):
        a, s = unit
        rows = pl.ds(*spans[a][s])
        return pltpu.make_async_remote_copy(
            src_ref=own[a].at[rows] if first else full[a].at[block, rows],
            dst_ref=full[a].at[block, rows],
            send_sem=sem,
            recv_sem=recv.at[a, block, s],
            device_id={"dp": target},
            device_id_type=MESH,
        )

    def to_core(unit, block, first=False):
        a, s = unit
        return copy(unit, block, core, send_core.at[a, block // 2, s], first)

    def to_pair(unit, block, first=False):
        a, s = unit
        return copy(unit, block, mate, send_pair.at[a, block // 4, s], first)

    def to_right(unit, block, first=False):
        a, s = unit
        return copy(unit, block, me + 4, send_right.at[a, block // 4, s], first)

    def to_left(unit, block, first=False):
        a, s = unit
        return copy(unit, block, me - 4, send_left.at[a, block // 4, s], first)

    def to_twin(unit, block):
        a, s = unit
        return copy(unit, block, me + 4 - 8 * (z % 2), send_twin.at[a])

    def shared(unit):
        return twins and unit[1] == 1

    def to_far(a, block):
        rows = pl.ds(*spans[a][0])
        return pltpu.make_async_remote_copy(
            src_ref=full[a].at[block, rows],
            dst_ref=full[a].at[block, rows],
            send_sem=far_sems[0].at[a, block // 2],
            recv_sem=far_sems[1].at[a, block],
            device_id={"loop": 1 - lax.axis_index("loop")},
            device_id_type=MESH,
        )

    def far_core(a, block, first=False):
        rows = pl.ds(*spans[a][2])
        return pltpu.make_async_remote_copy(
            src_ref=own[a].at[rows] if first else full[a].at[block, rows],
            dst_ref=full[a].at[block, rows],
            send_sem=far_sems[2].at[a, block // 2],
            recv_sem=far_sems[3].at[a, block],
            device_id={"dp": core},
            device_id_type=MESH,
        )

    def cross(unit, block):
        if far_sems is not None and unit[1] == 0:
            to_far(unit[0], block).start()

    local = [pltpu.make_async_copy(own[a], full[a].at[me], keep.at[a]) for a in range(arrays)]
    units = [(a, s) for a in range(arrays) for s in range(2 if far_sems else len(spans[a]))]

    def begin():
        for unit in units:

            @pl.when(z < depth - 1)
            def _(unit=unit):
                to_right(unit, me, True).start()

            @pl.when(z > 0)
            def _(unit=unit):
                to_left(unit, me, True).start()

            to_pair(unit, me, True).start()
            to_core(unit, me, True).start()
        if far_sems is not None:
            for a in range(arrays):
                far_core(a, me, True).start()
        for item in local:
            item.start()

    def from_line(k, unit):
        @pl.when(z - k >= 0)
        def _():
            block = me - 4 * k
            to_right(unit, block).wait_recv()

            @pl.when(z < depth - 1)
            def _():
                to_right(unit, block).start()

            if k == 1 and shared(unit):

                @pl.when(z % 2 == 0)
                def _():
                    to_pair(unit, block).start()

            else:
                to_pair(unit, block).start()
            to_core(unit, block).start()
            cross(unit, block)

        @pl.when(z + k < depth)
        def _():
            block = me + 4 * k
            to_left(unit, block).wait_recv()

            @pl.when(z > 0)
            def _():
                to_left(unit, block).start()

            if k == 1 and shared(unit):

                @pl.when(z % 2 == 1)
                def _():
                    to_pair(unit, block).start()

            else:
                to_pair(unit, block).start()
            to_core(unit, block).start()
            cross(unit, block)

    def pass_on(unit, block):
        to_pair(unit, block).wait_recv()
        to_core(unit, block).start()
        cross(unit, block)

    def from_pair(k, unit):
        if k == 0:
            pass_on(unit, mate)
            if shared(unit):
                to_twin(unit, mate).start()
            return

        @pl.when(z - k >= 0)
        def _():
            pass_on(unit, mate - 4 * k)

        @pl.when(z + k < depth)
        def _():
            pass_on(unit, mate + 4 * k)

    def far_on(a, block):
        to_far(a, block).wait_recv()
        far_core(a, block).start()

    def from_far(k, a):
        if k == 0:
            far_on(a, mate)
            return

        @pl.when(z - k >= 0)
        def _():
            far_on(a, me - 4 * k)
            far_on(a, mate - 4 * k)

        @pl.when(z + k < depth)
        def _():
            far_on(a, me + 4 * k)
            far_on(a, mate + 4 * k)

    def arrive(block=None, mine=True):
        for unit in units:
            for j in range(count // 2 if block is None else 1):
                to_core(unit, 2 * j + 1 - c if block is None else block).wait_recv()
        if far_sems is not None:
            for a in range(arrays):
                for j in range(count // 2):
                    far_core(a, 2 * j + 1 - c).wait_recv()
        if mine:
            for item in local:
                item.wait()

    def finish():
        for unit in units:
            for j in range(count // 2):
                to_core(unit, 2 * j + c).wait_send()
            for j in range(depth):
                block = 4 * j + 2 * y + c
                if shared(unit):

                    @pl.when(j != z + 1 - 2 * (z % 2))
                    def _():
                        to_pair(unit, block).wait_send()

                else:
                    to_pair(unit, block).wait_send()

                @pl.when((z >= j) & (z < depth - 1))
                def _():
                    to_right(unit, block).wait_send()

                @pl.when((z <= j) & (z > 0))
                def _():
                    to_left(unit, block).wait_send()

            if shared(unit):
                to_twin(unit, mate).wait_send()

        if far_sems is not None:
            for a in range(arrays):
                for j in range(count // 2):
                    far_core(a, 2 * j + c).wait_send()

                    @pl.when(2 * j + c != me)
                    def _():
                        to_far(a, 2 * j + c).wait_send()

    return units, begin, from_line, from_pair, from_far, arrive, finish


def gather_sems(count, number, parts):
    depth = count // 4
    sem = pltpu.SemaphoreType.DMA
    return [
        sem((number,)),
        sem((number, count, parts)),
        sem((number, count // 2, parts)),
        sem((number, depth, parts)),
        sem((number, depth, parts)),
        sem((number, depth, parts)),
        sem((number,)),
    ]


def even_spans(rows, parts):
    return [(s * (rows // parts), rows // parts) for s in range(parts)]


def kernel_params(ident):
    return pltpu.CompilerParams(
        collective_id=ident, has_side_effects=True, vmem_limit_bytes=VMEM_LIMIT
    )


def opening_body(count, shares, arrays, stream, gain, *refs):
    own = refs[:arrays]
    weights, factors, first, second = refs[arrays : arrays + 4]
    full = refs[arrays + 4 : 2 * arrays + 4]
    folded, normed, lowrank = refs[2 * arrays + 4 : 2 * arrays + 7]
    scratch = refs[2 * arrays + 7 :]
    (bank, factor_bank, first_bank, in_bank, second_bank, bank_sem, factor_sem, out_sem) = scratch[
        :8
    ]
    me, depth, z, y, c = place(count)
    rank = ADAPTER_RANK
    width, wide = bank.shape[1:]
    loop = lax.axis_index("loop")
    greet(count, True)
    spans = []
    for a in range(arrays):
        rows, share = own[a].shape[0], shares[a]
        spans.append(
            [
                (pl.multiple_of(loop * (rows - share), 16), share),
                (share, rows - 2 * share),
                (pl.multiple_of((1 - loop) * (rows - share), 16), share),
            ]
        )
    units, begin, from_line, from_pair, from_far, arrive, finish = gather_plan(
        count, spans, own, full, scratch[8:15], scratch[15:19]
    )
    begin()
    fills = [
        pltpu.make_async_copy(weights.at[i], bank.at[i], bank_sem.at[i]) for i in range(3)
    ]
    sources = [
        pltpu.make_async_copy(first.at[:, pl.ds(0, 3 * rank)], in_bank, factor_sem.at[0]),
        pltpu.make_async_copy(
            factors.at[pl.ds(me * width, width)], factor_bank, factor_sem.at[1]
        ),
        pltpu.make_async_copy(
            first.at[:, pl.ds(4 * rank, 2 * rank)], first_bank, factor_sem.at[2]
        ),
        pltpu.make_async_copy(
            second.at[:, pl.ds(PROJECTED_WIDTH + MODEL_WIDTH, wide)], second_bank, factor_sem.at[3]
        ),
    ]
    for item in sources + fills:
        item.start()

    def put(i):
        return pltpu.make_async_copy(bank.at[i], folded.at[i], out_sem.at[i])

    def fold(i):
        high, tile = 256, 512

        def inner(n, carry):
            rows = pl.ds(pl.multiple_of((n // (wide // tile)) * high, high), high)
            cols = pl.ds(pl.multiple_of((n % (wide // tile)) * tile, tile), tile)
            if i == 2:
                extra = contract(factor_bank[rows, :rank], second_bank[:, cols], 1, 0)
            else:
                extra = contract(
                    factor_bank[rows, (i + 1) * rank : (i + 2) * rank],
                    first_bank[cols, i * rank : (i + 1) * rank],
                    1,
                    1,
                )
            bank[i, rows, cols] = (bank[i, rows, cols].astype(jnp.float32) + extra).astype(
                bank.dtype
            )
            return carry

        lax.fori_loop(0, (width // high) * (wide // tile), inner, 0)
        put(i).start()

    rows = stream[...].astype(jnp.float32)
    inverse = lax.rsqrt(jnp.mean(rows * rows, axis=-1, keepdims=True) + EPSILON)
    normed[...] = (rows * inverse * gain[...]).astype(normed.dtype)
    sources[0].wait()
    lowrank[...] = contract(normed[...], in_bank[...], 1, 0).astype(lowrank.dtype)
    for item in sources[1:]:
        item.wait()
    for k in range(1, depth):
        for a in range(arrays):
            for unit in units:
                if unit[0] == a:
                    from_line(k, unit)
                    from_pair(k - 1, unit)
            if k > 1 or a > 0:
                stage = (k - 1) * arrays + a - 1
                from_far(stage // arrays, stage % arrays)
        fills[k - 1].wait()
        fold(k - 1)
    for unit in units:
        from_pair(depth - 1, unit)
    for stage in range((depth - 1) * arrays - 1, depth * arrays):
        from_far(stage // arrays, stage % arrays)
    arrive()
    finish()
    for i in range(3):
        put(i).wait()


def opening(count, ident, stream, gain, arrays, shares, weights, factors, first, second):
    number = len(arrays)
    _, width, wide = weights.shape
    low = jnp.bfloat16
    rank = ADAPTER_RANK
    sem = pltpu.SemaphoreType.DMA
    anywhere = pl.BlockSpec(memory_space=pl.ANY)
    inside = pl.BlockSpec(memory_space=pltpu.VMEM)
    out = pl.pallas_call(
        functools.partial(opening_body, count, shares, number),
        out_shape=[
            jax.ShapeDtypeStruct((count,) + item.shape, item.dtype) for item in arrays
        ]
        + [
            jax.ShapeDtypeStruct(weights.shape, low),
            jax.ShapeDtypeStruct(stream.shape, low),
            jax.ShapeDtypeStruct((stream.shape[0], 3 * rank), low),
        ],
        in_specs=[inside] * 2 + [anywhere] * (number + 4),
        out_specs=[anywhere] * (number + 1) + [inside] * 2,
        scratch_shapes=[
            pltpu.VMEM(weights.shape, low),
            pltpu.VMEM((width, factors.shape[1]), low),
            pltpu.VMEM((wide, 2 * rank), low),
            pltpu.VMEM((wide, 3 * rank), low),
            pltpu.VMEM((rank, wide), low),
            sem((3,)),
            sem((4,)),
            sem((3,)),
        ]
        + gather_sems(count, number, 2)
        + [
            sem((number, count // 2)),
            sem((number, count)),
            sem((number, count // 2)),
            sem((number, count)),
        ],
        compiler_params=kernel_params(ident),
        name="opening",
    )(stream, gain, *arrays, weights, factors, first, second)
    return [
        item.reshape((count * item.shape[1],) + item.shape[2:]) for item in out[:number]
    ] + list(out[number:])


def turn(values, cosine, sine):
    half = values.shape[-1] // 2
    first, second = values[:, :half], values[:, half:]
    return jnp.concatenate(
        [first * cosine - second * sine, first * sine + second * cosine], axis=1
    )


def attention_body(count, normed, lowrank, stream, active, gain, cosine, sine, own_seq, own_order,
                   all_seq, all_order, in_weight, out_weight, first, second, grads,
                   queries, attended, lowrank_out, level, middle, normed_next, keys_values, grads_all,
                   in_bank, out_bank, in_second, out_second, out_first, allowed, kv_own, kv_full,
                   load_sem, put_sem, *sems):
    me, depth, z, y, c = place(count)
    height, wide = normed.shape
    size = HEAD_SIZE
    scale = size ** (-0.5)
    rank = ADAPTER_RANK
    low = jnp.bfloat16
    greet(count)
    kv_units, kv_begin, kv_line, kv_pair, _, kv_arrive, kv_finish = gather_plan(
        count, [even_spans(height, 1)], (kv_own,), (kv_full,), sems[:7]
    )
    units, begin, from_line, from_pair, _, arrive, finish = gather_plan(
        count, [even_spans(height, 2)], (grads,), (grads_all,), sems[7:], twins=True
    )
    loads = [
        pltpu.make_async_copy(source, bank, load_sem.at[i])
        for i, (source, bank) in enumerate(
            (
                (in_weight, in_bank),
                (second.at[:, pl.ds(0, PROJECTED_WIDTH)], in_second),
                (out_weight, out_bank),
                (second.at[:, pl.ds(PROJECTED_WIDTH, MODEL_WIDTH)], out_second),
                (first.at[:, pl.ds(3 * rank, rank)], out_first),
            )
        )
    ]
    begin()
    for item in loads:
        item.start()
    loads[0].wait()
    loads[1].wait()

    def head(at, part):
        value = contract(normed[...], in_bank[:, at : at + size], 1, 0)
        return value + contract(
            lowrank[:, part * rank : (part + 1) * rank], in_second[:, at : at + size], 1, 0
        )

    kv_own[:, :size] = turn(head(QUERY_WIDTH, 1), cosine[...], sine[...]).astype(low)
    kv_own[:, size:] = head(QUERY_WIDTH + size, 2).astype(low)
    kv_begin()
    heads = wide // size

    def some_heads(start, stop):
        for i in range(start, stop):
            value = turn(head(i * size, 0), cosine[...], sine[...])
            queries[:, i * size : (i + 1) * size] = value.astype(low)

    some_heads(0, 4)
    (kv_unit,) = kv_units
    kv_line(1, kv_unit)
    kv_pair(0, kv_unit)
    some_heads(4, heads)
    same = own_seq[...] == all_seq[...]
    allowed[...] = jnp.where(same & (all_order[...] <= own_order[...]), 1.0, 0.0)
    kv_line(2, kv_unit)
    kv_pair(1, kv_unit)
    kv_line(3, kv_unit)
    kv_pair(2, kv_unit)
    kv_pair(3, kv_unit)
    for unit in units:
        from_line(1, unit)
        from_pair(0, unit)
    kv_arrive()
    put_kv = pltpu.make_async_copy(kv_full, keys_values, put_sem)
    put_kv.start()
    total = count * height
    keys = kv_full[:, :, :size].reshape(total, size)
    values = kv_full[:, :, size:].reshape(total, size)

    def attend(pair):
        query = jnp.concatenate(
            [
                queries[:, 2 * pair * size : (2 * pair + 1) * size],
                queries[:, (2 * pair + 1) * size : (2 * pair + 2) * size],
            ],
            axis=0,
        )
        keep = jnp.concatenate([allowed[...], allowed[...]], axis=0) > 0.5
        scores = jnp.where(keep, contract(query, keys, 1, 1) * scale, FLOOR_SCORE)
        top = jnp.max(scores, axis=-1, keepdims=True)
        expo = jnp.exp(scores - top)
        mass = jnp.sum(expo, axis=-1, keepdims=True)
        level[pair] = jnp.broadcast_to(top + jnp.log(mass), level.shape[1:])
        value = contract((expo / mass).astype(low), values, 1, 0).astype(low)
        for i in range(2):
            attended[:, (2 * pair + i) * size : (2 * pair + i + 1) * size] = value[
                i * height : (i + 1) * height
            ]

    for pair in range(heads // 2):
        attend(pair)
        if pair == 0:
            for unit in units:
                from_line(2, unit)
        if pair == 1:
            for unit in units:
                from_pair(1, unit)
        if pair == 2:
            for unit in units:
                from_line(3, unit)
        if pair == 3:
            for unit in units:
                from_pair(2, unit)
    for item in loads[2:]:
        item.wait()
    lowrank_out[...] = contract(attended[...], out_first[...], 1, 0).astype(low)
    tile = 256

    def product(n, carry):
        cols = pl.ds(pl.multiple_of(n * tile, tile), tile)
        value = contract(attended[...], out_bank[:, cols], 1, 0)
        value += contract(lowrank_out[...], out_second[:, cols], 1, 0)
        middle[:, cols] = stream[:, cols].astype(jnp.float32) + active[...] * value
        return carry

    lax.fori_loop(0, wide // tile, product, 0)
    rows = middle[...]
    inverse = lax.rsqrt(jnp.mean(rows * rows, axis=-1, keepdims=True) + EPSILON)
    normed_next[...] = (rows * inverse * gain[...]).astype(low)
    for unit in units:
        from_pair(3, unit)
    arrive()
    finish()
    kv_finish()
    put_kv.wait()


def attention(count, ident, normed, lowrank, stream, active, gain, cosine, sine, own_seq,
              own_order, all_seq, all_order, in_weight, out_weight, first, second, grads):
    height, wide = normed.shape
    low, high = jnp.bfloat16, jnp.float32
    inside = pl.BlockSpec(memory_space=pltpu.VMEM)
    anywhere = pl.BlockSpec(memory_space=pl.ANY)
    rank = ADAPTER_RANK
    both = 2 * HEAD_SIZE
    total = count * height
    sem = pltpu.SemaphoreType.DMA
    shape = jax.ShapeDtypeStruct
    return pl.pallas_call(
        functools.partial(attention_body, count),
        out_shape=[
            shape((height, wide), low),
            shape((height, wide), low),
            shape((height, rank), low),
            shape((wide // both, 2 * height, 128), high),
            shape((height, wide), high),
            shape((height, wide), low),
            shape((count, height, both), low),
            shape((count, height, wide), low),
        ],
        in_specs=[inside] * 11 + [anywhere] * 5,
        out_specs=[inside] * 6 + [anywhere] * 2,
        scratch_shapes=[
            pltpu.VMEM(in_weight.shape, low),
            pltpu.VMEM(out_weight.shape, low),
            pltpu.VMEM((rank, PROJECTED_WIDTH), low),
            pltpu.VMEM((rank, wide), low),
            pltpu.VMEM((wide, rank), low),
            pltpu.VMEM((height, total), high),
            pltpu.VMEM((height, both), low),
            pltpu.VMEM((count, height, both), low),
            sem((5,)),
            sem,
        ]
        + gather_sems(count, 1, 1)
        + gather_sems(count, 1, 2),
        compiler_params=kernel_params(ident),
        name="attention",
    )(
        normed, lowrank, stream, active, gain, cosine, sine, own_seq, own_order, all_seq,
        all_order, in_weight, out_weight, first, second, grads,
    )


def sum_plan(count, parts, mine, theirs, core_in, pair_in, line_in, twin_in, sems,
             twins=True):
    me, depth, z, y, c = place(count)
    core_send, core_recv, pair_send, pair_recv, line_send, line_recv, twin_sem = sems
    rows = core_in.shape[1]
    step = rows // parts
    near = z < 2
    order = [
        jnp.where(near, 3, 0),
        jnp.where(near, 0, 3),
        jnp.where(near, 2, 1),
        jnp.where(near, 1, 2),
    ]

    def rows_of(s):
        return pl.ds(s * step, step)

    def to_core(line, pair, s):
        at = 2 * line + pair
        return pltpu.make_async_remote_copy(
            src_ref=theirs(at, rows_of(s)),
            dst_ref=core_in.at[at, rows_of(s)],
            send_sem=core_send.at[at, s],
            recv_sem=core_recv.at[at, s],
            device_id={"dp": me + 1 - 2 * c},
            device_id_type=MESH,
        )

    def to_pair(line, s):
        return pltpu.make_async_remote_copy(
            src_ref=mine(2 * line + 1 - y, rows_of(s)),
            dst_ref=pair_in.at[line, rows_of(s)],
            send_sem=pair_send.at[line, s],
            recv_sem=pair_recv.at[line, s],
            device_id={"dp": me + 2 - 4 * y},
            device_id_type=MESH,
        )

    def along(line, slot, s, target):
        return pltpu.make_async_remote_copy(
            src_ref=mine(2 * line + y, rows_of(s)),
            dst_ref=line_in.at[slot, rows_of(s)],
            send_sem=line_send.at[line, s],
            recv_sem=line_recv.at[slot, s],
            device_id={"dp": target},
            device_id_type=MESH,
        )

    twin = z + 1 - 2 * (z % 2)

    def shared(s):
        return twins and parts > 1 and s == parts - 1

    def to_twin():
        return pltpu.make_async_remote_copy(
            src_ref=mine(2 * twin + 1 - y, rows_of(parts - 1)),
            dst_ref=twin_in,
            send_sem=twin_sem.at[0],
            recv_sem=twin_sem.at[1],
            device_id={"dp": me + 4 - 8 * (z % 2)},
            device_id_type=MESH,
        )

    if shared(parts - 1):
        pair_in[twin, rows_of(parts - 1)] = jnp.zeros((step, core_in.shape[2]), pair_in.dtype)

    def send_core(line, pair):
        for s in range(parts):
            to_core(line, pair, s).start()

    def core_left(line, pair):
        for s in range(parts):
            to_core(line, pair, s).wait_send()

    def pair_step(k):
        line = order[k]
        at = 2 * line + 1 - y
        for s in range(parts):
            to_core(line, 1 - y, s).wait_recv()
            block = mine(at, rows_of(s))
            block[...] = block[...] + core_in[at, rows_of(s)]
            if not shared(s):
                to_pair(line, s).start()
                continue

            @pl.when(line == twin)
            def _():
                to_twin().start()

            @pl.when((line != twin) & (line != z))
            def _():
                to_pair(line, s).start()

    def twin_step():
        block = mine(2 * z + 1 - y, rows_of(parts - 1))
        to_twin().wait_recv()
        block[...] = block[...] + twin_in[...]
        to_pair(z, parts - 1).start()

    def own_sum(line, s):
        at = 2 * line + y
        to_core(line, y, s).wait_recv()
        if shared(s):

            @pl.when(line != twin)
            def _():
                to_pair(line, s).wait_recv()

        else:
            to_pair(line, s).wait_recv()
        part = mine(at, rows_of(s))[...].astype(jnp.float32)
        part += core_in[at, rows_of(s)].astype(jnp.float32)
        return part + pair_in[line, rows_of(s)].astype(jnp.float32)

    def line_step(k):
        line = order[k]

        @pl.when(line != z)
        def _():
            for s in range(parts):
                block = mine(2 * line + y, rows_of(s))
                follows = ((line > z) & (z > 0)) | ((line < z) & (z < depth - 1))
                part = own_sum(line, s)

                @pl.when(follows)
                def _():
                    along(z, line, s, me + 4).wait_recv()
                    extra = line_in[line, rows_of(s)].astype(jnp.float32)
                    block[...] = (part + extra).astype(block.dtype)

                @pl.when(jnp.logical_not(follows))
                def _():
                    block[...] = part.astype(block.dtype)

                @pl.when(line > z)
                def _():
                    along(line, line, s, me + 4).start()

                @pl.when(line < z)
                def _():
                    along(line, jnp.where(line == z - 1, depth, line), s, me - 4).start()

    def last_step(total):
        for s in range(parts):
            total[rows_of(s)] = own_sum(z, s)

            @pl.when(z > 0)
            def _():
                along(z, z, s, me + 4).wait_recv()
                total[rows_of(s)] += line_in[z, rows_of(s)].astype(jnp.float32)

            @pl.when(z < depth - 1)
            def _():
                along(z, depth, s, me + 4).wait_recv()
                total[rows_of(s)] += line_in[depth, rows_of(s)].astype(jnp.float32)

    def finish(cores=True):
        if shared(parts - 1):
            to_twin().wait_send()
        for line in range(depth):
            for s in range(parts):
                for pair in range(2 if cores else 0):
                    to_core(line, pair, s).wait_send()
                if shared(s):

                    @pl.when(line != twin)
                    def _():
                        to_pair(line, s).wait_send()

                else:
                    to_pair(line, s).wait_send()

                @pl.when(z != line)
                def _():
                    along(line, line, s, me + 4).wait_send()

    return order, send_core, pair_step, line_step, last_step, finish, core_left, twin_step


def sum_sems(count, parts):
    depth = count // 4
    sem = pltpu.SemaphoreType.DMA
    return [
        sem((2 * depth, parts)),
        sem((2 * depth, parts)),
        sem((depth, parts)),
        sem((depth, parts)),
        sem((depth, parts)),
        sem((depth + 1, parts)),
        sem((2,)),
    ]


def sum_rooms(count, rows, cols, kind=jnp.bfloat16, parts=2):
    depth = count // 4
    return [
        pltpu.VMEM((2 * depth, rows, cols), kind),
        pltpu.VMEM((depth, rows, cols), kind),
        pltpu.VMEM((depth + 1, rows, cols), kind),
        pltpu.VMEM((rows // 2, cols) if parts > 1 else (16, 128), kind),
    ]


def sum_terms(count, parts, terms, rooms, sems):
    me, depth, z, y, c = place(count)

    def mine(at, rows):
        return terms.at[2 * at + c, rows]

    def theirs(at, rows):
        return terms.at[2 * at + 1 - c, rows]

    return sum_plan(count, parts, mine, theirs, *rooms, sems)


def turn_back(values, cosine, sine):
    half = values.shape[-1] // 2
    first, second = values[:, :half], values[:, half:]
    return jnp.concatenate(
        [first * cosine + second * sine, second * cosine - first * sine], axis=1
    )


def attention_grads_body(count, attended, grad_rows, weight, queries, keys_values, level,
                         cosine, sine, own_seq, own_order, all_seq, all_order, first, second,
                         joint_grads, lowrank_grads, out_sum,
                         weight_in, out_first, both_second, grad_att, allowed, kv_total, kv_terms, kv_sum, out_terms,
                         out_core, out_pair, out_line, out_twin, kv_core, kv_pair, kv_line, kv_twin,
                         weight_sem, *sems):
    me, depth, z, y, c = place(count)
    height, wide = grad_rows.shape
    size = HEAD_SIZE
    scale = size ** (-0.5)
    low = jnp.bfloat16
    greet(count)
    rank = ADAPTER_RANK
    loads = [
        pltpu.make_async_copy(source, bank, weight_sem.at[i])
        for i, (source, bank) in enumerate(
            (
                (weight, weight_in),
                (first.at[:, pl.ds(3 * rank, rank)], out_first),
                (second.at[:, pl.ds(0, PROJECTED_WIDTH + wide)], both_second),
            )
        )
    ]
    for item in loads:
        item.start()
    order, send_out, pair_out, line_out, last_out, finish_out, _, twin_out = sum_terms(
        count, 2, out_terms, (out_core, out_pair, out_line, out_twin), sems[:7]
    )
    _, send_kv, pair_kv, line_kv, last_kv, finish_kv, _, _ = sum_terms(
        count, 1, kv_terms, (kv_core, kv_pair, kv_line, kv_twin), sems[7:]
    )
    feature, some = out_terms.shape[1:]

    def out_product(line):
        def inner(n, carry):
            into = pl.ds(pl.multiple_of(n * 512, 512), 512)
            cols = pl.ds(pl.multiple_of(line * 4 * feature, 4 * feature), 4 * feature)
            value = contract(attended[:, cols], grad_rows[:, into], 0, 0).astype(low)
            out_terms[pl.ds(4 * line, 4), :, into] = value.reshape(4, feature, 512)
            return carry

        lax.fori_loop(0, some // 512, inner, 0)
        for pair in (1 - y, y):
            send_out(line, pair)

    for line in order:
        out_product(line)
    for item in loads:
        item.wait()
    tile = 256
    back_out = contract(grad_rows[...], both_second[:, PROJECTED_WIDTH:], 1, 1).astype(low)

    def product(n, carry):
        cols = pl.ds(pl.multiple_of(n * tile, tile), tile)
        value = contract(grad_rows[...], weight_in[cols], 1, 1)
        value += contract(back_out, out_first[cols], 1, 1)
        grad_att[:, cols] = value.astype(low)
        return carry

    lax.fori_loop(0, wide // tile, product, 0)
    same = own_seq[...] == all_seq[...]
    allowed[...] = jnp.where(same & (all_order[...] <= own_order[...]), 1.0, 0.0)
    for k in range(depth):
        pair_out(k)
    keys = keys_values[:, :size]
    values = keys_values[:, size:]

    def heads(pair):
        def both(ref):
            return jnp.concatenate(
                [
                    ref[:, 2 * pair * size : (2 * pair + 1) * size],
                    ref[:, (2 * pair + 1) * size : (2 * pair + 2) * size],
                ],
                axis=0,
            )

        query = both(queries)
        grad = both(grad_att)
        keep = jnp.concatenate([allowed[...], allowed[...]], axis=0) > 0.5
        scores = jnp.where(keep, contract(query, keys, 1, 1) * scale, FLOOR_SCORE)
        prob = jnp.exp(scores - level[pair][:, :1])
        grad_prob = contract(grad, values, 1, 1)
        centre = jnp.sum(prob * grad_prob, axis=-1, keepdims=True)
        grad_scores = (prob * (grad_prob - centre)).astype(low)
        back = contract(grad_scores, keys, 1, 0) * scale
        for i in range(2):
            part = turn_back(back[i * height : (i + 1) * height], cosine[...], sine[...])
            joint_grads[:, (2 * pair + i) * size : (2 * pair + i + 1) * size] = part.astype(low)
        key_part = contract(grad_scores, query, 0, 0) * scale
        value_part = contract(prob.astype(low), grad, 0, 0)
        if pair == 0:
            kv_total[:, :size] = key_part
            kv_total[:, size:] = value_part
        else:
            kv_total[:, :size] += key_part
            kv_total[:, size:] += value_part

    for pair in range(wide // size // 2):
        heads(pair)
        if pair == 0:
            twin_out()
    for block in range(count):
        kv_terms[block] = kv_total[block * height : (block + 1) * height].astype(low)
    for pair in (1 - y, y):
        for line in order:
            send_kv(line, pair)
    for k in range(depth):
        pair_kv(k)
    for k in range(depth):
        line_out(k)
    for k in range(depth):
        line_kv(k)
    last_kv(kv_sum)
    part = turn_back(kv_sum[:, :size], cosine[...], sine[...])
    joint_grads[:, wide : wide + size] = part.astype(low)
    joint_grads[:, wide + size :] = kv_sum[:, size:].astype(low)
    for i, (at, stop) in enumerate(
        ((0, wide), (wide, wide + size), (wide + size, wide + 2 * size))
    ):
        value = contract(joint_grads[:, at:stop], both_second[:, at:stop], 1, 1)
        lowrank_grads[:, i * rank : (i + 1) * rank] = value.astype(low)
    last_out(out_sum)
    finish_out()
    finish_kv()


def attention_grads(count, ident, attended, grad_rows, weight, queries, keys_values, level,
                    cosine, sine, own_seq, own_order, all_seq, all_order, first, second):
    height, wide = grad_rows.shape
    total = keys_values.shape[0]
    low = jnp.bfloat16
    inside = pl.BlockSpec(memory_space=pltpu.VMEM)
    anywhere = pl.BlockSpec(memory_space=pl.ANY)
    feature = attended.shape[1] // count
    both = 2 * HEAD_SIZE
    return pl.pallas_call(
        functools.partial(attention_grads_body, count),
        out_shape=[
            jax.ShapeDtypeStruct((height, wide + both), low),
            jax.ShapeDtypeStruct((height, 3 * ADAPTER_RANK), low),
            jax.ShapeDtypeStruct((feature, OUT_SPLIT), jnp.float32),
        ],
        in_specs=[inside] * 2 + [anywhere] + [inside] * 9 + [anywhere] * 2,
        out_specs=[inside] * 3,
        scratch_shapes=[
            pltpu.VMEM(weight.shape, low),
            pltpu.VMEM((wide, ADAPTER_RANK), low),
            pltpu.VMEM((ADAPTER_RANK, PROJECTED_WIDTH + wide), low),
            pltpu.VMEM(attended.shape, low),
            pltpu.VMEM((height, total), jnp.float32),
            pltpu.VMEM((total, both), jnp.float32),
            pltpu.VMEM((count, height, both), low),
            pltpu.VMEM((height, both), jnp.float32),
            pltpu.VMEM((count, feature, OUT_SPLIT), low),
        ]
        + sum_rooms(count, feature, OUT_SPLIT)
        + sum_rooms(count, height, both, parts=1)
        + [pltpu.SemaphoreType.DMA((3,))]
        + sum_sems(count, 2)
        + sum_sems(count, 1),
        compiler_params=kernel_params(ident),
        name="attention_grads",
    )(
        attended, grad_rows, weight, queries, keys_values, level,
        cosine, sine, own_seq, own_order, all_seq, all_order, first, second,
    )


def closing_body(count, normed, joint_grads, attended, grad_rows, lowrank, lowrank_out, stream,
                 gain, grad_middle, small, lowrank_grads, weight, gate_grads, up_grads, down_grads, factors,
                 first, second,
                 in_sum, out_sum, second_sum, first_sum, small_sum, stream_grad, factor_grads,
                 bank, in_bank, factor_bank, second_bank, made, in_terms, out_terms,
                 second_terms, first_terms, small_terms, *scratch):
    me, depth, z, y, c = place(count)
    height, wide = normed.shape
    rank = ADAPTER_RANK
    width = gate_grads.shape[0]
    low = jnp.bfloat16
    rooms = [scratch[4 * i : 4 * i + 4] for i in range(5)]
    weight_sem, grads_sem, factor_sem, made_sem, side_sem = scratch[20:25]
    sems = [scratch[25 + 7 * i : 32 + 7 * i] for i in range(5)]
    greet(count)
    halves = [
        pltpu.make_async_copy(weight.at[pl.ds(i * width, width)], bank, weight_sem.at[i])
        for i in range(wide // width)
    ]
    halves[0].start()
    loads = [
        pltpu.make_async_copy(
            factors.at[pl.ds(me * width, width), pl.ds(0, rank)], factor_bank, factor_sem.at[0]
        ),
        pltpu.make_async_copy(
            second.at[:, pl.ds(PROJECTED_WIDTH + MODEL_WIDTH, wide)], second_bank, factor_sem.at[2]
        ),
    ]
    in_load = pltpu.make_async_copy(first.at[:, pl.ds(0, 3 * rank)], in_bank, factor_sem.at[3])
    first_load = pltpu.make_async_copy(
        first.at[:, pl.ds(4 * rank, 2 * rank)], in_bank.at[:, pl.ds(0, 2 * rank)], factor_sem.at[1]
    )
    side_load = pltpu.make_async_copy(
        factors.at[pl.ds(me * width, width), pl.ds(rank, 2 * rank)],
        bank.at[:, pl.ds(wide, 2 * rank)],
        side_sem,
    )
    for item in [in_load] + loads:
        item.start()
    terms = (in_terms, out_terms, second_terms, first_terms, small_terms)
    parts = (2, 2, 1, 1, 1)
    plans = [sum_terms(count, parts[i], terms[i], rooms[i], sems[i]) for i in range(5)]
    order = plans[0][0]
    send = [plan[1] for plan in plans]
    pair_step = [plan[2] for plan in plans]
    line_step = [plan[3] for plan in plans]
    last_step = [plan[4] for plan in plans]
    finish = [plan[5] for plan in plans]

    def block_products(i, left, right, at):
        feature, some = terms[i].shape[1:]

        def product(line):
            def inner(n, carry):
                cols = pl.ds(pl.multiple_of(line * 4 * feature, 4 * feature), 4 * feature)
                into = pl.ds(pl.multiple_of(n * 512, 512), 512)
                from_ = pl.ds(pl.multiple_of(at + n * 512, 512), 512)
                value = contract(left[:, cols], right[:, from_], 0, 0).astype(low)
                terms[i][pl.ds(4 * line, 4), :, into] = value.reshape(4, feature, 512)
                return carry

            lax.fori_loop(0, some // 512, inner, 0)
            for pair in (1 - y, y):
                send[i](line, pair)

        for line in order:
            product(line)

    def send_all(i):
        for pair in (1 - y, y):
            for line in order:
                send[i](line, pair)
        for k in range(depth):
            pair_step[i](k)

    def put_second(at, value):
        size = second_terms.shape[1]
        value = value.astype(low)
        start = at
        while start < at + value.shape[0]:
            block, inner = start // size, start % size
            rows = min(size - inner, at + value.shape[0] - start)
            second_terms[block, inner : inner + rows, :] = value[start - at : start - at + rows]
            start += rows

    def half_product(i):
        halves[i].wait()

        def product(n, carry):
            some = pl.ds(pl.multiple_of(n * 256, 256), 256)
            cols = pl.ds(pl.multiple_of(i * width + n * 256, 256), 256)
            value = contract(joint_grads[...], bank[some], 1, 1)
            stream_grad[:, cols] = value + contract(lowrank_grads[...], in_bank[cols], 1, 1)
            return carry

        lax.fori_loop(0, width // 256, product, 0)
        if i + 1 < len(halves):
            halves[i + 1].start()

    block_products(0, normed, joint_grads, 0)
    for k in range(depth):
        pair_step[0](k)
    in_load.wait()
    half_product(0)
    plans[0][7]()
    block_products(1, attended, grad_rows, OUT_SPLIT)
    for k in range(depth):
        pair_step[1](k)
    for i in range(1, len(halves)):
        half_product(i)
    plans[1][7]()
    first_load.start()
    side_load.start()

    rows = stream[...].astype(jnp.float32)
    inverse = lax.rsqrt(jnp.mean(rows * rows, axis=-1, keepdims=True) + EPSILON)
    grad = stream_grad[...]
    unit = rows * inverse
    gain_grad = jnp.sum(grad * unit, axis=0, keepdims=True)
    scaled = grad * gain[...]
    centre = jnp.mean(scaled * unit, axis=-1, keepdims=True)
    stream_grad[...] = grad_middle[...] + inverse * (scaled - unit * centre)
    small_terms[...] = small[...]
    share = wide // count
    for block in range(count):
        small_terms[block, 0:1, :share] = gain_grad[:, block * share : (block + 1) * share]
    send_all(4)

    def bring(i):
        source = (gate_grads, up_grads, down_grads)[i]
        return pltpu.make_async_copy(source, bank.at[:, pl.ds(0, wide)], grads_sem.at[i])

    bring(0).start()
    line_step[0](0)
    value_at = QUERY_WIDTH + HEAD_SIZE
    for at, stop, left, own in (
        (0, QUERY_WIDTH, joint_grads, lowrank[:, :rank]),
        (QUERY_WIDTH, value_at, joint_grads, lowrank[:, rank : 2 * rank]),
        (value_at, PROJECTED_WIDTH, joint_grads, lowrank[:, 2 * rank :]),
    ):
        put_second(at, contract(left[:, at:stop], own, 0, 0))
    put_second(PROJECTED_WIDTH, contract(grad_rows[...], lowrank_out[...], 0, 0))
    for item in loads + [first_load, side_load]:
        item.wait()

    def put_factor(cols):
        return pltpu.make_async_copy(
            made, factor_grads.at[:, pl.ds(cols * rank, rank)], made_sem.at[cols]
        )

    line_step[0](1)
    held = bank.at[:, pl.ds(0, wide)]
    for i in range(2):
        bring(i).wait()
        if i > 0:
            put_factor(i).wait()
        made[...] = contract(held[...], in_bank[:, i * rank : (i + 1) * rank], 1, 0)
        put_factor(i + 1).start()
        value = contract(held[...], bank[:, wide + i * rank : wide + (i + 1) * rank], 0, 0)
        first_terms[:, :, i * rank : (i + 1) * rank] = value.astype(low).reshape(
            count, wide // count, rank
        )
        bring(i + 1).start()
        if i == 0:
            line_step[0](2)
    send_all(3)
    bring(2).wait()
    put_factor(2).wait()
    made[...] = contract(held[...], second_bank[...], 1, 1)
    put_factor(0).start()
    put_second(
        PROJECTED_WIDTH + MODEL_WIDTH, contract(held[...], factor_bank[...], 0, 0)
    )
    send_all(2)
    line_step[0](3)
    for k in range(depth):
        line_step[1](k)
    last_step[0](in_sum)
    last_step[1](out_sum)
    for i, total in ((4, small_sum), (3, first_sum), (2, second_sum)):
        for k in range(depth):
            line_step[i](k)
        last_step[i](total)
    for item in finish:
        item()
    put_factor(0).wait()


def closing(count, ident, normed, joint_grads, attended, grad_rows, lowrank, lowrank_out, stream,
            gain, grad_middle, small, lowrank_grads, weight, gate_grads, up_grads, down_grads, factors, first,
            second):
    height, wide = normed.shape
    width = gate_grads.shape[0]
    low, high = jnp.bfloat16, jnp.float32
    rank = ADAPTER_RANK
    inside = pl.BlockSpec(memory_space=pltpu.VMEM)
    anywhere = pl.BlockSpec(memory_space=pl.ANY)
    share = wide // count
    shapes = [
        (share, joint_grads.shape[1], low),
        (share, wide - OUT_SPLIT, low),
        (second.shape[1] // count, rank, low),
        (share, 2 * rank, low),
        (8, 128, high),
    ]
    sem = pltpu.SemaphoreType.DMA
    rooms, sems = [], []
    for (rows, cols, kind), parts in zip(shapes, (2, 2, 1, 1, 1)):
        rooms += sum_rooms(count, rows, cols, kind, parts)
        sems += sum_sems(count, parts)
    return pl.pallas_call(
        functools.partial(closing_body, count),
        out_shape=[jax.ShapeDtypeStruct((rows, cols), high) for rows, cols, _ in shapes]
        + [
            jax.ShapeDtypeStruct((height, wide), high),
            jax.ShapeDtypeStruct((width, 3 * rank), high),
        ],
        in_specs=[inside] * 11 + [anywhere] * 7,
        out_specs=[inside] * 6 + [anywhere],
        scratch_shapes=[
            pltpu.VMEM((width, weight.shape[1]), low),
            pltpu.VMEM((wide, 3 * rank), low),
            pltpu.VMEM((width, rank), low),
            pltpu.VMEM((rank, wide), low),
            pltpu.VMEM((width, rank), high),
        ]
        + [pltpu.VMEM((count, rows, cols), kind) for rows, cols, kind in shapes]
        + rooms
        + [sem((wide // width,)), sem((3,)), sem((4,)), sem((3,)), sem]
        + sems,
        compiler_params=kernel_params(ident),
        name="closing",
    )(
        normed, joint_grads, attended, grad_rows, lowrank, lowrank_out, stream, gain, grad_middle,
        small, lowrank_grads, weight, gate_grads, up_grads, down_grads, factors, first, second,
    )


def line_order(z):
    near = z < 2
    return [z, z + 1 - 2 * (z % 2), jnp.where(near, 2, 1), jnp.where(near, 3, 0)]


def unit_values(gate, up, grad):
    slope = 0.7978845608028654
    cubic = 0.044715
    square = gate * gate
    curve = jnp.tanh(slope * (gate + cubic * square * gate))
    half = 0.5 * (1.0 + curve)
    turned = gate * half
    rise = half + 0.5 * gate * (1.0 - curve * curve) * slope * (1.0 + 3.0 * cubic * square)
    low = jnp.bfloat16
    return (turned * up).astype(low), (grad * up * rise).astype(low), (grad * turned).astype(low)


def hidden_body(count, parts, own, grads, weights, units, gate_grads, up_grads, rows_out,
                held, bank, coming, done, bank_sem, coming_sem, done_sem, rows_sem, *sems):
    me, depth, z, y, c = place(count)
    height, wide = own.shape
    width = bank.shape[1]
    tile = 512
    lines = line_order(z)
    greet(count)
    pieces, begin, from_line, from_pair, _, arrive, finish = gather_plan(
        count, [even_spans(height, parts)], (own,), (held,), sems
    )
    begin()
    fills = [
        pltpu.make_async_copy(weights.at[i], bank.at[i], bank_sem.at[i]) for i in range(3)
    ]
    for fill in fills:
        fill.start()

    def first_of(line, pair):
        return 4 * line + 2 * pair

    steps = [(line, pair) for line in lines for pair in (y, 1 - y)]

    def fetch(index):
        some = pl.ds(first_of(*steps[index]), 2)
        return pltpu.make_async_copy(
            grads.at[some], coming.at[index % 2], coming_sem.at[index % 2]
        )

    def store(index):
        rows = pl.ds(first_of(*steps[index]) * height, 2 * height)
        slot = index % 2
        return [
            pltpu.make_async_copy(done.at[slot, i], out.at[rows], done_sem.at[slot, i])
            for i, out in enumerate((units, gate_grads, up_grads))
        ]

    def keep_rows(index):
        some = pl.ds(first_of(*steps[index]), 2)
        return pltpu.make_async_copy(held.at[some], rows_out.at[some], rows_sem.at[index])

    def work(index):
        line, pair = steps[index]
        slot = index % 2
        arrive(first_of(line, pair) + 1 - c, index == 0)
        if index == 0:
            fetch(0).start()
            for fill in fills:
                fill.wait()
        if index + 1 < len(steps):
            fetch(index + 1).start()
        fetch(index).wait()
        keep_rows(index).start()
        if index >= 2:
            for item in store(index - 2):
                item.wait()
        some = pl.ds(first_of(line, pair), 2)

        def inner(n, carry):
            cols = pl.ds(pl.multiple_of(n * tile, tile), tile)
            block = held[some].reshape(2 * height, wide)
            gate = contract(block, bank[0, cols], 1, 1)
            up = contract(block, bank[1, cols], 1, 1)
            grad = contract(coming[slot].reshape(2 * height, wide), bank[2, cols], 1, 1)
            for i, value in enumerate(unit_values(gate, up, grad)):
                done[slot, i, :, cols] = value
            return carry

        lax.fori_loop(0, width // tile, inner, 0)
        for item in store(index):
            item.start()

    work(0)
    for k in range(1, depth + 1):
        for piece in pieces:
            if k < depth:
                from_line(k, piece)
            from_pair(k - 1, piece)
        work(2 * k - 1)
        if k < depth:
            work(2 * k)

    for index in (len(steps) - 2, len(steps) - 1):
        for item in store(index):
            item.wait()
    for index in range(len(steps)):
        keep_rows(index).wait()
    finish()


def hidden_units(count, ident, own, grads, weights, parts=2):
    height, wide = own.shape
    width = weights.shape[1]
    low = jnp.bfloat16
    sem = pltpu.SemaphoreType.DMA
    anywhere = pl.BlockSpec(memory_space=pl.ANY)
    acts = jax.ShapeDtypeStruct((count * height, width), low)
    return pl.pallas_call(
        functools.partial(hidden_body, count, parts),
        out_shape=[acts, acts, acts, jax.ShapeDtypeStruct((count, height, wide), low)],
        in_specs=[anywhere] * 3,
        out_specs=[anywhere] * 4,
        scratch_shapes=[
            pltpu.VMEM((count, height, wide), low),
            pltpu.VMEM((3, width, wide), low),
            pltpu.VMEM((2, 2, height, wide), low),
            pltpu.VMEM((2, 3, 2 * height, width), low),
            sem((3,)),
            sem((2,)),
            sem((2, 3)),
            sem((count // 2,)),
        ]
        + gather_sems(count, 1, parts),
        compiler_params=kernel_params(ident),
        name="hidden_units",
    )(own, grads, weights)


def unit_grads_body(count, parts, units, gate_grads, up_grads, weights, rows_all, grads_all,
                    input_sum, output_sum, gate_out, up_out, down_out, gate_far,
                    bank, rows_in, units_in, made, loaded, leaving, core_in, pair_in, line_in,
                    twin_in, bank_sem, rows_sem, fill_sems, units_sem, made_sem, far_send,
                    far_recv, *sems):
    me, depth, z, y, c = place(count)
    height, wide = input_sum.shape
    width = weights.shape[1]
    step = height // parts
    low = jnp.bfloat16
    core, mate = me + 1 - 2 * c, me + 2 - 4 * y
    near = z < 2
    order = [jnp.where(near, 3, 0), jnp.where(near, 0, 3), jnp.where(near, 2, 1),
             jnp.where(near, 1, 2)]
    greet(count, True)

    def fill(source, at):
        return pltpu.make_async_copy(source, bank.at[at], bank_sem.at[at])

    blocks = width // height

    def fill_rows(source, half, at):
        return [
            pltpu.make_async_copy(
                source.at[half * blocks + i],
                bank.at[at, pl.ds(i * height, height)],
                fill_sems.at[at, i],
            )
            for i in range(blocks)
        ]

    first_fills = [fill(weights.at[i], i) for i in range(3)]
    for item in first_fills:
        item.start()
    grad_tail = fill_rows(grads_all, 1, 3)
    steps = [(line, pair) for line in order for pair in (1 - y, y)]

    def fetch(line, pair, slot, sources):
        rows = pl.ds((4 * line + 2 * pair) * height, 2 * height)
        return [
            pltpu.make_async_copy(source.at[rows], rows_in.at[slot, i], rows_sem.at[slot, i])
            for i, source in enumerate(sources)
        ]

    def plan(a):
        def mine(at, rows):
            return loaded.at[a, at, rows]

        def theirs(at, rows):
            return leaving.at[a, jnp.where(at % 2 == y, 1, 0), rows]

        return sum_plan(
            count, parts, mine, theirs, core_in.at[a], pair_in.at[a], line_in.at[a],
            twin_in.at[a], sems[7 * a : 7 * a + 7],
        )

    plans = [plan(a) for a in range(2)]

    def pair_step(a, k):
        plans[a][2](k)

    def line_step(a, k):
        plans[a][3](k)

    def last_step(a, total):
        plans[a][4](total)

    def to_core(a, line, pair):
        plans[a][1](line, pair)

    def core_left(a, line, pair):
        plans[a][6](line, pair)

    def product(a, index):
        line, pair = steps[index]
        slot = index % 2
        sources = (gate_grads, up_grads) if a == 0 else (units,)
        if index == 0:
            for item in fetch(line, pair, slot, sources):
                item.start()
        if index + 1 < len(steps):
            for item in fetch(*steps[index + 1], 1 - slot, sources):
                item.start()
        if index >= 2:
            core_left(a, *steps[index - 2])
        for item in fetch(line, pair, slot, sources):
            item.wait()
        tile = 512

        def inner(n, carry):
            cols = pl.ds(pl.multiple_of(n * tile, tile), tile)
            if a == 0:
                value = contract(rows_in[slot, 0], bank[0, :, cols], 1, 0)
                value += contract(rows_in[slot, 1], bank[1, :, cols], 1, 0)
            else:
                value = contract(rows_in[slot, 0], bank[2, :, cols], 1, 0)
            value = value.astype(low)

            @pl.when(c == 0)
            def _():
                loaded[a, 2 * line + pair, :, cols] = value[:height]
                leaving[a, slot, :, cols] = value[height:]

            @pl.when(c == 1)
            def _():
                loaded[a, 2 * line + pair, :, cols] = value[height:]
                leaving[a, slot, :, cols] = value[:height]

            return carry

        lax.fori_loop(0, wide // tile, inner, 0)
        to_core(a, line, pair)

    def finish_sends(a):
        for index in (len(steps) - 2, len(steps) - 1):
            core_left(a, *steps[index])

    tall = units_in.shape[2]
    each = width // tall

    def bring(g, slot):
        source = (gate_grads, up_grads, units)[g // each]
        cols = pl.ds((g % each) * tall, tall)
        return pltpu.make_async_copy(source.at[:, cols], units_in.at[slot], units_sem.at[slot])

    def put(g, slot):
        rows = pl.ds((g % each) * tall, tall)
        return pltpu.make_async_copy(
            made.at[slot], (gate_out, up_out, down_out)[g // each].at[rows], made_sem.at[slot]
        )

    def swap(g):
        rows = pl.ds(g * tall, tall)
        return pltpu.make_async_remote_copy(
            src_ref=gate_out.at[rows],
            dst_ref=gate_far.at[rows],
            send_sem=far_send.at[g],
            recv_sem=far_recv.at[g],
            device_id={"loop": 1 - lax.axis_index("loop")},
            device_id_type=MESH,
        )

    number = 3 * each

    def weight_product(g):
        slot = g % 2
        if g + 1 < number:
            bring(g + 1, 1 - slot).start()
        bring(g, slot).wait()
        if g >= 2:
            put(g - 2, slot).wait()
            if g - 2 < FAR_TILES:
                swap(g - 2).start()
        at = 0 if g < 2 * each else 2
        tile = 512

        def inner(n, carry):
            cols = pl.ds(pl.multiple_of(n * tile, tile), tile)
            whole = bank[at : at + 2, :, cols].reshape(2 * width, tile)
            made[slot, :, cols] = contract(units_in[slot], whole, 0, 0).astype(low)
            return carry

        lax.fori_loop(0, wide // tile, inner, 0)
        put(g, slot).start()

    for item in first_fills[:2]:
        item.wait()
    for index in range(8):
        product(0, index)
        if index >= 2 and index % 2 == 0:
            pair_step(0, index // 2 - 1)
    finish_sends(0)
    row_fills = fill_rows(rows_all, 0, 0) + fill_rows(rows_all, 1, 1)
    for item in row_fills:
        item.start()
    for item in grad_tail:
        item.start()
    bring(0, 0).start()
    first_fills[2].wait()
    product(1, 0)
    pair_step(0, 3)
    product(1, 1)
    plans[0][7]()
    for item in row_fills:
        item.wait()
    weight_product(0)
    weight_product(1)
    line_step(0, 0)
    weight_product(2)
    weight_product(3)
    line_step(0, 1)
    for index in range(2, 8):
        product(1, index)
        if index % 2 == 0:
            pair_step(1, index // 2 - 1)
        if index == 6:
            line_step(0, 2)
    finish_sends(1)
    grad_fills = fill_rows(grads_all, 0, 2)
    for item in grad_fills:
        item.start()
    weight_product(4)
    pair_step(1, 3)
    line_step(0, 3)
    weight_product(5)
    plans[1][7]()
    last_step(0, input_sum)
    weight_product(6)
    weight_product(7)
    line_step(1, 0)
    for item in grad_tail + grad_fills:
        item.wait()
    weight_product(8)
    weight_product(9)
    line_step(1, 1)
    weight_product(10)
    weight_product(11)
    line_step(1, 2)
    line_step(1, 3)
    last_step(1, output_sum)

    for g in (number - 2, number - 1):
        put(g, g % 2).wait()
    for g in range(FAR_TILES):
        swap(g).wait()
    for a in range(2):
        plans[a][5](False)


def unit_grads(count, ident, units, gate_grads, up_grads, weights, rows_all, grads_all, parts=2):
    width, wide = weights.shape[1:]
    height = rows_all.shape[1]
    depth = count // 4
    low = jnp.bfloat16
    sem = pltpu.SemaphoreType.DMA
    anywhere = pl.BlockSpec(memory_space=pl.ANY)
    inside = pl.BlockSpec(memory_space=pltpu.VMEM)
    total = jax.ShapeDtypeStruct((height, wide), jnp.float32)

    return pl.pallas_call(
        functools.partial(unit_grads_body, count, parts),
        out_shape=[total, total] + [jax.ShapeDtypeStruct((width, wide), low)] * 3
        + [jax.ShapeDtypeStruct((FAR_TILES * 256, wide), low)],
        in_specs=[anywhere] * 6,
        out_specs=[inside, inside] + [anywhere] * 4,
        scratch_shapes=[
            pltpu.VMEM((4, width, wide), low),
            pltpu.VMEM((2, 2, 2 * height, width), low),
            pltpu.VMEM((2, count * height, 256), low),
            pltpu.VMEM((2, 256, wide), low),
            pltpu.VMEM((2, 2 * depth, height, wide), low),
            pltpu.VMEM((2, 2, height, wide), low),
            pltpu.VMEM((2, 2 * depth, height, wide), low),
            pltpu.VMEM((2, depth, height, wide), low),
            pltpu.VMEM((2, depth + 1, height, wide), low),
            pltpu.VMEM((2, height // 2, wide), low),
            sem((4,)),
            sem((2, 2)),
            sem((4, width // height)),
            sem((2,)),
            sem((2,)),
            sem((FAR_TILES,)),
            sem((FAR_TILES,)),
        ]
        + sum_sems(count, parts)
        + sum_sems(count, parts),
        compiler_params=kernel_params(ident),
        name="unit_grads",
    )(units, gate_grads, up_grads, weights, rows_all, grads_all)


def swap_loops(values):
    return lax.ppermute(values, "loop", [(0, 1), (1, 0)])


def add_body(*refs):
    left, right, out = refs[-3], refs[-2], refs[-1]
    out[0] = left[...].astype(jnp.float32) + right[...].astype(jnp.float32)


def add_into(held, left, right, whole, which, skip):
    rows, wide = right.shape
    step = 256
    before = [] if held is None else [held]
    return pl.pallas_call(
        add_body,
        grid=(rows // step,),
        out_shape=jax.ShapeDtypeStruct(whole, jnp.float32),
        in_specs=[pl.BlockSpec(memory_space=pl.ANY)] * len(before)
        + [
            pl.BlockSpec((step, wide), lambda r: (r + skip // step, 0)),
            pl.BlockSpec((step, wide), lambda r: (r, 0)),
        ],
        out_specs=pl.BlockSpec((1, step, wide), lambda r: (which, r + skip // step, 0)),
        input_output_aliases={0: 0} if before else {},
        compiler_params=pltpu.CompilerParams(vmem_limit_bytes=VMEM_LIMIT),
        name="add_loops",
    )(*before, left, right)


def per_device(
    layer_input_stream,
    layer_output_gradient,
    attention_in_weight,
    attention_out_weight,
    feedforward_weight,
    layer_norm_gains,
    adapter_first_factors,
    adapter_second_factors,
    adapter_hidden_factors,
    group_sequence_lengths,
    token_per_row,
    token_exit_depth,
):
    current_loop = lax.axis_index("loop")
    dp_index = lax.axis_index("dp")
    loop_count = lax.axis_size("loop")
    count = lax.axis_size("dp")
    local_rows = layer_input_stream.shape[1]
    low = jnp.bfloat16
    key_at = QUERY_WIDTH
    value_at = QUERY_WIDTH + HEAD_SIZE
    down_at = PROJECTED_WIDTH + MODEL_WIDTH
    live_all, seq_all, order_all, pos_all = token_facts(token_per_row[0], group_sequence_lengths[0])
    first_row = dp_index * local_rows

    def own_slice(values):
        return lax.dynamic_slice_in_dim(values, first_row, local_rows, 0)

    live_own = own_slice(live_all)
    seq_own = own_slice(seq_all)
    order_own = own_slice(order_all)
    pos_own = own_slice(pos_all)
    active_mask = (live_own & (token_exit_depth[0] > current_loop)).astype(jnp.float32)[:, None]
    stream = layer_input_stream[0]
    residual_stream = stream.astype(jnp.float32)
    grad_out = layer_output_gradient[0].astype(jnp.float32)
    adapter_first = adapter_first_factors[0]
    adapter_second = adapter_second_factors[0]
    ffn_weight = jnp.swapaxes(feedforward_weight, 0, 1)
    feedforward_gradient = (active_mask * grad_out).astype(low)

    input_weight, output_weight, ffn_folded, normed_input, lowrank_projection = opening(
        count, 1, stream, layer_norm_gains[:1], (attention_in_weight, attention_out_weight),
        (IN_SHARE, OUT_SHARE), ffn_weight, adapter_hidden_factors[0], adapter_first,
        adapter_second,
    )
    half = HEAD_SIZE // 2
    freqs = 10000.0 ** (-jnp.arange(half, dtype=jnp.float32) / half)
    angles = pos_own.astype(jnp.float32)[:, None] * freqs
    cosine, sine = jnp.cos(angles), jnp.sin(angles)
    facts = (cosine, sine, seq_own[:, None], order_own[:, None], seq_all[None], order_all[None])
    (
        queries, attended_rows, output_projection, level, middle_state, second_normed_input,
        kv_blocks, grad_blocks,
    ) = attention(
        count, 2, normed_input, lowrank_projection, stream, active_mask, layer_norm_gains[1:],
        *facts, input_weight, output_weight, adapter_first, adapter_second, feedforward_gradient,
    )
    units_own, grad_gate_own, grad_up_own, normed_blocks = hidden_units(
        count, 3, second_normed_input, grad_blocks, ffn_folded
    )
    second_normed_gradient, ffn_sum, gate_grad, up_grad, down_grad, gate_other = unit_grads(
        count, 4, units_own, grad_gate_own, grad_up_own, ffn_folded, normed_blocks, grad_blocks
    )
    gate_last = swap_loops(gate_grad[FAR_TILES * 256 :])
    up_other = swap_loops(up_grad)
    down_other = swap_loops(down_grad)

    complete_output = middle_state + active_mask * ffn_sum
    confidence = root_mean(residual_stream) / (
        root_mean(residual_stream) + root_mean(complete_output - residual_stream)
    )
    conf_sum = jnp.sum(jnp.where(live_own, confidence, 0.0))
    depth_hits = (
        (token_exit_depth[0][:, None] == jnp.arange(loop_count + 1, dtype=jnp.int32)[None, :])
        & live_own[:, None]
    ).astype(jnp.float32)
    stats = jnp.concatenate([conf_sum[None], jnp.sum(depth_hits, axis=0)])
    grad_middle_part, grad_gain_two = jax.vjp(norm_rows, middle_state, layer_norm_gains[1])[1](
        second_normed_gradient
    )
    grad_middle = grad_out + grad_middle_part
    branch_gradient = (active_mask * grad_middle).astype(low)
    joint_grads, lowrank_grads, out_first = attention_grads(
        count, 5, attended_rows, branch_gradient, output_weight, queries,
        kv_blocks.reshape(count * local_rows, 2 * HEAD_SIZE), level, *facts, adapter_first,
        adapter_second,
    )
    width_own = MODEL_WIDTH // count
    small = jnp.zeros((count, 8, 128), jnp.float32)
    small = small.at[:, 1, :width_own].set(grad_gain_two.reshape(count, width_own))
    small = small.at[:, 2, : loop_count + 2].set(stats[None])
    (
        in_portion, out_last, second_grad, first_grad_hidden, small_sum, hidden_grad,
        adapter_hidden_gradient,
    ) = closing(
        count, 6, normed_input, joint_grads, attended_rows, branch_gradient, lowrank_projection,
        output_projection, stream, layer_norm_gains[:1], grad_middle, small, lowrank_grads,
        input_weight, gate_grad, up_grad, down_grad, adapter_hidden_factors[0], adapter_first,
        adapter_second,
    )
    gate_other, gate_last, up_other, down_other, small_sum = lax.optimization_barrier(
        (gate_other, gate_last, up_other, down_other, small_sum)
    )
    in_low = in_portion.astype(low)
    out_low = jnp.concatenate([out_first, out_last], axis=1).astype(low)
    in_far, out_far, small_far = swap_loops(in_low), swap_loops(out_low), swap_loops(small_sum)
    whole = ffn_weight.shape
    sum_mlp = add_into(None, gate_grad, gate_other, whole, 0, 0)
    sum_mlp = add_into(sum_mlp, gate_grad, gate_last, whole, 0, FAR_TILES * 256)
    sum_mlp = add_into(sum_mlp, up_grad, up_other, whole, 1, 0)
    sum_mlp = add_into(sum_mlp, down_grad, down_other, whole, 2, 0)
    adapter_first_gradient = jnp.concatenate(
        [
            outer_columns(in_low[:, :key_at], adapter_second[:, :key_at]),
            outer_columns(in_low[:, key_at:value_at], adapter_second[:, key_at:value_at]),
            outer_columns(in_low[:, value_at:], adapter_second[:, value_at:PROJECTED_WIDTH]),
            outer_columns(out_low, adapter_second[:, PROJECTED_WIDTH:down_at]),
            first_grad_hidden,
        ],
        axis=1,
    )
    in_far, out_far, small_far, sum_mlp, adapter_first_gradient = lax.optimization_barrier(
        (in_far, out_far, small_far, sum_mlp, adapter_first_gradient)
    )
    small_total = small_sum + small_far
    sum_gains = small_total[:2, :width_own]
    depth_total = small_total[2, 1 : loop_count + 2]
    mean_confidence = small_total[2, 0] / jnp.sum(depth_total)
    exit_counts = depth_total.astype(jnp.int32)
    return (
        complete_output.astype(low)[None],
        hidden_grad[None],
        in_low.astype(jnp.float32) + in_far.astype(jnp.float32),
        out_low.astype(jnp.float32) + out_far.astype(jnp.float32),
        jnp.swapaxes(sum_mlp, 0, 1),
        sum_gains,
        adapter_first_gradient[None],
        jnp.swapaxes(second_grad, 0, 1)[None],
        adapter_hidden_gradient[None],
        exit_counts,
        mean_confidence,
    )


def per_device_any(
    layer_input_stream,
    layer_output_gradient,
    attention_in_weight,
    attention_out_weight,
    feedforward_weight,
    layer_norm_gains,
    adapter_first_factors,
    adapter_second_factors,
    adapter_hidden_factors,
    group_sequence_lengths,
    token_per_row,
    token_exit_depth,
):
    current_loop = lax.axis_index("loop")
    dp_index = lax.axis_index("dp")
    loop_count = lax.axis_size("loop")
    local_rows = layer_input_stream.shape[1]
    ffn_rows = feedforward_weight.shape[0]
    scale = HEAD_SIZE ** (-0.5)
    live_all, seq_all, order_all, pos_all = token_facts(token_per_row[0], group_sequence_lengths[0])
    first_row = dp_index * local_rows

    def own_slice(values):
        return lax.dynamic_slice_in_dim(values, first_row, local_rows, 0)

    live_own = own_slice(live_all)
    seq_own = own_slice(seq_all)
    order_own = own_slice(order_all)
    pos_own = own_slice(pos_all)
    active_mask = (live_own & (token_exit_depth[0] > current_loop)).astype(jnp.float32)[:, None]
    residual_stream = layer_input_stream[0].astype(jnp.float32)
    adapter_first = adapter_first_factors[0]
    adapter_second = adapter_second_factors[0]
    adapter_feedforward = adapter_hidden_factors[0]
    ffn_own = lax.dynamic_slice_in_dim(adapter_feedforward, dp_index * ffn_rows, ffn_rows, 0)
    input_weight, output_weight = (
        lax.all_gather(attention_in_weight, "dp", axis=0, tiled=True),
        lax.all_gather(attention_out_weight, "dp", axis=0, tiled=True),
    )
    normed_input = norm_rows(residual_stream, layer_norm_gains[0]).astype(jnp.bfloat16)
    lowrank_projection = matrix_product(normed_input, adapter_first[:, : 3 * ADAPTER_RANK]).astype(
        jnp.bfloat16
    )
    adapter_query_key_value = jnp.concatenate(
        [
            matrix_product(lowrank_projection[:, :ADAPTER_RANK], adapter_second[:, :QUERY_WIDTH]),
            matrix_product(
                lowrank_projection[:, ADAPTER_RANK : 2 * ADAPTER_RANK],
                adapter_second[:, QUERY_WIDTH : QUERY_WIDTH + HEAD_SIZE],
            ),
            matrix_product(
                lowrank_projection[:, 2 * ADAPTER_RANK :],
                adapter_second[:, QUERY_WIDTH + HEAD_SIZE : PROJECTED_WIDTH],
            ),
        ],
        axis=1,
    )
    query_key_value_linear = matrix_product(normed_input, input_weight) + adapter_query_key_value
    queries = rotate(
        query_key_value_linear[:, :QUERY_WIDTH].reshape(local_rows, HEADS, HEAD_SIZE), pos_own
    ).astype(jnp.bfloat16)
    key_rot = rotate(
        query_key_value_linear[:, QUERY_WIDTH : QUERY_WIDTH + HEAD_SIZE].reshape(
            local_rows, 1, HEAD_SIZE
        ),
        pos_own,
    )[:, 0]
    kv_send = jnp.concatenate(
        [key_rot, query_key_value_linear[:, QUERY_WIDTH + HEAD_SIZE :]], axis=1
    ).astype(jnp.bfloat16)
    kv_all = lax.all_gather(kv_send, "dp", axis=0, tiled=True)
    keys = kv_all[:, :HEAD_SIZE]
    values = kv_all[:, HEAD_SIZE:]
    key_total = kv_all.shape[0]
    allowed = ((seq_own[:, None] == seq_all[None, :]) & (order_all[None, :] <= order_own[:, None]))[
        :, None, :
    ]
    query_rows = queries.reshape(local_rows * HEADS, HEAD_SIZE)

    def score_rows():
        raw_scores = (outer_columns(query_rows, keys) * scale).reshape(local_rows, HEADS, key_total)
        return jnp.where(allowed, raw_scores, FLOOR_SCORE)

    scores = score_rows()
    top_score = jnp.max(scores, axis=-1, keepdims=True)
    expo = jnp.exp(scores - top_score)
    mass = jnp.sum(expo, axis=-1, keepdims=True)
    prob_low = (expo / mass).astype(jnp.bfloat16)
    attended_rows = (
        matrix_product(prob_low.reshape(local_rows * HEADS, key_total), values)
        .reshape(local_rows, QUERY_WIDTH)
        .astype(jnp.bfloat16)
    )
    output_projection = matrix_product(
        attended_rows, adapter_first[:, 3 * ADAPTER_RANK : 4 * ADAPTER_RANK]
    ).astype(jnp.bfloat16)
    branch_output = matrix_product(attended_rows, output_weight) + matrix_product(
        output_projection, adapter_second[:, PROJECTED_WIDTH : PROJECTED_WIDTH + MODEL_WIDTH]
    )
    middle_state = residual_stream + active_mask * branch_output
    second_normed_input = norm_rows(middle_state, layer_norm_gains[1]).astype(jnp.bfloat16)
    feedforward_projection = matrix_product(
        second_normed_input, adapter_first[:, 4 * ADAPTER_RANK :]
    ).astype(jnp.bfloat16)
    normed_all, proj_all = (
        lax.all_gather(second_normed_input, "dp", axis=0, tiled=True),
        lax.all_gather(feedforward_projection, "dp", axis=0, tiled=True),
    )
    gate_own = outer_columns(normed_all, feedforward_weight[:, 0, :]) + outer_columns(
        proj_all[:, :ADAPTER_RANK], ffn_own[:, ADAPTER_RANK : 2 * ADAPTER_RANK]
    )
    up_own = outer_columns(normed_all, feedforward_weight[:, 1, :]) + outer_columns(
        proj_all[:, ADAPTER_RANK:], ffn_own[:, 2 * ADAPTER_RANK :]
    )
    units_own = geglu(gate_own, up_own).astype(jnp.bfloat16)
    ffn_sum, low_sum = (
        lax.psum_scatter(
            matrix_product(units_own, feedforward_weight[:, 2, :]),
            "dp",
            scatter_dimension=0,
            tiled=True,
        ),
        lax.psum_scatter(
            matrix_product(units_own, ffn_own[:, :ADAPTER_RANK]),
            "dp",
            scatter_dimension=0,
            tiled=True,
        ),
    )
    down_lowrank = low_sum.astype(jnp.bfloat16)
    complete_output = middle_state + active_mask * (
        ffn_sum + matrix_product(down_lowrank, adapter_second[:, PROJECTED_WIDTH + MODEL_WIDTH :])
    )
    confidence = root_mean(residual_stream) / (
        root_mean(residual_stream) + root_mean(complete_output - residual_stream)
    )
    conf_sum = jnp.sum(jnp.where(live_own, confidence, 0.0))
    depth_hits = (
        (token_exit_depth[0][:, None] == jnp.arange(loop_count + 1, dtype=jnp.int32)[None, :])
        & live_own[:, None]
    ).astype(jnp.float32)
    conf_total, depth_total = lax.psum((conf_sum, jnp.sum(depth_hits, axis=0)), ("loop", "dp"))
    mean_confidence = conf_total / jnp.sum(depth_total)
    exit_counts = depth_total.astype(jnp.int32)
    grad_out = layer_output_gradient[0].astype(jnp.float32)
    feedforward_gradient = (active_mask * grad_out).astype(jnp.bfloat16)
    lowrank_gradient = outer_columns(
        feedforward_gradient, adapter_second[:, PROJECTED_WIDTH + MODEL_WIDTH :]
    ).astype(jnp.bfloat16)
    grad_ffn_all, grad_low_all = (
        lax.all_gather(feedforward_gradient, "dp", axis=0, tiled=True),
        lax.all_gather(lowrank_gradient, "dp", axis=0, tiled=True),
    )
    hidden_unit_gradient = outer_columns(grad_ffn_all, feedforward_weight[:, 2, :]) + outer_columns(
        grad_low_all, ffn_own[:, :ADAPTER_RANK]
    )
    grad_gate_own, grad_up_own = jax.vjp(geglu, gate_own, up_own)[1](hidden_unit_gradient)
    grad_gate_own = grad_gate_own.astype(jnp.bfloat16)
    grad_up_own = grad_up_own.astype(jnp.bfloat16)
    input_terms = matrix_product(grad_gate_own, feedforward_weight[:, 0, :]) + matrix_product(
        grad_up_own, feedforward_weight[:, 1, :]
    )
    proj_terms = jnp.concatenate(
        [
            matrix_product(grad_gate_own, ffn_own[:, ADAPTER_RANK : 2 * ADAPTER_RANK]),
            matrix_product(grad_up_own, ffn_own[:, 2 * ADAPTER_RANK :]),
        ],
        axis=1,
    )
    grad_norm_base, grad_proj = (
        lax.psum_scatter(input_terms, "dp", scatter_dimension=0, tiled=True),
        lax.psum_scatter(proj_terms, "dp", scatter_dimension=0, tiled=True),
    )
    ffn_grad = jnp.concatenate(
        [
            inner_rows(grad_gate_own, normed_all),
            inner_rows(grad_up_own, normed_all),
            inner_rows(units_own, grad_ffn_all),
            inner_rows(units_own, grad_low_all),
            inner_rows(grad_gate_own, proj_all[:, :ADAPTER_RANK]),
            inner_rows(grad_up_own, proj_all[:, ADAPTER_RANK:]),
        ],
        axis=1,
    )
    lowrank_projection_gradient = grad_proj.astype(jnp.bfloat16)
    second_normed_gradient = grad_norm_base + outer_columns(
        lowrank_projection_gradient, adapter_first[:, 4 * ADAPTER_RANK :]
    )
    grad_middle_part, grad_gain_two = jax.vjp(norm_rows, middle_state, layer_norm_gains[1])[1](
        second_normed_gradient
    )
    grad_middle = grad_out + grad_middle_part
    branch_gradient = (active_mask * grad_middle).astype(jnp.bfloat16)
    output_projection_gradient = outer_columns(
        branch_gradient, adapter_second[:, PROJECTED_WIDTH : PROJECTED_WIDTH + MODEL_WIDTH]
    ).astype(jnp.bfloat16)
    grad_attended = (
        outer_columns(branch_gradient, output_weight)
        + outer_columns(
            output_projection_gradient, adapter_first[:, 3 * ADAPTER_RANK : 4 * ADAPTER_RANK]
        )
    ).astype(jnp.bfloat16)
    grad_att_rows = grad_attended.reshape(local_rows * HEADS, HEAD_SIZE)
    prob = jnp.exp(score_rows() - top_score) / mass
    grad_prob = outer_columns(grad_att_rows, values).reshape(local_rows, HEADS, key_total)
    centre = jnp.sum(prob * grad_prob, axis=-1, keepdims=True)
    grad_scores = (
        (prob * (grad_prob - centre)).astype(jnp.bfloat16).reshape(local_rows * HEADS, key_total)
    )
    grad_queries = (matrix_product(grad_scores, keys) * scale).reshape(local_rows, HEADS, HEAD_SIZE)
    prob_again = prob.astype(jnp.bfloat16).reshape(local_rows * HEADS, key_total)
    kv_terms = jnp.concatenate(
        [inner_rows(grad_scores, query_rows) * scale, inner_rows(prob_again, grad_att_rows)], axis=1
    )
    grad_kv = lax.psum_scatter(kv_terms, "dp", scatter_dimension=0, tiled=True)
    query_linear_gradient = (
        rotate_back(grad_queries, pos_own).reshape(local_rows, QUERY_WIDTH).astype(jnp.bfloat16)
    )
    key_linear_gradient = rotate_back(grad_kv[:, None, :HEAD_SIZE], pos_own)[:, 0].astype(
        jnp.bfloat16
    )
    value_linear_gradient = grad_kv[:, HEAD_SIZE:].astype(jnp.bfloat16)
    query_key_value_gradient = jnp.concatenate(
        [query_linear_gradient, key_linear_gradient, value_linear_gradient], axis=1
    )
    attention_projection_gradient = jnp.concatenate(
        [
            outer_columns(query_linear_gradient, adapter_second[:, :QUERY_WIDTH]),
            outer_columns(
                key_linear_gradient, adapter_second[:, QUERY_WIDTH : QUERY_WIDTH + HEAD_SIZE]
            ),
            outer_columns(
                value_linear_gradient, adapter_second[:, QUERY_WIDTH + HEAD_SIZE : PROJECTED_WIDTH]
            ),
        ],
        axis=1,
    ).astype(jnp.bfloat16)
    normed_gradient = outer_columns(query_key_value_gradient, input_weight) + outer_columns(
        attention_projection_gradient, adapter_first[:, : 3 * ADAPTER_RANK]
    )
    grad_resid_part, grad_gain_one = jax.vjp(norm_rows, residual_stream, layer_norm_gains[0])[1](
        normed_gradient
    )
    hidden_grad = grad_middle + grad_resid_part
    grad_w_in = inner_rows(normed_input, query_key_value_gradient)
    grad_w_out = inner_rows(attended_rows, branch_gradient)
    grad_gains = jnp.stack([grad_gain_one, grad_gain_two])
    adapter_first_gradient = jnp.concatenate(
        [
            inner_rows(normed_input, attention_projection_gradient),
            inner_rows(attended_rows, output_projection_gradient),
            inner_rows(second_normed_input, lowrank_projection_gradient),
        ],
        axis=1,
    )
    adapter_second_gradient = jnp.concatenate(
        [
            inner_rows(lowrank_projection[:, :ADAPTER_RANK], query_linear_gradient),
            inner_rows(lowrank_projection[:, ADAPTER_RANK : 2 * ADAPTER_RANK], key_linear_gradient),
            inner_rows(lowrank_projection[:, 2 * ADAPTER_RANK :], value_linear_gradient),
            inner_rows(output_projection, branch_gradient),
            inner_rows(down_lowrank, feedforward_gradient),
        ],
        axis=1,
    )
    input_portion, output_portion, gain_portion, adapter_first_grads, adapter_second_grads = (
        lax.psum_scatter(grad_w_in, "dp", scatter_dimension=0, tiled=True),
        lax.psum_scatter(grad_w_out, "dp", scatter_dimension=0, tiled=True),
        lax.psum_scatter(grad_gains, "dp", scatter_dimension=1, tiled=True),
        lax.psum_scatter(adapter_first_gradient, "dp", scatter_dimension=0, tiled=True),
        lax.psum_scatter(adapter_second_gradient, "dp", scatter_dimension=1, tiled=True),
    )
    mlp_part = ffn_grad[:, : 3 * MODEL_WIDTH].reshape(ffn_rows, 3, MODEL_WIDTH)
    sum_in, sum_out, sum_gains, sum_mlp = (
        lax.psum(input_portion.astype(jnp.bfloat16), "loop").astype(jnp.float32),
        lax.psum(output_portion.astype(jnp.bfloat16), "loop").astype(jnp.float32),
        lax.psum(gain_portion.astype(jnp.bfloat16), "loop").astype(jnp.float32),
        lax.psum(mlp_part.astype(jnp.bfloat16), "loop").astype(jnp.float32),
    )
    return (
        complete_output.astype(jnp.bfloat16)[None],
        hidden_grad[None],
        sum_in,
        sum_out,
        sum_mlp,
        sum_gains,
        adapter_first_grads[None],
        adapter_second_grads[None],
        ffn_grad[:, 3 * MODEL_WIDTH :][None],
        exit_counts,
        mean_confidence,
    )


def solution(mesh):
    return jax.shard_map(
        per_device if mesh.shape == {"loop": 2, "dp": LINE_DEVICES} else per_device_any,
        mesh=mesh,
        in_specs=(
            P("loop", "dp", None),
            P("loop", "dp", None),
            P("dp", None),
            P("dp", None),
            P("dp", None, None),
            P(),
            P("loop", None, None),
            P("loop", None, None),
            P("loop", None, None),
            P("loop", None),
            P("loop", None),
            P("loop", "dp"),
        ),
        out_specs=(
            P("loop", "dp", None),
            P("loop", "dp", None),
            P("dp", None),
            P("dp", None),
            P("dp", None, None),
            P(None, "dp"),
            P("loop", "dp", None),
            P("loop", None, "dp"),
            P("loop", "dp", None),
            P(),
            P(),
        ),
        check_vma=False,
    )
```

```python
import functools

import jax
import jax.numpy as jnp
from jax import lax
from jax.experimental import pallas as pl
from jax.experimental.pallas import tpu as pltpu
from jax.sharding import PartitionSpec as P

MODEL_WIDTH = 2048
HEADS = 8
HEAD_SIZE = 256
ADAPTER_RANK = 256
QUERY_WIDTH = 2048
PROJECTED_WIDTH = 2560


EPSILON = 1e-06
FLOOR_SCORE = -1e30
MESH = pl.DeviceIdType.MESH
VMEM_LIMIT = 60 * 1024 * 1024
LINE_DEVICES = 16
FAR_TILES = 3
OUT_SPLIT = 1536
IN_SHARE = 48
OUT_SHARE = 32
AB_PARTS = 2
CLOSING_PARTS = (2, 2, 1, 1, 1)


def matrix_product(left, right):
    return jnp.dot(left, right, preferred_element_type=jnp.float32)


def inner_rows(left, right):
    return lax.dot_general(
        left, right, (((0,), (0,)), ((), ())), preferred_element_type=jnp.float32
    )


def outer_columns(left, right):
    return lax.dot_general(
        left, right, (((1,), (1,)), ((), ())), preferred_element_type=jnp.float32
    )


def norm_rows(values, gain):
    return values * lax.rsqrt(jnp.mean(values * values, axis=-1, keepdims=True) + EPSILON) * gain


def rotate(values, positions):
    half_dim = values.shape[-1] // 2
    freqs = 10000.0 ** (-jnp.arange(half_dim, dtype=jnp.float32) / half_dim)
    angles = positions.astype(jnp.float32)[:, None, None] * freqs
    cosine = jnp.cos(angles)
    sine = jnp.sin(angles)
    first_half = values[..., :half_dim]
    second_half = values[..., half_dim:]
    return jnp.concatenate(
        [first_half * cosine - second_half * sine, first_half * sine + second_half * cosine],
        axis=-1,
    )


def rotate_back(grads, positions):

    def turned(values):
        return rotate(values, positions)

    return jax.vjp(turned, jnp.zeros_like(grads))[1](grads)[0]


def geglu(gate_values, up_projection_value):
    return jax.nn.gelu(gate_values, approximate=True) * up_projection_value


def root_mean(values):
    return jnp.sqrt(jnp.mean(values * values, axis=-1) + EPSILON)


def token_facts(row_of_tokens, sequence_length):
    row_total = row_of_tokens.shape[0]
    live_row = row_of_tokens >= 0
    seq_ends = jnp.cumsum(sequence_length)
    seq_index = jnp.sum((row_of_tokens[:, None] >= seq_ends[None, :]).astype(jnp.int32), axis=1)
    seq_starts = seq_ends - sequence_length
    own_start = jnp.sum(
        jnp.where(
            seq_index[:, None] == jnp.arange(sequence_length.shape[0], dtype=jnp.int32)[None, :],
            seq_starts[None, :],
            0,
        ),
        axis=1,
    )
    row_ids = jnp.arange(row_total, dtype=jnp.int32)
    sequence = jnp.where(live_row, seq_index, -1 - row_ids)
    ordering = jnp.where(live_row, row_of_tokens, 0)
    positions = jnp.where(live_row, row_of_tokens - own_start, 0)
    return (live_row, sequence, ordering, positions)


def place(count):
    me = lax.axis_index("dp")
    return me, count // 4, me // 4, (me // 2) % 2, me % 2


def greet(count, across=False):
    me, depth, z, y, c = place(count)
    barrier = pltpu.get_barrier_semaphore()

    def signal(where):
        pl.semaphore_signal(barrier, inc=1, device_id={"dp": where}, device_id_type=MESH)

    signal(me + 1 - 2 * c)
    signal(me + 2 - 4 * y)
    if across:
        other = 1 - lax.axis_index("loop")
        pl.semaphore_signal(barrier, inc=1, device_id={"loop": other}, device_id_type=MESH)

    @pl.when(z > 0)
    def _():
        signal(me - 4)

    @pl.when(z < depth - 1)
    def _():
        signal(me + 4)

    ends = jnp.where((z > 0) & (z < depth - 1), 4, 3)
    pl.semaphore_wait(barrier, ends + 1 if across else ends)


def contract(left, right, left_axis, right_axis):
    return lax.dot_general(
        left,
        right,
        (((left_axis,), (right_axis,)), ((), ())),
        preferred_element_type=jnp.float32,
    )


def gather_plan(count, spans, own, full, sems, far_sems=None, twins=False):
    keep, recv, send_core, send_pair, send_right, send_left, send_twin = sems
    arrays = len(own)
    me, depth, z, y, c = place(count)
    mate = me + 2 - 4 * y
    core = me + 1 - 2 * c

    def copy(unit, block, target, sem, first=False):
        a, s = unit
        rows = pl.ds(*spans[a][s])
        return pltpu.make_async_remote_copy(
            src_ref=own[a].at[rows] if first else full[a].at[block, rows],
            dst_ref=full[a].at[block, rows],
            send_sem=sem,
            recv_sem=recv.at[a, block, s],
            device_id={"dp": target},
            device_id_type=MESH,
        )

    def to_core(unit, block, first=False):
        a, s = unit
        return copy(unit, block, core, send_core.at[a, block // 2, s], first)

    def to_pair(unit, block, first=False):
        a, s = unit
        return copy(unit, block, mate, send_pair.at[a, block // 4, s], first)

    def to_right(unit, block, first=False):
        a, s = unit
        return copy(unit, block, me + 4, send_right.at[a, block // 4, s], first)

    def to_left(unit, block, first=False):
        a, s = unit
        return copy(unit, block, me - 4, send_left.at[a, block // 4, s], first)

    def to_twin(unit, block):
        a, s = unit
        return copy(unit, block, me + 4 - 8 * (z % 2), send_twin.at[a])

    def shared(unit):
        return twins and unit[1] == 1

    def to_far(a, block):
        rows = pl.ds(*spans[a][0])
        return pltpu.make_async_remote_copy(
            src_ref=full[a].at[block, rows],
            dst_ref=full[a].at[block, rows],
            send_sem=far_sems[0].at[a, block // 2],
            recv_sem=far_sems[1].at[a, block],
            device_id={"loop": 1 - lax.axis_index("loop")},
            device_id_type=MESH,
        )

    def far_core(a, block, first=False):
        rows = pl.ds(*spans[a][2])
        return pltpu.make_async_remote_copy(
            src_ref=own[a].at[rows] if first else full[a].at[block, rows],
            dst_ref=full[a].at[block, rows],
            send_sem=far_sems[2].at[a, block // 2],
            recv_sem=far_sems[3].at[a, block],
            device_id={"dp": core},
            device_id_type=MESH,
        )

    def cross(unit, block):
        if far_sems is not None and unit[1] == 0:
            to_far(unit[0], block).start()

    local = [pltpu.make_async_copy(own[a], full[a].at[me], keep.at[a]) for a in range(arrays)]
    units = [(a, s) for a in range(arrays) for s in range(2 if far_sems else len(spans[a]))]

    def begin():
        for unit in units:

            @pl.when(z < depth - 1)
            def _(unit=unit):
                to_right(unit, me, True).start()

            @pl.when(z > 0)
            def _(unit=unit):
                to_left(unit, me, True).start()

            to_pair(unit, me, True).start()
            to_core(unit, me, True).start()
        if far_sems is not None:
            for a in range(arrays):
                far_core(a, me, True).start()
        for item in local:
            item.start()

    def from_line(k, unit):
        @pl.when(z - k >= 0)
        def _():
            block = me - 4 * k
            to_right(unit, block).wait_recv()

            @pl.when(z < depth - 1)
            def _():
                to_right(unit, block).start()

            if k == 1 and shared(unit):

                @pl.when(z % 2 == 0)
                def _():
                    to_pair(unit, block).start()

            else:
                to_pair(unit, block).start()
            to_core(unit, block).start()
            cross(unit, block)

        @pl.when(z + k < depth)
        def _():
            block = me + 4 * k
            to_left(unit, block).wait_recv()

            @pl.when(z > 0)
            def _():
                to_left(unit, block).start()

            if k == 1 and shared(unit):

                @pl.when(z % 2 == 1)
                def _():
                    to_pair(unit, block).start()

            else:
                to_pair(unit, block).start()
            to_core(unit, block).start()
            cross(unit, block)

    def pass_on(unit, block):
        to_pair(unit, block).wait_recv()
        to_core(unit, block).start()
        cross(unit, block)

    def from_pair(k, unit):
        if k == 0:
            pass_on(unit, mate)
            if shared(unit):
                to_twin(unit, mate).start()
            return

        @pl.when(z - k >= 0)
        def _():
            pass_on(unit, mate - 4 * k)

        @pl.when(z + k < depth)
        def _():
            pass_on(unit, mate + 4 * k)

    def far_on(a, block):
        to_far(a, block).wait_recv()
        far_core(a, block).start()

    def from_far(k, a):
        if k == 0:
            far_on(a, mate)
            return

        @pl.when(z - k >= 0)
        def _():
            far_on(a, me - 4 * k)
            far_on(a, mate - 4 * k)

        @pl.when(z + k < depth)
        def _():
            far_on(a, me + 4 * k)
            far_on(a, mate + 4 * k)

    def arrive(block=None, mine=True):
        for unit in units:
            for j in range(count // 2 if block is None else 1):
                to_core(unit, 2 * j + 1 - c if block is None else block).wait_recv()
        if far_sems is not None:
            for a in range(arrays):
                for j in range(count // 2):
                    far_core(a, 2 * j + 1 - c).wait_recv()
        if mine:
            for item in local:
                item.wait()

    def finish():
        for unit in units:
            for j in range(count // 2):
                to_core(unit, 2 * j + c).wait_send()
            for j in range(depth):
                block = 4 * j + 2 * y + c
                if shared(unit):

                    @pl.when(j != z + 1 - 2 * (z % 2))
                    def _():
                        to_pair(unit, block).wait_send()

                else:
                    to_pair(unit, block).wait_send()

                @pl.when((z >= j) & (z < depth - 1))
                def _():
                    to_right(unit, block).wait_send()

                @pl.when((z <= j) & (z > 0))
                def _():
                    to_left(unit, block).wait_send()

            if shared(unit):
                to_twin(unit, mate).wait_send()

        if far_sems is not None:
            for a in range(arrays):
                for j in range(count // 2):
                    far_core(a, 2 * j + c).wait_send()

                    @pl.when(2 * j + c != me)
                    def _():
                        to_far(a, 2 * j + c).wait_send()

    return units, begin, from_line, from_pair, from_far, arrive, finish


def gather_sems(count, number, parts):
    depth = count // 4
    sem = pltpu.SemaphoreType.DMA
    return [
        sem((number,)),
        sem((number, count, parts)),
        sem((number, count // 2, parts)),
        sem((number, depth, parts)),
        sem((number, depth, parts)),
        sem((number, depth, parts)),
        sem((number,)),
    ]


def even_spans(rows, parts):
    return [(s * (rows // parts), rows // parts) for s in range(parts)]


def kernel_params(ident):
    return pltpu.CompilerParams(
        collective_id=ident, has_side_effects=True, vmem_limit_bytes=VMEM_LIMIT
    )


def opening_body(count, shares, arrays, stream, gain, tokens, depths, lengths, grads, *refs):
    own = refs[:arrays]
    weights, factors, first, second = refs[arrays : arrays + 4]
    full = refs[arrays + 4 : 2 * arrays + 4]
    folded, normed, lowrank = refs[2 * arrays + 4 : 2 * arrays + 7]
    all_seq, all_order, own_seq, own_order, own_place, active, live, masked = refs[
        2 * arrays + 7 : 2 * arrays + 15
    ]
    scratch = refs[2 * arrays + 15 :]
    (bank, factor_bank, first_bank, in_bank, second_bank, bank_sem, factor_sem, out_sem) = scratch[
        :8
    ]
    me, depth, z, y, c = place(count)
    rank = ADAPTER_RANK
    width, wide = bank.shape[1:]
    loop = lax.axis_index("loop")
    greet(count, True)
    spans = []
    for a in range(arrays):
        rows, share = own[a].shape[0], shares[a]
        spans.append(
            [
                (pl.multiple_of(loop * (rows - share), 16), share),
                (share, rows - 2 * share),
                (pl.multiple_of((1 - loop) * (rows - share), 16), share),
            ]
        )
    units, begin, from_line, from_pair, from_far, arrive, finish = gather_plan(
        count, spans, own, full, scratch[8:15], scratch[15:19]
    )
    begin()
    fills = [
        pltpu.make_async_copy(weights.at[i], bank.at[i], bank_sem.at[i]) for i in range(3)
    ]
    sources = [
        pltpu.make_async_copy(first.at[:, pl.ds(0, 3 * rank)], in_bank, factor_sem.at[0]),
        pltpu.make_async_copy(
            factors.at[pl.ds(me * width, width)], factor_bank, factor_sem.at[1]
        ),
        pltpu.make_async_copy(
            first.at[:, pl.ds(4 * rank, 2 * rank)], first_bank, factor_sem.at[2]
        ),
        pltpu.make_async_copy(
            second.at[:, pl.ds(PROJECTED_WIDTH + MODEL_WIDTH, wide)], second_bank, factor_sem.at[3]
        ),
    ]
    for item in sources + fills:
        item.start()

    def put(i):
        return pltpu.make_async_copy(bank.at[i], folded.at[i], out_sem.at[i])

    def fold(i):
        high, tile = 256, 512

        def inner(n, carry):
            rows = pl.ds(pl.multiple_of((n // (wide // tile)) * high, high), high)
            cols = pl.ds(pl.multiple_of((n % (wide // tile)) * tile, tile), tile)
            if i == 2:
                extra = contract(factor_bank[rows, :rank], second_bank[:, cols], 1, 0)
            else:
                extra = contract(
                    factor_bank[rows, (i + 1) * rank : (i + 2) * rank],
                    first_bank[cols, i * rank : (i + 1) * rank],
                    1,
                    1,
                )
            bank[i, rows, cols] = (bank[i, rows, cols].astype(jnp.float32) + extra).astype(
                bank.dtype
            )
            return carry

        lax.fori_loop(0, (width // high) * (wide // tile), inner, 0)
        put(i).start()

    starts, total = [], 0
    for i in range(lengths.shape[1]):
        starts.append(total)
        total = total + lengths[0, i]
    ends = starts[1:] + [total]

    def facts(token, row):
        alive = token >= 0
        sequence = sum((token >= end).astype(jnp.int32) for end in ends)
        start = sum(jnp.where(sequence == i, item, 0) for i, item in enumerate(starts))
        return (
            alive,
            jnp.where(alive, sequence, -1 - row),
            jnp.where(alive, token, 0),
            jnp.where(alive, token - start, 0),
        )

    every = tokens[...]
    _, all_seq[...], all_order[...], _ = facts(
        every, lax.broadcasted_iota(jnp.int32, every.shape, 1)
    )
    height = stream.shape[0]
    square = (height, height)
    on = lax.broadcasted_iota(jnp.int32, square, 0) == lax.broadcasted_iota(jnp.int32, square, 1)

    def upright(row):
        return jnp.sum(jnp.where(on, row, 0), axis=1, keepdims=True)

    token = upright(tokens[:, pl.ds(pl.multiple_of(me * height, height), height)])
    alive, own_seq[...], own_order[...], own_place[...] = facts(
        token, me * height + lax.broadcasted_iota(jnp.int32, token.shape, 0)
    )
    depth_own = upright(depths[...])
    live[...] = jnp.where(alive, 1.0, 0.0)
    moving = jnp.where(alive & (depth_own > loop), 1.0, 0.0)
    active[...] = moving
    masked[...] = (moving * grads[...].astype(jnp.float32)).astype(masked.dtype)

    rows = stream[...].astype(jnp.float32)
    inverse = lax.rsqrt(jnp.mean(rows * rows, axis=-1, keepdims=True) + EPSILON)
    normed[...] = (rows * inverse * gain[...]).astype(normed.dtype)
    sources[0].wait()
    lowrank[...] = contract(normed[...], in_bank[...], 1, 0).astype(lowrank.dtype)
    for item in sources[1:]:
        item.wait()
    for k in range(1, depth):
        for a in range(arrays):
            for unit in units:
                if unit[0] == a:
                    from_line(k, unit)
                    from_pair(k - 1, unit)
            if k > 1 or a > 0:
                stage = (k - 1) * arrays + a - 1
                from_far(stage // arrays, stage % arrays)
        fills[k - 1].wait()
        fold(k - 1)
    for unit in units:
        from_pair(depth - 1, unit)
    for stage in range((depth - 1) * arrays - 1, depth * arrays):
        from_far(stage // arrays, stage % arrays)
    arrive()
    finish()
    for i in range(3):
        put(i).wait()


def opening(count, ident, stream, gain, tokens, depths, lengths, grads, arrays, shares, weights,
            factors, first, second):
    number = len(arrays)
    _, width, wide = weights.shape
    low = jnp.bfloat16
    rank = ADAPTER_RANK
    sem = pltpu.SemaphoreType.DMA
    anywhere = pl.BlockSpec(memory_space=pl.ANY)
    inside = pl.BlockSpec(memory_space=pltpu.VMEM)
    out = pl.pallas_call(
        functools.partial(opening_body, count, shares, number),
        out_shape=[
            jax.ShapeDtypeStruct((count,) + item.shape, item.dtype) for item in arrays
        ]
        + [
            jax.ShapeDtypeStruct(weights.shape, low),
            jax.ShapeDtypeStruct(stream.shape, low),
            jax.ShapeDtypeStruct((stream.shape[0], 3 * rank), low),
            jax.ShapeDtypeStruct(tokens.shape, jnp.int32),
            jax.ShapeDtypeStruct(tokens.shape, jnp.int32),
        ]
        + [jax.ShapeDtypeStruct((stream.shape[0], 1), jnp.int32)] * 3
        + [jax.ShapeDtypeStruct((stream.shape[0], 1), jnp.float32)] * 2
        + [jax.ShapeDtypeStruct(grads.shape, low)],
        in_specs=[inside] * 4
        + [pl.BlockSpec(memory_space=pltpu.SMEM), inside]
        + [anywhere] * (number + 4),
        out_specs=[anywhere] * (number + 1) + [inside] * 10,
        scratch_shapes=[
            pltpu.VMEM(weights.shape, low),
            pltpu.VMEM((width, factors.shape[1]), low),
            pltpu.VMEM((wide, 2 * rank), low),
            pltpu.VMEM((wide, 3 * rank), low),
            pltpu.VMEM((rank, wide), low),
            sem((3,)),
            sem((4,)),
            sem((3,)),
        ]
        + gather_sems(count, number, 2)
        + [
            sem((number, count // 2)),
            sem((number, count)),
            sem((number, count // 2)),
            sem((number, count)),
        ],
        compiler_params=kernel_params(ident),
        name="opening",
    )(stream, gain, tokens, depths, lengths, grads, *arrays, weights, factors, first, second)
    return [
        item.reshape((count * item.shape[1],) + item.shape[2:]) for item in out[:number]
    ] + list(out[number:])


def turn(values, cosine, sine):
    half = values.shape[-1] // 2
    first, second = values[:, :half], values[:, half:]
    return jnp.concatenate(
        [first * cosine - second * sine, first * sine + second * cosine], axis=1
    )


def attention_body(count, normed, lowrank, stream, active, gain, cosine, sine, own_seq, own_order,
                   all_seq, all_order, in_weight, out_weight, first, second, grads,
                   queries, attended, lowrank_out, level, middle, normed_next, keys_values, grads_all,
                   in_bank, out_bank, in_second, out_second, out_first, allowed, kv_own, kv_full,
                   load_sem, put_sem, *sems):
    me, depth, z, y, c = place(count)
    height, wide = normed.shape
    size = HEAD_SIZE
    scale = size ** (-0.5)
    rank = ADAPTER_RANK
    low = jnp.bfloat16
    greet(count)
    kv_units, kv_begin, kv_line, kv_pair, _, kv_arrive, kv_finish = gather_plan(
        count, [even_spans(height, 1)], (kv_own,), (kv_full,), sems[:7]
    )
    units, begin, from_line, from_pair, _, arrive, finish = gather_plan(
        count, [even_spans(height, 2)], (grads,), (grads_all,), sems[7:], twins=True
    )
    loads = [
        pltpu.make_async_copy(source, bank, load_sem.at[i])
        for i, (source, bank) in enumerate(
            (
                (in_weight, in_bank),
                (second.at[:, pl.ds(0, PROJECTED_WIDTH)], in_second),
                (out_weight, out_bank),
                (second.at[:, pl.ds(PROJECTED_WIDTH, MODEL_WIDTH)], out_second),
                (first.at[:, pl.ds(3 * rank, rank)], out_first),
            )
        )
    ]
    begin()
    for item in loads:
        item.start()
    loads[0].wait()
    loads[1].wait()

    def head(at, part):
        value = contract(normed[...], in_bank[:, at : at + size], 1, 0)
        return value + contract(
            lowrank[:, part * rank : (part + 1) * rank], in_second[:, at : at + size], 1, 0
        )

    kv_own[:, :size] = turn(head(QUERY_WIDTH, 1), cosine[...], sine[...]).astype(low)
    kv_own[:, size:] = head(QUERY_WIDTH + size, 2).astype(low)
    kv_begin()
    heads = wide // size

    def some_heads(start, stop):
        for i in range(start, stop):
            value = turn(head(i * size, 0), cosine[...], sine[...])
            queries[:, i * size : (i + 1) * size] = value.astype(low)

    some_heads(0, 4)
    (kv_unit,) = kv_units
    kv_line(1, kv_unit)
    kv_pair(0, kv_unit)
    from_line(1, units[0])
    from_pair(0, units[0])
    some_heads(4, heads)
    same = own_seq[...] == all_seq[...]
    allowed[...] = jnp.where(same & (all_order[...] <= own_order[...]), 1.0, 0.0)
    kv_line(2, kv_unit)
    kv_pair(1, kv_unit)
    from_line(1, units[1])
    from_pair(0, units[1])
    kv_line(3, kv_unit)
    kv_pair(2, kv_unit)
    kv_pair(3, kv_unit)
    kv_arrive()
    put_kv = pltpu.make_async_copy(kv_full, keys_values, put_sem)
    put_kv.start()
    total = count * height
    keys = kv_full[:, :, :size].reshape(total, size)
    values = kv_full[:, :, size:].reshape(total, size)

    def attend(pair):
        query = jnp.concatenate(
            [
                queries[:, 2 * pair * size : (2 * pair + 1) * size],
                queries[:, (2 * pair + 1) * size : (2 * pair + 2) * size],
            ],
            axis=0,
        )
        keep = jnp.concatenate([allowed[...], allowed[...]], axis=0) > 0.5
        scores = jnp.where(keep, contract(query, keys, 1, 1) * scale, FLOOR_SCORE)
        top = jnp.max(scores, axis=-1, keepdims=True)
        expo = jnp.exp(scores - top)
        mass = jnp.sum(expo, axis=-1, keepdims=True)
        level[pair] = jnp.broadcast_to(top + jnp.log(mass), level.shape[1:])
        value = contract((expo / mass).astype(low), values, 1, 0).astype(low)
        for i in range(2):
            attended[:, (2 * pair + i) * size : (2 * pair + i + 1) * size] = value[
                i * height : (i + 1) * height
            ]

    for pair in range(heads // 2):
        attend(pair)
        if pair == 0:
            for unit in units:
                from_line(2, unit)
        if pair == 1:
            for unit in units:
                from_pair(1, unit)
        if pair == 2:
            for unit in units:
                from_line(3, unit)
        if pair == 3:
            for unit in units:
                from_pair(2, unit)
    for item in loads[2:]:
        item.wait()
    lowrank_out[...] = contract(attended[...], out_first[...], 1, 0).astype(low)
    tile = 256

    def product(n, carry):
        cols = pl.ds(pl.multiple_of(n * tile, tile), tile)
        value = contract(attended[...], out_bank[:, cols], 1, 0)
        value += contract(lowrank_out[...], out_second[:, cols], 1, 0)
        middle[:, cols] = stream[:, cols].astype(jnp.float32) + active[...] * value
        return carry

    lax.fori_loop(0, wide // tile, product, 0)
    rows = middle[...]
    inverse = lax.rsqrt(jnp.mean(rows * rows, axis=-1, keepdims=True) + EPSILON)
    normed_next[...] = (rows * inverse * gain[...]).astype(low)
    for unit in units:
        from_pair(3, unit)
    arrive()
    finish()
    kv_finish()
    put_kv.wait()


def attention(count, ident, normed, lowrank, stream, active, gain, cosine, sine, own_seq,
              own_order, all_seq, all_order, in_weight, out_weight, first, second, grads):
    height, wide = normed.shape
    low, high = jnp.bfloat16, jnp.float32
    inside = pl.BlockSpec(memory_space=pltpu.VMEM)
    anywhere = pl.BlockSpec(memory_space=pl.ANY)
    rank = ADAPTER_RANK
    both = 2 * HEAD_SIZE
    total = count * height
    sem = pltpu.SemaphoreType.DMA
    shape = jax.ShapeDtypeStruct
    return pl.pallas_call(
        functools.partial(attention_body, count),
        out_shape=[
            shape((height, wide), low),
            shape((height, wide), low),
            shape((height, rank), low),
            shape((wide // both, 2 * height, 128), high),
            shape((height, wide), high),
            shape((height, wide), low),
            shape((count, height, both), low),
            shape((count, height, wide), low),
        ],
        in_specs=[inside] * 11 + [anywhere] * 5,
        out_specs=[inside] * 6 + [anywhere] * 2,
        scratch_shapes=[
            pltpu.VMEM(in_weight.shape, low),
            pltpu.VMEM(out_weight.shape, low),
            pltpu.VMEM((rank, PROJECTED_WIDTH), low),
            pltpu.VMEM((rank, wide), low),
            pltpu.VMEM((wide, rank), low),
            pltpu.VMEM((height, total), high),
            pltpu.VMEM((height, both), low),
            pltpu.VMEM((count, height, both), low),
            sem((5,)),
            sem,
        ]
        + gather_sems(count, 1, 1)
        + gather_sems(count, 1, 2),
        compiler_params=kernel_params(ident),
        name="attention",
    )(
        normed, lowrank, stream, active, gain, cosine, sine, own_seq, own_order, all_seq,
        all_order, in_weight, out_weight, first, second, grads,
    )


def sum_plan(count, parts, mine, theirs, core_in, pair_in, line_in, twin_in, sems,
             twins=True):
    me, depth, z, y, c = place(count)
    core_send, core_recv, pair_send, pair_recv, line_send, line_recv, twin_sem = sems
    rows = core_in.shape[1]
    step = rows // parts
    near = z < 2
    order = [
        jnp.where(near, 3, 0),
        jnp.where(near, 0, 3),
        jnp.where(near, 2, 1),
        jnp.where(near, 1, 2),
    ]

    def rows_of(s):
        return pl.ds(s * step, step)

    def to_core(line, pair, s):
        at = 2 * line + pair
        return pltpu.make_async_remote_copy(
            src_ref=theirs(at, rows_of(s)),
            dst_ref=core_in.at[at, rows_of(s)],
            send_sem=core_send.at[at, s],
            recv_sem=core_recv.at[at, s],
            device_id={"dp": me + 1 - 2 * c},
            device_id_type=MESH,
        )

    def to_pair(line, s):
        return pltpu.make_async_remote_copy(
            src_ref=mine(2 * line + 1 - y, rows_of(s)),
            dst_ref=pair_in.at[line, rows_of(s)],
            send_sem=pair_send.at[line, s],
            recv_sem=pair_recv.at[line, s],
            device_id={"dp": me + 2 - 4 * y},
            device_id_type=MESH,
        )

    def along(line, slot, s, target):
        return pltpu.make_async_remote_copy(
            src_ref=mine(2 * line + y, rows_of(s)),
            dst_ref=line_in.at[slot, rows_of(s)],
            send_sem=line_send.at[line, s],
            recv_sem=line_recv.at[slot, s],
            device_id={"dp": target},
            device_id_type=MESH,
        )

    twin = z + 1 - 2 * (z % 2)

    def shared(s):
        return twins and parts > 1 and s == parts - 1

    def to_twin():
        return pltpu.make_async_remote_copy(
            src_ref=mine(2 * twin + 1 - y, rows_of(parts - 1)),
            dst_ref=twin_in,
            send_sem=twin_sem.at[0],
            recv_sem=twin_sem.at[1],
            device_id={"dp": me + 4 - 8 * (z % 2)},
            device_id_type=MESH,
        )

    if shared(parts - 1):
        pair_in[twin, rows_of(parts - 1)] = jnp.zeros((step, core_in.shape[2]), pair_in.dtype)

    def send_core(line, pair):
        for s in range(parts):
            to_core(line, pair, s).start()

    def core_left(line, pair):
        for s in range(parts):
            to_core(line, pair, s).wait_send()

    def pair_step(k):
        line = order[k]
        at = 2 * line + 1 - y
        for s in range(parts):
            to_core(line, 1 - y, s).wait_recv()
            block = mine(at, rows_of(s))
            block[...] = block[...] + core_in[at, rows_of(s)]
            if not shared(s):
                to_pair(line, s).start()
                continue

            @pl.when(line == twin)
            def _():
                to_twin().start()

            @pl.when((line != twin) & (line != z))
            def _():
                to_pair(line, s).start()

    def twin_step():
        block = mine(2 * z + 1 - y, rows_of(parts - 1))
        to_twin().wait_recv()
        block[...] = block[...] + twin_in[...]
        to_pair(z, parts - 1).start()

    def own_sum(line, s):
        at = 2 * line + y
        to_core(line, y, s).wait_recv()
        if shared(s):

            @pl.when(line != twin)
            def _():
                to_pair(line, s).wait_recv()

        else:
            to_pair(line, s).wait_recv()
        part = mine(at, rows_of(s))[...].astype(jnp.float32)
        part += core_in[at, rows_of(s)].astype(jnp.float32)
        return part + pair_in[line, rows_of(s)].astype(jnp.float32)

    def line_step(k):
        line = order[k]

        @pl.when(line != z)
        def _():
            for s in range(parts):
                block = mine(2 * line + y, rows_of(s))
                follows = ((line > z) & (z > 0)) | ((line < z) & (z < depth - 1))
                part = own_sum(line, s)

                @pl.when(follows)
                def _():
                    along(z, line, s, me + 4).wait_recv()
                    extra = line_in[line, rows_of(s)].astype(jnp.float32)
                    block[...] = (part + extra).astype(block.dtype)

                @pl.when(jnp.logical_not(follows))
                def _():
                    block[...] = part.astype(block.dtype)

                @pl.when(line > z)
                def _():
                    along(line, line, s, me + 4).start()

                @pl.when(line < z)
                def _():
                    along(line, jnp.where(line == z - 1, depth, line), s, me - 4).start()

    def last_step(total):
        for s in range(parts):
            total[rows_of(s)] = own_sum(z, s)

            @pl.when(z > 0)
            def _():
                along(z, z, s, me + 4).wait_recv()
                total[rows_of(s)] += line_in[z, rows_of(s)].astype(jnp.float32)

            @pl.when(z < depth - 1)
            def _():
                along(z, depth, s, me + 4).wait_recv()
                total[rows_of(s)] += line_in[depth, rows_of(s)].astype(jnp.float32)

    def finish(cores=True):
        if shared(parts - 1):
            to_twin().wait_send()
        for line in range(depth):
            for s in range(parts):
                for pair in range(2 if cores else 0):
                    to_core(line, pair, s).wait_send()
                if shared(s):

                    @pl.when(line != twin)
                    def _():
                        to_pair(line, s).wait_send()

                else:
                    to_pair(line, s).wait_send()

                @pl.when(z != line)
                def _():
                    along(line, line, s, me + 4).wait_send()

    return order, send_core, pair_step, line_step, last_step, finish, core_left, twin_step


def sum_sems(count, parts):
    depth = count // 4
    sem = pltpu.SemaphoreType.DMA
    return [
        sem((2 * depth, parts)),
        sem((2 * depth, parts)),
        sem((depth, parts)),
        sem((depth, parts)),
        sem((depth, parts)),
        sem((depth + 1, parts)),
        sem((2,)),
    ]


def sum_rooms(count, rows, cols, kind=jnp.bfloat16, parts=2):
    depth = count // 4
    return [
        pltpu.VMEM((2 * depth, rows, cols), kind),
        pltpu.VMEM((depth, rows, cols), kind),
        pltpu.VMEM((depth + 1, rows, cols), kind),
        pltpu.VMEM((rows // parts, cols) if parts > 1 else (16, 128), kind),
    ]


def sum_terms(count, parts, terms, rooms, sems):
    me, depth, z, y, c = place(count)

    def mine(at, rows):
        return terms.at[2 * at + c, rows]

    def theirs(at, rows):
        return terms.at[2 * at + 1 - c, rows]

    return sum_plan(count, parts, mine, theirs, *rooms, sems)


def turn_back(values, cosine, sine):
    half = values.shape[-1] // 2
    first, second = values[:, :half], values[:, half:]
    return jnp.concatenate(
        [first * cosine + second * sine, second * cosine - first * sine], axis=1
    )


def attention_grads_body(count, attended, grad_rows, weight, queries, keys_values, level,
                         cosine, sine, own_seq, own_order, all_seq, all_order, first, second,
                         joint_grads, lowrank_grads, out_sum,
                         weight_in, out_first, both_second, grad_att, allowed, kv_total, kv_terms, kv_sum, out_terms,
                         out_core, out_pair, out_line, out_twin, kv_core, kv_pair, kv_line, kv_twin,
                         weight_sem, *sems):
    me, depth, z, y, c = place(count)
    height, wide = grad_rows.shape
    size = HEAD_SIZE
    scale = size ** (-0.5)
    low = jnp.bfloat16
    greet(count)
    rank = ADAPTER_RANK
    loads = [
        pltpu.make_async_copy(source, bank, weight_sem.at[i])
        for i, (source, bank) in enumerate(
            (
                (weight, weight_in),
                (first.at[:, pl.ds(3 * rank, rank)], out_first),
                (second.at[:, pl.ds(0, PROJECTED_WIDTH + wide)], both_second),
            )
        )
    ]
    for item in loads:
        item.start()
    order, send_out, pair_out, line_out, last_out, finish_out, _, twin_out = sum_terms(
        count, AB_PARTS, out_terms, (out_core, out_pair, out_line, out_twin), sems[:7]
    )
    _, send_kv, pair_kv, line_kv, last_kv, finish_kv, _, _ = sum_terms(
        count, 1, kv_terms, (kv_core, kv_pair, kv_line, kv_twin), sems[7:]
    )
    feature, some = out_terms.shape[1:]

    def out_product(line):
        def inner(n, carry):
            into = pl.ds(pl.multiple_of(n * 512, 512), 512)
            cols = pl.ds(pl.multiple_of(line * 4 * feature, 4 * feature), 4 * feature)
            value = contract(attended[:, cols], grad_rows[:, into], 0, 0).astype(low)
            out_terms[pl.ds(4 * line, 4), :, into] = value.reshape(4, feature, 512)
            return carry

        lax.fori_loop(0, some // 512, inner, 0)
        for pair in (1 - y, y):
            send_out(line, pair)

    for line in order:
        out_product(line)
    for item in loads:
        item.wait()
    tile = 256
    back_out = contract(grad_rows[...], both_second[:, PROJECTED_WIDTH:], 1, 1).astype(low)

    def product(n, carry):
        cols = pl.ds(pl.multiple_of(n * tile, tile), tile)
        value = contract(grad_rows[...], weight_in[cols], 1, 1)
        value += contract(back_out, out_first[cols], 1, 1)
        grad_att[:, cols] = value.astype(low)
        return carry

    lax.fori_loop(0, wide // tile, product, 0)
    same = own_seq[...] == all_seq[...]
    allowed[...] = jnp.where(same & (all_order[...] <= own_order[...]), 1.0, 0.0)
    for k in range(depth):
        pair_out(k)
    keys = keys_values[:, :size]
    values = keys_values[:, size:]

    def heads(pair):
        def both(ref):
            return jnp.concatenate(
                [
                    ref[:, 2 * pair * size : (2 * pair + 1) * size],
                    ref[:, (2 * pair + 1) * size : (2 * pair + 2) * size],
                ],
                axis=0,
            )

        query = both(queries)
        grad = both(grad_att)
        keep = jnp.concatenate([allowed[...], allowed[...]], axis=0) > 0.5
        scores = jnp.where(keep, contract(query, keys, 1, 1) * scale, FLOOR_SCORE)
        prob = jnp.exp(scores - level[pair][:, :1])
        grad_prob = contract(grad, values, 1, 1)
        centre = jnp.sum(prob * grad_prob, axis=-1, keepdims=True)
        grad_scores = (prob * (grad_prob - centre)).astype(low)
        back = contract(grad_scores, keys, 1, 0) * scale
        for i in range(2):
            part = turn_back(back[i * height : (i + 1) * height], cosine[...], sine[...])
            joint_grads[:, (2 * pair + i) * size : (2 * pair + i + 1) * size] = part.astype(low)
        key_part = contract(grad_scores, query, 0, 0) * scale
        value_part = contract(prob.astype(low), grad, 0, 0)
        if pair == 0:
            kv_total[:, :size] = key_part
            kv_total[:, size:] = value_part
        else:
            kv_total[:, :size] += key_part
            kv_total[:, size:] += value_part

    for pair in range(wide // size // 2):
        heads(pair)
        if pair == 0:
            twin_out()
    for block in range(count):
        kv_terms[block] = kv_total[block * height : (block + 1) * height].astype(low)
    for pair in (1 - y, y):
        for line in order:
            send_kv(line, pair)
    for k in range(depth):
        pair_kv(k)
    line_out(0)
    line_out(1)
    for k in range(depth):
        line_kv(k)
        if k + 2 < depth:
            line_out(k + 2)
    last_kv(kv_sum)
    part = turn_back(kv_sum[:, :size], cosine[...], sine[...])
    joint_grads[:, wide : wide + size] = part.astype(low)
    joint_grads[:, wide + size :] = kv_sum[:, size:].astype(low)
    for i, (at, stop) in enumerate(
        ((0, wide), (wide, wide + size), (wide + size, wide + 2 * size))
    ):
        value = contract(joint_grads[:, at:stop], both_second[:, at:stop], 1, 1)
        lowrank_grads[:, i * rank : (i + 1) * rank] = value.astype(low)
    last_out(out_sum)
    finish_out()
    finish_kv()


def attention_grads(count, ident, attended, grad_rows, weight, queries, keys_values, level,
                    cosine, sine, own_seq, own_order, all_seq, all_order, first, second):
    height, wide = grad_rows.shape
    total = keys_values.shape[0]
    low = jnp.bfloat16
    inside = pl.BlockSpec(memory_space=pltpu.VMEM)
    anywhere = pl.BlockSpec(memory_space=pl.ANY)
    feature = attended.shape[1] // count
    both = 2 * HEAD_SIZE
    return pl.pallas_call(
        functools.partial(attention_grads_body, count),
        out_shape=[
            jax.ShapeDtypeStruct((height, wide + both), low),
            jax.ShapeDtypeStruct((height, 3 * ADAPTER_RANK), low),
            jax.ShapeDtypeStruct((feature, OUT_SPLIT), jnp.float32),
        ],
        in_specs=[inside] * 2 + [anywhere] + [inside] * 9 + [anywhere] * 2,
        out_specs=[inside] * 3,
        scratch_shapes=[
            pltpu.VMEM(weight.shape, low),
            pltpu.VMEM((wide, ADAPTER_RANK), low),
            pltpu.VMEM((ADAPTER_RANK, PROJECTED_WIDTH + wide), low),
            pltpu.VMEM(attended.shape, low),
            pltpu.VMEM((height, total), jnp.float32),
            pltpu.VMEM((total, both), jnp.float32),
            pltpu.VMEM((count, height, both), low),
            pltpu.VMEM((height, both), jnp.float32),
            pltpu.VMEM((count, feature, OUT_SPLIT), low),
        ]
        + sum_rooms(count, feature, OUT_SPLIT, parts=AB_PARTS)
        + sum_rooms(count, height, both, parts=1)
        + [pltpu.SemaphoreType.DMA((3,))]
        + sum_sems(count, AB_PARTS)
        + sum_sems(count, 1),
        compiler_params=kernel_params(ident),
        name="attention_grads",
    )(
        attended, grad_rows, weight, queries, keys_values, level,
        cosine, sine, own_seq, own_order, all_seq, all_order, first, second,
    )


def closing_body(count, normed, joint_grads, attended, grad_rows, lowrank, lowrank_out, stream,
                 gain, grad_middle, small, lowrank_grads, weight, gate_grads, up_grads, down_grads, factors,
                 first, second,
                 in_sum, out_sum, second_sum, first_sum, small_sum, stream_grad, factor_grads,
                 bank, in_bank, factor_bank, second_bank, made, in_terms, out_terms,
                 second_terms, first_terms, small_terms, *scratch):
    me, depth, z, y, c = place(count)
    height, wide = normed.shape
    rank = ADAPTER_RANK
    width = gate_grads.shape[0]
    low = jnp.bfloat16
    rooms = [scratch[4 * i : 4 * i + 4] for i in range(5)]
    weight_sem, grads_sem, factor_sem, made_sem, side_sem = scratch[20:25]
    sems = [scratch[25 + 7 * i : 32 + 7 * i] for i in range(5)]
    greet(count)
    halves = [
        pltpu.make_async_copy(weight.at[pl.ds(i * width, width)], bank, weight_sem.at[i])
        for i in range(wide // width)
    ]
    halves[0].start()
    loads = [
        pltpu.make_async_copy(
            factors.at[pl.ds(me * width, width), pl.ds(0, rank)], factor_bank, factor_sem.at[0]
        ),
        pltpu.make_async_copy(
            second.at[:, pl.ds(PROJECTED_WIDTH + MODEL_WIDTH, wide)], second_bank, factor_sem.at[2]
        ),
    ]
    in_load = pltpu.make_async_copy(first.at[:, pl.ds(0, 3 * rank)], in_bank, factor_sem.at[3])
    first_load = pltpu.make_async_copy(
        first.at[:, pl.ds(4 * rank, 2 * rank)], in_bank.at[:, pl.ds(0, 2 * rank)], factor_sem.at[1]
    )
    side_load = pltpu.make_async_copy(
        factors.at[pl.ds(me * width, width), pl.ds(rank, 2 * rank)],
        bank.at[:, pl.ds(wide, 2 * rank)],
        side_sem,
    )
    for item in [in_load] + loads:
        item.start()
    terms = (in_terms, out_terms, second_terms, first_terms, small_terms)
    parts = CLOSING_PARTS
    plans = [sum_terms(count, parts[i], terms[i], rooms[i], sems[i]) for i in range(5)]
    order = plans[0][0]
    send = [plan[1] for plan in plans]
    pair_step = [plan[2] for plan in plans]
    line_step = [plan[3] for plan in plans]
    last_step = [plan[4] for plan in plans]
    finish = [plan[5] for plan in plans]

    def block_products(i, left, right, at):
        feature, some = terms[i].shape[1:]

        def product(line):
            def inner(n, carry):
                cols = pl.ds(pl.multiple_of(line * 4 * feature, 4 * feature), 4 * feature)
                into = pl.ds(pl.multiple_of(n * 512, 512), 512)
                from_ = pl.ds(pl.multiple_of(at + n * 512, 512), 512)
                value = contract(left[:, cols], right[:, from_], 0, 0).astype(low)
                terms[i][pl.ds(4 * line, 4), :, into] = value.reshape(4, feature, 512)
                return carry

            lax.fori_loop(0, some // 512, inner, 0)
            for pair in (1 - y, y):
                send[i](line, pair)

        for line in order:
            product(line)

    def send_all(i):
        for pair in (1 - y, y):
            for line in order:
                send[i](line, pair)
        for k in range(depth):
            pair_step[i](k)

    def put_second(at, value):
        size = second_terms.shape[1]
        value = value.astype(low)
        start = at
        while start < at + value.shape[0]:
            block, inner = start // size, start % size
            rows = min(size - inner, at + value.shape[0] - start)
            second_terms[block, inner : inner + rows, :] = value[start - at : start - at + rows]
            start += rows

    def half_product(i):
        halves[i].wait()

        def product(n, carry):
            some = pl.ds(pl.multiple_of(n * 256, 256), 256)
            cols = pl.ds(pl.multiple_of(i * width + n * 256, 256), 256)
            value = contract(joint_grads[...], bank[some], 1, 1)
            stream_grad[:, cols] = value + contract(lowrank_grads[...], in_bank[cols], 1, 1)
            return carry

        lax.fori_loop(0, width // 256, product, 0)
        if i + 1 < len(halves):
            halves[i + 1].start()

    block_products(0, normed, joint_grads, 0)
    for k in range(depth):
        pair_step[0](k)
    in_load.wait()
    half_product(0)
    plans[0][7]()
    block_products(1, attended, grad_rows, OUT_SPLIT)
    for k in range(depth):
        pair_step[1](k)
    for i in range(1, len(halves)):
        half_product(i)
    plans[1][7]()
    first_load.start()
    side_load.start()

    rows = stream[...].astype(jnp.float32)
    inverse = lax.rsqrt(jnp.mean(rows * rows, axis=-1, keepdims=True) + EPSILON)
    grad = stream_grad[...]
    unit = rows * inverse
    gain_grad = jnp.sum(grad * unit, axis=0, keepdims=True)
    scaled = grad * gain[...]
    centre = jnp.mean(scaled * unit, axis=-1, keepdims=True)
    stream_grad[...] = grad_middle[...] + inverse * (scaled - unit * centre)
    small_terms[...] = small[...]
    share = wide // count
    for block in range(count):
        small_terms[block, 0:1, :share] = gain_grad[:, block * share : (block + 1) * share]
    send_all(4)

    def bring(i):
        source = (gate_grads, up_grads, down_grads)[i]
        return pltpu.make_async_copy(source, bank.at[:, pl.ds(0, wide)], grads_sem.at[i])

    bring(0).start()
    line_step[0](0)
    value_at = QUERY_WIDTH + HEAD_SIZE
    for at, stop, left, own in (
        (0, QUERY_WIDTH, joint_grads, lowrank[:, :rank]),
        (QUERY_WIDTH, value_at, joint_grads, lowrank[:, rank : 2 * rank]),
        (value_at, PROJECTED_WIDTH, joint_grads, lowrank[:, 2 * rank :]),
    ):
        put_second(at, contract(left[:, at:stop], own, 0, 0))
    put_second(PROJECTED_WIDTH, contract(grad_rows[...], lowrank_out[...], 0, 0))
    for item in loads + [first_load, side_load]:
        item.wait()

    def put_factor(cols):
        return pltpu.make_async_copy(
            made, factor_grads.at[:, pl.ds(cols * rank, rank)], made_sem.at[cols]
        )

    line_step[0](1)
    held = bank.at[:, pl.ds(0, wide)]
    for i in range(2):
        bring(i).wait()
        if i > 0:
            put_factor(i).wait()
        made[...] = contract(held[...], in_bank[:, i * rank : (i + 1) * rank], 1, 0)
        put_factor(i + 1).start()
        value = contract(held[...], bank[:, wide + i * rank : wide + (i + 1) * rank], 0, 0)
        first_terms[:, :, i * rank : (i + 1) * rank] = value.astype(low).reshape(
            count, wide // count, rank
        )
        bring(i + 1).start()
        if i == 0:
            line_step[0](2)
    send_all(3)
    bring(2).wait()
    put_factor(2).wait()
    made[...] = contract(held[...], second_bank[...], 1, 1)
    put_factor(0).start()
    put_second(
        PROJECTED_WIDTH + MODEL_WIDTH, contract(held[...], factor_bank[...], 0, 0)
    )
    send_all(2)
    if parts[3] > 1:
        plans[3][7]()
    line_step[0](3)
    for k in range(depth):
        line_step[1](k)
    last_step[0](in_sum)
    last_step[1](out_sum)
    if parts[2] > 1:
        plans[2][7]()
    for i, total in ((4, small_sum), (3, first_sum), (2, second_sum)):
        for k in range(depth):
            line_step[i](k)
        last_step[i](total)
    for item in finish:
        item()
    put_factor(0).wait()


def closing(count, ident, normed, joint_grads, attended, grad_rows, lowrank, lowrank_out, stream,
            gain, grad_middle, small, lowrank_grads, weight, gate_grads, up_grads, down_grads, factors, first,
            second):
    height, wide = normed.shape
    width = gate_grads.shape[0]
    low, high = jnp.bfloat16, jnp.float32
    rank = ADAPTER_RANK
    inside = pl.BlockSpec(memory_space=pltpu.VMEM)
    anywhere = pl.BlockSpec(memory_space=pl.ANY)
    share = wide // count
    shapes = [
        (share, joint_grads.shape[1], low),
        (share, wide - OUT_SPLIT, low),
        (second.shape[1] // count, rank, low),
        (share, 2 * rank, low),
        (8, 128, high),
    ]
    sem = pltpu.SemaphoreType.DMA
    rooms, sems = [], []
    for (rows, cols, kind), parts in zip(shapes, CLOSING_PARTS):
        rooms += sum_rooms(count, rows, cols, kind, parts)
        sems += sum_sems(count, parts)
    return pl.pallas_call(
        functools.partial(closing_body, count),
        out_shape=[jax.ShapeDtypeStruct((rows, cols), high) for rows, cols, _ in shapes]
        + [
            jax.ShapeDtypeStruct((height, wide), high),
            jax.ShapeDtypeStruct((width, 3 * rank), high),
        ],
        in_specs=[inside] * 11 + [anywhere] * 7,
        out_specs=[inside] * 6 + [anywhere],
        scratch_shapes=[
            pltpu.VMEM((width, weight.shape[1]), low),
            pltpu.VMEM((wide, 3 * rank), low),
            pltpu.VMEM((width, rank), low),
            pltpu.VMEM((rank, wide), low),
            pltpu.VMEM((width, rank), high),
        ]
        + [pltpu.VMEM((count, rows, cols), kind) for rows, cols, kind in shapes]
        + rooms
        + [sem((wide // width,)), sem((3,)), sem((4,)), sem((3,)), sem]
        + sems,
        compiler_params=kernel_params(ident),
        name="closing",
    )(
        normed, joint_grads, attended, grad_rows, lowrank, lowrank_out, stream, gain, grad_middle,
        small, lowrank_grads, weight, gate_grads, up_grads, down_grads, factors, first, second,
    )


def line_order(z):
    near = z < 2
    return [z, z + 1 - 2 * (z % 2), jnp.where(near, 2, 1), jnp.where(near, 3, 0)]


def unit_values(gate, up, grad):
    slope = 0.7978845608028654
    cubic = 0.044715
    square = gate * gate
    curve = jnp.tanh(slope * (gate + cubic * square * gate))
    half = 0.5 * (1.0 + curve)
    turned = gate * half
    rise = half + 0.5 * gate * (1.0 - curve * curve) * slope * (1.0 + 3.0 * cubic * square)
    low = jnp.bfloat16
    return (turned * up).astype(low), (grad * up * rise).astype(low), (grad * turned).astype(low)


def hidden_body(count, parts, own, grads, weights, units, gate_grads, up_grads, rows_out,
                held, bank, coming, done, bank_sem, coming_sem, done_sem, rows_sem, *sems):
    me, depth, z, y, c = place(count)
    height, wide = own.shape
    width = bank.shape[1]
    tile = 512
    lines = line_order(z)
    greet(count)
    pieces, begin, from_line, from_pair, _, arrive, finish = gather_plan(
        count, [even_spans(height, parts)], (own,), (held,), sems
    )
    begin()
    fills = [
        pltpu.make_async_copy(weights.at[i], bank.at[i], bank_sem.at[i]) for i in range(3)
    ]
    for fill in fills:
        fill.start()

    def first_of(line, pair):
        return 4 * line + 2 * pair

    steps = [(line, pair) for line in lines for pair in (y, 1 - y)]

    def fetch(index):
        some = pl.ds(first_of(*steps[index]), 2)
        return pltpu.make_async_copy(
            grads.at[some], coming.at[index % 2], coming_sem.at[index % 2]
        )

    def store(index):
        rows = pl.ds(first_of(*steps[index]) * height, 2 * height)
        slot = index % 2
        return [
            pltpu.make_async_copy(done.at[slot, i], out.at[rows], done_sem.at[slot, i])
            for i, out in enumerate((units, gate_grads, up_grads))
        ]

    def keep_rows(index):
        some = pl.ds(first_of(*steps[index]), 2)
        return pltpu.make_async_copy(held.at[some], rows_out.at[some], rows_sem.at[index])

    def work(index):
        line, pair = steps[index]
        slot = index % 2
        arrive(first_of(line, pair) + 1 - c, index == 0)
        if index == 0:
            fetch(0).start()
            for fill in fills:
                fill.wait()
        if index + 1 < len(steps):
            fetch(index + 1).start()
        fetch(index).wait()
        keep_rows(index).start()
        if index >= 2:
            for item in store(index - 2):
                item.wait()
        some = pl.ds(first_of(line, pair), 2)

        def inner(n, carry):
            cols = pl.ds(pl.multiple_of(n * tile, tile), tile)
            block = held[some].reshape(2 * height, wide)
            gate = contract(block, bank[0, cols], 1, 1)
            up = contract(block, bank[1, cols], 1, 1)
            grad = contract(coming[slot].reshape(2 * height, wide), bank[2, cols], 1, 1)
            for i, value in enumerate(unit_values(gate, up, grad)):
                done[slot, i, :, cols] = value
            return carry

        lax.fori_loop(0, width // tile, inner, 0)
        for item in store(index):
            item.start()

    work(0)
    for k in range(1, depth + 1):
        for piece in pieces:
            if k < depth:
                from_line(k, piece)
            from_pair(k - 1, piece)
        work(2 * k - 1)
        if k < depth:
            work(2 * k)

    for index in (len(steps) - 2, len(steps) - 1):
        for item in store(index):
            item.wait()
    for index in range(len(steps)):
        keep_rows(index).wait()
    finish()


def hidden_units(count, ident, own, grads, weights, parts=2):
    height, wide = own.shape
    width = weights.shape[1]
    low = jnp.bfloat16
    sem = pltpu.SemaphoreType.DMA
    anywhere = pl.BlockSpec(memory_space=pl.ANY)
    acts = jax.ShapeDtypeStruct((count * height, width), low)
    return pl.pallas_call(
        functools.partial(hidden_body, count, parts),
        out_shape=[acts, acts, acts, jax.ShapeDtypeStruct((count, height, wide), low)],
        in_specs=[anywhere] * 3,
        out_specs=[anywhere] * 4,
        scratch_shapes=[
            pltpu.VMEM((count, height, wide), low),
            pltpu.VMEM((3, width, wide), low),
            pltpu.VMEM((2, 2, height, wide), low),
            pltpu.VMEM((2, 3, 2 * height, width), low),
            sem((3,)),
            sem((2,)),
            sem((2, 3)),
            sem((count // 2,)),
        ]
        + gather_sems(count, 1, parts),
        compiler_params=kernel_params(ident),
        name="hidden_units",
    )(own, grads, weights)


def unit_grads_body(count, parts, units, gate_grads, up_grads, weights, rows_all, grads_all,
                    input_sum, output_sum, gate_out, up_out, down_out, gate_far,
                    bank, rows_in, units_in, made, loaded, leaving, core_in, pair_in, line_in,
                    twin_in, bank_sem, rows_sem, fill_sems, units_sem, made_sem, far_send,
                    far_recv, *sems):
    me, depth, z, y, c = place(count)
    height, wide = input_sum.shape
    width = weights.shape[1]
    step = height // parts
    low = jnp.bfloat16
    core, mate = me + 1 - 2 * c, me + 2 - 4 * y
    near = z < 2
    order = [jnp.where(near, 3, 0), jnp.where(near, 0, 3), jnp.where(near, 2, 1),
             jnp.where(near, 1, 2)]
    greet(count, True)

    def fill(source, at):
        return pltpu.make_async_copy(source, bank.at[at], bank_sem.at[at])

    blocks = width // height

    def fill_rows(source, half, at):
        return [
            pltpu.make_async_copy(
                source.at[half * blocks + i],
                bank.at[at, pl.ds(i * height, height)],
                fill_sems.at[at, i],
            )
            for i in range(blocks)
        ]

    first_fills = [fill(weights.at[i], i) for i in range(3)]
    for item in first_fills:
        item.start()
    grad_tail = fill_rows(grads_all, 1, 3)
    steps = [(line, pair) for line in order for pair in (1 - y, y)]

    def fetch(line, pair, slot, sources):
        rows = pl.ds((4 * line + 2 * pair) * height, 2 * height)
        return [
            pltpu.make_async_copy(source.at[rows], rows_in.at[slot, i], rows_sem.at[slot, i])
            for i, source in enumerate(sources)
        ]

    def plan(a):
        def mine(at, rows):
            return loaded.at[a, at, rows]

        def theirs(at, rows):
            return leaving.at[a, jnp.where(at % 2 == y, 1, 0), rows]

        return sum_plan(
            count, parts, mine, theirs, core_in.at[a], pair_in.at[a], line_in.at[a],
            twin_in.at[a], sems[7 * a : 7 * a + 7],
        )

    plans = [plan(a) for a in range(2)]

    def pair_step(a, k):
        plans[a][2](k)

    def line_step(a, k):
        plans[a][3](k)

    def last_step(a, total):
        plans[a][4](total)

    def to_core(a, line, pair):
        plans[a][1](line, pair)

    def core_left(a, line, pair):
        plans[a][6](line, pair)

    def product(a, index):
        line, pair = steps[index]
        slot = index % 2
        sources = (gate_grads, up_grads) if a == 0 else (units,)
        if index == 0:
            for item in fetch(line, pair, slot, sources):
                item.start()
        if index + 1 < len(steps):
            for item in fetch(*steps[index + 1], 1 - slot, sources):
                item.start()
        if index >= 2:
            core_left(a, *steps[index - 2])
        for item in fetch(line, pair, slot, sources):
            item.wait()
        tile = 512

        def inner(n, carry):
            cols = pl.ds(pl.multiple_of(n * tile, tile), tile)
            if a == 0:
                value = contract(rows_in[slot, 0], bank[0, :, cols], 1, 0)
                value += contract(rows_in[slot, 1], bank[1, :, cols], 1, 0)
            else:
                value = contract(rows_in[slot, 0], bank[2, :, cols], 1, 0)
            value = value.astype(low)

            @pl.when(c == 0)
            def _():
                loaded[a, 2 * line + pair, :, cols] = value[:height]
                leaving[a, slot, :, cols] = value[height:]

            @pl.when(c == 1)
            def _():
                loaded[a, 2 * line + pair, :, cols] = value[height:]
                leaving[a, slot, :, cols] = value[:height]

            return carry

        lax.fori_loop(0, wide // tile, inner, 0)
        to_core(a, line, pair)

    def finish_sends(a):
        for index in (len(steps) - 2, len(steps) - 1):
            core_left(a, *steps[index])

    tall = units_in.shape[2]
    each = width // tall

    def bring(g, slot):
        source = (gate_grads, up_grads, units)[g // each]
        cols = pl.ds((g % each) * tall, tall)
        return pltpu.make_async_copy(source.at[:, cols], units_in.at[slot], units_sem.at[slot])

    def put(g, slot):
        rows = pl.ds((g % each) * tall, tall)
        return pltpu.make_async_copy(
            made.at[slot], (gate_out, up_out, down_out)[g // each].at[rows], made_sem.at[slot]
        )

    def swap(g):
        rows = pl.ds(g * tall, tall)
        return pltpu.make_async_remote_copy(
            src_ref=gate_out.at[rows],
            dst_ref=gate_far.at[rows],
            send_sem=far_send.at[g],
            recv_sem=far_recv.at[g],
            device_id={"loop": 1 - lax.axis_index("loop")},
            device_id_type=MESH,
        )

    number = 3 * each

    def weight_product(g):
        slot = g % 2
        if g + 1 < number:
            bring(g + 1, 1 - slot).start()
        bring(g, slot).wait()
        if g >= 2:
            put(g - 2, slot).wait()
            if g - 2 < FAR_TILES:
                swap(g - 2).start()
        at = 0 if g < 2 * each else 2
        tile = 512

        def inner(n, carry):
            cols = pl.ds(pl.multiple_of(n * tile, tile), tile)
            whole = bank[at : at + 2, :, cols].reshape(2 * width, tile)
            made[slot, :, cols] = contract(units_in[slot], whole, 0, 0).astype(low)
            return carry

        lax.fori_loop(0, wide // tile, inner, 0)
        put(g, slot).start()

    for item in first_fills[:2]:
        item.wait()
    for index in range(8):
        product(0, index)
        if index >= 2 and index % 2 == 0:
            pair_step(0, index // 2 - 1)
    finish_sends(0)
    row_fills = fill_rows(rows_all, 0, 0) + fill_rows(rows_all, 1, 1)
    for item in row_fills:
        item.start()
    for item in grad_tail:
        item.start()
    bring(0, 0).start()
    first_fills[2].wait()
    product(1, 0)
    pair_step(0, 3)
    product(1, 1)
    plans[0][7]()
    for item in row_fills:
        item.wait()
    weight_product(0)
    weight_product(1)
    line_step(0, 0)
    weight_product(2)
    weight_product(3)
    line_step(0, 1)
    for index in range(2, 8):
        product(1, index)
        if index % 2 == 0:
            pair_step(1, index // 2 - 1)
        if index == 6:
            line_step(0, 2)
    finish_sends(1)
    grad_fills = fill_rows(grads_all, 0, 2)
    for item in grad_fills:
        item.start()
    weight_product(4)
    pair_step(1, 3)
    line_step(0, 3)
    weight_product(5)
    plans[1][7]()
    last_step(0, input_sum)
    weight_product(6)
    weight_product(7)
    line_step(1, 0)
    for item in grad_tail + grad_fills:
        item.wait()
    weight_product(8)
    weight_product(9)
    line_step(1, 1)
    weight_product(10)
    weight_product(11)
    line_step(1, 2)
    line_step(1, 3)
    last_step(1, output_sum)

    for g in (number - 2, number - 1):
        put(g, g % 2).wait()
    for g in range(FAR_TILES):
        swap(g).wait()
    for a in range(2):
        plans[a][5](False)


def unit_grads(count, ident, units, gate_grads, up_grads, weights, rows_all, grads_all, parts=2):
    width, wide = weights.shape[1:]
    height = rows_all.shape[1]
    depth = count // 4
    low = jnp.bfloat16
    sem = pltpu.SemaphoreType.DMA
    anywhere = pl.BlockSpec(memory_space=pl.ANY)
    inside = pl.BlockSpec(memory_space=pltpu.VMEM)
    total = jax.ShapeDtypeStruct((height, wide), jnp.float32)

    return pl.pallas_call(
        functools.partial(unit_grads_body, count, parts),
        out_shape=[total, total] + [jax.ShapeDtypeStruct((width, wide), low)] * 3
        + [jax.ShapeDtypeStruct((FAR_TILES * 256, wide), low)],
        in_specs=[anywhere] * 6,
        out_specs=[inside, inside] + [anywhere] * 4,
        scratch_shapes=[
            pltpu.VMEM((4, width, wide), low),
            pltpu.VMEM((2, 2, 2 * height, width), low),
            pltpu.VMEM((2, count * height, 256), low),
            pltpu.VMEM((2, 256, wide), low),
            pltpu.VMEM((2, 2 * depth, height, wide), low),
            pltpu.VMEM((2, 2, height, wide), low),
            pltpu.VMEM((2, 2 * depth, height, wide), low),
            pltpu.VMEM((2, depth, height, wide), low),
            pltpu.VMEM((2, depth + 1, height, wide), low),
            pltpu.VMEM((2, height // 2, wide), low),
            sem((4,)),
            sem((2, 2)),
            sem((4, width // height)),
            sem((2,)),
            sem((2,)),
            sem((FAR_TILES,)),
            sem((FAR_TILES,)),
        ]
        + sum_sems(count, parts)
        + sum_sems(count, parts),
        compiler_params=kernel_params(ident),
        name="unit_grads",
    )(units, gate_grads, up_grads, weights, rows_all, grads_all)


def swap_loops(values):
    return lax.ppermute(values, "loop", [(0, 1), (1, 0)])


def add_body(*refs):
    lefts, rights, out = refs[:3], refs[3:7], refs[7]
    left, right, made, load_sem, made_sem = refs[8:]
    step = made.shape[1]
    each = left.shape[1] // step
    chunks = [(i, n) for i in range(3) for n in range(each)]

    def loads(i, n):
        rows = pl.ds(n * step, step)
        far = rights[i + 1].at[rows] if i else rights[0].at[rows] if n < FAR_TILES else None
        if far is None:
            far = rights[1].at[pl.ds((n - FAR_TILES) * step, step)]
        return [
            pltpu.make_async_copy(lefts[i].at[rows], left.at[i, rows], load_sem.at[i, n, 0]),
            pltpu.make_async_copy(far, right.at[i, rows], load_sem.at[i, n, 1]),
        ]

    def put(at):
        i, n = chunks[at]
        return pltpu.make_async_copy(
            made.at[at % 2], out.at[i, pl.ds(n * step, step)], made_sem.at[at % 2]
        )

    for i, n in chunks:
        for item in loads(i, n):
            item.start()
    for at, (i, n) in enumerate(chunks):
        for item in loads(i, n):
            item.wait()
        if at >= 2:
            put(at - 2).wait()
        rows = pl.ds(n * step, step)
        made[at % 2] = left[i, rows].astype(jnp.float32) + right[i, rows].astype(jnp.float32)
        put(at).start()
    for at in (len(chunks) - 2, len(chunks) - 1):
        put(at).wait()


def add_loops(lefts, rights):
    rows, wide = lefts[0].shape
    step = 256
    anywhere = pl.BlockSpec(memory_space=pl.ANY)
    sem = pltpu.SemaphoreType.DMA
    return pl.pallas_call(
        add_body,
        out_shape=jax.ShapeDtypeStruct((3, rows, wide), jnp.float32),
        in_specs=[anywhere] * 7,
        out_specs=anywhere,
        scratch_shapes=[
            pltpu.VMEM((3, rows, wide), jnp.bfloat16),
            pltpu.VMEM((3, rows, wide), jnp.bfloat16),
            pltpu.VMEM((2, step, wide), jnp.float32),
            sem((3, rows // step, 2)),
            sem((2,)),
        ],
        compiler_params=pltpu.CompilerParams(vmem_limit_bytes=VMEM_LIMIT),
        name="add_loops",
    )(*lefts, *rights)


def per_device(
    layer_input_stream,
    layer_output_gradient,
    attention_in_weight,
    attention_out_weight,
    feedforward_weight,
    layer_norm_gains,
    adapter_first_factors,
    adapter_second_factors,
    adapter_hidden_factors,
    group_sequence_lengths,
    token_per_row,
    token_exit_depth,
):
    loop_count = lax.axis_size("loop")
    count = lax.axis_size("dp")
    local_rows = layer_input_stream.shape[1]
    low = jnp.bfloat16
    key_at = QUERY_WIDTH
    value_at = QUERY_WIDTH + HEAD_SIZE
    down_at = PROJECTED_WIDTH + MODEL_WIDTH
    stream = layer_input_stream[0]
    residual_stream = stream.astype(jnp.float32)
    grad_out = layer_output_gradient[0].astype(jnp.float32)
    adapter_first = adapter_first_factors[0]
    adapter_second = adapter_second_factors[0]
    ffn_weight = jnp.swapaxes(feedforward_weight, 0, 1)

    (
        input_weight, output_weight, ffn_folded, normed_input, lowrank_projection, seq_all,
        order_all, seq_own, order_own, pos_own, active_mask, live_mask, feedforward_gradient,
    ) = opening(
        count, 1, stream, layer_norm_gains[:1], token_per_row, token_exit_depth,
        group_sequence_lengths, layer_output_gradient[0],
        (attention_in_weight, attention_out_weight), (IN_SHARE, OUT_SHARE), ffn_weight,
        adapter_hidden_factors[0], adapter_first, adapter_second,
    )
    live_own = live_mask[:, 0] > 0.5
    half = HEAD_SIZE // 2
    freqs = 10000.0 ** (-jnp.arange(half, dtype=jnp.float32) / half)
    angles = pos_own.astype(jnp.float32) * freqs
    cosine, sine = jnp.cos(angles), jnp.sin(angles)
    facts = (cosine, sine, seq_own, order_own, seq_all, order_all)
    (
        queries, attended_rows, output_projection, level, middle_state, second_normed_input,
        kv_blocks, grad_blocks,
    ) = attention(
        count, 2, normed_input, lowrank_projection, stream, active_mask, layer_norm_gains[1:],
        *facts, input_weight, output_weight, adapter_first, adapter_second, feedforward_gradient,
    )
    units_own, grad_gate_own, grad_up_own, normed_blocks = hidden_units(
        count, 3, second_normed_input, grad_blocks, ffn_folded
    )
    second_normed_gradient, ffn_sum, gate_grad, up_grad, down_grad, gate_other = unit_grads(
        count, 4, units_own, grad_gate_own, grad_up_own, ffn_folded, normed_blocks, grad_blocks
    )
    gate_last = swap_loops(gate_grad[FAR_TILES * 256 :])
    up_other = swap_loops(up_grad)
    down_other = swap_loops(down_grad)

    complete_output = middle_state + active_mask * ffn_sum
    confidence = root_mean(residual_stream) / (
        root_mean(residual_stream) + root_mean(complete_output - residual_stream)
    )
    conf_sum = jnp.sum(jnp.where(live_own, confidence, 0.0))
    depth_hits = (
        (token_exit_depth[0][:, None] == jnp.arange(loop_count + 1, dtype=jnp.int32)[None, :])
        & live_own[:, None]
    ).astype(jnp.float32)
    stats = jnp.concatenate([conf_sum[None], jnp.sum(depth_hits, axis=0)])
    grad_middle_part, grad_gain_two = jax.vjp(norm_rows, middle_state, layer_norm_gains[1])[1](
        second_normed_gradient
    )
    grad_middle = grad_out + grad_middle_part
    branch_gradient = (active_mask * grad_middle).astype(low)
    joint_grads, lowrank_grads, out_first = attention_grads(
        count, 5, attended_rows, branch_gradient, output_weight, queries,
        kv_blocks.reshape(count * local_rows, 2 * HEAD_SIZE), level, *facts, adapter_first,
        adapter_second,
    )
    width_own = MODEL_WIDTH // count
    small = jnp.zeros((count, 8, 128), jnp.float32)
    small = small.at[:, 1, :width_own].set(grad_gain_two.reshape(count, width_own))
    small = small.at[:, 2, : loop_count + 2].set(stats[None])
    (
        in_portion, out_last, second_grad, first_grad_hidden, small_sum, hidden_grad,
        adapter_hidden_gradient,
    ) = closing(
        count, 6, normed_input, joint_grads, attended_rows, branch_gradient, lowrank_projection,
        output_projection, stream, layer_norm_gains[:1], grad_middle, small, lowrank_grads,
        input_weight, gate_grad, up_grad, down_grad, adapter_hidden_factors[0], adapter_first,
        adapter_second,
    )
    gate_other, gate_last, up_other, down_other, small_sum = lax.optimization_barrier(
        (gate_other, gate_last, up_other, down_other, small_sum)
    )
    in_low = in_portion.astype(low)
    out_low = jnp.concatenate([out_first, out_last], axis=1).astype(low)
    in_far, out_far, small_far = swap_loops(in_low), swap_loops(out_low), swap_loops(small_sum)
    sum_mlp = add_loops(
        (gate_grad, up_grad, down_grad), (gate_other, gate_last, up_other, down_other)
    )
    adapter_first_gradient = jnp.concatenate(
        [
            outer_columns(in_low[:, :key_at], adapter_second[:, :key_at]),
            outer_columns(in_low[:, key_at:value_at], adapter_second[:, key_at:value_at]),
            outer_columns(in_low[:, value_at:], adapter_second[:, value_at:PROJECTED_WIDTH]),
            outer_columns(out_low, adapter_second[:, PROJECTED_WIDTH:down_at]),
            first_grad_hidden,
        ],
        axis=1,
    )
    in_far, out_far, small_far, sum_mlp, adapter_first_gradient = lax.optimization_barrier(
        (in_far, out_far, small_far, sum_mlp, adapter_first_gradient)
    )
    small_total = small_sum + small_far
    sum_gains = small_total[:2, :width_own]
    depth_total = small_total[2, 1 : loop_count + 2]
    mean_confidence = small_total[2, 0] / jnp.sum(depth_total)
    exit_counts = depth_total.astype(jnp.int32)
    return (
        complete_output.astype(low)[None],
        hidden_grad[None],
        in_low.astype(jnp.float32) + in_far.astype(jnp.float32),
        out_low.astype(jnp.float32) + out_far.astype(jnp.float32),
        jnp.swapaxes(sum_mlp, 0, 1),
        sum_gains,
        adapter_first_gradient[None],
        jnp.swapaxes(second_grad, 0, 1)[None],
        adapter_hidden_gradient[None],
        exit_counts,
        mean_confidence,
    )


def per_device_any(
    layer_input_stream,
    layer_output_gradient,
    attention_in_weight,
    attention_out_weight,
    feedforward_weight,
    layer_norm_gains,
    adapter_first_factors,
    adapter_second_factors,
    adapter_hidden_factors,
    group_sequence_lengths,
    token_per_row,
    token_exit_depth,
):
    current_loop = lax.axis_index("loop")
    dp_index = lax.axis_index("dp")
    loop_count = lax.axis_size("loop")
    local_rows = layer_input_stream.shape[1]
    ffn_rows = feedforward_weight.shape[0]
    scale = HEAD_SIZE ** (-0.5)
    live_all, seq_all, order_all, pos_all = token_facts(token_per_row[0], group_sequence_lengths[0])
    first_row = dp_index * local_rows

    def own_slice(values):
        return lax.dynamic_slice_in_dim(values, first_row, local_rows, 0)

    live_own = own_slice(live_all)
    seq_own = own_slice(seq_all)
    order_own = own_slice(order_all)
    pos_own = own_slice(pos_all)
    active_mask = (live_own & (token_exit_depth[0] > current_loop)).astype(jnp.float32)[:, None]
    residual_stream = layer_input_stream[0].astype(jnp.float32)
    adapter_first = adapter_first_factors[0]
    adapter_second = adapter_second_factors[0]
    adapter_feedforward = adapter_hidden_factors[0]
    ffn_own = lax.dynamic_slice_in_dim(adapter_feedforward, dp_index * ffn_rows, ffn_rows, 0)
    input_weight, output_weight = (
        lax.all_gather(attention_in_weight, "dp", axis=0, tiled=True),
        lax.all_gather(attention_out_weight, "dp", axis=0, tiled=True),
    )
    normed_input = norm_rows(residual_stream, layer_norm_gains[0]).astype(jnp.bfloat16)
    lowrank_projection = matrix_product(normed_input, adapter_first[:, : 3 * ADAPTER_RANK]).astype(
        jnp.bfloat16
    )
    adapter_query_key_value = jnp.concatenate(
        [
            matrix_product(lowrank_projection[:, :ADAPTER_RANK], adapter_second[:, :QUERY_WIDTH]),
            matrix_product(
                lowrank_projection[:, ADAPTER_RANK : 2 * ADAPTER_RANK],
                adapter_second[:, QUERY_WIDTH : QUERY_WIDTH + HEAD_SIZE],
            ),
            matrix_product(
                lowrank_projection[:, 2 * ADAPTER_RANK :],
                adapter_second[:, QUERY_WIDTH + HEAD_SIZE : PROJECTED_WIDTH],
            ),
        ],
        axis=1,
    )
    query_key_value_linear = matrix_product(normed_input, input_weight) + adapter_query_key_value
    queries = rotate(
        query_key_value_linear[:, :QUERY_WIDTH].reshape(local_rows, HEADS, HEAD_SIZE), pos_own
    ).astype(jnp.bfloat16)
    key_rot = rotate(
        query_key_value_linear[:, QUERY_WIDTH : QUERY_WIDTH + HEAD_SIZE].reshape(
            local_rows, 1, HEAD_SIZE
        ),
        pos_own,
    )[:, 0]
    kv_send = jnp.concatenate(
        [key_rot, query_key_value_linear[:, QUERY_WIDTH + HEAD_SIZE :]], axis=1
    ).astype(jnp.bfloat16)
    kv_all = lax.all_gather(kv_send, "dp", axis=0, tiled=True)
    keys = kv_all[:, :HEAD_SIZE]
    values = kv_all[:, HEAD_SIZE:]
    key_total = kv_all.shape[0]
    allowed = ((seq_own[:, None] == seq_all[None, :]) & (order_all[None, :] <= order_own[:, None]))[
        :, None, :
    ]
    query_rows = queries.reshape(local_rows * HEADS, HEAD_SIZE)

    def score_rows():
        raw_scores = (outer_columns(query_rows, keys) * scale).reshape(local_rows, HEADS, key_total)
        return jnp.where(allowed, raw_scores, FLOOR_SCORE)

    scores = score_rows()
    top_score = jnp.max(scores, axis=-1, keepdims=True)
    expo = jnp.exp(scores - top_score)
    mass = jnp.sum(expo, axis=-1, keepdims=True)
    prob_low = (expo / mass).astype(jnp.bfloat16)
    attended_rows = (
        matrix_product(prob_low.reshape(local_rows * HEADS, key_total), values)
        .reshape(local_rows, QUERY_WIDTH)
        .astype(jnp.bfloat16)
    )
    output_projection = matrix_product(
        attended_rows, adapter_first[:, 3 * ADAPTER_RANK : 4 * ADAPTER_RANK]
    ).astype(jnp.bfloat16)
    branch_output = matrix_product(attended_rows, output_weight) + matrix_product(
        output_projection, adapter_second[:, PROJECTED_WIDTH : PROJECTED_WIDTH + MODEL_WIDTH]
    )
    middle_state = residual_stream + active_mask * branch_output
    second_normed_input = norm_rows(middle_state, layer_norm_gains[1]).astype(jnp.bfloat16)
    feedforward_projection = matrix_product(
        second_normed_input, adapter_first[:, 4 * ADAPTER_RANK :]
    ).astype(jnp.bfloat16)
    normed_all, proj_all = (
        lax.all_gather(second_normed_input, "dp", axis=0, tiled=True),
        lax.all_gather(feedforward_projection, "dp", axis=0, tiled=True),
    )
    gate_own = outer_columns(normed_all, feedforward_weight[:, 0, :]) + outer_columns(
        proj_all[:, :ADAPTER_RANK], ffn_own[:, ADAPTER_RANK : 2 * ADAPTER_RANK]
    )
    up_own = outer_columns(normed_all, feedforward_weight[:, 1, :]) + outer_columns(
        proj_all[:, ADAPTER_RANK:], ffn_own[:, 2 * ADAPTER_RANK :]
    )
    units_own = geglu(gate_own, up_own).astype(jnp.bfloat16)
    ffn_sum, low_sum = (
        lax.psum_scatter(
            matrix_product(units_own, feedforward_weight[:, 2, :]),
            "dp",
            scatter_dimension=0,
            tiled=True,
        ),
        lax.psum_scatter(
            matrix_product(units_own, ffn_own[:, :ADAPTER_RANK]),
            "dp",
            scatter_dimension=0,
            tiled=True,
        ),
    )
    down_lowrank = low_sum.astype(jnp.bfloat16)
    complete_output = middle_state + active_mask * (
        ffn_sum + matrix_product(down_lowrank, adapter_second[:, PROJECTED_WIDTH + MODEL_WIDTH :])
    )
    confidence = root_mean(residual_stream) / (
        root_mean(residual_stream) + root_mean(complete_output - residual_stream)
    )
    conf_sum = jnp.sum(jnp.where(live_own, confidence, 0.0))
    depth_hits = (
        (token_exit_depth[0][:, None] == jnp.arange(loop_count + 1, dtype=jnp.int32)[None, :])
        & live_own[:, None]
    ).astype(jnp.float32)
    conf_total, depth_total = lax.psum((conf_sum, jnp.sum(depth_hits, axis=0)), ("loop", "dp"))
    mean_confidence = conf_total / jnp.sum(depth_total)
    exit_counts = depth_total.astype(jnp.int32)
    grad_out = layer_output_gradient[0].astype(jnp.float32)
    feedforward_gradient = (active_mask * grad_out).astype(jnp.bfloat16)
    lowrank_gradient = outer_columns(
        feedforward_gradient, adapter_second[:, PROJECTED_WIDTH + MODEL_WIDTH :]
    ).astype(jnp.bfloat16)
    grad_ffn_all, grad_low_all = (
        lax.all_gather(feedforward_gradient, "dp", axis=0, tiled=True),
        lax.all_gather(lowrank_gradient, "dp", axis=0, tiled=True),
    )
    hidden_unit_gradient = outer_columns(grad_ffn_all, feedforward_weight[:, 2, :]) + outer_columns(
        grad_low_all, ffn_own[:, :ADAPTER_RANK]
    )
    grad_gate_own, grad_up_own = jax.vjp(geglu, gate_own, up_own)[1](hidden_unit_gradient)
    grad_gate_own = grad_gate_own.astype(jnp.bfloat16)
    grad_up_own = grad_up_own.astype(jnp.bfloat16)
    input_terms = matrix_product(grad_gate_own, feedforward_weight[:, 0, :]) + matrix_product(
        grad_up_own, feedforward_weight[:, 1, :]
    )
    proj_terms = jnp.concatenate(
        [
            matrix_product(grad_gate_own, ffn_own[:, ADAPTER_RANK : 2 * ADAPTER_RANK]),
            matrix_product(grad_up_own, ffn_own[:, 2 * ADAPTER_RANK :]),
        ],
        axis=1,
    )
    grad_norm_base, grad_proj = (
        lax.psum_scatter(input_terms, "dp", scatter_dimension=0, tiled=True),
        lax.psum_scatter(proj_terms, "dp", scatter_dimension=0, tiled=True),
    )
    ffn_grad = jnp.concatenate(
        [
            inner_rows(grad_gate_own, normed_all),
            inner_rows(grad_up_own, normed_all),
            inner_rows(units_own, grad_ffn_all),
            inner_rows(units_own, grad_low_all),
            inner_rows(grad_gate_own, proj_all[:, :ADAPTER_RANK]),
            inner_rows(grad_up_own, proj_all[:, ADAPTER_RANK:]),
        ],
        axis=1,
    )
    lowrank_projection_gradient = grad_proj.astype(jnp.bfloat16)
    second_normed_gradient = grad_norm_base + outer_columns(
        lowrank_projection_gradient, adapter_first[:, 4 * ADAPTER_RANK :]
    )
    grad_middle_part, grad_gain_two = jax.vjp(norm_rows, middle_state, layer_norm_gains[1])[1](
        second_normed_gradient
    )
    grad_middle = grad_out + grad_middle_part
    branch_gradient = (active_mask * grad_middle).astype(jnp.bfloat16)
    output_projection_gradient = outer_columns(
        branch_gradient, adapter_second[:, PROJECTED_WIDTH : PROJECTED_WIDTH + MODEL_WIDTH]
    ).astype(jnp.bfloat16)
    grad_attended = (
        outer_columns(branch_gradient, output_weight)
        + outer_columns(
            output_projection_gradient, adapter_first[:, 3 * ADAPTER_RANK : 4 * ADAPTER_RANK]
        )
    ).astype(jnp.bfloat16)
    grad_att_rows = grad_attended.reshape(local_rows * HEADS, HEAD_SIZE)
    prob = jnp.exp(score_rows() - top_score) / mass
    grad_prob = outer_columns(grad_att_rows, values).reshape(local_rows, HEADS, key_total)
    centre = jnp.sum(prob * grad_prob, axis=-1, keepdims=True)
    grad_scores = (
        (prob * (grad_prob - centre)).astype(jnp.bfloat16).reshape(local_rows * HEADS, key_total)
    )
    grad_queries = (matrix_product(grad_scores, keys) * scale).reshape(local_rows, HEADS, HEAD_SIZE)
    prob_again = prob.astype(jnp.bfloat16).reshape(local_rows * HEADS, key_total)
    kv_terms = jnp.concatenate(
        [inner_rows(grad_scores, query_rows) * scale, inner_rows(prob_again, grad_att_rows)], axis=1
    )
    grad_kv = lax.psum_scatter(kv_terms, "dp", scatter_dimension=0, tiled=True)
    query_linear_gradient = (
        rotate_back(grad_queries, pos_own).reshape(local_rows, QUERY_WIDTH).astype(jnp.bfloat16)
    )
    key_linear_gradient = rotate_back(grad_kv[:, None, :HEAD_SIZE], pos_own)[:, 0].astype(
        jnp.bfloat16
    )
    value_linear_gradient = grad_kv[:, HEAD_SIZE:].astype(jnp.bfloat16)
    query_key_value_gradient = jnp.concatenate(
        [query_linear_gradient, key_linear_gradient, value_linear_gradient], axis=1
    )
    attention_projection_gradient = jnp.concatenate(
        [
            outer_columns(query_linear_gradient, adapter_second[:, :QUERY_WIDTH]),
            outer_columns(
                key_linear_gradient, adapter_second[:, QUERY_WIDTH : QUERY_WIDTH + HEAD_SIZE]
            ),
            outer_columns(
                value_linear_gradient, adapter_second[:, QUERY_WIDTH + HEAD_SIZE : PROJECTED_WIDTH]
            ),
        ],
        axis=1,
    ).astype(jnp.bfloat16)
    normed_gradient = outer_columns(query_key_value_gradient, input_weight) + outer_columns(
        attention_projection_gradient, adapter_first[:, : 3 * ADAPTER_RANK]
    )
    grad_resid_part, grad_gain_one = jax.vjp(norm_rows, residual_stream, layer_norm_gains[0])[1](
        normed_gradient
    )
    hidden_grad = grad_middle + grad_resid_part
    grad_w_in = inner_rows(normed_input, query_key_value_gradient)
    grad_w_out = inner_rows(attended_rows, branch_gradient)
    grad_gains = jnp.stack([grad_gain_one, grad_gain_two])
    adapter_first_gradient = jnp.concatenate(
        [
            inner_rows(normed_input, attention_projection_gradient),
            inner_rows(attended_rows, output_projection_gradient),
            inner_rows(second_normed_input, lowrank_projection_gradient),
        ],
        axis=1,
    )
    adapter_second_gradient = jnp.concatenate(
        [
            inner_rows(lowrank_projection[:, :ADAPTER_RANK], query_linear_gradient),
            inner_rows(lowrank_projection[:, ADAPTER_RANK : 2 * ADAPTER_RANK], key_linear_gradient),
            inner_rows(lowrank_projection[:, 2 * ADAPTER_RANK :], value_linear_gradient),
            inner_rows(output_projection, branch_gradient),
            inner_rows(down_lowrank, feedforward_gradient),
        ],
        axis=1,
    )
    input_portion, output_portion, gain_portion, adapter_first_grads, adapter_second_grads = (
        lax.psum_scatter(grad_w_in, "dp", scatter_dimension=0, tiled=True),
        lax.psum_scatter(grad_w_out, "dp", scatter_dimension=0, tiled=True),
        lax.psum_scatter(grad_gains, "dp", scatter_dimension=1, tiled=True),
        lax.psum_scatter(adapter_first_gradient, "dp", scatter_dimension=0, tiled=True),
        lax.psum_scatter(adapter_second_gradient, "dp", scatter_dimension=1, tiled=True),
    )
    mlp_part = ffn_grad[:, : 3 * MODEL_WIDTH].reshape(ffn_rows, 3, MODEL_WIDTH)
    sum_in, sum_out, sum_gains, sum_mlp = (
        lax.psum(input_portion.astype(jnp.bfloat16), "loop").astype(jnp.float32),
        lax.psum(output_portion.astype(jnp.bfloat16), "loop").astype(jnp.float32),
        lax.psum(gain_portion.astype(jnp.bfloat16), "loop").astype(jnp.float32),
        lax.psum(mlp_part.astype(jnp.bfloat16), "loop").astype(jnp.float32),
    )
    return (
        complete_output.astype(jnp.bfloat16)[None],
        hidden_grad[None],
        sum_in,
        sum_out,
        sum_mlp,
        sum_gains,
        adapter_first_grads[None],
        adapter_second_grads[None],
        ffn_grad[:, 3 * MODEL_WIDTH :][None],
        exit_counts,
        mean_confidence,
    )


def solution(mesh):
    return jax.shard_map(
        per_device if mesh.shape == {"loop": 2, "dp": LINE_DEVICES} else per_device_any,
        mesh=mesh,
        in_specs=(
            P("loop", "dp", None),
            P("loop", "dp", None),
            P("dp", None),
            P("dp", None),
            P("dp", None, None),
            P(),
            P("loop", None, None),
            P("loop", None, None),
            P("loop", None, None),
            P("loop", None),
            P("loop", None),
            P("loop", "dp"),
        ),
        out_specs=(
            P("loop", "dp", None),
            P("loop", "dp", None),
            P("dp", None),
            P("dp", None),
            P("dp", None, None),
            P(None, "dp"),
            P("loop", "dp", None),
            P("loop", None, "dp"),
            P("loop", "dp", None),
            P(),
            P(),
        ),
        check_vma=False,
    )
```

```python
import functools

import jax
import jax.numpy as jnp
from jax import lax
from jax.experimental import pallas as pl
from jax.experimental.pallas import tpu as pltpu
from jax.sharding import PartitionSpec as P

MODEL_WIDTH = 2048
HEADS = 8
HEAD_SIZE = 256
ADAPTER_RANK = 256
QUERY_WIDTH = 2048
PROJECTED_WIDTH = 2560


EPSILON = 1e-06
FLOOR_SCORE = -1e30
MESH = pl.DeviceIdType.MESH
VMEM_LIMIT = 60 * 1024 * 1024
LINE_DEVICES = 16
FAR_TILES = 3
OUT_SPLIT = 1536
IN_SHARE = 48
OUT_SHARE = 32
AB_PARTS = 2
CLOSING_PARTS = (2, 2, 1, 1, 1)


def matrix_product(left, right):
    return jnp.dot(left, right, preferred_element_type=jnp.float32)


def inner_rows(left, right):
    return lax.dot_general(
        left, right, (((0,), (0,)), ((), ())), preferred_element_type=jnp.float32
    )


def outer_columns(left, right):
    return lax.dot_general(
        left, right, (((1,), (1,)), ((), ())), preferred_element_type=jnp.float32
    )


def norm_rows(values, gain):
    return values * lax.rsqrt(jnp.mean(values * values, axis=-1, keepdims=True) + EPSILON) * gain


def rotate(values, positions):
    half_dim = values.shape[-1] // 2
    freqs = 10000.0 ** (-jnp.arange(half_dim, dtype=jnp.float32) / half_dim)
    angles = positions.astype(jnp.float32)[:, None, None] * freqs
    cosine = jnp.cos(angles)
    sine = jnp.sin(angles)
    first_half = values[..., :half_dim]
    second_half = values[..., half_dim:]
    return jnp.concatenate(
        [first_half * cosine - second_half * sine, first_half * sine + second_half * cosine],
        axis=-1,
    )


def rotate_back(grads, positions):

    def turned(values):
        return rotate(values, positions)

    return jax.vjp(turned, jnp.zeros_like(grads))[1](grads)[0]


def geglu(gate_values, up_projection_value):
    return jax.nn.gelu(gate_values, approximate=True) * up_projection_value


def root_mean(values):
    return jnp.sqrt(jnp.mean(values * values, axis=-1) + EPSILON)


def token_facts(row_of_tokens, sequence_length):
    row_total = row_of_tokens.shape[0]
    live_row = row_of_tokens >= 0
    seq_ends = jnp.cumsum(sequence_length)
    seq_index = jnp.sum((row_of_tokens[:, None] >= seq_ends[None, :]).astype(jnp.int32), axis=1)
    seq_starts = seq_ends - sequence_length
    own_start = jnp.sum(
        jnp.where(
            seq_index[:, None] == jnp.arange(sequence_length.shape[0], dtype=jnp.int32)[None, :],
            seq_starts[None, :],
            0,
        ),
        axis=1,
    )
    row_ids = jnp.arange(row_total, dtype=jnp.int32)
    sequence = jnp.where(live_row, seq_index, -1 - row_ids)
    ordering = jnp.where(live_row, row_of_tokens, 0)
    positions = jnp.where(live_row, row_of_tokens - own_start, 0)
    return (live_row, sequence, ordering, positions)


def place(count):
    me = lax.axis_index("dp")
    return me, count // 4, me // 4, (me // 2) % 2, me % 2


def greet(count, across=False):
    me, depth, z, y, c = place(count)
    barrier = pltpu.get_barrier_semaphore()

    def signal(where):
        pl.semaphore_signal(barrier, inc=1, device_id={"dp": where}, device_id_type=MESH)

    signal(me + 1 - 2 * c)
    signal(me + 2 - 4 * y)
    if across:
        other = 1 - lax.axis_index("loop")
        pl.semaphore_signal(barrier, inc=1, device_id={"loop": other}, device_id_type=MESH)

    @pl.when(z > 0)
    def _():
        signal(me - 4)

    @pl.when(z < depth - 1)
    def _():
        signal(me + 4)

    ends = jnp.where((z > 0) & (z < depth - 1), 4, 3)
    pl.semaphore_wait(barrier, ends + 1 if across else ends)


def contract(left, right, left_axis, right_axis):
    return lax.dot_general(
        left,
        right,
        (((left_axis,), (right_axis,)), ((), ())),
        preferred_element_type=jnp.float32,
    )


def gather_plan(count, spans, own, full, sems, far_sems=None, twins=False):
    keep, recv, send_core, send_pair, send_right, send_left, send_twin = sems
    arrays = len(own)
    me, depth, z, y, c = place(count)
    mate = me + 2 - 4 * y
    core = me + 1 - 2 * c

    def copy(unit, block, target, sem, first=False):
        a, s = unit
        rows = pl.ds(*spans[a][s])
        return pltpu.make_async_remote_copy(
            src_ref=own[a].at[rows] if first else full[a].at[block, rows],
            dst_ref=full[a].at[block, rows],
            send_sem=sem,
            recv_sem=recv.at[a, block, s],
            device_id={"dp": target},
            device_id_type=MESH,
        )

    def to_core(unit, block, first=False):
        a, s = unit
        return copy(unit, block, core, send_core.at[a, block // 2, s], first)

    def to_pair(unit, block, first=False):
        a, s = unit
        return copy(unit, block, mate, send_pair.at[a, block // 4, s], first)

    def to_right(unit, block, first=False):
        a, s = unit
        return copy(unit, block, me + 4, send_right.at[a, block // 4, s], first)

    def to_left(unit, block, first=False):
        a, s = unit
        return copy(unit, block, me - 4, send_left.at[a, block // 4, s], first)

    def to_twin(unit, block):
        a, s = unit
        return copy(unit, block, me + 4 - 8 * (z % 2), send_twin.at[a])

    def shared(unit):
        return twins and unit[1] == 1

    def to_far(a, block):
        rows = pl.ds(*spans[a][0])
        return pltpu.make_async_remote_copy(
            src_ref=full[a].at[block, rows],
            dst_ref=full[a].at[block, rows],
            send_sem=far_sems[0].at[a, block // 2],
            recv_sem=far_sems[1].at[a, block],
            device_id={"loop": 1 - lax.axis_index("loop")},
            device_id_type=MESH,
        )

    def far_core(a, block, first=False):
        rows = pl.ds(*spans[a][2])
        return pltpu.make_async_remote_copy(
            src_ref=own[a].at[rows] if first else full[a].at[block, rows],
            dst_ref=full[a].at[block, rows],
            send_sem=far_sems[2].at[a, block // 2],
            recv_sem=far_sems[3].at[a, block],
            device_id={"dp": core},
            device_id_type=MESH,
        )

    def cross(unit, block):
        if far_sems is not None and unit[1] == 0:
            to_far(unit[0], block).start()

    local = [pltpu.make_async_copy(own[a], full[a].at[me], keep.at[a]) for a in range(arrays)]
    units = [(a, s) for a in range(arrays) for s in range(2 if far_sems else len(spans[a]))]

    def begin():
        for unit in units:

            @pl.when(z < depth - 1)
            def _(unit=unit):
                to_right(unit, me, True).start()

            @pl.when(z > 0)
            def _(unit=unit):
                to_left(unit, me, True).start()

            to_pair(unit, me, True).start()
            to_core(unit, me, True).start()
        if far_sems is not None:
            for a in range(arrays):
                far_core(a, me, True).start()
        for item in local:
            item.start()

    def from_line(k, unit):
        @pl.when(z - k >= 0)
        def _():
            block = me - 4 * k
            to_right(unit, block).wait_recv()

            @pl.when(z < depth - 1)
            def _():
                to_right(unit, block).start()

            if k == 1 and shared(unit):

                @pl.when(z % 2 == 0)
                def _():
                    to_pair(unit, block).start()

            else:
                to_pair(unit, block).start()
            to_core(unit, block).start()
            cross(unit, block)

        @pl.when(z + k < depth)
        def _():
            block = me + 4 * k
            to_left(unit, block).wait_recv()

            @pl.when(z > 0)
            def _():
                to_left(unit, block).start()

            if k == 1 and shared(unit):

                @pl.when(z % 2 == 1)
                def _():
                    to_pair(unit, block).start()

            else:
                to_pair(unit, block).start()
            to_core(unit, block).start()
            cross(unit, block)

    def pass_on(unit, block):
        to_pair(unit, block).wait_recv()
        to_core(unit, block).start()
        cross(unit, block)

    def from_pair(k, unit):
        if k == 0:
            pass_on(unit, mate)
            if shared(unit):
                to_twin(unit, mate).start()
            return

        @pl.when(z - k >= 0)
        def _():
            pass_on(unit, mate - 4 * k)

        @pl.when(z + k < depth)
        def _():
            pass_on(unit, mate + 4 * k)

    def far_on(a, block):
        to_far(a, block).wait_recv()
        far_core(a, block).start()

    def from_far(k, a):
        if k == 0:
            far_on(a, mate)
            return

        @pl.when(z - k >= 0)
        def _():
            far_on(a, me - 4 * k)
            far_on(a, mate - 4 * k)

        @pl.when(z + k < depth)
        def _():
            far_on(a, me + 4 * k)
            far_on(a, mate + 4 * k)

    def arrive(block=None, mine=True):
        for unit in units:
            for j in range(count // 2 if block is None else 1):
                to_core(unit, 2 * j + 1 - c if block is None else block).wait_recv()
        if far_sems is not None:
            for a in range(arrays):
                for j in range(count // 2):
                    far_core(a, 2 * j + 1 - c).wait_recv()
        if mine:
            for item in local:
                item.wait()

    def finish():
        for unit in units:
            for j in range(count // 2):
                to_core(unit, 2 * j + c).wait_send()
            for j in range(depth):
                block = 4 * j + 2 * y + c
                if shared(unit):

                    @pl.when(j != z + 1 - 2 * (z % 2))
                    def _():
                        to_pair(unit, block).wait_send()

                else:
                    to_pair(unit, block).wait_send()

                @pl.when((z >= j) & (z < depth - 1))
                def _():
                    to_right(unit, block).wait_send()

                @pl.when((z <= j) & (z > 0))
                def _():
                    to_left(unit, block).wait_send()

            if shared(unit):
                to_twin(unit, mate).wait_send()

        if far_sems is not None:
            for a in range(arrays):
                for j in range(count // 2):
                    far_core(a, 2 * j + c).wait_send()

                    @pl.when(2 * j + c != me)
                    def _():
                        to_far(a, 2 * j + c).wait_send()

    return units, begin, from_line, from_pair, from_far, arrive, finish


def gather_sems(count, number, parts):
    depth = count // 4
    sem = pltpu.SemaphoreType.DMA
    return [
        sem((number,)),
        sem((number, count, parts)),
        sem((number, count // 2, parts)),
        sem((number, depth, parts)),
        sem((number, depth, parts)),
        sem((number, depth, parts)),
        sem((number,)),
    ]


def even_spans(rows, parts):
    return [(s * (rows // parts), rows // parts) for s in range(parts)]


def kernel_params(ident):
    return pltpu.CompilerParams(
        collective_id=ident, has_side_effects=True, vmem_limit_bytes=VMEM_LIMIT
    )


def opening_body(count, shares, arrays, stream, gain, tokens, depths, lengths, grads, *refs):
    own = refs[:arrays]
    weights, factors, first, second = refs[arrays : arrays + 4]
    full = refs[arrays + 4 : 2 * arrays + 4]
    folded, normed, lowrank = refs[2 * arrays + 4 : 2 * arrays + 7]
    all_seq, all_order, own_seq, own_order, own_place, active, live, masked = refs[
        2 * arrays + 7 : 2 * arrays + 15
    ]
    scratch = refs[2 * arrays + 15 :]
    (bank, factor_bank, first_bank, in_bank, second_bank, bank_sem, factor_sem, out_sem) = scratch[
        :8
    ]
    me, depth, z, y, c = place(count)
    rank = ADAPTER_RANK
    width, wide = bank.shape[1:]
    loop = lax.axis_index("loop")
    greet(count, True)
    spans = []
    for a in range(arrays):
        rows, share = own[a].shape[0], shares[a]
        spans.append(
            [
                (pl.multiple_of(loop * (rows - share), 16), share),
                (share, rows - 2 * share),
                (pl.multiple_of((1 - loop) * (rows - share), 16), share),
            ]
        )
    units, begin, from_line, from_pair, from_far, arrive, finish = gather_plan(
        count, spans, own, full, scratch[8:15], scratch[15:19]
    )
    begin()
    fills = [
        pltpu.make_async_copy(weights.at[i], bank.at[i], bank_sem.at[i]) for i in range(3)
    ]
    sources = [
        pltpu.make_async_copy(first.at[:, pl.ds(0, 3 * rank)], in_bank, factor_sem.at[0]),
        pltpu.make_async_copy(
            factors.at[pl.ds(me * width, width)], factor_bank, factor_sem.at[1]
        ),
        pltpu.make_async_copy(
            first.at[:, pl.ds(4 * rank, 2 * rank)], first_bank, factor_sem.at[2]
        ),
        pltpu.make_async_copy(
            second.at[:, pl.ds(PROJECTED_WIDTH + MODEL_WIDTH, wide)], second_bank, factor_sem.at[3]
        ),
    ]
    for item in sources + fills:
        item.start()

    def put(i):
        return pltpu.make_async_copy(bank.at[i], folded.at[i], out_sem.at[i])

    def fold(i):
        high, tile = 256, 512

        def inner(n, carry):
            rows = pl.ds(pl.multiple_of((n // (wide // tile)) * high, high), high)
            cols = pl.ds(pl.multiple_of((n % (wide // tile)) * tile, tile), tile)
            if i == 2:
                extra = contract(factor_bank[rows, :rank], second_bank[:, cols], 1, 0)
            else:
                extra = contract(
                    factor_bank[rows, (i + 1) * rank : (i + 2) * rank],
                    first_bank[cols, i * rank : (i + 1) * rank],
                    1,
                    1,
                )
            bank[i, rows, cols] = (bank[i, rows, cols].astype(jnp.float32) + extra).astype(
                bank.dtype
            )
            return carry

        lax.fori_loop(0, (width // high) * (wide // tile), inner, 0)
        put(i).start()

    starts, total = [], 0
    for i in range(lengths.shape[1]):
        starts.append(total)
        total = total + lengths[0, i]
    ends = starts[1:] + [total]

    def facts(token, row):
        alive = token >= 0
        sequence = sum((token >= end).astype(jnp.int32) for end in ends)
        start = sum(jnp.where(sequence == i, item, 0) for i, item in enumerate(starts))
        return (
            alive,
            jnp.where(alive, sequence, -1 - row),
            jnp.where(alive, token, 0),
            jnp.where(alive, token - start, 0),
        )

    every = tokens[...]
    _, all_seq[...], all_order[...], _ = facts(
        every, lax.broadcasted_iota(jnp.int32, every.shape, 1)
    )
    height = stream.shape[0]
    square = (height, height)
    on = lax.broadcasted_iota(jnp.int32, square, 0) == lax.broadcasted_iota(jnp.int32, square, 1)

    def upright(row):
        return jnp.sum(jnp.where(on, row, 0), axis=1, keepdims=True)

    token = upright(tokens[:, pl.ds(pl.multiple_of(me * height, height), height)])
    alive, own_seq[...], own_order[...], own_place[...] = facts(
        token, me * height + lax.broadcasted_iota(jnp.int32, token.shape, 0)
    )
    depth_own = upright(depths[...])
    live[...] = jnp.where(alive, 1.0, 0.0)
    moving = jnp.where(alive & (depth_own > loop), 1.0, 0.0)
    active[...] = moving
    masked[...] = (moving * grads[...].astype(jnp.float32)).astype(masked.dtype)

    rows = stream[...].astype(jnp.float32)
    inverse = lax.rsqrt(jnp.mean(rows * rows, axis=-1, keepdims=True) + EPSILON)
    normed[...] = (rows * inverse * gain[...]).astype(normed.dtype)
    sources[0].wait()
    lowrank[...] = contract(normed[...], in_bank[...], 1, 0).astype(lowrank.dtype)
    for item in sources[1:]:
        item.wait()
    for k in range(1, depth):
        for a in range(arrays):
            for unit in units:
                if unit[0] == a:
                    from_line(k, unit)
                    from_pair(k - 1, unit)
            if k > 1 or a > 0:
                stage = (k - 1) * arrays + a - 1
                from_far(stage // arrays, stage % arrays)
        fills[k - 1].wait()
        fold(k - 1)
    for unit in units:
        from_pair(depth - 1, unit)
    for stage in range((depth - 1) * arrays - 1, depth * arrays):
        from_far(stage // arrays, stage % arrays)
    arrive()
    finish()
    for i in range(3):
        put(i).wait()


def opening(count, ident, stream, gain, tokens, depths, lengths, grads, arrays, shares, weights,
            factors, first, second):
    number = len(arrays)
    _, width, wide = weights.shape
    low = jnp.bfloat16
    rank = ADAPTER_RANK
    sem = pltpu.SemaphoreType.DMA
    anywhere = pl.BlockSpec(memory_space=pl.ANY)
    inside = pl.BlockSpec(memory_space=pltpu.VMEM)
    out = pl.pallas_call(
        functools.partial(opening_body, count, shares, number),
        out_shape=[
            jax.ShapeDtypeStruct((count,) + item.shape, item.dtype) for item in arrays
        ]
        + [
            jax.ShapeDtypeStruct(weights.shape, low),
            jax.ShapeDtypeStruct(stream.shape, low),
            jax.ShapeDtypeStruct((stream.shape[0], 3 * rank), low),
            jax.ShapeDtypeStruct(tokens.shape, jnp.int32),
            jax.ShapeDtypeStruct(tokens.shape, jnp.int32),
        ]
        + [jax.ShapeDtypeStruct((stream.shape[0], 1), jnp.int32)] * 3
        + [jax.ShapeDtypeStruct((stream.shape[0], 1), jnp.float32)] * 2
        + [jax.ShapeDtypeStruct(grads.shape, low)],
        in_specs=[inside] * 4
        + [pl.BlockSpec(memory_space=pltpu.SMEM), inside]
        + [anywhere] * (number + 4),
        out_specs=[anywhere] * (number + 1) + [inside] * 10,
        scratch_shapes=[
            pltpu.VMEM(weights.shape, low),
            pltpu.VMEM((width, factors.shape[1]), low),
            pltpu.VMEM((wide, 2 * rank), low),
            pltpu.VMEM((wide, 3 * rank), low),
            pltpu.VMEM((rank, wide), low),
            sem((3,)),
            sem((4,)),
            sem((3,)),
        ]
        + gather_sems(count, number, 2)
        + [
            sem((number, count // 2)),
            sem((number, count)),
            sem((number, count // 2)),
            sem((number, count)),
        ],
        compiler_params=kernel_params(ident),
        name="opening",
    )(stream, gain, tokens, depths, lengths, grads, *arrays, weights, factors, first, second)
    return [
        item.reshape((count * item.shape[1],) + item.shape[2:]) for item in out[:number]
    ] + list(out[number:])


def turn(values, cosine, sine):
    half = values.shape[-1] // 2
    first, second = values[:, :half], values[:, half:]
    return jnp.concatenate(
        [first * cosine - second * sine, first * sine + second * cosine], axis=1
    )


def attention_body(count, normed, lowrank, stream, active, gain, cosine, sine, own_seq, own_order,
                   all_seq, all_order, in_weight, out_weight, first, second, grads,
                   queries, attended, lowrank_out, level, middle, normed_next, keys_values, grads_all,
                   in_bank, out_bank, in_second, out_second, out_first, allowed, kv_own, kv_full,
                   load_sem, put_sem, *sems):
    me, depth, z, y, c = place(count)
    height, wide = normed.shape
    size = HEAD_SIZE
    scale = size ** (-0.5)
    rank = ADAPTER_RANK
    low = jnp.bfloat16
    greet(count)
    kv_units, kv_begin, kv_line, kv_pair, _, kv_arrive, kv_finish = gather_plan(
        count, [even_spans(height, 1)], (kv_own,), (kv_full,), sems[:7]
    )
    units, begin, from_line, from_pair, _, arrive, finish = gather_plan(
        count, [even_spans(height, 2)], (grads,), (grads_all,), sems[7:], twins=True
    )
    loads = [
        pltpu.make_async_copy(source, bank, load_sem.at[i])
        for i, (source, bank) in enumerate(
            (
                (in_weight, in_bank),
                (second.at[:, pl.ds(0, PROJECTED_WIDTH)], in_second),
                (out_weight, out_bank),
                (second.at[:, pl.ds(PROJECTED_WIDTH, MODEL_WIDTH)], out_second),
                (first.at[:, pl.ds(3 * rank, rank)], out_first),
            )
        )
    ]
    begin()
    for item in loads:
        item.start()
    loads[0].wait()
    loads[1].wait()

    def head(at, part):
        value = contract(normed[...], in_bank[:, at : at + size], 1, 0)
        return value + contract(
            lowrank[:, part * rank : (part + 1) * rank], in_second[:, at : at + size], 1, 0
        )

    kv_own[:, :size] = turn(head(QUERY_WIDTH, 1), cosine[...], sine[...]).astype(low)
    kv_own[:, size:] = head(QUERY_WIDTH + size, 2).astype(low)
    kv_begin()
    heads = wide // size

    def some_heads(start, stop):
        for i in range(start, stop):
            value = turn(head(i * size, 0), cosine[...], sine[...])
            queries[:, i * size : (i + 1) * size] = value.astype(low)

    some_heads(0, 4)
    (kv_unit,) = kv_units
    kv_line(1, kv_unit)
    kv_pair(0, kv_unit)
    from_line(1, units[0])
    from_pair(0, units[0])
    some_heads(4, heads)
    same = own_seq[...] == all_seq[...]
    allowed[...] = jnp.where(same & (all_order[...] <= own_order[...]), 1.0, 0.0)
    kv_line(2, kv_unit)
    kv_pair(1, kv_unit)
    from_line(1, units[1])
    from_pair(0, units[1])
    kv_line(3, kv_unit)
    kv_pair(2, kv_unit)
    kv_pair(3, kv_unit)
    kv_arrive()
    put_kv = pltpu.make_async_copy(kv_full, keys_values, put_sem)
    put_kv.start()
    total = count * height
    keys = kv_full[:, :, :size].reshape(total, size)
    values = kv_full[:, :, size:].reshape(total, size)

    def attend(pair):
        query = jnp.concatenate(
            [
                queries[:, 2 * pair * size : (2 * pair + 1) * size],
                queries[:, (2 * pair + 1) * size : (2 * pair + 2) * size],
            ],
            axis=0,
        )
        keep = jnp.concatenate([allowed[...], allowed[...]], axis=0) > 0.5
        scores = jnp.where(keep, contract(query, keys, 1, 1) * scale, FLOOR_SCORE)
        top = jnp.max(scores, axis=-1, keepdims=True)
        expo = jnp.exp(scores - top)
        mass = jnp.sum(expo, axis=-1, keepdims=True)
        level[pair] = jnp.broadcast_to(top + jnp.log(mass), level.shape[1:])
        value = contract((expo / mass).astype(low), values, 1, 0).astype(low)
        for i in range(2):
            attended[:, (2 * pair + i) * size : (2 * pair + i + 1) * size] = value[
                i * height : (i + 1) * height
            ]

    for pair in range(heads // 2):
        attend(pair)
        if pair == 0:
            for unit in units:
                from_line(2, unit)
        if pair == 1:
            for unit in units:
                from_pair(1, unit)
        if pair == 2:
            for unit in units:
                from_line(3, unit)
        if pair == 3:
            for unit in units:
                from_pair(2, unit)
    for item in loads[2:]:
        item.wait()
    lowrank_out[...] = contract(attended[...], out_first[...], 1, 0).astype(low)
    tile = 256

    def product(n, carry):
        cols = pl.ds(pl.multiple_of(n * tile, tile), tile)
        value = contract(attended[...], out_bank[:, cols], 1, 0)
        value += contract(lowrank_out[...], out_second[:, cols], 1, 0)
        middle[:, cols] = stream[:, cols].astype(jnp.float32) + active[...] * value
        return carry

    lax.fori_loop(0, wide // tile, product, 0)
    rows = middle[...]
    inverse = lax.rsqrt(jnp.mean(rows * rows, axis=-1, keepdims=True) + EPSILON)
    normed_next[...] = (rows * inverse * gain[...]).astype(low)
    for unit in units:
        from_pair(3, unit)
    arrive()
    finish()
    kv_finish()
    put_kv.wait()


def attention(count, ident, normed, lowrank, stream, active, gain, cosine, sine, own_seq,
              own_order, all_seq, all_order, in_weight, out_weight, first, second, grads):
    height, wide = normed.shape
    low, high = jnp.bfloat16, jnp.float32
    inside = pl.BlockSpec(memory_space=pltpu.VMEM)
    anywhere = pl.BlockSpec(memory_space=pl.ANY)
    rank = ADAPTER_RANK
    both = 2 * HEAD_SIZE
    total = count * height
    sem = pltpu.SemaphoreType.DMA
    shape = jax.ShapeDtypeStruct
    return pl.pallas_call(
        functools.partial(attention_body, count),
        out_shape=[
            shape((height, wide), low),
            shape((height, wide), low),
            shape((height, rank), low),
            shape((wide // both, 2 * height, 128), high),
            shape((height, wide), high),
            shape((height, wide), low),
            shape((count, height, both), low),
            shape((count, height, wide), low),
        ],
        in_specs=[inside] * 11 + [anywhere] * 5,
        out_specs=[inside] * 6 + [anywhere] * 2,
        scratch_shapes=[
            pltpu.VMEM(in_weight.shape, low),
            pltpu.VMEM(out_weight.shape, low),
            pltpu.VMEM((rank, PROJECTED_WIDTH), low),
            pltpu.VMEM((rank, wide), low),
            pltpu.VMEM((wide, rank), low),
            pltpu.VMEM((height, total), high),
            pltpu.VMEM((height, both), low),
            pltpu.VMEM((count, height, both), low),
            sem((5,)),
            sem,
        ]
        + gather_sems(count, 1, 1)
        + gather_sems(count, 1, 2),
        compiler_params=kernel_params(ident),
        name="attention",
    )(
        normed, lowrank, stream, active, gain, cosine, sine, own_seq, own_order, all_seq,
        all_order, in_weight, out_weight, first, second, grads,
    )


def sum_plan(count, parts, mine, theirs, core_in, pair_in, line_in, twin_in, sems,
             twins=True):
    me, depth, z, y, c = place(count)
    core_send, core_recv, pair_send, pair_recv, line_send, line_recv, twin_sem = sems
    rows = core_in.shape[1]
    step = rows // parts
    near = z < 2
    order = [
        jnp.where(near, 3, 0),
        jnp.where(near, 0, 3),
        jnp.where(near, 2, 1),
        jnp.where(near, 1, 2),
    ]

    def rows_of(s):
        return pl.ds(s * step, step)

    def to_core(line, pair, s):
        at = 2 * line + pair
        return pltpu.make_async_remote_copy(
            src_ref=theirs(at, rows_of(s)),
            dst_ref=core_in.at[at, rows_of(s)],
            send_sem=core_send.at[at, s],
            recv_sem=core_recv.at[at, s],
            device_id={"dp": me + 1 - 2 * c},
            device_id_type=MESH,
        )

    def to_pair(line, s):
        return pltpu.make_async_remote_copy(
            src_ref=mine(2 * line + 1 - y, rows_of(s)),
            dst_ref=pair_in.at[line, rows_of(s)],
            send_sem=pair_send.at[line, s],
            recv_sem=pair_recv.at[line, s],
            device_id={"dp": me + 2 - 4 * y},
            device_id_type=MESH,
        )

    def along(line, slot, s, target):
        return pltpu.make_async_remote_copy(
            src_ref=mine(2 * line + y, rows_of(s)),
            dst_ref=line_in.at[slot, rows_of(s)],
            send_sem=line_send.at[line, s],
            recv_sem=line_recv.at[slot, s],
            device_id={"dp": target},
            device_id_type=MESH,
        )

    twin = z + 1 - 2 * (z % 2)

    def shared(s):
        return twins and parts > 1 and s == parts - 1

    def to_twin():
        return pltpu.make_async_remote_copy(
            src_ref=mine(2 * twin + 1 - y, rows_of(parts - 1)),
            dst_ref=twin_in,
            send_sem=twin_sem.at[0],
            recv_sem=twin_sem.at[1],
            device_id={"dp": me + 4 - 8 * (z % 2)},
            device_id_type=MESH,
        )

    if shared(parts - 1):
        pair_in[twin, rows_of(parts - 1)] = jnp.zeros((step, core_in.shape[2]), pair_in.dtype)

    def send_core(line, pair):
        for s in range(parts):
            to_core(line, pair, s).start()

    def core_left(line, pair):
        for s in range(parts):
            to_core(line, pair, s).wait_send()

    def pair_step(k):
        line = order[k]
        at = 2 * line + 1 - y
        for s in range(parts):
            to_core(line, 1 - y, s).wait_recv()
            block = mine(at, rows_of(s))
            block[...] = block[...] + core_in[at, rows_of(s)]
            if not shared(s):
                to_pair(line, s).start()
                continue

            @pl.when(line == twin)
            def _():
                to_twin().start()

            @pl.when((line != twin) & (line != z))
            def _():
                to_pair(line, s).start()

    def twin_step():
        block = mine(2 * z + 1 - y, rows_of(parts - 1))
        to_twin().wait_recv()
        block[...] = block[...] + twin_in[...]
        to_pair(z, parts - 1).start()

    def own_sum(line, s):
        at = 2 * line + y
        to_core(line, y, s).wait_recv()
        if shared(s):

            @pl.when(line != twin)
            def _():
                to_pair(line, s).wait_recv()

        else:
            to_pair(line, s).wait_recv()
        part = mine(at, rows_of(s))[...].astype(jnp.float32)
        part += core_in[at, rows_of(s)].astype(jnp.float32)
        return part + pair_in[line, rows_of(s)].astype(jnp.float32)

    def line_step(k):
        line = order[k]

        @pl.when(line != z)
        def _():
            for s in range(parts):
                block = mine(2 * line + y, rows_of(s))
                follows = ((line > z) & (z > 0)) | ((line < z) & (z < depth - 1))
                part = own_sum(line, s)

                @pl.when(follows)
                def _():
                    along(z, line, s, me + 4).wait_recv()
                    extra = line_in[line, rows_of(s)].astype(jnp.float32)
                    block[...] = (part + extra).astype(block.dtype)

                @pl.when(jnp.logical_not(follows))
                def _():
                    block[...] = part.astype(block.dtype)

                @pl.when(line > z)
                def _():
                    along(line, line, s, me + 4).start()

                @pl.when(line < z)
                def _():
                    along(line, jnp.where(line == z - 1, depth, line), s, me - 4).start()

    def last_step(total):
        for s in range(parts):
            total[rows_of(s)] = own_sum(z, s)

            @pl.when(z > 0)
            def _():
                along(z, z, s, me + 4).wait_recv()
                total[rows_of(s)] += line_in[z, rows_of(s)].astype(jnp.float32)

            @pl.when(z < depth - 1)
            def _():
                along(z, depth, s, me + 4).wait_recv()
                total[rows_of(s)] += line_in[depth, rows_of(s)].astype(jnp.float32)

    def finish(cores=True):
        if shared(parts - 1):
            to_twin().wait_send()
        for line in range(depth):
            for s in range(parts):
                for pair in range(2 if cores else 0):
                    to_core(line, pair, s).wait_send()
                if shared(s):

                    @pl.when(line != twin)
                    def _():
                        to_pair(line, s).wait_send()

                else:
                    to_pair(line, s).wait_send()

                @pl.when(z != line)
                def _():
                    along(line, line, s, me + 4).wait_send()

    return order, send_core, pair_step, line_step, last_step, finish, core_left, twin_step


def sum_sems(count, parts):
    depth = count // 4
    sem = pltpu.SemaphoreType.DMA
    return [
        sem((2 * depth, parts)),
        sem((2 * depth, parts)),
        sem((depth, parts)),
        sem((depth, parts)),
        sem((depth, parts)),
        sem((depth + 1, parts)),
        sem((2,)),
    ]


def sum_rooms(count, rows, cols, kind=jnp.bfloat16, parts=2):
    depth = count // 4
    return [
        pltpu.VMEM((2 * depth, rows, cols), kind),
        pltpu.VMEM((depth, rows, cols), kind),
        pltpu.VMEM((depth + 1, rows, cols), kind),
        pltpu.VMEM((rows // parts, cols) if parts > 1 else (16, 128), kind),
    ]


def sum_terms(count, parts, terms, rooms, sems):
    me, depth, z, y, c = place(count)

    def mine(at, rows):
        return terms.at[2 * at + c, rows]

    def theirs(at, rows):
        return terms.at[2 * at + 1 - c, rows]

    return sum_plan(count, parts, mine, theirs, *rooms, sems)


def turn_back(values, cosine, sine):
    half = values.shape[-1] // 2
    first, second = values[:, :half], values[:, half:]
    return jnp.concatenate(
        [first * cosine + second * sine, second * cosine - first * sine], axis=1
    )


def attention_grads_body(count, attended, grad_rows, weight, queries, keys_values, level,
                         cosine, sine, own_seq, own_order, all_seq, all_order, first, second,
                         joint_grads, lowrank_grads, out_sum,
                         weight_in, out_first, both_second, grad_att, allowed, kv_total, kv_terms, kv_sum, out_terms,
                         out_core, out_pair, out_line, out_twin, kv_core, kv_pair, kv_line, kv_twin,
                         weight_sem, *sems):
    me, depth, z, y, c = place(count)
    height, wide = grad_rows.shape
    size = HEAD_SIZE
    scale = size ** (-0.5)
    low = jnp.bfloat16
    greet(count)
    rank = ADAPTER_RANK
    loads = [
        pltpu.make_async_copy(source, bank, weight_sem.at[i])
        for i, (source, bank) in enumerate(
            (
                (weight, weight_in),
                (first.at[:, pl.ds(3 * rank, rank)], out_first),
                (second.at[:, pl.ds(0, PROJECTED_WIDTH + wide)], both_second),
            )
        )
    ]
    for item in loads:
        item.start()
    order, send_out, pair_out, line_out, last_out, finish_out, _, twin_out = sum_terms(
        count, AB_PARTS, out_terms, (out_core, out_pair, out_line, out_twin), sems[:7]
    )
    _, send_kv, pair_kv, line_kv, last_kv, finish_kv, _, _ = sum_terms(
        count, 1, kv_terms, (kv_core, kv_pair, kv_line, kv_twin), sems[7:]
    )
    feature, some = out_terms.shape[1:]

    def out_product(line):
        def inner(n, carry):
            into = pl.ds(pl.multiple_of(n * 512, 512), 512)
            cols = pl.ds(pl.multiple_of(line * 4 * feature, 4 * feature), 4 * feature)
            value = contract(attended[:, cols], grad_rows[:, into], 0, 0).astype(low)
            out_terms[pl.ds(4 * line, 4), :, into] = value.reshape(4, feature, 512)
            return carry

        lax.fori_loop(0, some // 512, inner, 0)
        for pair in (1 - y, y):
            send_out(line, pair)

    for line in order:
        out_product(line)
    for item in loads:
        item.wait()
    tile = 256
    back_out = contract(grad_rows[...], both_second[:, PROJECTED_WIDTH:], 1, 1).astype(low)

    def product(n, carry):
        cols = pl.ds(pl.multiple_of(n * tile, tile), tile)
        value = contract(grad_rows[...], weight_in[cols], 1, 1)
        value += contract(back_out, out_first[cols], 1, 1)
        grad_att[:, cols] = value.astype(low)
        return carry

    lax.fori_loop(0, wide // tile, product, 0)
    same = own_seq[...] == all_seq[...]
    allowed[...] = jnp.where(same & (all_order[...] <= own_order[...]), 1.0, 0.0)
    for k in range(depth):
        pair_out(k)
    keys = keys_values[:, :size]
    values = keys_values[:, size:]

    def heads(pair):
        def both(ref):
            return jnp.concatenate(
                [
                    ref[:, 2 * pair * size : (2 * pair + 1) * size],
                    ref[:, (2 * pair + 1) * size : (2 * pair + 2) * size],
                ],
                axis=0,
            )

        query = both(queries)
        grad = both(grad_att)
        keep = jnp.concatenate([allowed[...], allowed[...]], axis=0) > 0.5
        scores = jnp.where(keep, contract(query, keys, 1, 1) * scale, FLOOR_SCORE)
        prob = jnp.exp(scores - level[pair][:, :1])
        grad_prob = contract(grad, values, 1, 1)
        centre = jnp.sum(prob * grad_prob, axis=-1, keepdims=True)
        grad_scores = (prob * (grad_prob - centre)).astype(low)
        back = contract(grad_scores, keys, 1, 0) * scale
        for i in range(2):
            part = turn_back(back[i * height : (i + 1) * height], cosine[...], sine[...])
            joint_grads[:, (2 * pair + i) * size : (2 * pair + i + 1) * size] = part.astype(low)
        key_part = contract(grad_scores, query, 0, 0) * scale
        value_part = contract(prob.astype(low), grad, 0, 0)
        if pair == 0:
            kv_total[:, :size] = key_part
            kv_total[:, size:] = value_part
        else:
            kv_total[:, :size] += key_part
            kv_total[:, size:] += value_part

    for pair in range(wide // size // 2):
        heads(pair)
        if pair == 0:
            twin_out()
    for block in range(count):
        kv_terms[block] = kv_total[block * height : (block + 1) * height].astype(low)
    for pair in (1 - y, y):
        for line in order:
            send_kv(line, pair)
    for k in range(depth):
        pair_kv(k)
    line_out(0)
    line_out(1)
    for k in range(depth):
        line_kv(k)
        if k + 2 < depth:
            line_out(k + 2)
    last_kv(kv_sum)
    part = turn_back(kv_sum[:, :size], cosine[...], sine[...])
    joint_grads[:, wide : wide + size] = part.astype(low)
    joint_grads[:, wide + size :] = kv_sum[:, size:].astype(low)
    for i, (at, stop) in enumerate(
        ((0, wide), (wide, wide + size), (wide + size, wide + 2 * size))
    ):
        value = contract(joint_grads[:, at:stop], both_second[:, at:stop], 1, 1)
        lowrank_grads[:, i * rank : (i + 1) * rank] = value.astype(low)
    last_out(out_sum)
    finish_out()
    finish_kv()


def attention_grads(count, ident, attended, grad_rows, weight, queries, keys_values, level,
                    cosine, sine, own_seq, own_order, all_seq, all_order, first, second):
    height, wide = grad_rows.shape
    total = keys_values.shape[0]
    low = jnp.bfloat16
    inside = pl.BlockSpec(memory_space=pltpu.VMEM)
    anywhere = pl.BlockSpec(memory_space=pl.ANY)
    feature = attended.shape[1] // count
    both = 2 * HEAD_SIZE
    return pl.pallas_call(
        functools.partial(attention_grads_body, count),
        out_shape=[
            jax.ShapeDtypeStruct((height, wide + both), low),
            jax.ShapeDtypeStruct((height, 3 * ADAPTER_RANK), low),
            jax.ShapeDtypeStruct((feature, OUT_SPLIT), jnp.float32),
        ],
        in_specs=[inside] * 2 + [anywhere] + [inside] * 9 + [anywhere] * 2,
        out_specs=[inside] * 3,
        scratch_shapes=[
            pltpu.VMEM(weight.shape, low),
            pltpu.VMEM((wide, ADAPTER_RANK), low),
            pltpu.VMEM((ADAPTER_RANK, PROJECTED_WIDTH + wide), low),
            pltpu.VMEM(attended.shape, low),
            pltpu.VMEM((height, total), jnp.float32),
            pltpu.VMEM((total, both), jnp.float32),
            pltpu.VMEM((count, height, both), low),
            pltpu.VMEM((height, both), jnp.float32),
            pltpu.VMEM((count, feature, OUT_SPLIT), low),
        ]
        + sum_rooms(count, feature, OUT_SPLIT, parts=AB_PARTS)
        + sum_rooms(count, height, both, parts=1)
        + [pltpu.SemaphoreType.DMA((3,))]
        + sum_sems(count, AB_PARTS)
        + sum_sems(count, 1),
        compiler_params=kernel_params(ident),
        name="attention_grads",
    )(
        attended, grad_rows, weight, queries, keys_values, level,
        cosine, sine, own_seq, own_order, all_seq, all_order, first, second,
    )


def closing_body(count, normed, joint_grads, attended, grad_rows, lowrank, lowrank_out, stream,
                 gain, grad_middle, small, lowrank_grads, weight, gate_grads, up_grads, down_grads, factors,
                 first, second,
                 in_sum, out_sum, second_sum, first_sum, small_sum, stream_grad, factor_grads,
                 bank, in_bank, factor_bank, second_bank, made, in_terms, out_terms,
                 second_terms, first_terms, small_terms, *scratch):
    me, depth, z, y, c = place(count)
    height, wide = normed.shape
    rank = ADAPTER_RANK
    width = gate_grads.shape[0]
    low = jnp.bfloat16
    rooms = [scratch[4 * i : 4 * i + 4] for i in range(5)]
    weight_sem, grads_sem, factor_sem, made_sem, side_sem = scratch[20:25]
    sems = [scratch[25 + 7 * i : 32 + 7 * i] for i in range(5)]
    greet(count)
    halves = [
        pltpu.make_async_copy(weight.at[pl.ds(i * width, width)], bank, weight_sem.at[i])
        for i in range(wide // width)
    ]
    halves[0].start()
    loads = [
        pltpu.make_async_copy(
            factors.at[pl.ds(me * width, width), pl.ds(0, rank)], factor_bank, factor_sem.at[0]
        ),
        pltpu.make_async_copy(
            second.at[:, pl.ds(PROJECTED_WIDTH + MODEL_WIDTH, wide)], second_bank, factor_sem.at[2]
        ),
    ]
    in_load = pltpu.make_async_copy(first.at[:, pl.ds(0, 3 * rank)], in_bank, factor_sem.at[3])
    first_load = pltpu.make_async_copy(
        first.at[:, pl.ds(4 * rank, 2 * rank)], in_bank.at[:, pl.ds(0, 2 * rank)], factor_sem.at[1]
    )
    side_load = pltpu.make_async_copy(
        factors.at[pl.ds(me * width, width), pl.ds(rank, 2 * rank)],
        bank.at[:, pl.ds(wide, 2 * rank)],
        side_sem,
    )
    for item in [in_load] + loads:
        item.start()
    terms = (in_terms, out_terms, second_terms, first_terms, small_terms)
    parts = CLOSING_PARTS
    plans = [sum_terms(count, parts[i], terms[i], rooms[i], sems[i]) for i in range(5)]
    order = plans[0][0]
    send = [plan[1] for plan in plans]
    pair_step = [plan[2] for plan in plans]
    line_step = [plan[3] for plan in plans]
    last_step = [plan[4] for plan in plans]
    finish = [plan[5] for plan in plans]

    def block_products(i, left, right, at):
        feature, some = terms[i].shape[1:]

        def product(line):
            def inner(n, carry):
                cols = pl.ds(pl.multiple_of(line * 4 * feature, 4 * feature), 4 * feature)
                into = pl.ds(pl.multiple_of(n * 512, 512), 512)
                from_ = pl.ds(pl.multiple_of(at + n * 512, 512), 512)
                value = contract(left[:, cols], right[:, from_], 0, 0).astype(low)
                terms[i][pl.ds(4 * line, 4), :, into] = value.reshape(4, feature, 512)
                return carry

            lax.fori_loop(0, some // 512, inner, 0)
            for pair in (1 - y, y):
                send[i](line, pair)

        for line in order:
            product(line)

    def send_all(i):
        for pair in (1 - y, y):
            for line in order:
                send[i](line, pair)
        for k in range(depth):
            pair_step[i](k)

    def put_second(at, value):
        size = second_terms.shape[1]
        value = value.astype(low)
        start = at
        while start < at + value.shape[0]:
            block, inner = start // size, start % size
            rows = min(size - inner, at + value.shape[0] - start)
            second_terms[block, inner : inner + rows, :] = value[start - at : start - at + rows]
            start += rows

    def half_product(i):
        halves[i].wait()

        def product(n, carry):
            some = pl.ds(pl.multiple_of(n * 256, 256), 256)
            cols = pl.ds(pl.multiple_of(i * width + n * 256, 256), 256)
            value = contract(joint_grads[...], bank[some], 1, 1)
            stream_grad[:, cols] = value + contract(lowrank_grads[...], in_bank[cols], 1, 1)
            return carry

        lax.fori_loop(0, width // 256, product, 0)
        if i + 1 < len(halves):
            halves[i + 1].start()

    block_products(0, normed, joint_grads, 0)
    for k in range(depth):
        pair_step[0](k)
    in_load.wait()
    half_product(0)
    plans[0][7]()
    block_products(1, attended, grad_rows, OUT_SPLIT)
    for k in range(depth):
        pair_step[1](k)
    for i in range(1, len(halves)):
        half_product(i)
    plans[1][7]()
    first_load.start()
    side_load.start()

    rows = stream[...].astype(jnp.float32)
    inverse = lax.rsqrt(jnp.mean(rows * rows, axis=-1, keepdims=True) + EPSILON)
    grad = stream_grad[...]
    unit = rows * inverse
    gain_grad = jnp.sum(grad * unit, axis=0, keepdims=True)
    scaled = grad * gain[...]
    centre = jnp.mean(scaled * unit, axis=-1, keepdims=True)
    stream_grad[...] = grad_middle[...] + inverse * (scaled - unit * centre)
    small_terms[...] = small[...]
    share = wide // count
    for block in range(count):
        small_terms[block, 0:1, :share] = gain_grad[:, block * share : (block + 1) * share]
    send_all(4)

    def bring(i):
        source = (gate_grads, up_grads, down_grads)[i]
        return pltpu.make_async_copy(source, bank.at[:, pl.ds(0, wide)], grads_sem.at[i])

    bring(0).start()
    line_step[0](0)
    value_at = QUERY_WIDTH + HEAD_SIZE
    for at, stop, left, own in (
        (0, QUERY_WIDTH, joint_grads, lowrank[:, :rank]),
        (QUERY_WIDTH, value_at, joint_grads, lowrank[:, rank : 2 * rank]),
        (value_at, PROJECTED_WIDTH, joint_grads, lowrank[:, 2 * rank :]),
    ):
        put_second(at, contract(left[:, at:stop], own, 0, 0))
    put_second(PROJECTED_WIDTH, contract(grad_rows[...], lowrank_out[...], 0, 0))
    for item in loads + [first_load, side_load]:
        item.wait()

    def put_factor(cols):
        return pltpu.make_async_copy(
            made, factor_grads.at[:, pl.ds(cols * rank, rank)], made_sem.at[cols]
        )

    line_step[0](1)
    held = bank.at[:, pl.ds(0, wide)]
    for i in range(2):
        bring(i).wait()
        if i > 0:
            put_factor(i).wait()
        made[...] = contract(held[...], in_bank[:, i * rank : (i + 1) * rank], 1, 0)
        put_factor(i + 1).start()
        value = contract(held[...], bank[:, wide + i * rank : wide + (i + 1) * rank], 0, 0)
        first_terms[:, :, i * rank : (i + 1) * rank] = value.astype(low).reshape(
            count, wide // count, rank
        )
        bring(i + 1).start()
        if i == 0:
            line_step[0](2)
    send_all(3)
    bring(2).wait()
    put_factor(2).wait()
    made[...] = contract(held[...], second_bank[...], 1, 1)
    put_factor(0).start()
    put_second(
        PROJECTED_WIDTH + MODEL_WIDTH, contract(held[...], factor_bank[...], 0, 0)
    )
    send_all(2)
    if parts[3] > 1:
        plans[3][7]()
    line_step[0](3)
    for k in range(depth):
        line_step[1](k)
    last_step[0](in_sum)
    last_step[1](out_sum)
    if parts[2] > 1:
        plans[2][7]()
    for i, total in ((4, small_sum), (3, first_sum), (2, second_sum)):
        for k in range(depth):
            line_step[i](k)
        last_step[i](total)
    for item in finish:
        item()
    put_factor(0).wait()


def closing(count, ident, normed, joint_grads, attended, grad_rows, lowrank, lowrank_out, stream,
            gain, grad_middle, small, lowrank_grads, weight, gate_grads, up_grads, down_grads, factors, first,
            second):
    height, wide = normed.shape
    width = gate_grads.shape[0]
    low, high = jnp.bfloat16, jnp.float32
    rank = ADAPTER_RANK
    inside = pl.BlockSpec(memory_space=pltpu.VMEM)
    anywhere = pl.BlockSpec(memory_space=pl.ANY)
    share = wide // count
    shapes = [
        (share, joint_grads.shape[1], low),
        (share, wide - OUT_SPLIT, low),
        (second.shape[1] // count, rank, low),
        (share, 2 * rank, low),
        (8, 128, high),
    ]
    sem = pltpu.SemaphoreType.DMA
    rooms, sems = [], []
    for (rows, cols, kind), parts in zip(shapes, CLOSING_PARTS):
        rooms += sum_rooms(count, rows, cols, kind, parts)
        sems += sum_sems(count, parts)
    return pl.pallas_call(
        functools.partial(closing_body, count),
        out_shape=[jax.ShapeDtypeStruct((rows, cols), high) for rows, cols, _ in shapes]
        + [
            jax.ShapeDtypeStruct((height, wide), high),
            jax.ShapeDtypeStruct((width, 3 * rank), high),
        ],
        in_specs=[inside] * 11 + [anywhere] * 7,
        out_specs=[inside] * 6 + [anywhere],
        scratch_shapes=[
            pltpu.VMEM((width, weight.shape[1]), low),
            pltpu.VMEM((wide, 3 * rank), low),
            pltpu.VMEM((width, rank), low),
            pltpu.VMEM((rank, wide), low),
            pltpu.VMEM((width, rank), high),
        ]
        + [pltpu.VMEM((count, rows, cols), kind) for rows, cols, kind in shapes]
        + rooms
        + [sem((wide // width,)), sem((3,)), sem((4,)), sem((3,)), sem]
        + sems,
        compiler_params=kernel_params(ident),
        name="closing",
    )(
        normed, joint_grads, attended, grad_rows, lowrank, lowrank_out, stream, gain, grad_middle,
        small, lowrank_grads, weight, gate_grads, up_grads, down_grads, factors, first, second,
    )


def line_order(z):
    near = z < 2
    return [z, z + 1 - 2 * (z % 2), jnp.where(near, 2, 1), jnp.where(near, 3, 0)]


def unit_values(gate, up, grad):
    slope = 0.7978845608028654
    cubic = 0.044715
    square = gate * gate
    curve = jnp.tanh(slope * (gate + cubic * square * gate))
    half = 0.5 * (1.0 + curve)
    turned = gate * half
    rise = half + 0.5 * gate * (1.0 - curve * curve) * slope * (1.0 + 3.0 * cubic * square)
    low = jnp.bfloat16
    return (turned * up).astype(low), (grad * up * rise).astype(low), (grad * turned).astype(low)


def hidden_body(count, parts, own, grads, weights, units, gate_grads, up_grads, rows_out,
                held, bank, coming, done, bank_sem, coming_sem, done_sem, rows_sem, *sems):
    me, depth, z, y, c = place(count)
    height, wide = own.shape
    width = bank.shape[1]
    tile = 512
    lines = line_order(z)
    greet(count)
    pieces, begin, from_line, from_pair, _, arrive, finish = gather_plan(
        count, [even_spans(height, parts)], (own,), (held,), sems
    )
    begin()
    fills = [
        pltpu.make_async_copy(weights.at[i], bank.at[i], bank_sem.at[i]) for i in range(3)
    ]
    for fill in fills:
        fill.start()

    def first_of(line, pair):
        return 4 * line + 2 * pair

    steps = [(line, pair) for line in lines for pair in (y, 1 - y)]

    def fetch(index):
        some = pl.ds(first_of(*steps[index]), 2)
        return pltpu.make_async_copy(
            grads.at[some], coming.at[index % 2], coming_sem.at[index % 2]
        )

    def store(index):
        rows = pl.ds(first_of(*steps[index]) * height, 2 * height)
        slot = index % 2
        return [
            pltpu.make_async_copy(done.at[slot, i], out.at[rows], done_sem.at[slot, i])
            for i, out in enumerate((units, gate_grads, up_grads))
        ]

    def keep_rows(index):
        some = pl.ds(first_of(*steps[index]), 2)
        return pltpu.make_async_copy(held.at[some], rows_out.at[some], rows_sem.at[index])

    def work(index):
        line, pair = steps[index]
        slot = index % 2
        arrive(first_of(line, pair) + 1 - c, index == 0)
        if index == 0:
            fetch(0).start()
            for fill in fills:
                fill.wait()
        if index + 1 < len(steps):
            fetch(index + 1).start()
        fetch(index).wait()
        keep_rows(index).start()
        if index >= 2:
            for item in store(index - 2):
                item.wait()
        some = pl.ds(first_of(line, pair), 2)

        def inner(n, carry):
            cols = pl.ds(pl.multiple_of(n * tile, tile), tile)
            block = held[some].reshape(2 * height, wide)
            gate = contract(block, bank[0, cols], 1, 1)
            up = contract(block, bank[1, cols], 1, 1)
            grad = contract(coming[slot].reshape(2 * height, wide), bank[2, cols], 1, 1)
            for i, value in enumerate(unit_values(gate, up, grad)):
                done[slot, i, :, cols] = value
            return carry

        lax.fori_loop(0, width // tile, inner, 0)
        for item in store(index):
            item.start()

    work(0)
    for k in range(1, depth + 1):
        for piece in pieces:
            if k < depth:
                from_line(k, piece)
            from_pair(k - 1, piece)
        work(2 * k - 1)
        if k < depth:
            work(2 * k)

    for index in (len(steps) - 2, len(steps) - 1):
        for item in store(index):
            item.wait()
    for index in range(len(steps)):
        keep_rows(index).wait()
    finish()


def hidden_units(count, ident, own, grads, weights, parts=2):
    height, wide = own.shape
    width = weights.shape[1]
    low = jnp.bfloat16
    sem = pltpu.SemaphoreType.DMA
    anywhere = pl.BlockSpec(memory_space=pl.ANY)
    acts = jax.ShapeDtypeStruct((count * height, width), low)
    return pl.pallas_call(
        functools.partial(hidden_body, count, parts),
        out_shape=[acts, acts, acts, jax.ShapeDtypeStruct((count, height, wide), low)],
        in_specs=[anywhere] * 3,
        out_specs=[anywhere] * 4,
        scratch_shapes=[
            pltpu.VMEM((count, height, wide), low),
            pltpu.VMEM((3, width, wide), low),
            pltpu.VMEM((2, 2, height, wide), low),
            pltpu.VMEM((2, 3, 2 * height, width), low),
            sem((3,)),
            sem((2,)),
            sem((2, 3)),
            sem((count // 2,)),
        ]
        + gather_sems(count, 1, parts),
        compiler_params=kernel_params(ident),
        name="hidden_units",
    )(own, grads, weights)


def unit_grads_body(count, parts, units, gate_grads, up_grads, weights, rows_all, grads_all,
                    input_sum, output_sum, gate_out, up_out, down_out, gate_far,
                    gate_tail,
                    bank, rows_in, units_in, made, loaded, leaving, core_in, pair_in, line_in,
                    twin_in, bank_sem, rows_sem, fill_sems, units_sem, made_sem, far_send,
                    far_recv, tail_sem, *sems):
    me, depth, z, y, c = place(count)
    height, wide = input_sum.shape
    width = weights.shape[1]
    step = height // parts
    low = jnp.bfloat16
    core, mate = me + 1 - 2 * c, me + 2 - 4 * y
    near = z < 2
    order = [jnp.where(near, 3, 0), jnp.where(near, 0, 3), jnp.where(near, 2, 1),
             jnp.where(near, 1, 2)]
    greet(count, True)

    def fill(source, at):
        return pltpu.make_async_copy(source, bank.at[at], bank_sem.at[at])

    blocks = width // height

    def fill_rows(source, half, at):
        return [
            pltpu.make_async_copy(
                source.at[half * blocks + i],
                bank.at[at, pl.ds(i * height, height)],
                fill_sems.at[at, i],
            )
            for i in range(blocks)
        ]

    first_fills = [fill(weights.at[i], i) for i in range(3)]
    for item in first_fills:
        item.start()
    grad_tail = fill_rows(grads_all, 1, 3)
    steps = [(line, pair) for line in order for pair in (1 - y, y)]

    def fetch(line, pair, slot, sources):
        rows = pl.ds((4 * line + 2 * pair) * height, 2 * height)
        return [
            pltpu.make_async_copy(source.at[rows], rows_in.at[slot, i], rows_sem.at[slot, i])
            for i, source in enumerate(sources)
        ]

    def plan(a):
        def mine(at, rows):
            return loaded.at[a, at, rows]

        def theirs(at, rows):
            return leaving.at[a, jnp.where(at % 2 == y, 1, 0), rows]

        return sum_plan(
            count, parts, mine, theirs, core_in.at[a], pair_in.at[a], line_in.at[a],
            twin_in.at[a], sems[7 * a : 7 * a + 7],
        )

    plans = [plan(a) for a in range(2)]

    def pair_step(a, k):
        plans[a][2](k)

    def line_step(a, k):
        plans[a][3](k)

    def last_step(a, total):
        plans[a][4](total)

    def to_core(a, line, pair):
        plans[a][1](line, pair)

    def core_left(a, line, pair):
        plans[a][6](line, pair)

    def product(a, index):
        line, pair = steps[index]
        slot = index % 2
        sources = (gate_grads, up_grads) if a == 0 else (units,)
        if index == 0:
            for item in fetch(line, pair, slot, sources):
                item.start()
        if index + 1 < len(steps):
            for item in fetch(*steps[index + 1], 1 - slot, sources):
                item.start()
        if index >= 2:
            core_left(a, *steps[index - 2])
        for item in fetch(line, pair, slot, sources):
            item.wait()
        tile = 512

        def inner(n, carry):
            cols = pl.ds(pl.multiple_of(n * tile, tile), tile)
            if a == 0:
                value = contract(rows_in[slot, 0], bank[0, :, cols], 1, 0)
                value += contract(rows_in[slot, 1], bank[1, :, cols], 1, 0)
            else:
                value = contract(rows_in[slot, 0], bank[2, :, cols], 1, 0)
            value = value.astype(low)

            @pl.when(c == 0)
            def _():
                loaded[a, 2 * line + pair, :, cols] = value[:height]
                leaving[a, slot, :, cols] = value[height:]

            @pl.when(c == 1)
            def _():
                loaded[a, 2 * line + pair, :, cols] = value[height:]
                leaving[a, slot, :, cols] = value[:height]

            return carry

        lax.fori_loop(0, wide // tile, inner, 0)
        to_core(a, line, pair)

    def finish_sends(a):
        for index in (len(steps) - 2, len(steps) - 1):
            core_left(a, *steps[index])

    tall = units_in.shape[2]
    each = width // tall

    def bring(g, slot):
        source = (gate_grads, up_grads, units)[g // each]
        cols = pl.ds((g % each) * tall, tall)
        return pltpu.make_async_copy(source.at[:, cols], units_in.at[slot], units_sem.at[slot])

    def put(g, slot):
        rows = pl.ds((g % each) * tall, tall)
        return pltpu.make_async_copy(
            made.at[slot], (gate_out, up_out, down_out)[g // each].at[rows], made_sem.at[slot]
        )

    def put_tail(slot):
        return pltpu.make_async_copy(made.at[slot], gate_tail, tail_sem)

    def swap(g):
        rows = pl.ds(g * tall, tall)
        return pltpu.make_async_remote_copy(
            src_ref=gate_out.at[rows],
            dst_ref=gate_far.at[rows],
            send_sem=far_send.at[g],
            recv_sem=far_recv.at[g],
            device_id={"loop": 1 - lax.axis_index("loop")},
            device_id_type=MESH,
        )

    number = 3 * each

    def weight_product(g):
        slot = g % 2
        if g + 1 < number:
            bring(g + 1, 1 - slot).start()
        bring(g, slot).wait()
        if g >= 2:
            put(g - 2, slot).wait()
            if g - 2 == FAR_TILES:
                put_tail(slot).wait()
            if g - 2 < FAR_TILES:
                swap(g - 2).start()
        at = 0 if g < 2 * each else 2
        tile = 512

        def inner(n, carry):
            cols = pl.ds(pl.multiple_of(n * tile, tile), tile)
            whole = bank[at : at + 2, :, cols].reshape(2 * width, tile)
            made[slot, :, cols] = contract(units_in[slot], whole, 0, 0).astype(low)
            return carry

        lax.fori_loop(0, wide // tile, inner, 0)
        put(g, slot).start()
        if g == FAR_TILES:
            put_tail(slot).start()

    for item in first_fills[:2]:
        item.wait()
    for index in range(8):
        product(0, index)
        if index >= 2 and index % 2 == 0:
            pair_step(0, index // 2 - 1)
    finish_sends(0)
    row_fills = fill_rows(rows_all, 0, 0) + fill_rows(rows_all, 1, 1)
    for item in row_fills:
        item.start()
    for item in grad_tail:
        item.start()
    bring(0, 0).start()
    first_fills[2].wait()
    product(1, 0)
    pair_step(0, 3)
    product(1, 1)
    plans[0][7]()
    for item in row_fills:
        item.wait()
    weight_product(0)
    weight_product(1)
    line_step(0, 0)
    weight_product(2)
    weight_product(3)
    line_step(0, 1)
    for index in range(2, 8):
        product(1, index)
        if index % 2 == 0:
            pair_step(1, index // 2 - 1)
        if index == 6:
            line_step(0, 2)
    finish_sends(1)
    grad_fills = fill_rows(grads_all, 0, 2)
    for item in grad_fills:
        item.start()
    weight_product(4)
    pair_step(1, 3)
    line_step(0, 3)
    weight_product(5)
    plans[1][7]()
    last_step(0, input_sum)
    weight_product(6)
    weight_product(7)
    line_step(1, 0)
    for item in grad_tail + grad_fills:
        item.wait()
    weight_product(8)
    weight_product(9)
    line_step(1, 1)
    weight_product(10)
    weight_product(11)
    line_step(1, 2)
    line_step(1, 3)
    last_step(1, output_sum)

    for g in (number - 2, number - 1):
        put(g, g % 2).wait()
    for g in range(FAR_TILES):
        swap(g).wait()
    for a in range(2):
        plans[a][5](False)


def unit_grads(count, ident, units, gate_grads, up_grads, weights, rows_all, grads_all, parts=2):
    width, wide = weights.shape[1:]
    height = rows_all.shape[1]
    depth = count // 4
    low = jnp.bfloat16
    sem = pltpu.SemaphoreType.DMA
    anywhere = pl.BlockSpec(memory_space=pl.ANY)
    inside = pl.BlockSpec(memory_space=pltpu.VMEM)
    total = jax.ShapeDtypeStruct((height, wide), jnp.float32)

    return pl.pallas_call(
        functools.partial(unit_grads_body, count, parts),
        out_shape=[total, total] + [jax.ShapeDtypeStruct((width, wide), low)] * 3
        + [
            jax.ShapeDtypeStruct((FAR_TILES * 256, wide), low),
            jax.ShapeDtypeStruct((width - FAR_TILES * 256, wide), low),
        ],
        in_specs=[anywhere] * 6,
        out_specs=[inside, inside] + [anywhere] * 5,
        scratch_shapes=[
            pltpu.VMEM((4, width, wide), low),
            pltpu.VMEM((2, 2, 2 * height, width), low),
            pltpu.VMEM((2, count * height, 256), low),
            pltpu.VMEM((2, 256, wide), low),
            pltpu.VMEM((2, 2 * depth, height, wide), low),
            pltpu.VMEM((2, 2, height, wide), low),
            pltpu.VMEM((2, 2 * depth, height, wide), low),
            pltpu.VMEM((2, depth, height, wide), low),
            pltpu.VMEM((2, depth + 1, height, wide), low),
            pltpu.VMEM((2, height // 2, wide), low),
            sem((4,)),
            sem((2, 2)),
            sem((4, width // height)),
            sem((2,)),
            sem((2,)),
            sem((FAR_TILES,)),
            sem((FAR_TILES,)),
            sem,
        ]
        + sum_sems(count, parts)
        + sum_sems(count, parts),
        compiler_params=kernel_params(ident),
        name="unit_grads",
    )(units, gate_grads, up_grads, weights, rows_all, grads_all)


def swap_loops(values):
    return lax.ppermute(values, "loop", [(0, 1), (1, 0)])


def add_body(*refs):
    lefts, rights, out = refs[:3], refs[3:7], refs[7]
    left, right, made, load_sem, made_sem = refs[8:]
    step = made.shape[1]
    each = left.shape[1] // step
    chunks = [(i, n) for i in range(3) for n in range(each)]

    def loads(i, n):
        rows = pl.ds(n * step, step)
        far = rights[i + 1].at[rows] if i else rights[0].at[rows] if n < FAR_TILES else None
        if far is None:
            far = rights[1].at[pl.ds((n - FAR_TILES) * step, step)]
        return [
            pltpu.make_async_copy(lefts[i].at[rows], left.at[i, rows], load_sem.at[i, n, 0]),
            pltpu.make_async_copy(far, right.at[i, rows], load_sem.at[i, n, 1]),
        ]

    def put(at):
        i, n = chunks[at]
        return pltpu.make_async_copy(
            made.at[at % 2], out.at[i, pl.ds(n * step, step)], made_sem.at[at % 2]
        )

    for i, n in chunks:
        for item in loads(i, n):
            item.start()
    for at, (i, n) in enumerate(chunks):
        for item in loads(i, n):
            item.wait()
        if at >= 2:
            put(at - 2).wait()
        rows = pl.ds(n * step, step)
        made[at % 2] = left[i, rows].astype(jnp.float32) + right[i, rows].astype(jnp.float32)
        put(at).start()
    for at in (len(chunks) - 2, len(chunks) - 1):
        put(at).wait()


def add_loops(lefts, rights):
    rows, wide = lefts[0].shape
    step = 256
    anywhere = pl.BlockSpec(memory_space=pl.ANY)
    sem = pltpu.SemaphoreType.DMA
    return pl.pallas_call(
        add_body,
        out_shape=jax.ShapeDtypeStruct((3, rows, wide), jnp.float32),
        in_specs=[anywhere] * 7,
        out_specs=anywhere,
        scratch_shapes=[
            pltpu.VMEM((3, rows, wide), jnp.bfloat16),
            pltpu.VMEM((3, rows, wide), jnp.bfloat16),
            pltpu.VMEM((2, step, wide), jnp.float32),
            sem((3, rows // step, 2)),
            sem((2,)),
        ],
        compiler_params=pltpu.CompilerParams(vmem_limit_bytes=VMEM_LIMIT),
        name="add_loops",
    )(*lefts, *rights)


def per_device(
    layer_input_stream,
    layer_output_gradient,
    attention_in_weight,
    attention_out_weight,
    feedforward_weight,
    layer_norm_gains,
    adapter_first_factors,
    adapter_second_factors,
    adapter_hidden_factors,
    group_sequence_lengths,
    token_per_row,
    token_exit_depth,
):
    loop_count = lax.axis_size("loop")
    count = lax.axis_size("dp")
    local_rows = layer_input_stream.shape[1]
    low = jnp.bfloat16
    key_at = QUERY_WIDTH
    value_at = QUERY_WIDTH + HEAD_SIZE
    down_at = PROJECTED_WIDTH + MODEL_WIDTH
    stream = layer_input_stream[0]
    residual_stream = stream.astype(jnp.float32)
    grad_out = layer_output_gradient[0].astype(jnp.float32)
    adapter_first = adapter_first_factors[0]
    adapter_second = adapter_second_factors[0]
    ffn_weight = jnp.swapaxes(feedforward_weight, 0, 1)

    (
        input_weight, output_weight, ffn_folded, normed_input, lowrank_projection, seq_all,
        order_all, seq_own, order_own, pos_own, active_mask, live_mask, feedforward_gradient,
    ) = opening(
        count, 1, stream, layer_norm_gains[:1], token_per_row, token_exit_depth,
        group_sequence_lengths, layer_output_gradient[0],
        (attention_in_weight, attention_out_weight), (IN_SHARE, OUT_SHARE), ffn_weight,
        adapter_hidden_factors[0], adapter_first, adapter_second,
    )
    live_own = live_mask[:, 0] > 0.5
    half = HEAD_SIZE // 2
    freqs = 10000.0 ** (-jnp.arange(half, dtype=jnp.float32) / half)
    angles = pos_own.astype(jnp.float32) * freqs
    cosine, sine = jnp.cos(angles), jnp.sin(angles)
    facts = (cosine, sine, seq_own, order_own, seq_all, order_all)
    (
        queries, attended_rows, output_projection, level, middle_state, second_normed_input,
        kv_blocks, grad_blocks,
    ) = attention(
        count, 2, normed_input, lowrank_projection, stream, active_mask, layer_norm_gains[1:],
        *facts, input_weight, output_weight, adapter_first, adapter_second, feedforward_gradient,
    )
    units_own, grad_gate_own, grad_up_own, normed_blocks = hidden_units(
        count, 3, second_normed_input, grad_blocks, ffn_folded
    )
    second_normed_gradient, ffn_sum, gate_grad, up_grad, down_grad, gate_other, gate_tail = unit_grads(
        count, 4, units_own, grad_gate_own, grad_up_own, ffn_folded, normed_blocks, grad_blocks
    )
    gate_last = swap_loops(gate_tail)
    up_other = swap_loops(up_grad)
    down_other = swap_loops(down_grad)

    complete_output = middle_state + active_mask * ffn_sum
    confidence = root_mean(residual_stream) / (
        root_mean(residual_stream) + root_mean(complete_output - residual_stream)
    )
    conf_sum = jnp.sum(jnp.where(live_own, confidence, 0.0))
    depth_hits = (
        (token_exit_depth[0][:, None] == jnp.arange(loop_count + 1, dtype=jnp.int32)[None, :])
        & live_own[:, None]
    ).astype(jnp.float32)
    stats = jnp.concatenate([conf_sum[None], jnp.sum(depth_hits, axis=0)])
    grad_middle_part, grad_gain_two = jax.vjp(norm_rows, middle_state, layer_norm_gains[1])[1](
        second_normed_gradient
    )
    grad_middle = grad_out + grad_middle_part
    branch_gradient = (active_mask * grad_middle).astype(low)
    joint_grads, lowrank_grads, out_first = attention_grads(
        count, 5, attended_rows, branch_gradient, output_weight, queries,
        kv_blocks.reshape(count * local_rows, 2 * HEAD_SIZE), level, *facts, adapter_first,
        adapter_second,
    )
    width_own = MODEL_WIDTH // count
    small = jnp.zeros((count, 8, 128), jnp.float32)
    small = small.at[:, 1, :width_own].set(grad_gain_two.reshape(count, width_own))
    small = small.at[:, 2, : loop_count + 2].set(stats[None])
    (
        in_portion, out_last, second_grad, first_grad_hidden, small_sum, hidden_grad,
        adapter_hidden_gradient,
    ) = closing(
        count, 6, normed_input, joint_grads, attended_rows, branch_gradient, lowrank_projection,
        output_projection, stream, layer_norm_gains[:1], grad_middle, small, lowrank_grads,
        input_weight, gate_grad, up_grad, down_grad, adapter_hidden_factors[0], adapter_first,
        adapter_second,
    )
    gate_other, gate_last, up_other, down_other, small_sum = lax.optimization_barrier(
        (gate_other, gate_last, up_other, down_other, small_sum)
    )
    in_low = in_portion.astype(low)
    out_low = jnp.concatenate([out_first, out_last], axis=1).astype(low)
    in_far, out_far, small_far = swap_loops(in_low), swap_loops(out_low), swap_loops(small_sum)
    sum_mlp = add_loops(
        (gate_grad, up_grad, down_grad), (gate_other, gate_last, up_other, down_other)
    )
    adapter_first_gradient = jnp.concatenate(
        [
            outer_columns(in_low[:, :key_at], adapter_second[:, :key_at]),
            outer_columns(in_low[:, key_at:value_at], adapter_second[:, key_at:value_at]),
            outer_columns(in_low[:, value_at:], adapter_second[:, value_at:PROJECTED_WIDTH]),
            outer_columns(out_low, adapter_second[:, PROJECTED_WIDTH:down_at]),
            first_grad_hidden,
        ],
        axis=1,
    )
    in_far, out_far, small_far, sum_mlp, adapter_first_gradient = lax.optimization_barrier(
        (in_far, out_far, small_far, sum_mlp, adapter_first_gradient)
    )
    small_total = small_sum + small_far
    sum_gains = small_total[:2, :width_own]
    depth_total = small_total[2, 1 : loop_count + 2]
    mean_confidence = small_total[2, 0] / jnp.sum(depth_total)
    exit_counts = depth_total.astype(jnp.int32)
    return (
        complete_output.astype(low)[None],
        hidden_grad[None],
        in_low.astype(jnp.float32) + in_far.astype(jnp.float32),
        out_low.astype(jnp.float32) + out_far.astype(jnp.float32),
        jnp.swapaxes(sum_mlp, 0, 1),
        sum_gains,
        adapter_first_gradient[None],
        jnp.swapaxes(second_grad, 0, 1)[None],
        adapter_hidden_gradient[None],
        exit_counts,
        mean_confidence,
    )


def per_device_any(
    layer_input_stream,
    layer_output_gradient,
    attention_in_weight,
    attention_out_weight,
    feedforward_weight,
    layer_norm_gains,
    adapter_first_factors,
    adapter_second_factors,
    adapter_hidden_factors,
    group_sequence_lengths,
    token_per_row,
    token_exit_depth,
):
    current_loop = lax.axis_index("loop")
    dp_index = lax.axis_index("dp")
    loop_count = lax.axis_size("loop")
    local_rows = layer_input_stream.shape[1]
    ffn_rows = feedforward_weight.shape[0]
    scale = HEAD_SIZE ** (-0.5)
    live_all, seq_all, order_all, pos_all = token_facts(token_per_row[0], group_sequence_lengths[0])
    first_row = dp_index * local_rows

    def own_slice(values):
        return lax.dynamic_slice_in_dim(values, first_row, local_rows, 0)

    live_own = own_slice(live_all)
    seq_own = own_slice(seq_all)
    order_own = own_slice(order_all)
    pos_own = own_slice(pos_all)
    active_mask = (live_own & (token_exit_depth[0] > current_loop)).astype(jnp.float32)[:, None]
    residual_stream = layer_input_stream[0].astype(jnp.float32)
    adapter_first = adapter_first_factors[0]
    adapter_second = adapter_second_factors[0]
    adapter_feedforward = adapter_hidden_factors[0]
    ffn_own = lax.dynamic_slice_in_dim(adapter_feedforward, dp_index * ffn_rows, ffn_rows, 0)
    input_weight, output_weight = (
        lax.all_gather(attention_in_weight, "dp", axis=0, tiled=True),
        lax.all_gather(attention_out_weight, "dp", axis=0, tiled=True),
    )
    normed_input = norm_rows(residual_stream, layer_norm_gains[0]).astype(jnp.bfloat16)
    lowrank_projection = matrix_product(normed_input, adapter_first[:, : 3 * ADAPTER_RANK]).astype(
        jnp.bfloat16
    )
    adapter_query_key_value = jnp.concatenate(
        [
            matrix_product(lowrank_projection[:, :ADAPTER_RANK], adapter_second[:, :QUERY_WIDTH]),
            matrix_product(
                lowrank_projection[:, ADAPTER_RANK : 2 * ADAPTER_RANK],
                adapter_second[:, QUERY_WIDTH : QUERY_WIDTH + HEAD_SIZE],
            ),
            matrix_product(
                lowrank_projection[:, 2 * ADAPTER_RANK :],
                adapter_second[:, QUERY_WIDTH + HEAD_SIZE : PROJECTED_WIDTH],
            ),
        ],
        axis=1,
    )
    query_key_value_linear = matrix_product(normed_input, input_weight) + adapter_query_key_value
    queries = rotate(
        query_key_value_linear[:, :QUERY_WIDTH].reshape(local_rows, HEADS, HEAD_SIZE), pos_own
    ).astype(jnp.bfloat16)
    key_rot = rotate(
        query_key_value_linear[:, QUERY_WIDTH : QUERY_WIDTH + HEAD_SIZE].reshape(
            local_rows, 1, HEAD_SIZE
        ),
        pos_own,
    )[:, 0]
    kv_send = jnp.concatenate(
        [key_rot, query_key_value_linear[:, QUERY_WIDTH + HEAD_SIZE :]], axis=1
    ).astype(jnp.bfloat16)
    kv_all = lax.all_gather(kv_send, "dp", axis=0, tiled=True)
    keys = kv_all[:, :HEAD_SIZE]
    values = kv_all[:, HEAD_SIZE:]
    key_total = kv_all.shape[0]
    allowed = ((seq_own[:, None] == seq_all[None, :]) & (order_all[None, :] <= order_own[:, None]))[
        :, None, :
    ]
    query_rows = queries.reshape(local_rows * HEADS, HEAD_SIZE)

    def score_rows():
        raw_scores = (outer_columns(query_rows, keys) * scale).reshape(local_rows, HEADS, key_total)
        return jnp.where(allowed, raw_scores, FLOOR_SCORE)

    scores = score_rows()
    top_score = jnp.max(scores, axis=-1, keepdims=True)
    expo = jnp.exp(scores - top_score)
    mass = jnp.sum(expo, axis=-1, keepdims=True)
    prob_low = (expo / mass).astype(jnp.bfloat16)
    attended_rows = (
        matrix_product(prob_low.reshape(local_rows * HEADS, key_total), values)
        .reshape(local_rows, QUERY_WIDTH)
        .astype(jnp.bfloat16)
    )
    output_projection = matrix_product(
        attended_rows, adapter_first[:, 3 * ADAPTER_RANK : 4 * ADAPTER_RANK]
    ).astype(jnp.bfloat16)
    branch_output = matrix_product(attended_rows, output_weight) + matrix_product(
        output_projection, adapter_second[:, PROJECTED_WIDTH : PROJECTED_WIDTH + MODEL_WIDTH]
    )
    middle_state = residual_stream + active_mask * branch_output
    second_normed_input = norm_rows(middle_state, layer_norm_gains[1]).astype(jnp.bfloat16)
    feedforward_projection = matrix_product(
        second_normed_input, adapter_first[:, 4 * ADAPTER_RANK :]
    ).astype(jnp.bfloat16)
    normed_all, proj_all = (
        lax.all_gather(second_normed_input, "dp", axis=0, tiled=True),
        lax.all_gather(feedforward_projection, "dp", axis=0, tiled=True),
    )
    gate_own = outer_columns(normed_all, feedforward_weight[:, 0, :]) + outer_columns(
        proj_all[:, :ADAPTER_RANK], ffn_own[:, ADAPTER_RANK : 2 * ADAPTER_RANK]
    )
    up_own = outer_columns(normed_all, feedforward_weight[:, 1, :]) + outer_columns(
        proj_all[:, ADAPTER_RANK:], ffn_own[:, 2 * ADAPTER_RANK :]
    )
    units_own = geglu(gate_own, up_own).astype(jnp.bfloat16)
    ffn_sum, low_sum = (
        lax.psum_scatter(
            matrix_product(units_own, feedforward_weight[:, 2, :]),
            "dp",
            scatter_dimension=0,
            tiled=True,
        ),
        lax.psum_scatter(
            matrix_product(units_own, ffn_own[:, :ADAPTER_RANK]),
            "dp",
            scatter_dimension=0,
            tiled=True,
        ),
    )
    down_lowrank = low_sum.astype(jnp.bfloat16)
    complete_output = middle_state + active_mask * (
        ffn_sum + matrix_product(down_lowrank, adapter_second[:, PROJECTED_WIDTH + MODEL_WIDTH :])
    )
    confidence = root_mean(residual_stream) / (
        root_mean(residual_stream) + root_mean(complete_output - residual_stream)
    )
    conf_sum = jnp.sum(jnp.where(live_own, confidence, 0.0))
    depth_hits = (
        (token_exit_depth[0][:, None] == jnp.arange(loop_count + 1, dtype=jnp.int32)[None, :])
        & live_own[:, None]
    ).astype(jnp.float32)
    conf_total, depth_total = lax.psum((conf_sum, jnp.sum(depth_hits, axis=0)), ("loop", "dp"))
    mean_confidence = conf_total / jnp.sum(depth_total)
    exit_counts = depth_total.astype(jnp.int32)
    grad_out = layer_output_gradient[0].astype(jnp.float32)
    feedforward_gradient = (active_mask * grad_out).astype(jnp.bfloat16)
    lowrank_gradient = outer_columns(
        feedforward_gradient, adapter_second[:, PROJECTED_WIDTH + MODEL_WIDTH :]
    ).astype(jnp.bfloat16)
    grad_ffn_all, grad_low_all = (
        lax.all_gather(feedforward_gradient, "dp", axis=0, tiled=True),
        lax.all_gather(lowrank_gradient, "dp", axis=0, tiled=True),
    )
    hidden_unit_gradient = outer_columns(grad_ffn_all, feedforward_weight[:, 2, :]) + outer_columns(
        grad_low_all, ffn_own[:, :ADAPTER_RANK]
    )
    grad_gate_own, grad_up_own = jax.vjp(geglu, gate_own, up_own)[1](hidden_unit_gradient)
    grad_gate_own = grad_gate_own.astype(jnp.bfloat16)
    grad_up_own = grad_up_own.astype(jnp.bfloat16)
    input_terms = matrix_product(grad_gate_own, feedforward_weight[:, 0, :]) + matrix_product(
        grad_up_own, feedforward_weight[:, 1, :]
    )
    proj_terms = jnp.concatenate(
        [
            matrix_product(grad_gate_own, ffn_own[:, ADAPTER_RANK : 2 * ADAPTER_RANK]),
            matrix_product(grad_up_own, ffn_own[:, 2 * ADAPTER_RANK :]),
        ],
        axis=1,
    )
    grad_norm_base, grad_proj = (
        lax.psum_scatter(input_terms, "dp", scatter_dimension=0, tiled=True),
        lax.psum_scatter(proj_terms, "dp", scatter_dimension=0, tiled=True),
    )
    ffn_grad = jnp.concatenate(
        [
            inner_rows(grad_gate_own, normed_all),
            inner_rows(grad_up_own, normed_all),
            inner_rows(units_own, grad_ffn_all),
            inner_rows(units_own, grad_low_all),
            inner_rows(grad_gate_own, proj_all[:, :ADAPTER_RANK]),
            inner_rows(grad_up_own, proj_all[:, ADAPTER_RANK:]),
        ],
        axis=1,
    )
    lowrank_projection_gradient = grad_proj.astype(jnp.bfloat16)
    second_normed_gradient = grad_norm_base + outer_columns(
        lowrank_projection_gradient, adapter_first[:, 4 * ADAPTER_RANK :]
    )
    grad_middle_part, grad_gain_two = jax.vjp(norm_rows, middle_state, layer_norm_gains[1])[1](
        second_normed_gradient
    )
    grad_middle = grad_out + grad_middle_part
    branch_gradient = (active_mask * grad_middle).astype(jnp.bfloat16)
    output_projection_gradient = outer_columns(
        branch_gradient, adapter_second[:, PROJECTED_WIDTH : PROJECTED_WIDTH + MODEL_WIDTH]
    ).astype(jnp.bfloat16)
    grad_attended = (
        outer_columns(branch_gradient, output_weight)
        + outer_columns(
            output_projection_gradient, adapter_first[:, 3 * ADAPTER_RANK : 4 * ADAPTER_RANK]
        )
    ).astype(jnp.bfloat16)
    grad_att_rows = grad_attended.reshape(local_rows * HEADS, HEAD_SIZE)
    prob = jnp.exp(score_rows() - top_score) / mass
    grad_prob = outer_columns(grad_att_rows, values).reshape(local_rows, HEADS, key_total)
    centre = jnp.sum(prob * grad_prob, axis=-1, keepdims=True)
    grad_scores = (
        (prob * (grad_prob - centre)).astype(jnp.bfloat16).reshape(local_rows * HEADS, key_total)
    )
    grad_queries = (matrix_product(grad_scores, keys) * scale).reshape(local_rows, HEADS, HEAD_SIZE)
    prob_again = prob.astype(jnp.bfloat16).reshape(local_rows * HEADS, key_total)
    kv_terms = jnp.concatenate(
        [inner_rows(grad_scores, query_rows) * scale, inner_rows(prob_again, grad_att_rows)], axis=1
    )
    grad_kv = lax.psum_scatter(kv_terms, "dp", scatter_dimension=0, tiled=True)
    query_linear_gradient = (
        rotate_back(grad_queries, pos_own).reshape(local_rows, QUERY_WIDTH).astype(jnp.bfloat16)
    )
    key_linear_gradient = rotate_back(grad_kv[:, None, :HEAD_SIZE], pos_own)[:, 0].astype(
        jnp.bfloat16
    )
    value_linear_gradient = grad_kv[:, HEAD_SIZE:].astype(jnp.bfloat16)
    query_key_value_gradient = jnp.concatenate(
        [query_linear_gradient, key_linear_gradient, value_linear_gradient], axis=1
    )
    attention_projection_gradient = jnp.concatenate(
        [
            outer_columns(query_linear_gradient, adapter_second[:, :QUERY_WIDTH]),
            outer_columns(
                key_linear_gradient, adapter_second[:, QUERY_WIDTH : QUERY_WIDTH + HEAD_SIZE]
            ),
            outer_columns(
                value_linear_gradient, adapter_second[:, QUERY_WIDTH + HEAD_SIZE : PROJECTED_WIDTH]
            ),
        ],
        axis=1,
    ).astype(jnp.bfloat16)
    normed_gradient = outer_columns(query_key_value_gradient, input_weight) + outer_columns(
        attention_projection_gradient, adapter_first[:, : 3 * ADAPTER_RANK]
    )
    grad_resid_part, grad_gain_one = jax.vjp(norm_rows, residual_stream, layer_norm_gains[0])[1](
        normed_gradient
    )
    hidden_grad = grad_middle + grad_resid_part
    grad_w_in = inner_rows(normed_input, query_key_value_gradient)
    grad_w_out = inner_rows(attended_rows, branch_gradient)
    grad_gains = jnp.stack([grad_gain_one, grad_gain_two])
    adapter_first_gradient = jnp.concatenate(
        [
            inner_rows(normed_input, attention_projection_gradient),
            inner_rows(attended_rows, output_projection_gradient),
            inner_rows(second_normed_input, lowrank_projection_gradient),
        ],
        axis=1,
    )
    adapter_second_gradient = jnp.concatenate(
        [
            inner_rows(lowrank_projection[:, :ADAPTER_RANK], query_linear_gradient),
            inner_rows(lowrank_projection[:, ADAPTER_RANK : 2 * ADAPTER_RANK], key_linear_gradient),
            inner_rows(lowrank_projection[:, 2 * ADAPTER_RANK :], value_linear_gradient),
            inner_rows(output_projection, branch_gradient),
            inner_rows(down_lowrank, feedforward_gradient),
        ],
        axis=1,
    )
    input_portion, output_portion, gain_portion, adapter_first_grads, adapter_second_grads = (
        lax.psum_scatter(grad_w_in, "dp", scatter_dimension=0, tiled=True),
        lax.psum_scatter(grad_w_out, "dp", scatter_dimension=0, tiled=True),
        lax.psum_scatter(grad_gains, "dp", scatter_dimension=1, tiled=True),
        lax.psum_scatter(adapter_first_gradient, "dp", scatter_dimension=0, tiled=True),
        lax.psum_scatter(adapter_second_gradient, "dp", scatter_dimension=1, tiled=True),
    )
    mlp_part = ffn_grad[:, : 3 * MODEL_WIDTH].reshape(ffn_rows, 3, MODEL_WIDTH)
    sum_in, sum_out, sum_gains, sum_mlp = (
        lax.psum(input_portion.astype(jnp.bfloat16), "loop").astype(jnp.float32),
        lax.psum(output_portion.astype(jnp.bfloat16), "loop").astype(jnp.float32),
        lax.psum(gain_portion.astype(jnp.bfloat16), "loop").astype(jnp.float32),
        lax.psum(mlp_part.astype(jnp.bfloat16), "loop").astype(jnp.float32),
    )
    return (
        complete_output.astype(jnp.bfloat16)[None],
        hidden_grad[None],
        sum_in,
        sum_out,
        sum_mlp,
        sum_gains,
        adapter_first_grads[None],
        adapter_second_grads[None],
        ffn_grad[:, 3 * MODEL_WIDTH :][None],
        exit_counts,
        mean_confidence,
    )


def solution(mesh):
    return jax.shard_map(
        per_device if mesh.shape == {"loop": 2, "dp": LINE_DEVICES} else per_device_any,
        mesh=mesh,
        in_specs=(
            P("loop", "dp", None),
            P("loop", "dp", None),
            P("dp", None),
            P("dp", None),
            P("dp", None, None),
            P(),
            P("loop", None, None),
            P("loop", None, None),
            P("loop", None, None),
            P("loop", None),
            P("loop", None),
            P("loop", "dp"),
        ),
        out_specs=(
            P("loop", "dp", None),
            P("loop", "dp", None),
            P("dp", None),
            P("dp", None),
            P("dp", None, None),
            P(None, "dp"),
            P("loop", "dp", None),
            P("loop", None, "dp"),
            P("loop", "dp", None),
            P(),
            P(),
        ),
        check_vma=False,
    )
```
